32 devices in a mesh: gx: 8 (over y, x, core), gy: 4 (over z).
Axes of the slice: x: 2, y: 2, z: 4, core: 2. Of those that a mesh axis runs over, the one named last changes fastest.
Arguments:
- solution: float32 [8, 4, 8, 8, 8, 128], P('gx', 'gy'), as said below
- residual: float32 [8, 4, 8, 8, 8, 128], P('gx', 'gy'), as said below
- grain_counts: int32 [8, 4, 128], P('gx', 'gy'), may hold values from 0 to 16
Outputs:
- solution_out: float32 [8, 4, 8, 8, 8, 128], P('gx', 'gy')
- residual_out: float32 [8, 4, 8, 8, 8, 128], P('gx', 'gy')
- direction_out: float32 [8, 4, 8, 8, 8, 128], P('gx', 'gy')
- step_sizes: float32 [2], replicated
The draws below stay inside these ranges and needn't reach their ends.
Inputs may be any that keep to these rules, and one draw needn't show every extreme that they name: `solution`: every node shared by neighbouring elements holds the same value in all of its copies. `residual`: every node shared by neighbouring elements holds the same value in all of its copies.
All inputs are finite; a program needn't handle non-finite values.
Results may differ from the reference program's by a relative error of at most 0.003.
Values sent between devices are 32-bit elements; how exact they have to be, the bound alone decides.
No kernel may reach another device: no remote copies, remote signals or barrier semaphores. Data moves between devices by JAX's collectives and lax.ppermute only.
A program may use at most 64 MiB of HBM per device.

```python
import math
import jax
import jax.numpy as jnp
import numpy as np
from jax import lax

NODES = 8
EZ = 128
MOST_GRAINS = 16
ITERS = 2
NXE = 8
NYE = 4


def continuous_field(key):
    span = NODES - 1
    grid_shape = (span * NXE + 1, span * NYE + 1, span * EZ + 1)
    grid = jax.random.normal(key, grid_shape, jnp.float32)
    along_first = jnp.stack([grid[offset:offset + span * NXE:span] for offset in range(NODES)], axis=1)
    along_second = jnp.stack([along_first[:, :, offset:offset + span * NYE:span] for offset in range(NODES)], axis=3)
    along_third = jnp.stack([along_second[..., offset:offset + span * EZ:span] for offset in range(NODES)], axis=5)
    return jnp.transpose(along_third, (0, 2, 1, 3, 5, 4))


def draw_solution(key, part):
    return continuous_field(jax.random.fold_in(key, 11))


def draw_residual(key, part):
    return continuous_field(jax.random.fold_in(key, 23))


def touch_ends(values, key, smallest, high):
    index_at = [jax.random.randint(jax.random.fold_in(key, axis), (), 0, length) for axis, length in enumerate(values.shape)]
    widest = values.shape.index(max(values.shape))
    next_to = index_at[:widest] + [(index_at[widest] + 1) % values.shape[widest]] + index_at[widest + 1:]
    return values.at[tuple(index_at)].set(smallest).at[tuple(next_to)].set(high)


def setup_inputs(seed: int = 0) -> dict:
    seeds = jax.random.split(jax.random.key(seed), 4)
    return {
        "solution": draw_solution(jax.random.fold_in(seeds[3], 71), 0),
        "residual": draw_residual(jax.random.fold_in(seeds[3], 71), 0),
        "grain_counts": touch_ends(jax.random.randint(seeds[2], (NXE, NYE, EZ), 0, MOST_GRAINS + 1), jax.random.fold_in(seeds[2], 1), 0, MOST_GRAINS).astype(jnp.int32),
    }


shift_mass = 0.1
mean_porosity = 0.7
exact_mode = lax.Precision.HIGHEST

def legendre_columns(node_set, degree):
    table = [node_set * 0.0 + 1.0, node_set]
    for order in range(2, degree + 1):
        table.append(((2 * order - 1) * node_set * table[order - 1] - (order - 1) * table[order - 2]) / order)
    return table

def gll_tables():
    degree = NODES - 1
    node_set = np.cos(math.pi * np.arange(degree + 1) / degree)
    for sweep in range(100):
        table = legendre_columns(node_set, degree)
        node_set = node_set - (node_set * table[degree] - table[degree - 1]) / ((degree + 1) * table[degree])
    node_set = node_set[::-1].copy()
    values = legendre_columns(node_set, degree)[degree]
    weights = 2.0 / (degree * (degree + 1) * values ** 2)
    derivative = np.zeros((NODES, NODES))
    for row_index in range(NODES):
        for column_index in range(NODES):
            if row_index != column_index:
                derivative[row_index, column_index] = values[row_index] / (values[column_index] * (node_set[row_index] - node_set[column_index]))
    derivative[0, 0] = -degree * (degree + 1) / 4.0
    derivative[NODES - 1, NODES - 1] = degree * (degree + 1) / 4.0
    return (weights, derivative)

def jacobi_eigen(matrix):
    size_now = matrix.shape[0]
    current = matrix.copy()
    vectors = np.eye(size_now)
    for sweep in range(12):
        for first in range(size_now - 1):
            for second in range(first + 1, size_now):
                off_value = current[first, second]
                safe_value = np.where(off_value == 0.0, 1e-300, off_value)
                theta = (current[second, second] - current[first, first]) / (2.0 * safe_value)
                sign_value = np.where(theta >= 0.0, 1.0, -1.0)
                tangent = sign_value / (np.abs(theta) + np.sqrt(theta * theta + 1.0))
                cosine = 1.0 / np.sqrt(tangent * tangent + 1.0)
                sine = tangent * cosine
                rotation = np.eye(size_now)
                rotation[first, first] = cosine
                rotation[second, second] = cosine
                rotation[first, second] = sine
                rotation[second, first] = -sine
                current = rotation.T @ current @ rotation
                vectors = vectors @ rotation
    eigen_values = np.array([current[index, index] for index in range(size_now)])
    return (eigen_values, vectors)

def schwarz_tables():
    weights, derivative = gll_tables()
    stiffness = derivative.T @ (weights[:, None] * derivative)
    total_nodes = 3 * (NODES - 1) + 1
    three_stiffness = np.zeros((total_nodes, total_nodes))
    three_mass = np.zeros(total_nodes)
    for element in range(3):
        start_node = element * (NODES - 1)
        three_stiffness[start_node:start_node + NODES, start_node:start_node + NODES] += stiffness
        three_mass[start_node:start_node + NODES] += weights
    chosen = np.array([NODES - 2] + list(range(NODES - 1, 2 * NODES - 1)) + [2 * NODES - 1])
    local_stiffness = three_stiffness[chosen][:, chosen]
    local_mass = three_mass[chosen]
    scaling = 1.0 / np.sqrt(local_mass)
    symmetric = scaling[:, None] * local_stiffness * scaling[None, :]
    symmetric = 0.5 * (symmetric + symmetric.T)
    eigen_values, eigen_vectors = jacobi_eigen(symmetric)
    return (scaling[:, None] * eigen_vectors, eigen_values)

def cosine_basis(column_count):
    position = jnp.arange(column_count, dtype=jnp.float32)
    phase_table = math.pi * (position[:, None] + 0.5) * position[None, :] / column_count
    norm_factor = jnp.where(position == 0, math.sqrt(1.0 / column_count), math.sqrt(2.0 / column_count))
    eigen_basis = jnp.cos(phase_table) * norm_factor[None, :]
    eigen_values = 2.0 - 2.0 * jnp.cos(math.pi * position / column_count)
    return (eigen_basis, eigen_values)

def coarse_solve(coarse_source, column_length):
    basis_first, eigen_first = cosine_basis(coarse_source.shape[0])
    basis_second, eigen_second = cosine_basis(coarse_source.shape[1])
    spectrum = jnp.einsum('pa,pq,qb->ab', basis_first, coarse_source, basis_second, precision=exact_mode)
    divisor = 2.0 * mean_porosity * column_length * (eigen_first[:, None] + eigen_second[None, :]) + 8.0 * shift_mass * column_length
    return jnp.einsum('pa,ab,qb->pq', basis_first, spectrum / divisor, basis_second, precision=exact_mode)

def share_weights(column_count, points):
    column = jnp.arange(column_count)
    identity = (column[:, None] == column[None, :]).astype(jnp.float32)
    left_side = (column[None, :] == column[:, None] - 1).astype(jnp.float32)
    right_side = (column[None, :] == column[:, None] + 1).astype(jnp.float32)
    has_left = (column > 0).astype(jnp.float32)
    has_right = (column < column_count - 1).astype(jnp.float32)
    lowest = identity * (1.0 - 0.5 * has_left[:, None]) + 0.5 * left_side
    highest = identity * (1.0 - 0.5 * has_right[:, None]) + 0.5 * right_side
    table = jnp.broadcast_to(identity[:, None, :], (column_count, points, column_count))
    return table.at[:, 0, :].set(lowest).at[:, points - 1, :].set(highest)

def multiplicity_inverse(column_count, points):
    column = jnp.arange(column_count)[:, None]
    node_index = jnp.arange(points)[None, :]
    shared = (node_index == 0) & (column > 0) | (node_index == points - 1) & (column < column_count - 1)
    return 1.0 / (1.0 + shared.astype(jnp.float32))

def shift_elements(layers, element_axis, toward):
    extent = layers.shape[element_axis]
    widths = [(0, 0)] * layers.ndim
    if toward > 0:
        retained = lax.slice_in_dim(layers, 0, extent - 1, axis=element_axis)
        widths[element_axis] = (1, 0)
    else:
        retained = lax.slice_in_dim(layers, 1, extent, axis=element_axis)
        widths[element_axis] = (0, 1)
    return jnp.pad(retained, widths)

def extend(nodal_field, node_axis, element_axis):
    points = nodal_field.shape[node_axis]
    lower_layer = shift_elements(lax.slice_in_dim(nodal_field, points - 2, points - 1, axis=node_axis), element_axis, 1)
    upper_layer = shift_elements(lax.slice_in_dim(nodal_field, 1, 2, axis=node_axis), element_axis, -1)
    return jnp.concatenate([lower_layer, nodal_field, upper_layer], axis=node_axis)

def spread(extended, node_axis, element_axis):
    points = extended.shape[node_axis] - 2
    own_part = lax.slice_in_dim(extended, 1, points + 1, axis=node_axis)
    lower_layer = shift_elements(lax.slice_in_dim(extended, points, points + 2, axis=node_axis), element_axis, 1)
    upper_layer = shift_elements(lax.slice_in_dim(extended, 0, 2, axis=node_axis), element_axis, -1)
    lower_widths = [(0, 0)] * extended.ndim
    lower_widths[node_axis] = (0, points - 2)
    upper_widths = [(0, 0)] * extended.ndim
    upper_widths[node_axis] = (points - 2, 0)
    return own_part + jnp.pad(lower_layer, lower_widths) + jnp.pad(upper_layer, upper_widths)

def schwarz_solve(extended, eigen_basis, eigen_values):
    first_pass = jnp.einsum('ia,...ijke->...ajke', eigen_basis, extended, precision=exact_mode)
    second_pass = jnp.einsum('jb,...ajke->...abke', eigen_basis, first_pass, precision=exact_mode)
    third_pass = jnp.einsum('kc,...abke->...abce', eigen_basis, second_pass, precision=exact_mode)
    divisor = mean_porosity * (eigen_values[:, None, None] + eigen_values[None, :, None] + eigen_values[None, None, :]) + shift_mass
    scaled = third_pass / divisor[..., None]
    back_first = jnp.einsum('ia,...abce->...ibce', eigen_basis, scaled, precision=exact_mode)
    back_second = jnp.einsum('jb,...ibce->...ijce', eigen_basis, back_first, precision=exact_mode)
    return jnp.einsum('kc,...ijce->...ijke', eigen_basis, back_second, precision=exact_mode)

def apply_local(nodal_field, coupling, derivative, weights_cube):
    grad_first = jnp.einsum('ai,...ijke->...ajke', derivative, nodal_field, precision=exact_mode)
    flux_first = jnp.einsum('ai,...ajke->...ijke', derivative, coupling * grad_first, precision=exact_mode)
    grad_second = jnp.einsum('bj,...ijke->...ibke', derivative, nodal_field, precision=exact_mode)
    flux_second = jnp.einsum('bj,...ibke->...ijke', derivative, coupling * grad_second, precision=exact_mode)
    grad_third = jnp.einsum('ck,...ijke->...ijce', derivative, nodal_field, precision=exact_mode)
    flux_third = jnp.einsum('ck,...ijce->...ijke', derivative, coupling * grad_third, precision=exact_mode)
    return flux_first + flux_second + flux_third + shift_mass * weights_cube[..., None] * nodal_field

def assemble_z(nodal_field):
    points = nodal_field.shape[-2]
    shared = nodal_field[..., points - 1, :-1] + nodal_field[..., 0, 1:]
    return nodal_field.at[..., points - 1, :-1].set(shared).at[..., 0, 1:].set(shared)

def assemble(nodal_field):
    points = nodal_field.shape[2]
    shared = nodal_field[:-1, :, points - 1] + nodal_field[1:, :, 0]
    nodal_field = nodal_field.at[:-1, :, points - 1].set(shared).at[1:, :, 0].set(shared)
    shared = nodal_field[:, :-1, :, points - 1] + nodal_field[:, 1:, :, 0]
    nodal_field = nodal_field.at[:, :-1, :, points - 1].set(shared).at[:, 1:, :, 0].set(shared)
    return assemble_z(nodal_field)

def reference(solution, residual, grain_counts):
    weights_np, derivative_np = gll_tables()
    weights = jnp.asarray(weights_np, dtype=jnp.float32)
    derivative = jnp.asarray(derivative_np, dtype=jnp.float32)
    weights_cube = weights[:, None, None] * weights[None, :, None] * weights[None, None, :]
    basis_np, eigen_np = schwarz_tables()
    eigen_basis = jnp.asarray(basis_np, dtype=jnp.float32)
    eigen_values = jnp.asarray(eigen_np, dtype=jnp.float32)
    porosity = 1.0 - 0.6 * grain_counts.astype(jnp.float32) / MOST_GRAINS
    coupling = weights_cube[None, None, :, :, :, None] * porosity[:, :, None, None, None, :]
    inverse_first = multiplicity_inverse(NXE, NODES)
    inverse_second = multiplicity_inverse(NYE, NODES)
    inverse_third = multiplicity_inverse(EZ, NODES).T
    inverse_all = inverse_first[:, None, :, None, None, None] * inverse_second[None, :, None, :, None, None] * inverse_third[None, None, None, None, :, :]
    share_first = share_weights(NXE, NODES)
    share_second = share_weights(NYE, NODES)

    def precondition(residual_now):
        extended = extend(extend(extend(residual_now, 2, 0), 3, 1), 4, 5)
        local_solution = schwarz_solve(extended, eigen_basis, eigen_values)
        schwarz_part = spread(spread(spread(local_solution, 2, 0), 3, 1), 4, 5)
        columns = lax.optimization_barrier(jnp.sum(inverse_all * residual_now, axis=(4, 5)))
        coarse_source = jnp.einsum('xyij,xia,yjb->ab', columns, share_first, share_second, precision=exact_mode)
        coarse_field = coarse_solve(coarse_source, EZ)
        lifted = jnp.einsum('xia,ab,yjb->xyij', share_first, coarse_field, share_second, precision=exact_mode)
        return schwarz_part + lifted[..., None, None]
    direction = residual
    previous_inner = jnp.float32(1.0)
    step_list = []
    for step_index in range(ITERS):
        preconditioned = precondition(residual)
        precond_inner = jnp.sum(inverse_all * residual * preconditioned)
        if step_index == 0:
            direction = preconditioned
        else:
            direction = preconditioned + precond_inner / previous_inner * direction
        image = assemble(apply_local(direction, coupling, derivative, weights_cube))
        step_size = precond_inner / jnp.sum(inverse_all * direction * image)
        solution = solution + step_size * direction
        residual = residual - step_size * image
        previous_inner = precond_inner
        step_list.append(step_size)
    return (solution, residual, direction, jnp.stack(step_list))
```

```python
import math

import jax
import jax.numpy as jnp
import numpy as np
from jax import lax
from jax.experimental import pallas as pl
from jax.experimental.pallas import tpu as pltpu
from jax.sharding import PartitionSpec as P

NODES = 8
MOST_GRAINS = 16
EXT = NODES + 2
ROWS = 112
MODES = 104
AXES = ("gx", "gy")

shift_mass = 0.1
mean_porosity = 0.7
exact_mode = lax.Precision.HIGHEST


def legendre_columns(node_set, degree):
    table = [node_set * 0.0 + 1.0, node_set]
    for order in range(2, degree + 1):
        table.append(
            ((2 * order - 1) * node_set * table[order - 1] - (order - 1) * table[order - 2]) / order
        )
    return table


def gll_tables():
    degree = NODES - 1
    node_set = np.cos(math.pi * np.arange(degree + 1) / degree)
    for sweep in range(100):
        table = legendre_columns(node_set, degree)
        node_set = node_set - (node_set * table[degree] - table[degree - 1]) / (
            (degree + 1) * table[degree]
        )
    node_set = node_set[::-1].copy()
    values = legendre_columns(node_set, degree)[degree]
    weights = 2.0 / (degree * (degree + 1) * values**2)
    derivative = np.zeros((NODES, NODES))
    for row_index in range(NODES):
        for column_index in range(NODES):
            if row_index != column_index:
                derivative[row_index, column_index] = values[row_index] / (
                    values[column_index] * (node_set[row_index] - node_set[column_index])
                )
    derivative[0, 0] = -degree * (degree + 1) / 4.0
    derivative[NODES - 1, NODES - 1] = degree * (degree + 1) / 4.0
    return (weights, derivative)


def jacobi_eigen(matrix):
    size_now = matrix.shape[0]
    current = matrix.copy()
    vectors = np.eye(size_now)
    for sweep in range(12):
        for first in range(size_now - 1):
            for second in range(first + 1, size_now):
                off_value = current[first, second]
                safe_value = np.where(off_value == 0.0, 1e-300, off_value)
                theta = (current[second, second] - current[first, first]) / (2.0 * safe_value)
                sign_value = np.where(theta >= 0.0, 1.0, -1.0)
                tangent = sign_value / (np.abs(theta) + np.sqrt(theta * theta + 1.0))
                cosine = 1.0 / np.sqrt(tangent * tangent + 1.0)
                sine = tangent * cosine
                rotation = np.eye(size_now)
                rotation[first, first] = cosine
                rotation[second, second] = cosine
                rotation[first, second] = sine
                rotation[second, first] = -sine
                current = rotation.T @ current @ rotation
                vectors = vectors @ rotation
    eigen_values = np.array([current[index, index] for index in range(size_now)])
    return (eigen_values, vectors)


def schwarz_tables():
    weights, derivative = gll_tables()
    stiffness = derivative.T @ (weights[:, None] * derivative)
    total_nodes = 3 * (NODES - 1) + 1
    three_stiffness = np.zeros((total_nodes, total_nodes))
    three_mass = np.zeros(total_nodes)
    for element in range(3):
        start_node = element * (NODES - 1)
        three_stiffness[
            start_node : start_node + NODES, start_node : start_node + NODES
        ] += stiffness
        three_mass[start_node : start_node + NODES] += weights
    chosen = np.array([NODES - 2] + list(range(NODES - 1, 2 * NODES - 1)) + [2 * NODES - 1])
    local_stiffness = three_stiffness[chosen][:, chosen]
    local_mass = three_mass[chosen]
    scaling = 1.0 / np.sqrt(local_mass)
    symmetric = scaling[:, None] * local_stiffness * scaling[None, :]
    symmetric = 0.5 * (symmetric + symmetric.T)
    eigen_values, eigen_vectors = jacobi_eigen(symmetric)
    return (scaling[:, None] * eigen_vectors, eigen_values)


WEIGHTS, DERIVATIVE = gll_tables()
STIFF = DERIVATIVE.T @ (WEIGHTS[:, None] * DERIVATIVE)
BASIS, EIGEN = schwarz_tables()


def plane_tables():
    forward = np.zeros((MODES, ROWS))
    inverse = np.zeros((MODES, EXT))
    for mode_b in range(EXT):
        for mode_c in range(EXT):
            mode = mode_b * EXT + mode_c
            for b in range(EXT):
                for k in range(NODES):
                    forward[mode, b * NODES + k] = BASIS[b, mode_b] * BASIS[k + 1, mode_c]
                forward[mode, 80 + b] = BASIS[b, mode_b] * BASIS[0, mode_c]
                forward[mode, 96 + b] = BASIS[b, mode_b] * BASIS[EXT - 1, mode_c]
            inverse[mode] = 1.0 / (
                mean_porosity * (EIGEN + EIGEN[mode_b] + EIGEN[mode_c]) + shift_mass
            )
    lanes = np.repeat(inverse.T[:, :, None], 128, axis=2)
    return (
        forward.astype(np.float32),
        forward.T.astype(np.float32).copy(),
        lanes.astype(np.float32),
    )


def tile_tables():
    table = np.zeros((NODES + 1, NODES, 128))
    table[0] = WEIGHTS[:, None]
    for shift in range(NODES):
        for k in range(NODES):
            table[1 + shift, k] = STIFF[k, (k - shift) % NODES]
    return table.astype(np.float32)


def share_table(count):
    table = np.zeros((count, 3, count))
    for column in range(count):
        table[column, :, column] = 1.0
        if column > 0:
            table[column, 0, column] = 0.5
            table[column, 0, column - 1] = 0.5
        if column < count - 1:
            table[column, 2, column] = 0.5
            table[column, 2, column + 1] = 0.5
    return table


def cosine_inverse(count):
    position = np.arange(count)
    basis = np.cos(math.pi * (position[:, None] + 0.5) * position[None, :] / count)
    basis = basis * np.where(position == 0, math.sqrt(1.0 / count), math.sqrt(2.0 / count))[None, :]
    return basis, 2.0 - 2.0 * np.cos(math.pi * position / count)


def side_even(axis):
    return lax.rem(lax.axis_index(axis), 2) == 0


def shift_up(rows):
    lane = lax.broadcasted_iota(jnp.int32, rows.shape, 1)
    return jnp.where(lane == 0, 0.0, pltpu.roll(rows, 1, 1))


def shift_down(rows):
    lane = lax.broadcasted_iota(jnp.int32, rows.shape, 1)
    return jnp.where(lane == 127, 0.0, pltpu.roll(rows, 127, 1))


class Sides:
    def __init__(self, axis, count):
        index = lax.axis_index(axis)
        self.even = lax.rem(index, 2) == 0
        self.no_low = index == 0
        self.no_high = index == count - 1

    def low(self, first, second):
        return jnp.where(self.no_low, 0.0, jnp.where(self.even, second, first))

    def high(self, first, second):
        return jnp.where(self.no_high, 0.0, jnp.where(self.even, first, second))

    def send_first(self, low_face, high_face):
        return jnp.where(self.even, high_face, low_face)

    def send_second(self, low_face, high_face):
        return jnp.where(self.even, low_face, high_face)


def multiplicity_tile():
    row = lax.broadcasted_iota(jnp.int32, (NODES, 128), 0)
    lane = lax.broadcasted_iota(jnp.int32, (NODES, 128), 1)
    shared = ((row == 0) & (lane > 0)) | ((row == NODES - 1) & (lane < 127))
    return jnp.where(shared, 0.5, 1.0)


def class_of(node):
    return 0 if node == 0 else (2 if node == NODES - 1 else 1)


def axis_factor(node, side):
    if node == 0:
        return jnp.where(side.no_low, 1.0, 0.5)
    if node == NODES - 1:
        return jnp.where(side.no_high, 1.0, 0.5)
    return None


def scaled(value, *factors):
    for factor in factors:
        if factor is not None:
            value = value * factor
    return value


def add_to(total, key, value):
    total[key] = value if key not in total else total[key] + value


def stats_row(tiles):
    columns = jnp.concatenate([jnp.sum(tile, axis=0, keepdims=True) for tile in tiles], axis=0)
    pad = 16 - len(tiles)
    columns = jnp.concatenate([columns, jnp.zeros((pad, 128), jnp.float32)], axis=0)
    sums = jnp.sum(columns, axis=1, keepdims=True)
    row = lax.broadcasted_iota(jnp.int32, (16, 128), 0)
    lane = lax.broadcasted_iota(jnp.int32, (16, 128), 1)
    return jnp.sum(jnp.where(row == lane, sums, 0.0), axis=0, keepdims=True)


def class_tiles(sums):
    return [sums[(i, j)] for i in range(3) for j in range(3)]


def start_kernel(counts, r_ref, sy_first, sy_second, stats_ref):
    side_x, side_y = Sides("gx", counts[0]), Sides("gy", counts[1])
    tile = multiplicity_tile()
    for a in range(NODES):
        low, high = r_ref[a, 1], r_ref[a, NODES - 2]
        sy_first[a] = side_y.send_first(low, high)
        sy_second[a] = side_y.send_second(low, high)
    sums = {}
    for a in range(NODES):
        for b in range(NODES):
            add_to(sums, (class_of(a), class_of(b)), r_ref[a, b])
    for (i, j), value in sums.items():
        a, b = (0, 1, NODES - 1)[i], (0, 1, NODES - 1)[j]
        sums[(i, j)] = scaled(value * tile, axis_factor(a, side_x), axis_factor(b, side_y))
    stats_ref[...] = stats_row(class_tiles(sums))


def planes(ref):
    return jnp.concatenate([ref[a] for a in range(EXT)], axis=1)


def local_solve(x_ref, h_ref, forward_ref, back_ref, inverse_ref, part_ref):
    zero = jnp.zeros((6, 128), jnp.float32)
    for a in range(EXT):
        x_ref[a, 80:90] = shift_up(x_ref[a, pl.ds(6, EXT, stride=NODES), :])
        x_ref[a, 96:106] = shift_down(x_ref[a, pl.ds(1, EXT, stride=NODES), :])
        x_ref[a, 90:96] = zero
        x_ref[a, 106:112] = zero
    spectrum = jnp.dot(
        forward_ref[...], planes(x_ref), precision=exact_mode, preferred_element_type=jnp.float32
    )
    for a in range(EXT):
        h_ref[a] = spectrum[:, a * 128 : (a + 1) * 128]
    for block in range(MODES // 8):
        rows = pl.ds(block * 8, 8)
        values = [h_ref[a, rows] for a in range(EXT)]
        modes = []
        for mode in range(EXT):
            total = values[0] * float(BASIS[0, mode])
            for a in range(1, EXT):
                total = total + values[a] * float(BASIS[a, mode])
            modes.append(total * inverse_ref[mode, rows])
        for a in range(EXT):
            total = modes[0] * float(BASIS[a, 0])
            for mode in range(1, EXT):
                total = total + modes[mode] * float(BASIS[a, mode])
            h_ref[a, rows] = total
    values = jnp.dot(
        back_ref[...], planes(h_ref), precision=exact_mode, preferred_element_type=jnp.float32
    )
    for a in range(EXT):
        part_ref[a] = values[:, a * 128 : (a + 1) * 128]
    for a in range(EXT):

        def layer(k):
            return (a, pl.ds(k, EXT, stride=NODES), slice(None))

        bottom, top = part_ref[layer(0)], part_ref[layer(NODES - 1)]
        part_ref[layer(0)] = bottom + shift_up(top)
        part_ref[layer(NODES - 1)] = top + shift_down(bottom)
        part_ref[layer(1)] = part_ref[layer(1)] + shift_up(part_ref[a, 96:106])
        part_ref[layer(NODES - 2)] = part_ref[layer(NODES - 2)] + shift_down(part_ref[a, 80:90])


def send_parts(part_ref, side_x, side_y, sy_first, sy_second, fx_first, fx_second):
    for a in range(EXT):
        low, high = part_ref[a, 0:16], part_ref[a, 64:80]
        sy_first[a] = side_y.send_first(low, high).reshape(2, NODES, 128)
        sy_second[a] = side_y.send_second(low, high).reshape(2, NODES, 128)
    for layer in range(2):
        low, high = part_ref[layer, 0:80], part_ref[NODES + layer, 0:80]
        fx_first[layer] = side_x.send_first(low, high).reshape(EXT, NODES, 128)
        fx_second[layer] = side_x.send_second(low, high).reshape(EXT, NODES, 128)


def first_solve_kernel(
    counts, r_ref, ry_first, ry_second, rx_first, rx_second, forward_ref, back_ref, inverse_ref,
    part_ref, sy_first, sy_second, fx_first, fx_second, x_ref, h_ref,
):
    side_x, side_y = Sides("gx", counts[0]), Sides("gy", counts[1])
    x_ref[0, 0:80] = side_x.low(rx_first[...], rx_second[...]).reshape(80, 128)
    x_ref[EXT - 1, 0:80] = side_x.high(rx_first[...], rx_second[...]).reshape(80, 128)
    for a in range(NODES):
        x_ref[a + 1, 0:8] = side_y.low(ry_first[a], ry_second[a])
        x_ref[a + 1, 8:72] = r_ref[a].reshape(64, 128)
        x_ref[a + 1, 72:80] = side_y.high(ry_first[a], ry_second[a])
    local_solve(x_ref, h_ref, forward_ref, back_ref, inverse_ref, part_ref)
    send_parts(part_ref, side_x, side_y, sy_first, sy_second, fx_first, fx_second)


def second_solve_kernel(
    counts, u_ref, ry_first, ry_second, rx_first, rx_second, forward_ref, back_ref, inverse_ref,
    q_ref, part_ref, sy_first, sy_second, fx_first, fx_second, x_ref, h_ref,
):
    side_x, side_y = Sides("gx", counts[0]), Sides("gy", counts[1])
    low_x = side_x.low(rx_first[...], rx_second[...])
    high_x = side_x.high(rx_first[...], rx_second[...])
    x_ref[0, 0:80] = low_x[0].reshape(80, 128)
    x_ref[EXT - 1, 0:80] = high_x[1].reshape(80, 128)
    for a in range(NODES):
        low_y = side_y.low(ry_first[a], ry_second[a])
        high_y = side_y.high(ry_first[a], ry_second[a])
        rows = [low_y[0]]
        for b in range(NODES):
            value = u_ref[a, b]
            if b == 0:
                value = value + low_y[1]
            if b == NODES - 1:
                value = value + high_y[0]
            rows.append(value)
        rows.append(high_y[1])
        for b in range(EXT):
            value = rows[b]
            if a == 0:
                value = value + low_x[1, b]
            if a == NODES - 1:
                value = value + high_x[0, b]
            x_ref[a + 1, b * 8 : b * 8 + 8] = value
            if 0 < b < EXT - 1:
                q_ref[a, b - 1] = value
    local_solve(x_ref, h_ref, forward_ref, back_ref, inverse_ref, part_ref)
    send_parts(part_ref, side_x, side_y, sy_first, sy_second, fx_first, fx_second)


def collect_parts(part_ref, ry_first, ry_second, rx_first, rx_second, side_x, side_y, field_ref):
    low_x = side_x.low(rx_first[...], rx_second[...])
    high_x = side_x.high(rx_first[...], rx_second[...])
    result = {}
    for a in range(NODES):
        low_y = side_y.low(ry_first[a + 1], ry_second[a + 1])
        high_y = side_y.high(ry_first[a + 1], ry_second[a + 1])
        for b in range(NODES):
            value = part_ref[a + 1, (b + 1) * 8 : (b + 2) * 8]
            if b < 2:
                value = value + low_y[b]
            if b >= NODES - 2:
                value = value + high_y[b - (NODES - 2)]
            if a < 2:
                value = value + low_x[a, b]
            if a >= NODES - 2:
                value = value + high_x[a - (NODES - 2), b]
            field = 3 * class_of(a) + class_of(b)
            result[(a, b)] = value + field_ref[field : field + 1, :]
    return result


def apply_tiles(z_ref, u_ref, y_ref, tiles_ref, por):
    for a in range(NODES):
        for b in range(NODES):
            y_ref[a, b] = z_ref[a, b] * tiles_ref[0]
    for a in range(NODES):
        for b in range(NODES):
            z = z_ref[a, b]
            third = z * tiles_ref[1]
            for shift in range(1, NODES):
                third = third + pltpu.roll(z, shift, 0) * tiles_ref[1 + shift]
            first = y_ref[0, b] * float(STIFF[a, 0] * WEIGHTS[b])
            second = y_ref[a, 0] * float(STIFF[b, 0] * WEIGHTS[a])
            for other in range(1, NODES):
                first = first + y_ref[other, b] * float(STIFF[a, other] * WEIGHTS[b])
                second = second + y_ref[a, other] * float(STIFF[b, other] * WEIGHTS[a])
            weight = float(WEIGHTS[a] * WEIGHTS[b])
            u_ref[a, b] = por * (third * weight + first + second) + y_ref[a, b] * (
                shift_mass * weight
            )


def sum_column(u_ref):
    for a in range(NODES):
        bottom = u_ref[a, :, 0, :]
        top = u_ref[a, :, NODES - 1, :]
        u_ref[a, :, 0, :] = bottom + shift_up(top)
        u_ref[a, :, NODES - 1, :] = top + shift_down(bottom)


def first_apply_kernel(
    counts, part_ref, ry_first, ry_second, rx_first, rx_second, field_ref, por_ref, r_ref,
    tiles_ref, z_ref, u_ref, sy_first, sy_second, fx_first, fx_second, stats_ref, y_ref,
):
    side_x, side_y = Sides("gx", counts[0]), Sides("gy", counts[1])
    z = collect_parts(
        part_ref, ry_first, ry_second, rx_first, rx_second, side_x, side_y, field_ref
    )
    inner = None
    for (a, b), value in z.items():
        z_ref[a, b] = value
        term = scaled(value * r_ref[a, b], axis_factor(a, side_x), axis_factor(b, side_y))
        inner = term if inner is None else inner + term
    inner = inner * multiplicity_tile()
    apply_tiles(z_ref, u_ref, y_ref, tiles_ref, por_ref[...])
    sums = {}
    curvature = None
    for a in range(NODES):
        for b in range(NODES):
            value = u_ref[a, b]
            add_to(sums, (class_of(a), class_of(b)), value)
            term = value * z_ref[a, b]
            curvature = term if curvature is None else curvature + term
    stats_ref[...] = stats_row(class_tiles(sums) + [inner, curvature])
    sum_column(u_ref)
    for a in range(NODES):
        for layer in range(2):
            low, high = u_ref[a, layer], u_ref[a, NODES - 2 + layer]
            sy_first[a, layer] = side_y.send_first(low, high)
            sy_second[a, layer] = side_y.send_second(low, high)
    for layer in range(2):
        low, high = u_ref[layer], u_ref[NODES - 2 + layer]
        fx_first[layer] = side_x.send_first(low, high)
        fx_second[layer] = side_x.send_second(low, high)


def second_apply_kernel(
    counts, part_ref, ry_first, ry_second, rx_first, rx_second, field_ref, por_ref, r_ref, q_ref,
    z_ref, tiles_ref, z1_ref, u_ref, sy_first, sy_second, fx_first, fx_second, stats_ref, y_ref,
):
    side_x, side_y = Sides("gx", counts[0]), Sides("gy", counts[1])
    step = field_ref[9:10, :]
    w = collect_parts(
        part_ref, ry_first, ry_second, rx_first, rx_second, side_x, side_y, field_ref
    )
    inner = None
    for (a, b), value in w.items():
        next_z = z_ref[a, b] - step * value
        next_r = r_ref[a, b] - step * q_ref[a, b]
        z1_ref[a, b] = next_z
        term = scaled(next_z * next_r, axis_factor(a, side_x), axis_factor(b, side_y))
        inner = term if inner is None else inner + term
    inner = inner * multiplicity_tile()
    apply_tiles(z1_ref, u_ref, y_ref, tiles_ref, por_ref[...])
    own = None
    cross = None
    for a in range(NODES):
        for b in range(NODES):
            value = u_ref[a, b]
            own_term = value * z1_ref[a, b]
            cross_term = value * z_ref[a, b]
            own = own_term if own is None else own + own_term
            cross = cross_term if cross is None else cross + cross_term
    stats_ref[...] = stats_row([inner, own, cross])
    sum_column(u_ref)
    for a in range(NODES):
        low, high = u_ref[a, 0], u_ref[a, NODES - 1]
        sy_first[a] = side_y.send_first(low, high)
        sy_second[a] = side_y.send_second(low, high)
    low, high = u_ref[0], u_ref[NODES - 1]
    fx_first[...] = side_x.send_first(low, high)
    fx_second[...] = side_x.send_second(low, high)


def final_kernel(
    counts, sol_ref, r_ref, q_ref, z_ref, z1_ref, u_ref, ry_first, ry_second, rx_first, rx_second,
    scalars_ref, sol_out, r_out, d_out,
):
    side_x, side_y = Sides("gx", counts[0]), Sides("gy", counts[1])
    first_step = scalars_ref[0:1, :]
    second_step = scalars_ref[1:2, :]
    ratio = scalars_ref[2:3, :]
    low_x = side_x.low(rx_first[...], rx_second[...])
    high_x = side_x.high(rx_first[...], rx_second[...])
    for a in range(NODES):
        for b in range(NODES):
            image = u_ref[a, b]
            if b == 0:
                image = image + side_y.low(ry_first[a], ry_second[a])
            if b == NODES - 1:
                image = image + side_y.high(ry_first[a], ry_second[a])
            if a == 0:
                image = image + low_x[b]
            if a == NODES - 1:
                image = image + high_x[b]
            z, q = z_ref[a, b], q_ref[a, b]
            direction = z1_ref[a, b] + ratio * z
            image = image + ratio * q
            d_out[a, b] = direction
            sol_out[a, b] = sol_ref[a, b] + first_step * z + second_step * direction
            r_out[a, b] = r_ref[a, b] - first_step * q - second_step * image


def call(kernel, counts, name, shapes, scratch, *operands):
    def body(*refs):
        kernel(counts, *refs)

    return pl.pallas_call(
        body,
        name=name,
        out_shape=[jax.ShapeDtypeStruct(shape, jnp.float32) for shape in shapes],
        in_specs=[pl.BlockSpec(memory_space=pltpu.VMEM)] * len(operands),
        out_specs=[pl.BlockSpec(memory_space=pltpu.VMEM)] * len(shapes),
        scratch_shapes=[pltpu.VMEM(shape, jnp.float32) for shape in scratch],
        compiler_params=pltpu.CompilerParams(vmem_limit_bytes=24 * 1024 * 1024),
    )(*operands)


def swap_pairs(counts, axis, parity):
    count_x, count_y = counts
    pairs = []
    for x in range(count_x):
        for y in range(count_y):
            if axis == 0:
                to = ((x + 1 if x % 2 == parity else x - 1) % count_x, y)
            else:
                other = y + 1 if y % 2 == parity else y - 1
                to = (x, other) if 0 <= other < count_y else (x ^ 1, y)
            pairs.append((x * count_y + y, to[0] * count_y + to[1]))
    return pairs


def trade(counts, axis, first, second):
    return (
        lax.ppermute(first, AXES, swap_pairs(counts, axis, 0)),
        lax.ppermute(second, AXES, swap_pairs(counts, axis, 1)),
    )


def gather_stats(counts, row):
    total = counts[0] * counts[1]
    return lax.all_to_all(jnp.broadcast_to(row[None], (total, 1, 128)), AXES, 0, 0)[:, 0, :]


def coarse_tables(counts, column_length):
    share_x, share_y = share_table(counts[0]), share_table(counts[1])
    basis_x, eigen_x = cosine_inverse(counts[0])
    basis_y, eigen_y = cosine_inverse(counts[1])
    divisor = (
        2.0 * mean_porosity * column_length * (eigen_x[:, None] + eigen_y[None, :])
        + 8.0 * shift_mass * column_length
    )
    to_modes_x = np.einsum("xip,pa->xia", share_x, basis_x)
    to_modes_y = np.einsum("yjq,qb->yjb", share_y, basis_y)
    return to_modes_x, to_modes_y, divisor


def coarse_field(counts, tables, stats):
    to_modes_x, to_modes_y, divisor = tables
    sums = stats[:, :9].reshape(counts[0], counts[1], 3, 3)
    modes_x, modes_y = jnp.asarray(to_modes_x, jnp.float32), jnp.asarray(to_modes_y, jnp.float32)
    spectrum = jnp.einsum("xyij,xia,yjb->ab", sums, modes_x, modes_y, precision=exact_mode)
    spectrum = spectrum / jnp.asarray(divisor, jnp.float32)
    own_x = lax.dynamic_index_in_dim(modes_x, lax.axis_index("gx"), 0, keepdims=False)
    own_y = lax.dynamic_index_in_dim(modes_y, lax.axis_index("gy"), 0, keepdims=False)
    return jnp.einsum("ia,ab,jb->ij", own_x, spectrum, own_y, precision=exact_mode).reshape(9)


def rows_of(values, count):
    values = jnp.concatenate([values, jnp.zeros((count - values.shape[0],), jnp.float32)])
    return jnp.broadcast_to(values[:, None], (count, 128))


def shards_of(counts):
    forward_np, back_np, inverse_np = plane_tables()
    tiles_np = tile_tables()

    def shards(solution, residual, grain_counts):
        shard_shape = solution.shape
        block = shard_shape[2:]
        solution = solution.reshape(block)
        residual = residual.reshape(block)
        tables = coarse_tables(counts, block[-1])
        plane = [jnp.asarray(table) for table in (forward_np, back_np, inverse_np)]
        tiles = jnp.asarray(tiles_np)
        porosity = 1.0 - 0.6 * grain_counts.reshape(1, 128).astype(jnp.float32) / MOST_GRAINS
        side_x, side_y = Sides("gx", counts[0]), Sides("gy", counts[1])
        even_x = side_x.even
        row = (1, 128)
        face = (NODES, NODES, 128)
        part_shapes = [
            (EXT, ROWS, 128),
            (EXT, 2, NODES, 128), (EXT, 2, NODES, 128),
            (2, EXT, NODES, 128), (2, EXT, NODES, 128),
        ]
        solve_scratch = [(EXT, ROWS, 128), (EXT, MODES, 128)]

        y_first, y_second, stats = call(
            start_kernel, counts, "start", [face, face, row], [], residual
        )
        ry = trade(counts, 1, y_first, y_second)
        low_y, high_y = side_y.low(*ry), side_y.high(*ry)

        def with_layers(index):
            return jnp.concatenate([low_y[index][None], residual[index], high_y[index][None]])

        low_face, high_face = with_layers(1), with_layers(NODES - 2)
        rx = trade(
            counts, 0, side_x.send_first(low_face, high_face),
            side_x.send_second(low_face, high_face),
        )
        first_stats = gather_stats(counts, stats)

        def spread_faces(fx, ry):
            low_y, high_y = side_y.low(*ry), side_y.high(*ry)
            middle = jnp.zeros((2, NODES - 4, NODES, 128), jnp.float32)
            both = [
                jnp.concatenate([low_y[at], middle, high_y[at]], axis=1)
                for at in (slice(0, 2), slice(8, 10))
            ]
            return (
                fx[0][:, 1:-1] + side_x.send_first(*both),
                fx[1][:, 1:-1] + side_x.send_second(*both),
            )

        part, y_first, y_second, *fx = call(
            first_solve_kernel, counts, "first_solve", part_shapes, solve_scratch,
            residual, *ry, *rx, *plane,
        )
        ry = trade(counts, 1, y_first, y_second)
        rx = trade(counts, 0, *spread_faces(fx, ry))
        field = rows_of(coarse_field(counts, tables, first_stats), 16)
        z, u, y_first, y_second, *fx, stats = call(
            first_apply_kernel, counts, "first_apply",
            [block, block, (NODES, 2, NODES, 128), (NODES, 2, NODES, 128),
             (2, NODES, NODES, 128), (2, NODES, NODES, 128), row],
            [block],
            part, *ry, *rx, field, porosity, residual, tiles,
        )
        ry = trade(counts, 1, y_first, y_second)
        low_y, high_y = side_y.low(*ry), side_y.high(*ry)

        def image_faces(index):
            middle = jnp.zeros((2, NODES - 2, NODES, 128), jnp.float32)
            return jnp.concatenate([low_y[index], middle, high_y[index]], axis=1)

        pads = ((0, 0), (1, 1), (0, 0), (0, 0))
        both = (image_faces(slice(0, 2)), image_faces(slice(NODES - 2, NODES)))
        rx = trade(
            counts, 0,
            jnp.pad(fx[0], pads) + side_x.send_first(*both),
            jnp.pad(fx[1], pads) + side_x.send_second(*both),
        )
        second_stats = gather_stats(counts, stats)
        q, part, y_first, y_second, *fx = call(
            second_solve_kernel, counts, "second_solve", [block] + part_shapes, solve_scratch,
            u, *ry, *rx, *plane,
        )
        ry = trade(counts, 1, y_first, y_second)
        rx = trade(counts, 0, *spread_faces(fx, ry))
        first_inner = jnp.sum(second_stats[:, 9])
        first_curvature = jnp.sum(second_stats[:, 10])
        first_step = first_inner / first_curvature
        field = rows_of(
            jnp.concatenate([coarse_field(counts, tables, second_stats), first_step[None]]), 16
        )
        z1, u, y_first, y_second, *fx, stats = call(
            second_apply_kernel, counts, "second_apply",
            [block, block, face, face, face, face, row],
            [block],
            part, *ry, *rx, field, porosity, residual, q, z, tiles,
        )
        ry = trade(counts, 1, y_first, y_second)
        low_y, high_y = side_y.low(*ry), side_y.high(*ry)

        def edge_rows(index):
            middle = jnp.zeros((NODES - 2, NODES, 128), jnp.float32)
            return jnp.concatenate([low_y[index][None], middle, high_y[index][None]])

        both = (edge_rows(0), edge_rows(NODES - 1))
        rx = trade(
            counts, 0, fx[0] + side_x.send_first(*both), fx[1] + side_x.send_second(*both)
        )
        last_stats = gather_stats(counts, stats)
        second_inner, own, cross = (jnp.sum(last_stats[:, i]) for i in range(3))
        ratio = second_inner / first_inner
        second_step = second_inner / (own + ratio * (2.0 * cross + ratio * first_curvature))
        scalars = rows_of(jnp.stack([first_step, second_step, ratio]), 8)
        solution_out, residual_out, direction = call(
            final_kernel, counts, "final", [block] * 3, [],
            solution, residual, q, z, z1, u, *ry, *rx, scalars,
        )
        return (
            solution_out.reshape(shard_shape),
            residual_out.reshape(shard_shape),
            direction.reshape(shard_shape),
            jnp.stack([first_step, second_step]),
        )

    return shards


def solution(mesh):
    counts = (mesh.shape["gx"], mesh.shape["gy"])
    return jax.shard_map(
        shards_of(counts),
        mesh=mesh,
        in_specs=(
            P("gx", "gy", None, None, None, None),
            P("gx", "gy", None, None, None, None),
            P("gx", "gy", None),
        ),
        out_specs=(
            P("gx", "gy", None, None, None, None),
            P("gx", "gy", None, None, None, None),
            P("gx", "gy", None, None, None, None),
            P(),
        ),
        check_vma=False,
    )
```

```python
import math

import jax
import jax.numpy as jnp
import numpy as np
from jax import lax
from jax.experimental import pallas as pl
from jax.experimental.pallas import tpu as pltpu
from jax.sharding import PartitionSpec as P

NODES = 8
MOST_GRAINS = 16
EXT = NODES + 2
ROWS = 112
MODES = 104
AXES = ("gx", "gy")

shift_mass = 0.1
mean_porosity = 0.7
exact_mode = lax.Precision.HIGHEST


def legendre_columns(node_set, degree):
    table = [node_set * 0.0 + 1.0, node_set]
    for order in range(2, degree + 1):
        table.append(
            ((2 * order - 1) * node_set * table[order - 1] - (order - 1) * table[order - 2]) / order
        )
    return table


def gll_tables():
    degree = NODES - 1
    node_set = np.cos(math.pi * np.arange(degree + 1) / degree)
    for sweep in range(100):
        table = legendre_columns(node_set, degree)
        node_set = node_set - (node_set * table[degree] - table[degree - 1]) / (
            (degree + 1) * table[degree]
        )
    node_set = node_set[::-1].copy()
    values = legendre_columns(node_set, degree)[degree]
    weights = 2.0 / (degree * (degree + 1) * values**2)
    derivative = np.zeros((NODES, NODES))
    for row_index in range(NODES):
        for column_index in range(NODES):
            if row_index != column_index:
                derivative[row_index, column_index] = values[row_index] / (
                    values[column_index] * (node_set[row_index] - node_set[column_index])
                )
    derivative[0, 0] = -degree * (degree + 1) / 4.0
    derivative[NODES - 1, NODES - 1] = degree * (degree + 1) / 4.0
    return (weights, derivative)


def jacobi_eigen(matrix):
    size_now = matrix.shape[0]
    current = matrix.copy()
    vectors = np.eye(size_now)
    for sweep in range(12):
        for first in range(size_now - 1):
            for second in range(first + 1, size_now):
                off_value = current[first, second]
                safe_value = np.where(off_value == 0.0, 1e-300, off_value)
                theta = (current[second, second] - current[first, first]) / (2.0 * safe_value)
                sign_value = np.where(theta >= 0.0, 1.0, -1.0)
                tangent = sign_value / (np.abs(theta) + np.sqrt(theta * theta + 1.0))
                cosine = 1.0 / np.sqrt(tangent * tangent + 1.0)
                sine = tangent * cosine
                rotation = np.eye(size_now)
                rotation[first, first] = cosine
                rotation[second, second] = cosine
                rotation[first, second] = sine
                rotation[second, first] = -sine
                current = rotation.T @ current @ rotation
                vectors = vectors @ rotation
    eigen_values = np.array([current[index, index] for index in range(size_now)])
    return (eigen_values, vectors)


def schwarz_tables():
    weights, derivative = gll_tables()
    stiffness = derivative.T @ (weights[:, None] * derivative)
    total_nodes = 3 * (NODES - 1) + 1
    three_stiffness = np.zeros((total_nodes, total_nodes))
    three_mass = np.zeros(total_nodes)
    for element in range(3):
        start_node = element * (NODES - 1)
        three_stiffness[
            start_node : start_node + NODES, start_node : start_node + NODES
        ] += stiffness
        three_mass[start_node : start_node + NODES] += weights
    chosen = np.array([NODES - 2] + list(range(NODES - 1, 2 * NODES - 1)) + [2 * NODES - 1])
    local_stiffness = three_stiffness[chosen][:, chosen]
    local_mass = three_mass[chosen]
    scaling = 1.0 / np.sqrt(local_mass)
    symmetric = scaling[:, None] * local_stiffness * scaling[None, :]
    symmetric = 0.5 * (symmetric + symmetric.T)
    eigen_values, eigen_vectors = jacobi_eigen(symmetric)
    return (scaling[:, None] * eigen_vectors, eigen_values)


WEIGHTS, DERIVATIVE = gll_tables()
STIFF = DERIVATIVE.T @ (WEIGHTS[:, None] * DERIVATIVE)
BASIS, EIGEN = schwarz_tables()


def plane_tables():
    forward = np.zeros((MODES, ROWS))
    inverse = np.zeros((MODES, EXT))
    for mode_b in range(EXT):
        for mode_c in range(EXT):
            mode = mode_b * EXT + mode_c
            for b in range(EXT):
                for k in range(NODES):
                    forward[mode, b * NODES + k] = BASIS[b, mode_b] * BASIS[k + 1, mode_c]
                forward[mode, 80 + b] = BASIS[b, mode_b] * BASIS[0, mode_c]
                forward[mode, 96 + b] = BASIS[b, mode_b] * BASIS[EXT - 1, mode_c]
            inverse[mode] = 1.0 / (
                mean_porosity * (EIGEN + EIGEN[mode_b] + EIGEN[mode_c]) + shift_mass
            )
    lanes = np.repeat(inverse.T[:, :, None], 128, axis=2)
    return (
        forward.astype(np.float32),
        forward.T.astype(np.float32).copy(),
        lanes.astype(np.float32),
    )


def tile_tables():
    table = np.zeros((NODES + 1, NODES, 128))
    table[0] = WEIGHTS[:, None]
    for shift in range(NODES):
        for k in range(NODES):
            table[1 + shift, k] = STIFF[k, (k - shift) % NODES]
    return table.astype(np.float32)


def share_table(count):
    table = np.zeros((count, 3, count))
    for column in range(count):
        table[column, :, column] = 1.0
        if column > 0:
            table[column, 0, column] = 0.5
            table[column, 0, column - 1] = 0.5
        if column < count - 1:
            table[column, 2, column] = 0.5
            table[column, 2, column + 1] = 0.5
    return table


def cosine_inverse(count):
    position = np.arange(count)
    basis = np.cos(math.pi * (position[:, None] + 0.5) * position[None, :] / count)
    basis = basis * np.where(position == 0, math.sqrt(1.0 / count), math.sqrt(2.0 / count))[None, :]
    return basis, 2.0 - 2.0 * np.cos(math.pi * position / count)


def side_even(axis):
    return lax.rem(lax.axis_index(axis), 2) == 0


def shift_up(rows):
    lane = lax.broadcasted_iota(jnp.int32, rows.shape, 1)
    return jnp.where(lane == 0, 0.0, pltpu.roll(rows, 1, 1))


def shift_down(rows):
    lane = lax.broadcasted_iota(jnp.int32, rows.shape, 1)
    return jnp.where(lane == 127, 0.0, pltpu.roll(rows, 127, 1))


class Sides:
    def __init__(self, axis, count):
        index = lax.axis_index(axis)
        self.even = lax.rem(index, 2) == 0
        self.no_low = index == 0
        self.no_high = index == count - 1

    def low(self, first, second):
        return jnp.where(self.no_low, 0.0, jnp.where(self.even, second, first))

    def high(self, first, second):
        return jnp.where(self.no_high, 0.0, jnp.where(self.even, first, second))

    def send_first(self, low_face, high_face):
        return jnp.where(self.even, high_face, low_face)

    def send_second(self, low_face, high_face):
        return jnp.where(self.even, low_face, high_face)


def multiplicity_tile():
    row = lax.broadcasted_iota(jnp.int32, (NODES, 128), 0)
    lane = lax.broadcasted_iota(jnp.int32, (NODES, 128), 1)
    shared = ((row == 0) & (lane > 0)) | ((row == NODES - 1) & (lane < 127))
    return jnp.where(shared, 0.5, 1.0)


def class_of(node):
    return 0 if node == 0 else (2 if node == NODES - 1 else 1)


def axis_factor(node, side):
    if node == 0:
        return jnp.where(side.no_low, 1.0, 0.5)
    if node == NODES - 1:
        return jnp.where(side.no_high, 1.0, 0.5)
    return None


def scaled(value, *factors):
    for factor in factors:
        if factor is not None:
            value = value * factor
    return value


def add_to(total, key, value):
    total[key] = value if key not in total else total[key] + value


def lane_sums(tiles):
    columns = [jnp.sum(tile, axis=0, keepdims=True) for tile in tiles]
    columns.append(jnp.zeros((16 - len(tiles), 128), jnp.float32))
    sums = jnp.sum(jnp.concatenate(columns, axis=0), axis=1, keepdims=True)
    return jnp.broadcast_to(sums, (16, 128))


def write_stats(stats_ref, tiles):
    row = lax.broadcasted_iota(jnp.int32, (16, 128), 0)
    lane = lax.broadcasted_iota(jnp.int32, (16, 128), 1)
    sums = jnp.sum(jnp.where(row == lane, lane_sums(tiles), 0.0), axis=0, keepdims=True)
    for index in range(stats_ref.shape[0]):
        stats_ref[index] = sums


def gathered(stats_ref):
    return stats_ref[:, 0, :]


def stat_columns(stats, first, count):
    lane = lax.broadcasted_iota(jnp.int32, stats.shape, 1)
    sums = lane_sums([jnp.where(lane == first + i, stats, 0.0) for i in range(count)])
    return [sums[i : i + 1] for i in range(count)]


def lifted_rows(stats, lift_ref):
    return lane_sums([lift_ref[i] * stats for i in range(9)])


def class_tiles(sums):
    return [sums[(i, j)] for i in range(3) for j in range(3)]


def start_kernel(counts, r_ref, sy_first, sy_second, stats_ref):
    side_x, side_y = Sides("gx", counts[0]), Sides("gy", counts[1])
    tile = multiplicity_tile()
    for a in range(NODES):
        low, high = r_ref[a, 1], r_ref[a, NODES - 2]
        sy_first[a] = side_y.send_first(low, high)
        sy_second[a] = side_y.send_second(low, high)
    sums = {}
    for a in range(NODES):
        for b in range(NODES):
            add_to(sums, (class_of(a), class_of(b)), r_ref[a, b])
    for (i, j), value in sums.items():
        a, b = (0, 1, NODES - 1)[i], (0, 1, NODES - 1)[j]
        sums[(i, j)] = scaled(value * tile, axis_factor(a, side_x), axis_factor(b, side_y))
    write_stats(stats_ref, class_tiles(sums))


def planes(ref):
    return jnp.concatenate([ref[a] for a in range(EXT)], axis=1)


def local_solve(x_ref, h_ref, forward_ref, back_ref, inverse_ref, part_ref):
    zero = jnp.zeros((6, 128), jnp.float32)
    for a in range(EXT):
        x_ref[a, 80:90] = shift_up(x_ref[a, pl.ds(6, EXT, stride=NODES), :])
        x_ref[a, 96:106] = shift_down(x_ref[a, pl.ds(1, EXT, stride=NODES), :])
        x_ref[a, 90:96] = zero
        x_ref[a, 106:112] = zero
    spectrum = jnp.dot(
        forward_ref[...], planes(x_ref), precision=exact_mode, preferred_element_type=jnp.float32
    )
    for a in range(EXT):
        h_ref[a] = spectrum[:, a * 128 : (a + 1) * 128]
    for block in range(MODES // 8):
        rows = pl.ds(block * 8, 8)
        values = [h_ref[a, rows] for a in range(EXT)]
        modes = []
        for mode in range(EXT):
            total = values[0] * float(BASIS[0, mode])
            for a in range(1, EXT):
                total = total + values[a] * float(BASIS[a, mode])
            modes.append(total * inverse_ref[mode, rows])
        for a in range(EXT):
            total = modes[0] * float(BASIS[a, 0])
            for mode in range(1, EXT):
                total = total + modes[mode] * float(BASIS[a, mode])
            h_ref[a, rows] = total
    values = jnp.dot(
        back_ref[...], planes(h_ref), precision=exact_mode, preferred_element_type=jnp.float32
    )
    for a in range(EXT):
        part_ref[a] = values[:, a * 128 : (a + 1) * 128]
    for a in range(EXT):

        def layer(k):
            return (a, pl.ds(k, EXT, stride=NODES), slice(None))

        bottom, top = part_ref[layer(0)], part_ref[layer(NODES - 1)]
        part_ref[layer(0)] = bottom + shift_up(top)
        part_ref[layer(NODES - 1)] = top + shift_down(bottom)
        part_ref[layer(1)] = part_ref[layer(1)] + shift_up(part_ref[a, 96:106])
        part_ref[layer(NODES - 2)] = part_ref[layer(NODES - 2)] + shift_down(part_ref[a, 80:90])


def send_parts(part_ref, side_x, side_y, sy_first, sy_second, fx_first, fx_second):
    for a in range(EXT):
        low, high = part_ref[a, 0:16], part_ref[a, 64:80]
        sy_first[a] = side_y.send_first(low, high).reshape(2, NODES, 128)
        sy_second[a] = side_y.send_second(low, high).reshape(2, NODES, 128)
    for layer in range(2):
        low, high = part_ref[layer, 0:80], part_ref[NODES + layer, 0:80]
        fx_first[layer] = side_x.send_first(low, high).reshape(EXT, NODES, 128)
        fx_second[layer] = side_x.send_second(low, high).reshape(EXT, NODES, 128)


def first_solve_kernel(
    counts, r_ref, ry_first, ry_second, rx_first, rx_second, forward_ref, back_ref, inverse_ref,
    part_ref, sy_first, sy_second, fx_first, fx_second, x_ref, h_ref,
):
    side_x, side_y = Sides("gx", counts[0]), Sides("gy", counts[1])
    x_ref[0, 0:80] = side_x.low(rx_first[...], rx_second[...]).reshape(80, 128)
    x_ref[EXT - 1, 0:80] = side_x.high(rx_first[...], rx_second[...]).reshape(80, 128)
    for a in range(NODES):
        x_ref[a + 1, 0:8] = side_y.low(ry_first[a], ry_second[a])
        x_ref[a + 1, 8:72] = r_ref[a].reshape(64, 128)
        x_ref[a + 1, 72:80] = side_y.high(ry_first[a], ry_second[a])
    local_solve(x_ref, h_ref, forward_ref, back_ref, inverse_ref, part_ref)
    send_parts(part_ref, side_x, side_y, sy_first, sy_second, fx_first, fx_second)


def second_solve_kernel(
    counts, u_ref, ry_first, ry_second, rx_first, rx_second, forward_ref, back_ref, inverse_ref,
    q_ref, part_ref, sy_first, sy_second, fx_first, fx_second, x_ref, h_ref,
):
    side_x, side_y = Sides("gx", counts[0]), Sides("gy", counts[1])
    low_x = side_x.low(rx_first[...], rx_second[...])
    high_x = side_x.high(rx_first[...], rx_second[...])
    x_ref[0, 0:80] = low_x[0].reshape(80, 128)
    x_ref[EXT - 1, 0:80] = high_x[1].reshape(80, 128)
    for a in range(NODES):
        low_y = side_y.low(ry_first[a], ry_second[a])
        high_y = side_y.high(ry_first[a], ry_second[a])
        rows = [low_y[0]]
        for b in range(NODES):
            value = u_ref[a, b]
            if b == 0:
                value = value + low_y[1]
            if b == NODES - 1:
                value = value + high_y[0]
            rows.append(value)
        rows.append(high_y[1])
        for b in range(EXT):
            value = rows[b]
            if a == 0:
                value = value + low_x[1, b]
            if a == NODES - 1:
                value = value + high_x[0, b]
            x_ref[a + 1, b * 8 : b * 8 + 8] = value
            if 0 < b < EXT - 1:
                q_ref[a, b - 1] = value
    local_solve(x_ref, h_ref, forward_ref, back_ref, inverse_ref, part_ref)
    send_parts(part_ref, side_x, side_y, sy_first, sy_second, fx_first, fx_second)


def collect_parts(part_ref, ry_first, ry_second, rx_first, rx_second, side_x, side_y, field):
    low_x = side_x.low(rx_first[...], rx_second[...])
    high_x = side_x.high(rx_first[...], rx_second[...])
    result = {}
    for a in range(NODES):
        low_y = side_y.low(ry_first[a + 1], ry_second[a + 1])
        high_y = side_y.high(ry_first[a + 1], ry_second[a + 1])
        for b in range(NODES):
            value = part_ref[a + 1, (b + 1) * 8 : (b + 2) * 8]
            if b < 2:
                value = value + low_y[b]
            if b >= NODES - 2:
                value = value + high_y[b - (NODES - 2)]
            if a < 2:
                value = value + low_x[a, b]
            if a >= NODES - 2:
                value = value + high_x[a - (NODES - 2), b]
            node_class = 3 * class_of(a) + class_of(b)
            result[(a, b)] = value + field[node_class : node_class + 1, :]
    return result


def porosity_row(grains_ref):
    return 1.0 - 0.6 * grains_ref[...].astype(jnp.float32) / MOST_GRAINS


def apply_tiles(z_ref, u_ref, y_ref, tiles_ref, por):
    for a in range(NODES):
        for b in range(NODES):
            y_ref[a, b] = z_ref[a, b] * tiles_ref[0]
    for a in range(NODES):
        for b in range(NODES):
            z = z_ref[a, b]
            third = z * tiles_ref[1]
            for shift in range(1, NODES):
                third = third + pltpu.roll(z, shift, 0) * tiles_ref[1 + shift]
            first = y_ref[0, b] * float(STIFF[a, 0] * WEIGHTS[b])
            second = y_ref[a, 0] * float(STIFF[b, 0] * WEIGHTS[a])
            for other in range(1, NODES):
                first = first + y_ref[other, b] * float(STIFF[a, other] * WEIGHTS[b])
                second = second + y_ref[a, other] * float(STIFF[b, other] * WEIGHTS[a])
            weight = float(WEIGHTS[a] * WEIGHTS[b])
            u_ref[a, b] = por * (third * weight + first + second) + y_ref[a, b] * (
                shift_mass * weight
            )


def sum_column(u_ref):
    for a in range(NODES):
        bottom = u_ref[a, :, 0, :]
        top = u_ref[a, :, NODES - 1, :]
        u_ref[a, :, 0, :] = bottom + shift_up(top)
        u_ref[a, :, NODES - 1, :] = top + shift_down(bottom)


def first_apply_kernel(
    counts, part_ref, ry_first, ry_second, rx_first, rx_second, gathered_ref, lift_ref, grains_ref,
    r_ref, tiles_ref, z_ref, u_ref, sy_first, sy_second, fx_first, fx_second, stats_ref, y_ref,
):
    side_x, side_y = Sides("gx", counts[0]), Sides("gy", counts[1])
    field = lifted_rows(gathered(gathered_ref), lift_ref)
    z = collect_parts(part_ref, ry_first, ry_second, rx_first, rx_second, side_x, side_y, field)
    inner = None
    for (a, b), value in z.items():
        z_ref[a, b] = value
        term = scaled(value * r_ref[a, b], axis_factor(a, side_x), axis_factor(b, side_y))
        inner = term if inner is None else inner + term
    inner = inner * multiplicity_tile()
    apply_tiles(z_ref, u_ref, y_ref, tiles_ref, porosity_row(grains_ref))
    sums = {}
    curvature = None
    for a in range(NODES):
        for b in range(NODES):
            value = u_ref[a, b]
            add_to(sums, (class_of(a), class_of(b)), value)
            term = value * z_ref[a, b]
            curvature = term if curvature is None else curvature + term
    write_stats(stats_ref, class_tiles(sums) + [inner, curvature])
    sum_column(u_ref)
    for a in range(NODES):
        for layer in range(2):
            low, high = u_ref[a, layer], u_ref[a, NODES - 2 + layer]
            sy_first[a, layer] = side_y.send_first(low, high)
            sy_second[a, layer] = side_y.send_second(low, high)
    for layer in range(2):
        low, high = u_ref[layer], u_ref[NODES - 2 + layer]
        fx_first[layer] = side_x.send_first(low, high)
        fx_second[layer] = side_x.send_second(low, high)


def second_apply_kernel(
    counts, part_ref, ry_first, ry_second, rx_first, rx_second, gathered_ref, lift_ref, grains_ref,
    r_ref, q_ref, z_ref, tiles_ref, z1_ref, u_ref, sy_first, sy_second, fx_first, fx_second, stats_ref, y_ref,
):
    side_x, side_y = Sides("gx", counts[0]), Sides("gy", counts[1])
    stats = gathered(gathered_ref)
    field = lifted_rows(stats, lift_ref)
    first_inner, first_curvature = stat_columns(stats, 9, 2)
    step = first_inner / first_curvature
    w = collect_parts(part_ref, ry_first, ry_second, rx_first, rx_second, side_x, side_y, field)
    inner = None
    for (a, b), value in w.items():
        next_z = z_ref[a, b] - step * value
        next_r = r_ref[a, b] - step * q_ref[a, b]
        z1_ref[a, b] = next_z
        term = scaled(next_z * next_r, axis_factor(a, side_x), axis_factor(b, side_y))
        inner = term if inner is None else inner + term
    inner = inner * multiplicity_tile()
    apply_tiles(z1_ref, u_ref, y_ref, tiles_ref, porosity_row(grains_ref))
    own = None
    cross = None
    for a in range(NODES):
        for b in range(NODES):
            value = u_ref[a, b]
            own_term = value * z1_ref[a, b]
            cross_term = value * z_ref[a, b]
            own = own_term if own is None else own + own_term
            cross = cross_term if cross is None else cross + cross_term
    write_stats(stats_ref, [inner, own, cross])
    sum_column(u_ref)
    for a in range(NODES):
        low, high = u_ref[a, 0], u_ref[a, NODES - 1]
        sy_first[a] = side_y.send_first(low, high)
        sy_second[a] = side_y.send_second(low, high)
    low, high = u_ref[0], u_ref[NODES - 1]
    fx_first[...] = side_x.send_first(low, high)
    fx_second[...] = side_x.send_second(low, high)


def final_kernel(
    counts, sol_ref, r_ref, q_ref, z_ref, z1_ref, u_ref, ry_first, ry_second, rx_first, rx_second,
    second_ref, last_ref, sol_out, r_out, d_out, steps_out,
):
    side_x, side_y = Sides("gx", counts[0]), Sides("gy", counts[1])
    first_inner, first_curvature = stat_columns(gathered(second_ref), 9, 2)
    second_inner, own, cross = stat_columns(gathered(last_ref), 0, 3)
    first_step = first_inner / first_curvature
    ratio = second_inner / first_inner
    second_step = second_inner / (own + ratio * (2.0 * cross + ratio * first_curvature))
    steps_out[0] = first_step[0, 0]
    steps_out[1] = second_step[0, 0]
    low_x = side_x.low(rx_first[...], rx_second[...])
    high_x = side_x.high(rx_first[...], rx_second[...])
    for a in range(NODES):
        for b in range(NODES):
            image = u_ref[a, b]
            if b == 0:
                image = image + side_y.low(ry_first[a], ry_second[a])
            if b == NODES - 1:
                image = image + side_y.high(ry_first[a], ry_second[a])
            if a == 0:
                image = image + low_x[b]
            if a == NODES - 1:
                image = image + high_x[b]
            z, q = z_ref[a, b], q_ref[a, b]
            direction = z1_ref[a, b] + ratio * z
            image = image + ratio * q
            d_out[a, b] = direction
            sol_out[a, b] = sol_ref[a, b] + first_step * z + second_step * direction
            r_out[a, b] = r_ref[a, b] - first_step * q - second_step * image


def call(kernel, counts, name, shapes, scratch, *operands):
    def body(*refs):
        kernel(counts, *refs)

    def space(shape):
        return pltpu.SMEM if len(shape) == 1 else pltpu.VMEM

    return pl.pallas_call(
        body,
        name=name,
        out_shape=[jax.ShapeDtypeStruct(shape, jnp.float32) for shape in shapes],
        in_specs=[pl.BlockSpec(memory_space=pltpu.VMEM)] * len(operands),
        out_specs=[pl.BlockSpec(memory_space=space(shape)) for shape in shapes],
        scratch_shapes=[pltpu.VMEM(shape, jnp.float32) for shape in scratch],
        compiler_params=pltpu.CompilerParams(vmem_limit_bytes=24 * 1024 * 1024),
    )(*operands)


def swap_pairs(counts, axis, parity):
    count_x, count_y = counts
    pairs = []
    for x in range(count_x):
        for y in range(count_y):
            if axis == 0:
                to = ((x + 1 if x % 2 == parity else x - 1) % count_x, y)
            else:
                other = y + 1 if y % 2 == parity else y - 1
                to = (x, other) if 0 <= other < count_y else (x ^ 1, y)
            pairs.append((x * count_y + y, to[0] * count_y + to[1]))
    return pairs


def trade(counts, axis, first, second):
    return (
        lax.ppermute(first, AXES, swap_pairs(counts, axis, 0)),
        lax.ppermute(second, AXES, swap_pairs(counts, axis, 1)),
    )


def gather_stats(stats):
    return lax.all_to_all(stats, AXES, 0, 0)


def lift_tables(counts, column_length):
    share_x, share_y = share_table(counts[0]), share_table(counts[1])
    basis_x, eigen_x = cosine_inverse(counts[0])
    basis_y, eigen_y = cosine_inverse(counts[1])
    divisor = (
        2.0 * mean_porosity * column_length * (eigen_x[:, None] + eigen_y[None, :])
        + 8.0 * shift_mass * column_length
    )
    modes_x = np.einsum("xip,pa->xia", share_x, basis_x)
    modes_y = np.einsum("yjq,qb->yjb", share_y, basis_y)
    total = counts[0] * counts[1]
    to_modes = np.einsum("xia,yjb->abxyij", modes_x, modes_y).reshape(total, total, 9)
    to_modes = np.pad(to_modes, ((0, 0), (0, 0), (0, 7))).reshape(total, total * 16)
    return [table.astype(np.float32) for table in (modes_x, modes_y, 1.0 / divisor, to_modes)]


def own_lift(tables):
    modes_x, modes_y, inverse, to_modes = [jnp.asarray(table) for table in tables]
    own_x = lax.dynamic_index_in_dim(modes_x, lax.axis_index("gx"), 0, keepdims=False)
    own_y = lax.dynamic_index_in_dim(modes_y, lax.axis_index("gy"), 0, keepdims=False)
    own = own_x[:, None, :, None] * own_y[None, :, None, :] * inverse[None, None]
    total = to_modes.shape[0]
    lift = jnp.dot(own.reshape(9, total), to_modes, precision=exact_mode)
    return jnp.pad(lift.reshape(9, total, 16), ((0, 0), (0, 0), (0, 112)))


def shards_of(counts):
    forward_np, back_np, inverse_np = plane_tables()
    tiles_np = tile_tables()

    def shards(solution, residual, grain_counts):
        shard_shape = solution.shape
        block = shard_shape[2:]
        solution = solution.reshape(block)
        residual = residual.reshape(block)
        lift = own_lift(lift_tables(counts, block[-1]))
        grains = grain_counts.reshape(1, 128)
        plane = [jnp.asarray(table) for table in (forward_np, back_np, inverse_np)]
        tiles = jnp.asarray(tiles_np)
        side_x, side_y = Sides("gx", counts[0]), Sides("gy", counts[1])
        row = (counts[0] * counts[1], 1, 128)
        face = (NODES, NODES, 128)
        part_shapes = [
            (EXT, ROWS, 128),
            (EXT, 2, NODES, 128), (EXT, 2, NODES, 128),
            (2, EXT, NODES, 128), (2, EXT, NODES, 128),
        ]
        solve_scratch = [(EXT, ROWS, 128), (EXT, MODES, 128)]

        y_first, y_second, stats = call(
            start_kernel, counts, "start", [face, face, row], [], residual
        )
        ry = trade(counts, 1, y_first, y_second)
        low_y, high_y = side_y.low(*ry), side_y.high(*ry)

        def with_layers(index):
            return jnp.concatenate([low_y[index][None], residual[index], high_y[index][None]])

        low_face, high_face = with_layers(1), with_layers(NODES - 2)
        rx = trade(
            counts, 0, side_x.send_first(low_face, high_face),
            side_x.send_second(low_face, high_face),
        )
        first_stats = gather_stats(stats)

        def spread_faces(fx, ry):
            low_y, high_y = side_y.low(*ry), side_y.high(*ry)
            middle = jnp.zeros((2, NODES - 4, NODES, 128), jnp.float32)
            both = [
                jnp.concatenate([low_y[at], middle, high_y[at]], axis=1)
                for at in (slice(0, 2), slice(8, 10))
            ]
            return (
                fx[0][:, 1:-1] + side_x.send_first(*both),
                fx[1][:, 1:-1] + side_x.send_second(*both),
            )

        part, y_first, y_second, *fx = call(
            first_solve_kernel, counts, "first_solve", part_shapes, solve_scratch,
            residual, *ry, *rx, *plane,
        )
        ry = trade(counts, 1, y_first, y_second)
        rx = trade(counts, 0, *spread_faces(fx, ry))
        z, u, y_first, y_second, *fx, stats = call(
            first_apply_kernel, counts, "first_apply",
            [block, block, (NODES, 2, NODES, 128), (NODES, 2, NODES, 128),
             (2, NODES, NODES, 128), (2, NODES, NODES, 128), row],
            [block],
            part, *ry, *rx, first_stats, lift, grains, residual, tiles,
        )
        ry = trade(counts, 1, y_first, y_second)
        low_y, high_y = side_y.low(*ry), side_y.high(*ry)

        def image_faces(index):
            middle = jnp.zeros((2, NODES - 2, NODES, 128), jnp.float32)
            return jnp.concatenate([low_y[index], middle, high_y[index]], axis=1)

        pads = ((0, 0), (1, 1), (0, 0), (0, 0))
        both = (image_faces(slice(0, 2)), image_faces(slice(NODES - 2, NODES)))
        rx = trade(
            counts, 0,
            jnp.pad(fx[0], pads) + side_x.send_first(*both),
            jnp.pad(fx[1], pads) + side_x.send_second(*both),
        )
        second_stats = gather_stats(stats)
        q, part, y_first, y_second, *fx = call(
            second_solve_kernel, counts, "second_solve", [block] + part_shapes, solve_scratch,
            u, *ry, *rx, *plane,
        )
        ry = trade(counts, 1, y_first, y_second)
        rx = trade(counts, 0, *spread_faces(fx, ry))
        z1, u, y_first, y_second, *fx, stats = call(
            second_apply_kernel, counts, "second_apply",
            [block, block, face, face, face, face, row],
            [block],
            part, *ry, *rx, second_stats, lift, grains, residual, q, z, tiles,
        )
        ry = trade(counts, 1, y_first, y_second)
        low_y, high_y = side_y.low(*ry), side_y.high(*ry)

        def edge_rows(index):
            middle = jnp.zeros((NODES - 2, NODES, 128), jnp.float32)
            return jnp.concatenate([low_y[index][None], middle, high_y[index][None]])

        both = (edge_rows(0), edge_rows(NODES - 1))
        rx = trade(
            counts, 0, fx[0] + side_x.send_first(*both), fx[1] + side_x.send_second(*both)
        )
        last_stats = gather_stats(stats)
        solution_out, residual_out, direction, steps = call(
            final_kernel, counts, "final", [block] * 3 + [(2,)], [],
            solution, residual, q, z, z1, u, *ry, *rx, second_stats, last_stats,
        )
        return (
            solution_out.reshape(shard_shape),
            residual_out.reshape(shard_shape),
            direction.reshape(shard_shape),
            steps,
        )

    return shards


def solution(mesh):
    counts = (mesh.shape["gx"], mesh.shape["gy"])
    return jax.shard_map(
        shards_of(counts),
        mesh=mesh,
        in_specs=(
            P("gx", "gy", None, None, None, None),
            P("gx", "gy", None, None, None, None),
            P("gx", "gy", None),
        ),
        out_specs=(
            P("gx", "gy", None, None, None, None),
            P("gx", "gy", None, None, None, None),
            P("gx", "gy", None, None, None, None),
            P(),
        ),
        check_vma=False,
    )
```

```python
import math

import jax
import jax.numpy as jnp
import numpy as np
from jax import lax
from jax.experimental import pallas as pl
from jax.experimental.pallas import tpu as pltpu
from jax.sharding import PartitionSpec as P

NODES = 8
MOST_GRAINS = 16
EXT = NODES + 2
ROWS = 112
MODES = 104
AXES = ("gx", "gy")

shift_mass = 0.1
mean_porosity = 0.7
exact_mode = lax.Precision.HIGHEST


def legendre_columns(node_set, degree):
    table = [node_set * 0.0 + 1.0, node_set]
    for order in range(2, degree + 1):
        table.append(
            ((2 * order - 1) * node_set * table[order - 1] - (order - 1) * table[order - 2]) / order
        )
    return table


def gll_tables():
    degree = NODES - 1
    node_set = np.cos(math.pi * np.arange(degree + 1) / degree)
    for sweep in range(100):
        table = legendre_columns(node_set, degree)
        node_set = node_set - (node_set * table[degree] - table[degree - 1]) / (
            (degree + 1) * table[degree]
        )
    node_set = node_set[::-1].copy()
    values = legendre_columns(node_set, degree)[degree]
    weights = 2.0 / (degree * (degree + 1) * values**2)
    derivative = np.zeros((NODES, NODES))
    for row_index in range(NODES):
        for column_index in range(NODES):
            if row_index != column_index:
                derivative[row_index, column_index] = values[row_index] / (
                    values[column_index] * (node_set[row_index] - node_set[column_index])
                )
    derivative[0, 0] = -degree * (degree + 1) / 4.0
    derivative[NODES - 1, NODES - 1] = degree * (degree + 1) / 4.0
    return (weights, derivative)


def jacobi_eigen(matrix):
    size_now = matrix.shape[0]
    current = matrix.copy()
    vectors = np.eye(size_now)
    for sweep in range(12):
        for first in range(size_now - 1):
            for second in range(first + 1, size_now):
                off_value = current[first, second]
                safe_value = np.where(off_value == 0.0, 1e-300, off_value)
                theta = (current[second, second] - current[first, first]) / (2.0 * safe_value)
                sign_value = np.where(theta >= 0.0, 1.0, -1.0)
                tangent = sign_value / (np.abs(theta) + np.sqrt(theta * theta + 1.0))
                cosine = 1.0 / np.sqrt(tangent * tangent + 1.0)
                sine = tangent * cosine
                rotation = np.eye(size_now)
                rotation[first, first] = cosine
                rotation[second, second] = cosine
                rotation[first, second] = sine
                rotation[second, first] = -sine
                current = rotation.T @ current @ rotation
                vectors = vectors @ rotation
    eigen_values = np.array([current[index, index] for index in range(size_now)])
    return (eigen_values, vectors)


def schwarz_tables():
    weights, derivative = gll_tables()
    stiffness = derivative.T @ (weights[:, None] * derivative)
    total_nodes = 3 * (NODES - 1) + 1
    three_stiffness = np.zeros((total_nodes, total_nodes))
    three_mass = np.zeros(total_nodes)
    for element in range(3):
        start_node = element * (NODES - 1)
        three_stiffness[
            start_node : start_node + NODES, start_node : start_node + NODES
        ] += stiffness
        three_mass[start_node : start_node + NODES] += weights
    chosen = np.array([NODES - 2] + list(range(NODES - 1, 2 * NODES - 1)) + [2 * NODES - 1])
    local_stiffness = three_stiffness[chosen][:, chosen]
    local_mass = three_mass[chosen]
    scaling = 1.0 / np.sqrt(local_mass)
    symmetric = scaling[:, None] * local_stiffness * scaling[None, :]
    symmetric = 0.5 * (symmetric + symmetric.T)
    eigen_values, eigen_vectors = jacobi_eigen(symmetric)
    return (scaling[:, None] * eigen_vectors, eigen_values)


WEIGHTS, DERIVATIVE = gll_tables()
STIFF = DERIVATIVE.T @ (WEIGHTS[:, None] * DERIVATIVE)
BASIS, EIGEN = schwarz_tables()


def plane_tables():
    forward = np.zeros((MODES, ROWS))
    inverse = np.zeros((MODES, EXT))
    for mode_b in range(EXT):
        for mode_c in range(EXT):
            mode = mode_b * EXT + mode_c
            for b in range(EXT):
                for k in range(NODES):
                    forward[mode, b * NODES + k] = BASIS[b, mode_b] * BASIS[k + 1, mode_c]
                forward[mode, 80 + b] = BASIS[b, mode_b] * BASIS[0, mode_c]
                forward[mode, 96 + b] = BASIS[b, mode_b] * BASIS[EXT - 1, mode_c]
            inverse[mode] = 1.0 / (
                mean_porosity * (EIGEN + EIGEN[mode_b] + EIGEN[mode_c]) + shift_mass
            )
    lanes = np.repeat(inverse.T[:, :, None], 128, axis=2)
    return (
        forward.astype(np.float32),
        forward.T.astype(np.float32).copy(),
        lanes.astype(np.float32),
    )


def tile_tables():
    table = np.zeros((NODES + 1, NODES, 128))
    table[0] = WEIGHTS[:, None]
    for shift in range(NODES):
        for k in range(NODES):
            table[1 + shift, k] = STIFF[k, (k - shift) % NODES]
    return table.astype(np.float32)


def share_table(count):
    table = np.zeros((count, 3, count))
    for column in range(count):
        table[column, :, column] = 1.0
        if column > 0:
            table[column, 0, column] = 0.5
            table[column, 0, column - 1] = 0.5
        if column < count - 1:
            table[column, 2, column] = 0.5
            table[column, 2, column + 1] = 0.5
    return table


def cosine_inverse(count):
    position = np.arange(count)
    basis = np.cos(math.pi * (position[:, None] + 0.5) * position[None, :] / count)
    basis = basis * np.where(position == 0, math.sqrt(1.0 / count), math.sqrt(2.0 / count))[None, :]
    return basis, 2.0 - 2.0 * np.cos(math.pi * position / count)


def shift_up(rows):
    lane = lax.broadcasted_iota(jnp.int32, rows.shape, 1)
    return jnp.where(lane == 0, 0.0, pltpu.roll(rows, 1, 1))


def shift_down(rows):
    lane = lax.broadcasted_iota(jnp.int32, rows.shape, 1)
    return jnp.where(lane == 127, 0.0, pltpu.roll(rows, 127, 1))


class Sides:
    def __init__(self, axis, count):
        self.index = lax.axis_index(axis)
        self.even = lax.rem(self.index, 2) == 0
        self.no_low = self.index == 0
        self.no_high = self.index == count - 1

    def low(self, first, second):
        return jnp.where(self.no_low, 0.0, jnp.where(self.even, second, first))

    def high(self, first, second):
        return jnp.where(self.no_high, 0.0, jnp.where(self.even, first, second))

    def send_first(self, low_face, high_face):
        return jnp.where(self.even, high_face, low_face)

    def send_second(self, low_face, high_face):
        return jnp.where(self.even, low_face, high_face)


def multiplicity_tile():
    row = lax.broadcasted_iota(jnp.int32, (NODES, 128), 0)
    lane = lax.broadcasted_iota(jnp.int32, (NODES, 128), 1)
    shared = ((row == 0) & (lane > 0)) | ((row == NODES - 1) & (lane < 127))
    return jnp.where(shared, 0.5, 1.0)


def class_of(node):
    return 0 if node == 0 else (2 if node == NODES - 1 else 1)


def axis_factor(node, side):
    if node == 0:
        return jnp.where(side.no_low, 1.0, 0.5)
    if node == NODES - 1:
        return jnp.where(side.no_high, 1.0, 0.5)
    return None


def scaled(value, *factors):
    for factor in factors:
        if factor is not None:
            value = value * factor
    return value


def add_to(total, key, value):
    total[key] = value if key not in total else total[key] + value


def lane_sums(tiles):
    columns = [jnp.sum(tile, axis=0, keepdims=True) for tile in tiles]
    columns.append(jnp.zeros((16 - len(tiles), 128), jnp.float32))
    sums = jnp.sum(jnp.concatenate(columns, axis=0), axis=1, keepdims=True)
    return jnp.broadcast_to(sums, (16, 128))


def write_stats(stats_ref, tiles):
    row = lax.broadcasted_iota(jnp.int32, (16, 128), 0)
    lane = lax.broadcasted_iota(jnp.int32, (16, 128), 1)
    sums = jnp.sum(jnp.where(row == lane, lane_sums(tiles), 0.0), axis=0, keepdims=True)
    for index in range(stats_ref.shape[0]):
        stats_ref[index] = jnp.broadcast_to(sums, stats_ref.shape[1:])


def stat_columns(stats, first, count):
    lane = lax.broadcasted_iota(jnp.int32, stats.shape, 1)
    sums = lane_sums([jnp.where(lane == first + i, stats, 0.0) for i in range(count)])
    return [sums[i : i + 1] for i in range(count)]


def sum_lanes(counts):
    return -(-(counts[0] * counts[1] + 2) // 128) * 128


def share_rows(counts, side_x, side_y):
    lane = lax.broadcasted_iota(jnp.int32, (1, sum_lanes(counts)), 1)
    column_y = lax.rem(lane, counts[1])
    first_x = lane - column_y

    def weights(side, place, step, count):
        own = jnp.where(place == side.index * step, 1.0, 0.0)
        below = jnp.where(place == (side.index - 1) * step, 1.0, 0.0)
        above = jnp.where(place == (side.index + 1) * step, 1.0, 0.0)
        return (
            jnp.where(side.no_low, own, 0.5 * (own + below)),
            own,
            jnp.where(side.no_high, own, 0.5 * (own + above)),
        )

    inside = lane < counts[0] * counts[1]
    along_x = weights(side_x, first_x, counts[1], counts[0])
    along_y = weights(side_y, column_y, 1, counts[1])
    return [jnp.where(inside, wx * wy, 0.0) for wx in along_x for wy in along_y]


def summed_row(counts, tiles, side_x, side_y):
    sums = lane_sums(tiles)
    lane = lax.broadcasted_iota(jnp.int32, (1, sum_lanes(counts)), 1)
    total = None
    for i, share in enumerate(share_rows(counts, side_x, side_y)):
        term = share * sums[i : i + 1, 0:1]
        total = term if total is None else total + term
    for i in range(9, len(tiles)):
        total = total + jnp.where(lane == counts[0] * counts[1] + i - 9, sums[i : i + 1, 0:1], 0.0)
    pieces = [total[:, at : at + 128] for at in range(0, sum_lanes(counts), 128)]
    pieces.append(jnp.zeros((NODES - len(pieces), 128), jnp.float32))
    return jnp.concatenate(pieces, axis=0)


def row_of(counts, tile_ref):
    rows = [tile_ref[i : i + 1, :] for i in range(sum_lanes(counts) // 128)]
    return rows[0] if len(rows) == 1 else jnp.concatenate(rows, axis=1)


def lifted_rows(counts, row, lift_ref):
    sums = jnp.sum(lift_ref[...] * row, axis=1, keepdims=True)
    return jnp.broadcast_to(sums, (16, 128))


def row_value(counts, row, index):
    lane = lax.broadcasted_iota(jnp.int32, row.shape, 1)
    chosen = jnp.where(lane == counts[0] * counts[1] + index, row, 0.0)
    return jnp.broadcast_to(jnp.sum(chosen, axis=1, keepdims=True), (1, 128))


def class_tiles(sums):
    return [sums[(i, j)] for i in range(3) for j in range(3)]


def start_kernel(counts, r_ref, sy_first, sy_second):
    side_x, side_y = Sides("gx", counts[0]), Sides("gy", counts[1])
    tile = multiplicity_tile()
    for a in range(NODES):
        low, high = r_ref[a, 1], r_ref[a, NODES - 2]
        sy_first[a] = side_y.send_first(low, high)
        sy_second[a] = side_y.send_second(low, high)
    sums = {}
    for a in range(NODES):
        for b in range(NODES):
            add_to(sums, (class_of(a), class_of(b)), r_ref[a, b])
    for (i, j), value in sums.items():
        a, b = (0, 1, NODES - 1)[i], (0, 1, NODES - 1)[j]
        sums[(i, j)] = scaled(value * tile, axis_factor(a, side_x), axis_factor(b, side_y))
    sy_first[NODES] = summed_row(counts, class_tiles(sums), side_x, side_y)


def planes(ref):
    return jnp.concatenate([ref[a] for a in range(EXT)], axis=1)


def local_solve(x_ref, h_ref, forward_ref, back_ref, inverse_ref, part_ref):
    zero = jnp.zeros((6, 128), jnp.float32)
    for a in range(EXT):
        x_ref[a, 80:90] = shift_up(x_ref[a, pl.ds(6, EXT, stride=NODES), :])
        x_ref[a, 96:106] = shift_down(x_ref[a, pl.ds(1, EXT, stride=NODES), :])
        x_ref[a, 90:96] = zero
        x_ref[a, 106:112] = zero
    spectrum = jnp.dot(
        forward_ref[...], planes(x_ref), precision=exact_mode, preferred_element_type=jnp.float32
    )
    for a in range(EXT):
        h_ref[a] = spectrum[:, a * 128 : (a + 1) * 128]
    for block in range(MODES // 8):
        rows = pl.ds(block * 8, 8)
        values = [h_ref[a, rows] for a in range(EXT)]
        modes = []
        for mode in range(EXT):
            total = values[0] * float(BASIS[0, mode])
            for a in range(1, EXT):
                total = total + values[a] * float(BASIS[a, mode])
            modes.append(total * inverse_ref[mode, rows])
        for a in range(EXT):
            total = modes[0] * float(BASIS[a, 0])
            for mode in range(1, EXT):
                total = total + modes[mode] * float(BASIS[a, mode])
            h_ref[a, rows] = total
    values = jnp.dot(
        back_ref[...], planes(h_ref), precision=exact_mode, preferred_element_type=jnp.float32
    )
    for a in range(EXT):
        part_ref[a] = values[:, a * 128 : (a + 1) * 128]
    for a in range(EXT):

        def layer(k):
            return (a, pl.ds(k, EXT, stride=NODES), slice(None))

        bottom, top = part_ref[layer(0)], part_ref[layer(NODES - 1)]
        part_ref[layer(0)] = bottom + shift_up(top)
        part_ref[layer(NODES - 1)] = top + shift_down(bottom)
        part_ref[layer(1)] = part_ref[layer(1)] + shift_up(part_ref[a, 96:106])
        part_ref[layer(NODES - 2)] = part_ref[layer(NODES - 2)] + shift_down(part_ref[a, 80:90])


def send_parts(part_ref, side_x, side_y, sy_first, sy_second, fx_first, fx_second):
    for a in range(EXT):
        low, high = part_ref[a, 0:16], part_ref[a, 64:80]
        sy_first[a] = side_y.send_first(low, high).reshape(2, NODES, 128)
        sy_second[a] = side_y.send_second(low, high).reshape(2, NODES, 128)
    for layer in range(2):
        low, high = part_ref[layer, 0:80], part_ref[NODES + layer, 0:80]
        fx_first[layer] = side_x.send_first(low, high).reshape(EXT, NODES, 128)
        fx_second[layer] = side_x.send_second(low, high).reshape(EXT, NODES, 128)


def first_solve_kernel(
    counts, r_ref, ry_first, ry_second, rx_first, rx_second, forward_ref, back_ref, inverse_ref,
    part_ref, sy_first, sy_second, fx_first, fx_second, x_ref, h_ref,
):
    side_x, side_y = Sides("gx", counts[0]), Sides("gy", counts[1])
    x_ref[0, 0:80] = side_x.low(rx_first[...], rx_second[...]).reshape(80, 128)
    x_ref[EXT - 1, 0:80] = side_x.high(rx_first[...], rx_second[...]).reshape(80, 128)
    for a in range(NODES):
        x_ref[a + 1, 0:8] = side_y.low(ry_first[a], ry_second[a])
        x_ref[a + 1, 8:72] = r_ref[a].reshape(64, 128)
        x_ref[a + 1, 72:80] = side_y.high(ry_first[a], ry_second[a])
    local_solve(x_ref, h_ref, forward_ref, back_ref, inverse_ref, part_ref)
    send_parts(part_ref, side_x, side_y, sy_first, sy_second, fx_first, fx_second)


def second_solve_kernel(
    counts, u_ref, ry_first, ry_second, rx_first, rx_second, forward_ref, back_ref, inverse_ref,
    q_ref, part_ref, sy_first, sy_second, fx_first, fx_second, x_ref, h_ref,
):
    side_x, side_y = Sides("gx", counts[0]), Sides("gy", counts[1])
    low_x = side_x.low(rx_first[...], rx_second[...])
    high_x = side_x.high(rx_first[...], rx_second[...])
    x_ref[0, 0:80] = low_x[0].reshape(80, 128)
    x_ref[EXT - 1, 0:80] = high_x[1].reshape(80, 128)
    for a in range(NODES):
        low_y = side_y.low(ry_first[a], ry_second[a])
        high_y = side_y.high(ry_first[a], ry_second[a])
        rows = [low_y[0]]
        for b in range(NODES):
            value = u_ref[a, b]
            if b == 0:
                value = value + low_y[1]
            if b == NODES - 1:
                value = value + high_y[0]
            rows.append(value)
        rows.append(high_y[1])
        for b in range(EXT):
            value = rows[b]
            if a == 0:
                value = value + low_x[1, b]
            if a == NODES - 1:
                value = value + high_x[0, b]
            x_ref[a + 1, b * 8 : b * 8 + 8] = value
            if 0 < b < EXT - 1:
                q_ref[a, b - 1] = value
    local_solve(x_ref, h_ref, forward_ref, back_ref, inverse_ref, part_ref)
    send_parts(part_ref, side_x, side_y, sy_first, sy_second, fx_first, fx_second)


def collect_parts(part_ref, ry_first, ry_second, rx_first, rx_second, side_x, side_y, field):
    low_x = side_x.low(rx_first[...], rx_second[...])
    high_x = side_x.high(rx_first[...], rx_second[...])
    result = {}
    for a in range(NODES):
        low_y = side_y.low(ry_first[a + 1], ry_second[a + 1])
        high_y = side_y.high(ry_first[a + 1], ry_second[a + 1])
        for b in range(NODES):
            value = part_ref[a + 1, (b + 1) * 8 : (b + 2) * 8]
            if b < 2:
                value = value + low_y[b]
            if b >= NODES - 2:
                value = value + high_y[b - (NODES - 2)]
            if a < 2:
                value = value + low_x[a, b]
            if a >= NODES - 2:
                value = value + high_x[a - (NODES - 2), b]
            node_class = 3 * class_of(a) + class_of(b)
            result[(a, b)] = value + field[node_class : node_class + 1, :]
    return result


def porosity_row(grains_ref):
    return 1.0 - 0.6 * grains_ref[...].astype(jnp.float32) / MOST_GRAINS


def apply_tiles(z_ref, u_ref, y_ref, tiles_ref, por):
    for a in range(NODES):
        for b in range(NODES):
            y_ref[a, b] = z_ref[a, b] * tiles_ref[0]
    for a in range(NODES):
        for b in range(NODES):
            z = z_ref[a, b]
            third = z * tiles_ref[1]
            for shift in range(1, NODES):
                third = third + pltpu.roll(z, shift, 0) * tiles_ref[1 + shift]
            first = y_ref[0, b] * float(STIFF[a, 0] * WEIGHTS[b])
            second = y_ref[a, 0] * float(STIFF[b, 0] * WEIGHTS[a])
            for other in range(1, NODES):
                first = first + y_ref[other, b] * float(STIFF[a, other] * WEIGHTS[b])
                second = second + y_ref[a, other] * float(STIFF[b, other] * WEIGHTS[a])
            weight = float(WEIGHTS[a] * WEIGHTS[b])
            u_ref[a, b] = por * (third * weight + first + second) + y_ref[a, b] * (
                shift_mass * weight
            )


def sum_column(u_ref):
    for a in range(NODES):
        bottom = u_ref[a, :, 0, :]
        top = u_ref[a, :, NODES - 1, :]
        u_ref[a, :, 0, :] = bottom + shift_up(top)
        u_ref[a, :, NODES - 1, :] = top + shift_down(bottom)


def first_apply_kernel(
    counts, part_ref, ry_first, ry_second, rx_first, rx_second, sum_ref, lift_ref, grains_ref,
    r_ref, tiles_ref, z_ref, u_ref, sy_first, sy_second, fx_first, fx_second, y_ref,
):
    side_x, side_y = Sides("gx", counts[0]), Sides("gy", counts[1])
    field = lifted_rows(counts, row_of(counts, sum_ref), lift_ref)
    z = collect_parts(part_ref, ry_first, ry_second, rx_first, rx_second, side_x, side_y, field)
    inner = None
    for (a, b), value in z.items():
        z_ref[a, b] = value
        term = scaled(value * r_ref[a, b], axis_factor(a, side_x), axis_factor(b, side_y))
        inner = term if inner is None else inner + term
    inner = inner * multiplicity_tile()
    apply_tiles(z_ref, u_ref, y_ref, tiles_ref, porosity_row(grains_ref))
    sums = {}
    curvature = None
    for a in range(NODES):
        for b in range(NODES):
            value = u_ref[a, b]
            add_to(sums, (class_of(a), class_of(b)), value)
            term = value * z_ref[a, b]
            curvature = term if curvature is None else curvature + term
    tiles = class_tiles(sums) + [inner, curvature]
    sy_first[2 * NODES] = summed_row(counts, tiles, side_x, side_y)
    sum_column(u_ref)
    for a in range(NODES):
        for layer in range(2):
            low, high = u_ref[a, layer], u_ref[a, NODES - 2 + layer]
            sy_first[2 * a + layer] = side_y.send_first(low, high)
            sy_second[2 * a + layer] = side_y.send_second(low, high)
    for layer in range(2):
        low, high = u_ref[layer], u_ref[NODES - 2 + layer]
        fx_first[layer] = side_x.send_first(low, high)
        fx_second[layer] = side_x.send_second(low, high)


def second_apply_kernel(
    counts, part_ref, ry_first, ry_second, rx_first, rx_second, sum_ref, lift_ref, grains_ref,
    r_ref, q_ref, z_ref, tiles_ref, z1_ref, u_ref, sy_first, sy_second, fx_first, fx_second, stats_ref, y_ref,
):
    side_x, side_y = Sides("gx", counts[0]), Sides("gy", counts[1])
    summed = row_of(counts, sum_ref)
    field = lifted_rows(counts, summed, lift_ref)
    step = row_value(counts, summed, 0) / row_value(counts, summed, 1)
    w = collect_parts(part_ref, ry_first, ry_second, rx_first, rx_second, side_x, side_y, field)
    inner = None
    for (a, b), value in w.items():
        next_z = z_ref[a, b] - step * value
        next_r = r_ref[a, b] - step * q_ref[a, b]
        z1_ref[a, b] = next_z
        term = scaled(next_z * next_r, axis_factor(a, side_x), axis_factor(b, side_y))
        inner = term if inner is None else inner + term
    inner = inner * multiplicity_tile()
    apply_tiles(z1_ref, u_ref, y_ref, tiles_ref, porosity_row(grains_ref))
    own = None
    cross = None
    for a in range(NODES):
        for b in range(NODES):
            value = u_ref[a, b]
            own_term = value * z1_ref[a, b]
            cross_term = value * z_ref[a, b]
            own = own_term if own is None else own + own_term
            cross = cross_term if cross is None else cross + cross_term
    write_stats(stats_ref, [inner, own, cross])
    sum_column(u_ref)
    for a in range(NODES):
        low, high = u_ref[a, 0], u_ref[a, NODES - 1]
        sy_first[a] = side_y.send_first(low, high)
        sy_second[a] = side_y.send_second(low, high)
    low, high = u_ref[0], u_ref[NODES - 1]
    fx_first[...] = side_x.send_first(low, high)
    fx_second[...] = side_x.send_second(low, high)


def final_kernel(
    counts, sol_ref, r_ref, q_ref, z_ref, z1_ref, u_ref, ry_first, ry_second, rx_first, rx_second,
    sum_ref, last_ref, sol_out, r_out, d_out, steps_out,
):
    side_x, side_y = Sides("gx", counts[0]), Sides("gy", counts[1])
    summed = row_of(counts, sum_ref)
    first_inner, first_curvature = row_value(counts, summed, 0), row_value(counts, summed, 1)
    second_inner, own, cross = stat_columns(last_ref[:, 0, :], 0, 3)
    first_step = first_inner / first_curvature
    ratio = second_inner / first_inner
    second_step = second_inner / (own + ratio * (2.0 * cross + ratio * first_curvature))
    steps_out[0] = first_step[0, 0]
    steps_out[1] = second_step[0, 0]
    low_x = side_x.low(rx_first[...], rx_second[...])
    high_x = side_x.high(rx_first[...], rx_second[...])
    for a in range(NODES):
        for b in range(NODES):
            image = u_ref[a, b]
            if b == 0:
                image = image + side_y.low(ry_first[a], ry_second[a])
            if b == NODES - 1:
                image = image + side_y.high(ry_first[a], ry_second[a])
            if a == 0:
                image = image + low_x[b]
            if a == NODES - 1:
                image = image + high_x[b]
            z, q = z_ref[a, b], q_ref[a, b]
            direction = z1_ref[a, b] + ratio * z
            image = image + ratio * q
            d_out[a, b] = direction
            sol_out[a, b] = sol_ref[a, b] + first_step * z + second_step * direction
            r_out[a, b] = r_ref[a, b] - first_step * q - second_step * image


def call(kernel, counts, name, shapes, scratch, *operands):
    def body(*refs):
        kernel(counts, *refs)

    def space(shape):
        return pltpu.SMEM if len(shape) == 1 else pltpu.VMEM

    return pl.pallas_call(
        body,
        name=name,
        out_shape=[jax.ShapeDtypeStruct(shape, jnp.float32) for shape in shapes],
        in_specs=[pl.BlockSpec(memory_space=pltpu.VMEM)] * len(operands),
        out_specs=[pl.BlockSpec(memory_space=space(shape)) for shape in shapes],
        scratch_shapes=[pltpu.VMEM(shape, jnp.float32) for shape in scratch],
        compiler_params=pltpu.CompilerParams(vmem_limit_bytes=24 * 1024 * 1024),
    )(*operands)


def swap_pairs(counts, axis, parity):
    count_x, count_y = counts
    pairs = []
    for x in range(count_x):
        for y in range(count_y):
            if axis == 0:
                to = ((x + 1 if x % 2 == parity else x - 1) % count_x, y)
            else:
                other = y + 1 if y % 2 == parity else y - 1
                to = (x, other) if 0 <= other < count_y else (x ^ 1, y)
            pairs.append((x * count_y + y, to[0] * count_y + to[1]))
    return pairs


def trade(counts, axis, first, second):
    return (
        lax.ppermute(first, AXES, swap_pairs(counts, axis, 0)),
        lax.ppermute(second, AXES, swap_pairs(counts, axis, 1)),
    )


def trade_far(counts, value, far_x, far_y):
    pairs = [
        (x * counts[1] + y, (x ^ far_x) * counts[1] + (y ^ far_y))
        for x in range(counts[0])
        for y in range(counts[1])
    ]
    return lax.ppermute(value, AXES, pairs)


class RunningSum:
    def __init__(self, counts, tile):
        self.counts = counts
        self.carried = counts == (8, 4)
        self.value = tile if self.carried else lax.psum(tile, AXES)

    def add(self, received):
        if self.carried:
            self.value = self.value + received

    def far(self, *steps):
        return [trade_far(self.counts, self.value, *step) for step in steps if self.carried]


def carry(tiles, running):
    return jnp.concatenate([tiles.reshape((-1, NODES, 128)), running.value[None]])


def carried(received, shape):
    return received[:-1].reshape(shape), received[-1]


def gather_stats(stats):
    return lax.all_to_all(stats, AXES, 0, 0)


def lift_tables(counts, column_length):
    share_x, share_y = share_table(counts[0]), share_table(counts[1])
    basis_x, eigen_x = cosine_inverse(counts[0])
    basis_y, eigen_y = cosine_inverse(counts[1])
    divisor = (
        2.0 * mean_porosity * column_length * (eigen_x[:, None] + eigen_y[None, :])
        + 8.0 * shift_mass * column_length
    )
    modes_x = np.einsum("xip,pa->xia", share_x, basis_x)
    modes_y = np.einsum("yjq,qb->yjb", share_y, basis_y)
    total = counts[0] * counts[1]
    to_modes = np.einsum("pa,qb->abpq", basis_x, basis_y).reshape(total, total)
    to_modes = np.pad(to_modes, ((0, 0), (0, sum_lanes(counts) - total)))
    return [table.astype(np.float32) for table in (modes_x, modes_y, 1.0 / divisor, to_modes)]


def own_lift(tables):
    modes_x, modes_y, inverse, to_modes = [jnp.asarray(table) for table in tables]
    own_x = lax.dynamic_index_in_dim(modes_x, lax.axis_index("gx"), 0, keepdims=False)
    own_y = lax.dynamic_index_in_dim(modes_y, lax.axis_index("gy"), 0, keepdims=False)
    own = own_x[:, None, :, None] * own_y[None, :, None, :] * inverse[None, None]
    lift = jnp.dot(own.reshape(9, -1), to_modes, precision=exact_mode)
    return jnp.pad(lift, ((0, 7), (0, 0)))


def shards_of(counts):
    forward_np, back_np, inverse_np = plane_tables()
    tiles_np = tile_tables()

    def shards(solution, residual, grain_counts):
        shard_shape = solution.shape
        block = shard_shape[2:]
        solution = solution.reshape(block)
        residual = residual.reshape(block)
        lift = own_lift(lift_tables(counts, block[-1]))
        grains = grain_counts.reshape(1, 128)
        plane = [jnp.asarray(table) for table in (forward_np, back_np, inverse_np)]
        tiles = jnp.asarray(tiles_np)
        side_x, side_y = Sides("gx", counts[0]), Sides("gy", counts[1])
        row = (counts[0] * counts[1], 4, 128)
        face = (NODES, NODES, 128)
        part_shapes = [
            (EXT, ROWS, 128),
            (EXT, 2, NODES, 128), (EXT, 2, NODES, 128),
            (2, EXT, NODES, 128), (2, EXT, NODES, 128),
        ]
        solve_scratch = [(EXT, ROWS, 128), (EXT, MODES, 128)]

        y_first, y_second = call(
            start_kernel, counts, "start", [(NODES + 1,) + face[1:], face], [], residual
        )
        running = RunningSum(counts, y_first[-1])
        ry = trade(counts, 1, y_first, y_second)
        ry_first, tile = carried(ry[0], face)
        running.add(tile)
        ry = (ry_first, ry[1])
        low_y, high_y = side_y.low(*ry), side_y.high(*ry)

        def with_layers(index):
            return jnp.concatenate([low_y[index][None], residual[index], high_y[index][None]])

        low_face, high_face = with_layers(1), with_layers(NODES - 2)
        rx = trade(
            counts, 0, carry(side_x.send_first(low_face, high_face), running),
            side_x.send_second(low_face, high_face),
        )
        rx, far = lax.optimization_barrier((rx, running.far((4, 0), (5, 0))))
        rx_first, tile = carried(rx[0], low_face.shape)
        for value in [tile] + far:
            running.add(value)
        rx = (rx_first, rx[1])
        part, y_first, y_second, *fx = call(
            first_solve_kernel, counts, "first_solve", part_shapes, solve_scratch,
            residual, *ry, *rx, *plane,
        )

        def spread_faces(fx, ry):
            low_y, high_y = side_y.low(*ry), side_y.high(*ry)
            middle = jnp.zeros((2, NODES - 4, NODES, 128), jnp.float32)
            both = [
                jnp.concatenate([low_y[at], middle, high_y[at]], axis=1)
                for at in (slice(0, 2), slice(8, 10))
            ]
            return (
                fx[0][:, 1:-1] + side_x.send_first(*both),
                fx[1][:, 1:-1] + side_x.send_second(*both),
            )

        def trade_spread(y_first, y_second, fx, running):
            ry = trade(counts, 1, y_first, y_second)
            for value in running.far((0, 2)):
                running.add(value)
            first, second = spread_faces(fx, ry)
            rx = trade(counts, 0, first, carry(second, running))
            rx_second, tile = carried(rx[1], second.shape)
            running.add(tile)
            return ry, (rx[0], rx_second)

        ry, rx = trade_spread(y_first, y_second, fx, running)
        z, u, y_first, y_second, *fx = call(
            first_apply_kernel, counts, "first_apply",
            [block, block, (2 * NODES + 1, NODES, 128), (2 * NODES, NODES, 128),
             (2, NODES, NODES, 128), (2, NODES, NODES, 128)],
            [block],
            part, *ry, *rx, running.value, lift, grains, residual, tiles,
        )
        running = RunningSum(counts, y_first[-1])
        ry = trade(counts, 1, y_first, y_second)
        two = (NODES, 2, NODES, 128)
        ry_first, tile = carried(ry[0], two)
        running.add(tile)
        ry = (ry_first, ry[1].reshape(two))
        low_y, high_y = side_y.low(*ry), side_y.high(*ry)

        def image_faces(index):
            middle = jnp.zeros((2, NODES - 2, NODES, 128), jnp.float32)
            return jnp.concatenate([low_y[index], middle, high_y[index]], axis=1)

        pads = ((0, 0), (1, 1), (0, 0), (0, 0))
        both = (image_faces(slice(0, 2)), image_faces(slice(NODES - 2, NODES)))
        first = jnp.pad(fx[0], pads) + side_x.send_first(*both)
        second = jnp.pad(fx[1], pads) + side_x.send_second(*both)
        rx = trade(counts, 0, carry(first, running), second)
        rx, far = lax.optimization_barrier((rx, running.far((4, 0), (5, 0))))
        rx_first, tile = carried(rx[0], first.shape)
        for value in [tile] + far:
            running.add(value)
        rx = (rx_first, rx[1])
        q, part, y_first, y_second, *fx = call(
            second_solve_kernel, counts, "second_solve", [block] + part_shapes, solve_scratch,
            u, *ry, *rx, *plane,
        )
        ry, rx = trade_spread(y_first, y_second, fx, running)
        z1, u, y_first, y_second, *fx, stats = call(
            second_apply_kernel, counts, "second_apply",
            [block, block, face, face, face, face, row],
            [block],
            part, *ry, *rx, running.value, lift, grains, residual, q, z, tiles,
        )
        ry = trade(counts, 1, y_first, y_second)
        low_y, high_y = side_y.low(*ry), side_y.high(*ry)

        def edge_rows(index):
            middle = jnp.zeros((NODES - 2, NODES, 128), jnp.float32)
            return jnp.concatenate([low_y[index][None], middle, high_y[index][None]])

        both = (edge_rows(0), edge_rows(NODES - 1))
        rx = trade(
            counts, 0, fx[0] + side_x.send_first(*both), fx[1] + side_x.send_second(*both)
        )
        last_stats = gather_stats(stats)
        solution_out, residual_out, direction, steps = call(
            final_kernel, counts, "final", [block] * 3 + [(2,)], [],
            solution, residual, q, z, z1, u, *ry, *rx, running.value, last_stats,
        )
        return (
            solution_out.reshape(shard_shape),
            residual_out.reshape(shard_shape),
            direction.reshape(shard_shape),
            steps,
        )

    return shards


def solution(mesh):
    counts = (mesh.shape["gx"], mesh.shape["gy"])
    return jax.shard_map(
        shards_of(counts),
        mesh=mesh,
        in_specs=(
            P("gx", "gy", None, None, None, None),
            P("gx", "gy", None, None, None, None),
            P("gx", "gy", None),
        ),
        out_specs=(
            P("gx", "gy", None, None, None, None),
            P("gx", "gy", None, None, None, None),
            P("gx", "gy", None, None, None, None),
            P(),
        ),
        check_vma=False,
    )
```

```python
import math

import jax
import jax.numpy as jnp
import numpy as np
from jax import lax
from jax.experimental import pallas as pl
from jax.experimental.pallas import tpu as pltpu
from jax.sharding import PartitionSpec as P

NODES = 8
MOST_GRAINS = 16
EXT = NODES + 2
ROWS = 112
MODES = 104
AXES = ("gx", "gy")

shift_mass = 0.1
mean_porosity = 0.7
exact_mode = lax.Precision.HIGHEST
plane_mode = lax.Precision.HIGH


def legendre_columns(node_set, degree):
    table = [node_set * 0.0 + 1.0, node_set]
    for order in range(2, degree + 1):
        table.append(
            ((2 * order - 1) * node_set * table[order - 1] - (order - 1) * table[order - 2]) / order
        )
    return table


def gll_tables():
    degree = NODES - 1
    node_set = np.cos(math.pi * np.arange(degree + 1) / degree)
    for sweep in range(100):
        table = legendre_columns(node_set, degree)
        node_set = node_set - (node_set * table[degree] - table[degree - 1]) / (
            (degree + 1) * table[degree]
        )
    node_set = node_set[::-1].copy()
    values = legendre_columns(node_set, degree)[degree]
    weights = 2.0 / (degree * (degree + 1) * values**2)
    derivative = np.zeros((NODES, NODES))
    for row_index in range(NODES):
        for column_index in range(NODES):
            if row_index != column_index:
                derivative[row_index, column_index] = values[row_index] / (
                    values[column_index] * (node_set[row_index] - node_set[column_index])
                )
    derivative[0, 0] = -degree * (degree + 1) / 4.0
    derivative[NODES - 1, NODES - 1] = degree * (degree + 1) / 4.0
    return (weights, derivative)


def jacobi_eigen(matrix):
    size_now = matrix.shape[0]
    current = matrix.copy()
    vectors = np.eye(size_now)
    for sweep in range(12):
        for first in range(size_now - 1):
            for second in range(first + 1, size_now):
                off_value = current[first, second]
                safe_value = np.where(off_value == 0.0, 1e-300, off_value)
                theta = (current[second, second] - current[first, first]) / (2.0 * safe_value)
                sign_value = np.where(theta >= 0.0, 1.0, -1.0)
                tangent = sign_value / (np.abs(theta) + np.sqrt(theta * theta + 1.0))
                cosine = 1.0 / np.sqrt(tangent * tangent + 1.0)
                sine = tangent * cosine
                rotation = np.eye(size_now)
                rotation[first, first] = cosine
                rotation[second, second] = cosine
                rotation[first, second] = sine
                rotation[second, first] = -sine
                current = rotation.T @ current @ rotation
                vectors = vectors @ rotation
    eigen_values = np.array([current[index, index] for index in range(size_now)])
    return (eigen_values, vectors)


def schwarz_tables():
    weights, derivative = gll_tables()
    stiffness = derivative.T @ (weights[:, None] * derivative)
    total_nodes = 3 * (NODES - 1) + 1
    three_stiffness = np.zeros((total_nodes, total_nodes))
    three_mass = np.zeros(total_nodes)
    for element in range(3):
        start_node = element * (NODES - 1)
        three_stiffness[
            start_node : start_node + NODES, start_node : start_node + NODES
        ] += stiffness
        three_mass[start_node : start_node + NODES] += weights
    chosen = np.array([NODES - 2] + list(range(NODES - 1, 2 * NODES - 1)) + [2 * NODES - 1])
    local_stiffness = three_stiffness[chosen][:, chosen]
    local_mass = three_mass[chosen]
    scaling = 1.0 / np.sqrt(local_mass)
    symmetric = scaling[:, None] * local_stiffness * scaling[None, :]
    symmetric = 0.5 * (symmetric + symmetric.T)
    eigen_values, eigen_vectors = jacobi_eigen(symmetric)
    return (scaling[:, None] * eigen_vectors, eigen_values)


WEIGHTS, DERIVATIVE = gll_tables()
STIFF = DERIVATIVE.T @ (WEIGHTS[:, None] * DERIVATIVE)
BASIS, EIGEN = schwarz_tables()
PARITY = {
    sign: [mode for mode in range(EXT) if BASIS[0, mode] * BASIS[EXT - 1, mode] * sign > 0]
    for sign in (1, -1)
}


def plane_tables():
    forward = np.zeros((MODES, ROWS))
    inverse = np.zeros((MODES, EXT))
    for mode_b in range(EXT):
        for mode_c in range(EXT):
            mode = mode_b * EXT + mode_c
            for b in range(EXT):
                for k in range(NODES):
                    forward[mode, b * NODES + k] = BASIS[b, mode_b] * BASIS[k + 1, mode_c]
                forward[mode, 80 + b] = BASIS[b, mode_b] * BASIS[0, mode_c]
                forward[mode, 96 + b] = BASIS[b, mode_b] * BASIS[EXT - 1, mode_c]
            inverse[mode] = 1.0 / (
                mean_porosity * (EIGEN + EIGEN[mode_b] + EIGEN[mode_c]) + shift_mass
            )
    lanes = np.repeat(inverse.T[:, :, None], 128, axis=2)
    return (
        forward.astype(np.float32),
        forward.T.astype(np.float32).copy(),
        lanes.astype(np.float32),
    )


def row_tile(values):
    row = lax.broadcasted_iota(jnp.int32, (NODES, 128), 0)
    tile = jnp.full((NODES, 128), float(values[0]), jnp.float32)
    for k in range(1, NODES):
        tile = jnp.where(row == k, float(values[k]), tile)
    return tile


def share_table(count):
    table = np.zeros((count, 3, count))
    for column in range(count):
        table[column, :, column] = 1.0
        if column > 0:
            table[column, 0, column] = 0.5
            table[column, 0, column - 1] = 0.5
        if column < count - 1:
            table[column, 2, column] = 0.5
            table[column, 2, column + 1] = 0.5
    return table


def cosine_inverse(count):
    position = np.arange(count)
    basis = np.cos(math.pi * (position[:, None] + 0.5) * position[None, :] / count)
    basis = basis * np.where(position == 0, math.sqrt(1.0 / count), math.sqrt(2.0 / count))[None, :]
    return basis, 2.0 - 2.0 * np.cos(math.pi * position / count)


def shift_up(rows):
    lane = lax.broadcasted_iota(jnp.int32, rows.shape, 1)
    return jnp.where(lane == 0, 0.0, pltpu.roll(rows, 1, 1))


def shift_down(rows):
    lane = lax.broadcasted_iota(jnp.int32, rows.shape, 1)
    return jnp.where(lane == 127, 0.0, pltpu.roll(rows, 127, 1))


class Sides:
    def __init__(self, axis, count):
        self.index = lax.axis_index(axis)
        self.even = lax.rem(self.index, 2) == 0
        self.no_low = self.index == 0
        self.no_high = self.index == count - 1

    def low(self, first, second):
        return jnp.where(self.no_low, 0.0, jnp.where(self.even, second, first))

    def high(self, first, second):
        return jnp.where(self.no_high, 0.0, jnp.where(self.even, first, second))

    def send_first(self, low_face, high_face):
        return jnp.where(self.even, high_face, low_face)

    def send_second(self, low_face, high_face):
        return jnp.where(self.even, low_face, high_face)


def multiplicity_tile():
    row = lax.broadcasted_iota(jnp.int32, (NODES, 128), 0)
    lane = lax.broadcasted_iota(jnp.int32, (NODES, 128), 1)
    shared = ((row == 0) & (lane > 0)) | ((row == NODES - 1) & (lane < 127))
    return jnp.where(shared, 0.5, 1.0)


def class_of(node):
    return 0 if node == 0 else (2 if node == NODES - 1 else 1)


def axis_factor(node, side):
    if node == 0:
        return jnp.where(side.no_low, 1.0, 0.5)
    if node == NODES - 1:
        return jnp.where(side.no_high, 1.0, 0.5)
    return None


def scaled(value, *factors):
    for factor in factors:
        if factor is not None:
            value = value * factor
    return value


def add_to(total, key, value):
    total[key] = value if key not in total else total[key] + value


def lane_sums(tiles):
    columns = [jnp.sum(tile, axis=0, keepdims=True) for tile in tiles]
    columns.append(jnp.zeros((16 - len(tiles), 128), jnp.float32))
    sums = jnp.sum(jnp.concatenate(columns, axis=0), axis=1, keepdims=True)
    return jnp.broadcast_to(sums, (16, 128))


def write_stats(stats_ref, tiles):
    row = lax.broadcasted_iota(jnp.int32, (16, 128), 0)
    lane = lax.broadcasted_iota(jnp.int32, (16, 128), 1)
    sums = jnp.sum(jnp.where(row == lane, lane_sums(tiles), 0.0), axis=0, keepdims=True)
    for index in range(stats_ref.shape[0]):
        stats_ref[index] = jnp.broadcast_to(sums, stats_ref.shape[1:])


def stat_columns(stats, first, count):
    lane = lax.broadcasted_iota(jnp.int32, stats.shape, 1)
    sums = lane_sums([jnp.where(lane == first + i, stats, 0.0) for i in range(count)])
    return [sums[i : i + 1] for i in range(count)]


def sum_lanes(counts):
    return -(-(counts[0] * counts[1] + 2) // 128) * 128


def share_rows(counts, side_x, side_y):
    lane = lax.broadcasted_iota(jnp.int32, (1, sum_lanes(counts)), 1)
    column_y = lax.rem(lane, counts[1])
    first_x = lane - column_y

    def weights(side, place, step, count):
        own = jnp.where(place == side.index * step, 1.0, 0.0)
        below = jnp.where(place == (side.index - 1) * step, 1.0, 0.0)
        above = jnp.where(place == (side.index + 1) * step, 1.0, 0.0)
        return (
            jnp.where(side.no_low, own, 0.5 * (own + below)),
            own,
            jnp.where(side.no_high, own, 0.5 * (own + above)),
        )

    inside = lane < counts[0] * counts[1]
    along_x = weights(side_x, first_x, counts[1], counts[0])
    along_y = weights(side_y, column_y, 1, counts[1])
    return [jnp.where(inside, wx * wy, 0.0) for wx in along_x for wy in along_y]


def summed_row(counts, tiles, side_x, side_y):
    sums = lane_sums(tiles)
    lane = lax.broadcasted_iota(jnp.int32, (1, sum_lanes(counts)), 1)
    total = None
    for i, share in enumerate(share_rows(counts, side_x, side_y)):
        term = share * sums[i : i + 1, 0:1]
        total = term if total is None else total + term
    for i in range(9, len(tiles)):
        total = total + jnp.where(lane == counts[0] * counts[1] + i - 9, sums[i : i + 1, 0:1], 0.0)
    pieces = [total[:, at : at + 128] for at in range(0, sum_lanes(counts), 128)]
    pieces.append(jnp.zeros((NODES - len(pieces), 128), jnp.float32))
    return jnp.concatenate(pieces, axis=0)


def row_of(counts, tile_ref):
    rows = [tile_ref[i : i + 1, :] for i in range(sum_lanes(counts) // 128)]
    return rows[0] if len(rows) == 1 else jnp.concatenate(rows, axis=1)


def lifted_rows(counts, row, lift_ref):
    sums = jnp.sum(lift_ref[...] * row, axis=1, keepdims=True)
    return jnp.broadcast_to(sums, (16, 128))


def row_value(counts, row, index):
    lane = lax.broadcasted_iota(jnp.int32, row.shape, 1)
    chosen = jnp.where(lane == counts[0] * counts[1] + index, row, 0.0)
    return jnp.broadcast_to(jnp.sum(chosen, axis=1, keepdims=True), (1, 128))


def class_tiles(sums):
    return [sums[(i, j)] for i in range(3) for j in range(3)]


def start_kernel(counts, r_ref, sy_first, sy_second):
    side_x, side_y = Sides("gx", counts[0]), Sides("gy", counts[1])
    tile = multiplicity_tile()
    for a in range(NODES):
        low, high = r_ref[a, 1], r_ref[a, NODES - 2]
        sy_first[a] = side_y.send_first(low, high)
        sy_second[a] = side_y.send_second(low, high)
    sums = {}
    for a in range(NODES):
        for b in range(NODES):
            add_to(sums, (class_of(a), class_of(b)), r_ref[a, b])
    for (i, j), value in sums.items():
        a, b = (0, 1, NODES - 1)[i], (0, 1, NODES - 1)[j]
        sums[(i, j)] = scaled(value * tile, axis_factor(a, side_x), axis_factor(b, side_y))
    sy_first[NODES] = summed_row(counts, class_tiles(sums), side_x, side_y)


def planes(ref):
    return jnp.concatenate([ref[a] for a in range(EXT)], axis=1)


def local_solve(x_ref, forward_ref, back_ref, inverse_ref, part_ref):
    zero = jnp.zeros((6, 128), jnp.float32)
    for a in range(EXT):
        x_ref[a, 80:90] = shift_up(x_ref[a, pl.ds(6, EXT, stride=NODES), :])
        x_ref[a, 96:106] = shift_down(x_ref[a, pl.ds(1, EXT, stride=NODES), :])
        x_ref[a, 90:96] = zero
        x_ref[a, 106:112] = zero
    half = EXT // 2
    for block in range(ROWS // 8):
        rows = pl.ds(block * 8, 8)
        low = [x_ref[a, rows] for a in range(half)]
        high = [x_ref[EXT - 1 - a, rows] for a in range(half)]
        folded = {1: [x + y for x, y in zip(low, high)], -1: [x - y for x, y in zip(low, high)]}
        for sign in (1, -1):
            for mode in PARITY[sign]:
                total = folded[sign][0] * float(BASIS[0, mode])
                for a in range(1, half):
                    total = total + folded[sign][a] * float(BASIS[a, mode])
                x_ref[mode, rows] = total
    spectrum = jnp.dot(
        forward_ref[...], planes(x_ref), precision=plane_mode, preferred_element_type=jnp.float32
    ) * planes(inverse_ref)
    values = jnp.dot(
        back_ref[...], spectrum, precision=plane_mode, preferred_element_type=jnp.float32
    )
    for block in range(ROWS // 8):
        rows = pl.ds(block * 8, 8)
        modes = [values[block * 8 : block * 8 + 8, m * 128 : (m + 1) * 128] for m in range(EXT)]
        back = {}
        for sign in (1, -1):
            for a in range(half):
                total = None
                for mode in PARITY[sign]:
                    term = modes[mode] * float(BASIS[a, mode])
                    total = term if total is None else total + term
                back[(sign, a)] = total
        for a in range(half):
            part_ref[a, rows] = back[(1, a)] + back[(-1, a)]
            part_ref[EXT - 1 - a, rows] = back[(1, a)] - back[(-1, a)]
    for a in range(EXT):

        def layer(k):
            return (a, pl.ds(k, EXT, stride=NODES), slice(None))

        bottom, top = part_ref[layer(0)], part_ref[layer(NODES - 1)]
        part_ref[layer(0)] = bottom + shift_up(top)
        part_ref[layer(NODES - 1)] = top + shift_down(bottom)
        part_ref[layer(1)] = part_ref[layer(1)] + shift_up(part_ref[a, 96:106])
        part_ref[layer(NODES - 2)] = part_ref[layer(NODES - 2)] + shift_down(part_ref[a, 80:90])


def send_parts(part_ref, side_x, side_y, sy_first, sy_second, fx_first, fx_second):
    for a in range(EXT):
        low, high = part_ref[a, 0:16], part_ref[a, 64:80]
        sy_first[a] = side_y.send_first(low, high).reshape(2, NODES, 128)
        sy_second[a] = side_y.send_second(low, high).reshape(2, NODES, 128)
    for layer in range(2):
        low, high = part_ref[layer, 0:80], part_ref[NODES + layer, 0:80]
        fx_first[layer] = side_x.send_first(low, high).reshape(EXT, NODES, 128)
        fx_second[layer] = side_x.send_second(low, high).reshape(EXT, NODES, 128)


def first_solve_kernel(
    counts, r_ref, grains_ref, ry_first, ry_second, rx_first, rx_second, forward_ref, back_ref,
    inverse_ref, part_ref, sy_first, sy_second, fx_first, fx_second, porosity_ref, x_ref,
):
    porosity_ref[...] = 1.0 - 0.6 * grains_ref[...].astype(jnp.float32) / MOST_GRAINS
    side_x, side_y = Sides("gx", counts[0]), Sides("gy", counts[1])
    x_ref[0, 0:80] = side_x.low(rx_first[...], rx_second[...]).reshape(80, 128)
    x_ref[EXT - 1, 0:80] = side_x.high(rx_first[...], rx_second[...]).reshape(80, 128)
    for a in range(NODES):
        x_ref[a + 1, 0:8] = side_y.low(ry_first[a], ry_second[a])
        x_ref[a + 1, 8:72] = r_ref[a].reshape(64, 128)
        x_ref[a + 1, 72:80] = side_y.high(ry_first[a], ry_second[a])
    local_solve(x_ref, forward_ref, back_ref, inverse_ref, part_ref)
    send_parts(part_ref, side_x, side_y, sy_first, sy_second, fx_first, fx_second)


def second_solve_kernel(
    counts, u_ref, ry_first, ry_second, rx_first, rx_second, forward_ref, back_ref, inverse_ref,
    q_ref, part_ref, sy_first, sy_second, fx_first, fx_second, x_ref,
):
    side_x, side_y = Sides("gx", counts[0]), Sides("gy", counts[1])
    low_x = side_x.low(rx_first[...], rx_second[...])
    high_x = side_x.high(rx_first[...], rx_second[...])
    x_ref[0, 0:80] = low_x[0].reshape(80, 128)
    x_ref[EXT - 1, 0:80] = high_x[1].reshape(80, 128)
    for a in range(NODES):
        low_y = side_y.low(ry_first[a], ry_second[a])
        high_y = side_y.high(ry_first[a], ry_second[a])
        rows = [low_y[0]]
        for b in range(NODES):
            value = u_ref[a, b]
            if b == 0:
                value = value + low_y[1]
            if b == NODES - 1:
                value = value + high_y[0]
            rows.append(value)
        rows.append(high_y[1])
        for b in range(EXT):
            value = rows[b]
            if a == 0:
                value = value + low_x[1, b]
            if a == NODES - 1:
                value = value + high_x[0, b]
            x_ref[a + 1, b * 8 : b * 8 + 8] = value
            if 0 < b < EXT - 1:
                q_ref[a, b - 1] = value
    local_solve(x_ref, forward_ref, back_ref, inverse_ref, part_ref)
    send_parts(part_ref, side_x, side_y, sy_first, sy_second, fx_first, fx_second)


def collect_parts(part_ref, ry_first, ry_second, rx_first, rx_second, side_x, side_y, field):
    low_x = side_x.low(rx_first[...], rx_second[...])
    high_x = side_x.high(rx_first[...], rx_second[...])
    result = {}
    for a in range(NODES):
        low_y = side_y.low(ry_first[a + 1], ry_second[a + 1])
        high_y = side_y.high(ry_first[a + 1], ry_second[a + 1])
        for b in range(NODES):
            value = part_ref[a + 1, (b + 1) * 8 : (b + 2) * 8]
            if b < 2:
                value = value + low_y[b]
            if b >= NODES - 2:
                value = value + high_y[b - (NODES - 2)]
            if a < 2:
                value = value + low_x[a, b]
            if a >= NODES - 2:
                value = value + high_x[a - (NODES - 2), b]
            node_class = 3 * class_of(a) + class_of(b)
            result[(a, b)] = value + field[node_class : node_class + 1, :]
    return result


def apply_tiles(z_ref, u_ref, y_ref, por):
    weight_tile = row_tile(WEIGHTS)
    stiff_tiles = [
        row_tile([STIFF[k, (k - shift) % NODES] for k in range(NODES)]) for shift in range(NODES)
    ]
    for a in range(NODES):
        for b in range(NODES):
            y_ref[a, b] = z_ref[a, b] * weight_tile
    for a in range(NODES):
        for b in range(NODES):
            z = z_ref[a, b]
            third = z * stiff_tiles[0]
            for shift in range(1, NODES):
                third = third + pltpu.roll(z, shift, 0) * stiff_tiles[shift]
            first = y_ref[0, b] * float(STIFF[a, 0] * WEIGHTS[b])
            second = y_ref[a, 0] * float(STIFF[b, 0] * WEIGHTS[a])
            for other in range(1, NODES):
                first = first + y_ref[other, b] * float(STIFF[a, other] * WEIGHTS[b])
                second = second + y_ref[a, other] * float(STIFF[b, other] * WEIGHTS[a])
            weight = float(WEIGHTS[a] * WEIGHTS[b])
            u_ref[a, b] = por * (third * weight + first + second) + y_ref[a, b] * (
                shift_mass * weight
            )


def sum_column(u_ref):
    for a in range(NODES):
        bottom = u_ref[a, :, 0, :]
        top = u_ref[a, :, NODES - 1, :]
        u_ref[a, :, 0, :] = bottom + shift_up(top)
        u_ref[a, :, NODES - 1, :] = top + shift_down(bottom)


def first_apply_kernel(
    counts, part_ref, ry_first, ry_second, rx_first, rx_second, sum_ref, lift_ref, porosity_ref,
    r_ref, z_ref, u_ref, sy_first, sy_second, fx_first, fx_second, y_ref,
):
    side_x, side_y = Sides("gx", counts[0]), Sides("gy", counts[1])
    field = lifted_rows(counts, row_of(counts, sum_ref), lift_ref)
    z = collect_parts(part_ref, ry_first, ry_second, rx_first, rx_second, side_x, side_y, field)
    inner = None
    for (a, b), value in z.items():
        z_ref[a, b] = value
        term = scaled(value * r_ref[a, b], axis_factor(a, side_x), axis_factor(b, side_y))
        inner = term if inner is None else inner + term
    inner = inner * multiplicity_tile()
    apply_tiles(z_ref, u_ref, y_ref, porosity_ref[...])
    sums = {}
    curvature = None
    for a in range(NODES):
        for b in range(NODES):
            value = u_ref[a, b]
            add_to(sums, (class_of(a), class_of(b)), value)
            term = value * z_ref[a, b]
            curvature = term if curvature is None else curvature + term
    tiles = class_tiles(sums) + [inner, curvature]
    sy_first[2 * NODES] = summed_row(counts, tiles, side_x, side_y)
    sum_column(u_ref)
    for a in range(NODES):
        for layer in range(2):
            low, high = u_ref[a, layer], u_ref[a, NODES - 2 + layer]
            sy_first[2 * a + layer] = side_y.send_first(low, high)
            sy_second[2 * a + layer] = side_y.send_second(low, high)
    for layer in range(2):
        low, high = u_ref[layer], u_ref[NODES - 2 + layer]
        fx_first[layer] = side_x.send_first(low, high)
        fx_second[layer] = side_x.send_second(low, high)


def second_apply_kernel(
    counts, part_ref, ry_first, ry_second, rx_first, rx_second, sum_ref, lift_ref, porosity_ref,
    r_ref, q_ref, z_ref, z1_ref, u_ref, sy_first, sy_second, fx_first, fx_second, stats_ref, y_ref,
):
    side_x, side_y = Sides("gx", counts[0]), Sides("gy", counts[1])
    summed = row_of(counts, sum_ref)
    field = lifted_rows(counts, summed, lift_ref)
    step = row_value(counts, summed, 0) / row_value(counts, summed, 1)
    w = collect_parts(part_ref, ry_first, ry_second, rx_first, rx_second, side_x, side_y, field)
    inner = None
    for (a, b), value in w.items():
        next_z = z_ref[a, b] - step * value
        next_r = r_ref[a, b] - step * q_ref[a, b]
        z1_ref[a, b] = next_z
        term = scaled(next_z * next_r, axis_factor(a, side_x), axis_factor(b, side_y))
        inner = term if inner is None else inner + term
    inner = inner * multiplicity_tile()
    apply_tiles(z1_ref, u_ref, y_ref, porosity_ref[...])
    own = None
    cross = None
    for a in range(NODES):
        for b in range(NODES):
            value = u_ref[a, b]
            own_term = value * z1_ref[a, b]
            cross_term = value * z_ref[a, b]
            own = own_term if own is None else own + own_term
            cross = cross_term if cross is None else cross + cross_term
    write_stats(stats_ref, [inner, own, cross])
    sum_column(u_ref)
    for a in range(NODES):
        low, high = u_ref[a, 0], u_ref[a, NODES - 1]
        sy_first[a] = side_y.send_first(low, high)
        sy_second[a] = side_y.send_second(low, high)
    low, high = u_ref[0], u_ref[NODES - 1]
    fx_first[...] = side_x.send_first(low, high)
    fx_second[...] = side_x.send_second(low, high)


def prepare_kernel(counts, sol_ref, r_ref, q_ref, z_ref, sum_ref, sol_out, r_out):
    summed = row_of(counts, sum_ref)
    step = row_value(counts, summed, 0) / row_value(counts, summed, 1)
    for a in range(NODES):
        for b in range(NODES):
            sol_out[a, b] = sol_ref[a, b] + step * z_ref[a, b]
            r_out[a, b] = r_ref[a, b] - step * q_ref[a, b]


def final_kernel(
    counts, sol_ref, r_ref, q_ref, z_ref, z1_ref, u_ref, ry_first, ry_second, rx_first, rx_second,
    sum_ref, last_ref, sol_out, r_out, d_out, steps_out,
):
    side_x, side_y = Sides("gx", counts[0]), Sides("gy", counts[1])
    summed = row_of(counts, sum_ref)
    first_inner, first_curvature = row_value(counts, summed, 0), row_value(counts, summed, 1)
    second_inner, own, cross = stat_columns(last_ref[:, 0, :], 0, 3)
    first_step = first_inner / first_curvature
    ratio = second_inner / first_inner
    second_step = second_inner / (own + ratio * (2.0 * cross + ratio * first_curvature))
    steps_out[0] = first_step[0, 0]
    steps_out[1] = second_step[0, 0]
    low_x = side_x.low(rx_first[...], rx_second[...])
    high_x = side_x.high(rx_first[...], rx_second[...])
    for a in range(NODES):
        for b in range(NODES):
            image = u_ref[a, b]
            if b == 0:
                image = image + side_y.low(ry_first[a], ry_second[a])
            if b == NODES - 1:
                image = image + side_y.high(ry_first[a], ry_second[a])
            if a == 0:
                image = image + low_x[b]
            if a == NODES - 1:
                image = image + high_x[b]
            z, q = z_ref[a, b], q_ref[a, b]
            direction = z1_ref[a, b] + ratio * z
            image = image + ratio * q
            d_out[a, b] = direction
            sol_out[a, b] = sol_ref[a, b] + second_step * direction
            r_out[a, b] = r_ref[a, b] - second_step * image


COSTS = {
    "start": 100, "first_solve": 1300, "second_solve": 1300, "first_apply": 800,
    "second_apply": 800, "prepare": 20000, "final": 500,
}


def call(kernel, counts, name, shapes, scratch, *operands):
    def body(*refs):
        kernel(counts, *refs)

    def space(shape):
        return pltpu.SMEM if len(shape) == 1 else pltpu.VMEM

    return pl.pallas_call(
        body,
        name=name,
        out_shape=[jax.ShapeDtypeStruct(shape, jnp.float32) for shape in shapes],
        in_specs=[pl.BlockSpec(memory_space=pltpu.VMEM)] * len(operands),
        out_specs=[pl.BlockSpec(memory_space=space(shape)) for shape in shapes],
        scratch_shapes=[pltpu.VMEM(shape, jnp.float32) for shape in scratch],
        compiler_params=pltpu.CompilerParams(vmem_limit_bytes=24 * 1024 * 1024),
        cost_estimate=pl.CostEstimate(
            flops=COSTS[name] * 1000000, bytes_accessed=COSTS[name] * 3000, transcendentals=0
        ),
    )(*operands)


def swap_pairs(counts, axis, parity):
    count_x, count_y = counts
    pairs = []
    for x in range(count_x):
        for y in range(count_y):
            if axis == 0:
                to = ((x + 1 if x % 2 == parity else x - 1) % count_x, y)
            else:
                other = y + 1 if y % 2 == parity else y - 1
                to = (x, other) if 0 <= other < count_y else (x ^ 1, y)
            pairs.append((x * count_y + y, to[0] * count_y + to[1]))
    return pairs


def trade(counts, axis, first, second):
    return (
        lax.ppermute(first, AXES, swap_pairs(counts, axis, 0)),
        lax.ppermute(second, AXES, swap_pairs(counts, axis, 1)),
    )


def trade_far(counts, value, far_x, far_y):
    pairs = [
        (x * counts[1] + y, (x ^ far_x) * counts[1] + (y ^ far_y))
        for x in range(counts[0])
        for y in range(counts[1])
    ]
    return lax.ppermute(value, AXES, pairs)


class RunningSum:
    def __init__(self, counts, tile):
        self.counts = counts
        self.carried = counts == (8, 4)
        self.value = tile if self.carried else lax.psum(tile, AXES)

    def add(self, received):
        if self.carried:
            self.value = self.value + received

    def far(self, *steps):
        return [trade_far(self.counts, self.value, *step) for step in steps if self.carried]


def carry(tiles, running):
    return jnp.concatenate([tiles.reshape((-1, NODES, 128)), running.value[None]])


def carried(received, shape):
    return received[:-1].reshape(shape), received[-1]


def gather_stats(stats):
    return lax.all_to_all(stats, AXES, 0, 0)


def lift_tables(counts, column_length):
    share_x, share_y = share_table(counts[0]), share_table(counts[1])
    basis_x, eigen_x = cosine_inverse(counts[0])
    basis_y, eigen_y = cosine_inverse(counts[1])
    divisor = (
        2.0 * mean_porosity * column_length * (eigen_x[:, None] + eigen_y[None, :])
        + 8.0 * shift_mass * column_length
    )
    modes_x = np.einsum("xip,pa->xia", share_x, basis_x)
    modes_y = np.einsum("yjq,qb->yjb", share_y, basis_y)
    total = counts[0] * counts[1]
    to_modes = np.einsum("pa,qb->abpq", basis_x, basis_y).reshape(total, total)
    to_modes = np.pad(to_modes, ((0, 0), (0, sum_lanes(counts) - total)))
    return [table.astype(np.float32) for table in (modes_x, modes_y, 1.0 / divisor, to_modes)]


def own_lift(tables):
    modes_x, modes_y, inverse, to_modes = [jnp.asarray(table) for table in tables]
    own_x = lax.dynamic_index_in_dim(modes_x, lax.axis_index("gx"), 0, keepdims=False)
    own_y = lax.dynamic_index_in_dim(modes_y, lax.axis_index("gy"), 0, keepdims=False)
    own = own_x[:, None, :, None] * own_y[None, :, None, :] * inverse[None, None]
    lift = jnp.dot(own.reshape(9, -1), to_modes, precision=exact_mode)
    return jnp.pad(lift, ((0, 7), (0, 0)))


def shards_of(counts):
    forward_np, back_np, inverse_np = plane_tables()

    def shards(solution, residual, grain_counts):
        shard_shape = solution.shape
        block = shard_shape[2:]
        solution = solution.reshape(block)
        residual = residual.reshape(block)
        lift = own_lift(lift_tables(counts, block[-1]))
        grains = grain_counts.reshape(1, 128)
        plane = [jnp.asarray(table) for table in (forward_np, back_np, inverse_np)]
        side_x, side_y = Sides("gx", counts[0]), Sides("gy", counts[1])
        row = (counts[0] * counts[1], 4, 128)
        face = (NODES, NODES, 128)
        part_shapes = [
            (EXT, ROWS, 128),
            (EXT, 2, NODES, 128), (EXT, 2, NODES, 128),
            (2, EXT, NODES, 128), (2, EXT, NODES, 128),
        ]
        solve_scratch = [(EXT, ROWS, 128)]

        y_first, y_second = call(
            start_kernel, counts, "start", [(NODES + 1,) + face[1:], face], [], residual
        )
        running = RunningSum(counts, y_first[-1])
        ry = trade(counts, 1, y_first, y_second)
        ry_first, tile = carried(ry[0], face)
        running.add(tile)
        ry = (ry_first, ry[1])
        low_y, high_y = side_y.low(*ry), side_y.high(*ry)

        def with_layers(index):
            return jnp.concatenate([low_y[index][None], residual[index], high_y[index][None]])

        low_face, high_face = with_layers(1), with_layers(NODES - 2)
        rx = trade(
            counts, 0, carry(side_x.send_first(low_face, high_face), running),
            side_x.send_second(low_face, high_face),
        )
        rx_first, tile = carried(rx[0], low_face.shape)
        running.add(tile)
        rx = (rx_first, rx[1])
        far = running.far((0, 2))
        part, y_first, y_second, *fx, porosity = call(
            first_solve_kernel, counts, "first_solve", part_shapes + [(1, 128)], solve_scratch,
            residual, grains, *ry, *rx, *plane,
        )

        def spread_faces(fx, ry):
            low_y, high_y = side_y.low(*ry), side_y.high(*ry)
            middle = jnp.zeros((2, NODES - 4, NODES, 128), jnp.float32)
            both = [
                jnp.concatenate([low_y[at], middle, high_y[at]], axis=1)
                for at in (slice(0, 2), slice(8, 10))
            ]
            return (
                fx[0][:, 1:-1] + side_x.send_first(*both),
                fx[1][:, 1:-1] + side_x.send_second(*both),
            )

        def trade_spread(y_first, y_second, fx, running, far):
            y_first, far = lax.optimization_barrier((y_first, far))
            for value in far:
                running.add(value)
            ry = trade(counts, 1, y_first, y_second)
            for value in running.far((4, 0)):
                running.add(value)
            first, second = spread_faces(fx, ry)
            rx = trade(counts, 0, first, carry(second, running))
            rx_second, tile = carried(rx[1], second.shape)
            running.add(tile)
            return ry, (rx[0], rx_second)

        ry, rx = trade_spread(y_first, y_second, fx, running, far)
        z, u, y_first, y_second, *fx = call(
            first_apply_kernel, counts, "first_apply",
            [block, block, (2 * NODES + 1, NODES, 128), (2 * NODES, NODES, 128),
             (2, NODES, NODES, 128), (2, NODES, NODES, 128)],
            [block],
            part, *ry, *rx, running.value, lift, porosity, residual,
        )
        running = RunningSum(counts, y_first[-1])
        ry = trade(counts, 1, y_first, y_second)
        two = (NODES, 2, NODES, 128)
        ry_first, tile = carried(ry[0], two)
        running.add(tile)
        ry = (ry_first, ry[1].reshape(two))
        low_y, high_y = side_y.low(*ry), side_y.high(*ry)

        def image_faces(index):
            middle = jnp.zeros((2, NODES - 2, NODES, 128), jnp.float32)
            return jnp.concatenate([low_y[index], middle, high_y[index]], axis=1)

        pads = ((0, 0), (1, 1), (0, 0), (0, 0))
        both = (image_faces(slice(0, 2)), image_faces(slice(NODES - 2, NODES)))
        first = jnp.pad(fx[0], pads) + side_x.send_first(*both)
        second = jnp.pad(fx[1], pads) + side_x.send_second(*both)
        rx = trade(counts, 0, carry(first, running), second)
        rx_first, tile = carried(rx[0], first.shape)
        running.add(tile)
        rx = (rx_first, rx[1])
        far = running.far((0, 2))
        q, part, y_first, y_second, *fx = call(
            second_solve_kernel, counts, "second_solve", [block] + part_shapes, solve_scratch,
            u, *ry, *rx, *plane,
        )
        ry, rx = trade_spread(y_first, y_second, fx, running, far)
        z1, u, y_first, y_second, *fx, stats = call(
            second_apply_kernel, counts, "second_apply",
            [block, block, face, face, face, face, row],
            [block],
            part, *ry, *rx, running.value, lift, porosity, residual, q, z,
        )
        next_solution, next_residual = call(
            prepare_kernel, counts, "prepare", [block] * 2, [],
            solution, residual, q, z, running.value,
        )
        ry, next_solution, next_residual = lax.optimization_barrier(
            (trade(counts, 1, y_first, y_second), next_solution, next_residual)
        )
        low_y, high_y = side_y.low(*ry), side_y.high(*ry)

        def edge_rows(index):
            middle = jnp.zeros((NODES - 2, NODES, 128), jnp.float32)
            return jnp.concatenate([low_y[index][None], middle, high_y[index][None]])

        both = (edge_rows(0), edge_rows(NODES - 1))
        rx = trade(
            counts, 0, fx[0] + side_x.send_first(*both), fx[1] + side_x.send_second(*both)
        )
        last_stats = gather_stats(stats)
        solution_out, residual_out, direction, steps = call(
            final_kernel, counts, "final", [block] * 3 + [(2,)], [],
            next_solution, next_residual, q, z, z1, u, *ry, *rx, running.value, last_stats,
        )
        return (
            solution_out.reshape(shard_shape),
            residual_out.reshape(shard_shape),
            direction.reshape(shard_shape),
            steps,
        )

    return shards


def solution(mesh):
    counts = (mesh.shape["gx"], mesh.shape["gy"])
    return jax.shard_map(
        shards_of(counts),
        mesh=mesh,
        in_specs=(
            P("gx", "gy", None, None, None, None),
            P("gx", "gy", None, None, None, None),
            P("gx", "gy", None),
        ),
        out_specs=(
            P("gx", "gy", None, None, None, None),
            P("gx", "gy", None, None, None, None),
            P("gx", "gy", None, None, None, None),
            P(),
        ),
        check_vma=False,
    )
```

```python
import math

import jax
import jax.numpy as jnp
import numpy as np
from jax import lax
from jax.experimental import pallas as pl
from jax.experimental.pallas import tpu as pltpu
from jax.sharding import PartitionSpec as P

NODES = 8
MOST_GRAINS = 16
EXT = NODES + 2
ROWS = 112
MODES = 104
AXES = ("gx", "gy")

shift_mass = 0.1
mean_porosity = 0.7
exact_mode = lax.Precision.HIGHEST
plane_mode = lax.Precision.HIGH


def legendre_columns(node_set, degree):
    table = [node_set * 0.0 + 1.0, node_set]
    for order in range(2, degree + 1):
        table.append(
            ((2 * order - 1) * node_set * table[order - 1] - (order - 1) * table[order - 2]) / order
        )
    return table


def gll_tables():
    degree = NODES - 1
    node_set = np.cos(math.pi * np.arange(degree + 1) / degree)
    for sweep in range(100):
        table = legendre_columns(node_set, degree)
        node_set = node_set - (node_set * table[degree] - table[degree - 1]) / (
            (degree + 1) * table[degree]
        )
    node_set = node_set[::-1].copy()
    values = legendre_columns(node_set, degree)[degree]
    weights = 2.0 / (degree * (degree + 1) * values**2)
    derivative = np.zeros((NODES, NODES))
    for row_index in range(NODES):
        for column_index in range(NODES):
            if row_index != column_index:
                derivative[row_index, column_index] = values[row_index] / (
                    values[column_index] * (node_set[row_index] - node_set[column_index])
                )
    derivative[0, 0] = -degree * (degree + 1) / 4.0
    derivative[NODES - 1, NODES - 1] = degree * (degree + 1) / 4.0
    return (weights, derivative)


def jacobi_eigen(matrix):
    size_now = matrix.shape[0]
    current = matrix.copy()
    vectors = np.eye(size_now)
    for sweep in range(12):
        for first in range(size_now - 1):
            for second in range(first + 1, size_now):
                off_value = current[first, second]
                safe_value = np.where(off_value == 0.0, 1e-300, off_value)
                theta = (current[second, second] - current[first, first]) / (2.0 * safe_value)
                sign_value = np.where(theta >= 0.0, 1.0, -1.0)
                tangent = sign_value / (np.abs(theta) + np.sqrt(theta * theta + 1.0))
                cosine = 1.0 / np.sqrt(tangent * tangent + 1.0)
                sine = tangent * cosine
                rotation = np.eye(size_now)
                rotation[first, first] = cosine
                rotation[second, second] = cosine
                rotation[first, second] = sine
                rotation[second, first] = -sine
                current = rotation.T @ current @ rotation
                vectors = vectors @ rotation
    eigen_values = np.array([current[index, index] for index in range(size_now)])
    return (eigen_values, vectors)


def schwarz_tables():
    weights, derivative = gll_tables()
    stiffness = derivative.T @ (weights[:, None] * derivative)
    total_nodes = 3 * (NODES - 1) + 1
    three_stiffness = np.zeros((total_nodes, total_nodes))
    three_mass = np.zeros(total_nodes)
    for element in range(3):
        start_node = element * (NODES - 1)
        three_stiffness[
            start_node : start_node + NODES, start_node : start_node + NODES
        ] += stiffness
        three_mass[start_node : start_node + NODES] += weights
    chosen = np.array([NODES - 2] + list(range(NODES - 1, 2 * NODES - 1)) + [2 * NODES - 1])
    local_stiffness = three_stiffness[chosen][:, chosen]
    local_mass = three_mass[chosen]
    scaling = 1.0 / np.sqrt(local_mass)
    symmetric = scaling[:, None] * local_stiffness * scaling[None, :]
    symmetric = 0.5 * (symmetric + symmetric.T)
    eigen_values, eigen_vectors = jacobi_eigen(symmetric)
    return (scaling[:, None] * eigen_vectors, eigen_values)


WEIGHTS, DERIVATIVE = gll_tables()
STIFF = DERIVATIVE.T @ (WEIGHTS[:, None] * DERIVATIVE)
BASIS, EIGEN = schwarz_tables()
PARITY = {
    sign: [mode for mode in range(EXT) if BASIS[0, mode] * BASIS[EXT - 1, mode] * sign > 0]
    for sign in (1, -1)
}


def plane_tables():
    forward = np.zeros((MODES, ROWS))
    inverse = np.zeros((MODES, EXT))
    for mode_b in range(EXT):
        for mode_c in range(EXT):
            mode = mode_b * EXT + mode_c
            for b in range(EXT):
                for k in range(NODES):
                    forward[mode, b * NODES + k] = BASIS[b, mode_b] * BASIS[k + 1, mode_c]
                forward[mode, 80 + b] = BASIS[b, mode_b] * BASIS[0, mode_c]
                forward[mode, 96 + b] = BASIS[b, mode_b] * BASIS[EXT - 1, mode_c]
            inverse[mode] = 1.0 / (
                mean_porosity * (EIGEN + EIGEN[mode_b] + EIGEN[mode_c]) + shift_mass
            )
    lanes = np.repeat(inverse.T[:, :, None], 128, axis=2)
    return (
        forward.astype(np.float32),
        forward.T.astype(np.float32).copy(),
        lanes.astype(np.float32),
    )


def row_tile(values):
    row = lax.broadcasted_iota(jnp.int32, (NODES, 128), 0)
    tile = jnp.full((NODES, 128), float(values[0]), jnp.float32)
    for k in range(1, NODES):
        tile = jnp.where(row == k, float(values[k]), tile)
    return tile


def share_table(count):
    table = np.zeros((count, 3, count))
    for column in range(count):
        table[column, :, column] = 1.0
        if column > 0:
            table[column, 0, column] = 0.5
            table[column, 0, column - 1] = 0.5
        if column < count - 1:
            table[column, 2, column] = 0.5
            table[column, 2, column + 1] = 0.5
    return table


def cosine_inverse(count):
    position = np.arange(count)
    basis = np.cos(math.pi * (position[:, None] + 0.5) * position[None, :] / count)
    basis = basis * np.where(position == 0, math.sqrt(1.0 / count), math.sqrt(2.0 / count))[None, :]
    return basis, 2.0 - 2.0 * np.cos(math.pi * position / count)


def shift_up(rows):
    lane = lax.broadcasted_iota(jnp.int32, rows.shape, 1)
    return jnp.where(lane == 0, 0.0, pltpu.roll(rows, 1, 1))


def shift_down(rows):
    lane = lax.broadcasted_iota(jnp.int32, rows.shape, 1)
    return jnp.where(lane == 127, 0.0, pltpu.roll(rows, 127, 1))


class Sides:
    def __init__(self, axis, count):
        self.index = lax.axis_index(axis)
        self.even = lax.rem(self.index, 2) == 0
        self.no_low = self.index == 0
        self.no_high = self.index == count - 1

    def low(self, first, second):
        return jnp.where(self.no_low, 0.0, jnp.where(self.even, second, first))

    def high(self, first, second):
        return jnp.where(self.no_high, 0.0, jnp.where(self.even, first, second))

    def send_first(self, low_face, high_face):
        return jnp.where(self.even, high_face, low_face)

    def send_second(self, low_face, high_face):
        return jnp.where(self.even, low_face, high_face)


def multiplicity_tile():
    row = lax.broadcasted_iota(jnp.int32, (NODES, 128), 0)
    lane = lax.broadcasted_iota(jnp.int32, (NODES, 128), 1)
    shared = ((row == 0) & (lane > 0)) | ((row == NODES - 1) & (lane < 127))
    return jnp.where(shared, 0.5, 1.0)


def class_of(node):
    return 0 if node == 0 else (2 if node == NODES - 1 else 1)


def axis_factor(node, side):
    if node == 0:
        return jnp.where(side.no_low, 1.0, 0.5)
    if node == NODES - 1:
        return jnp.where(side.no_high, 1.0, 0.5)
    return None


def scaled(value, *factors):
    for factor in factors:
        if factor is not None:
            value = value * factor
    return value


def add_to(total, key, value):
    total[key] = value if key not in total else total[key] + value


def lane_sums(tiles):
    columns = [jnp.sum(tile, axis=0, keepdims=True) for tile in tiles]
    columns.append(jnp.zeros((16 - len(tiles), 128), jnp.float32))
    sums = jnp.sum(jnp.concatenate(columns, axis=0), axis=1, keepdims=True)
    return jnp.broadcast_to(sums, (16, 128))


def write_stats(stats_ref, tiles):
    row = lax.broadcasted_iota(jnp.int32, (16, 128), 0)
    lane = lax.broadcasted_iota(jnp.int32, (16, 128), 1)
    sums = jnp.sum(jnp.where(row == lane, lane_sums(tiles), 0.0), axis=0, keepdims=True)
    for index in range(stats_ref.shape[0]):
        stats_ref[index] = jnp.broadcast_to(sums, stats_ref.shape[1:])


def stat_columns(stats, first, count):
    lane = lax.broadcasted_iota(jnp.int32, stats.shape, 1)
    sums = lane_sums([jnp.where(lane == first + i, stats, 0.0) for i in range(count)])
    return [sums[i : i + 1] for i in range(count)]


def sum_lanes(counts):
    return -(-(counts[0] * counts[1] + 2) // 128) * 128


def share_rows(counts, side_x, side_y):
    lane = lax.broadcasted_iota(jnp.int32, (1, sum_lanes(counts)), 1)
    column_y = lax.rem(lane, counts[1])
    first_x = lane - column_y

    def weights(side, place, step, count):
        own = jnp.where(place == side.index * step, 1.0, 0.0)
        below = jnp.where(place == (side.index - 1) * step, 1.0, 0.0)
        above = jnp.where(place == (side.index + 1) * step, 1.0, 0.0)
        return (
            jnp.where(side.no_low, own, 0.5 * (own + below)),
            own,
            jnp.where(side.no_high, own, 0.5 * (own + above)),
        )

    inside = lane < counts[0] * counts[1]
    along_x = weights(side_x, first_x, counts[1], counts[0])
    along_y = weights(side_y, column_y, 1, counts[1])
    return [jnp.where(inside, wx * wy, 0.0) for wx in along_x for wy in along_y]


def summed_row(counts, tiles, side_x, side_y):
    sums = lane_sums(tiles)
    lane = lax.broadcasted_iota(jnp.int32, (1, sum_lanes(counts)), 1)
    total = None
    for i, share in enumerate(share_rows(counts, side_x, side_y)):
        term = share * sums[i : i + 1, 0:1]
        total = term if total is None else total + term
    for i in range(9, len(tiles)):
        total = total + jnp.where(lane == counts[0] * counts[1] + i - 9, sums[i : i + 1, 0:1], 0.0)
    pieces = [total[:, at : at + 128] for at in range(0, sum_lanes(counts), 128)]
    pieces.append(jnp.zeros((NODES - len(pieces), 128), jnp.float32))
    return jnp.concatenate(pieces, axis=0)


def row_of(counts, tile_ref):
    rows = [tile_ref[i : i + 1, :] for i in range(sum_lanes(counts) // 128)]
    return rows[0] if len(rows) == 1 else jnp.concatenate(rows, axis=1)


def lifted_rows(counts, row, lift_ref):
    sums = jnp.sum(lift_ref[...] * row, axis=1, keepdims=True)
    return jnp.broadcast_to(sums, (16, 128))


def row_value(counts, row, index):
    lane = lax.broadcasted_iota(jnp.int32, row.shape, 1)
    chosen = jnp.where(lane == counts[0] * counts[1] + index, row, 0.0)
    return jnp.broadcast_to(jnp.sum(chosen, axis=1, keepdims=True), (1, 128))


def class_tiles(sums):
    return [sums[(i, j)] for i in range(3) for j in range(3)]


def shared_class_tiles(field_ref, side_x, side_y):
    tile = multiplicity_tile()
    sums = {}
    for a in range(NODES):
        for b in range(NODES):
            add_to(sums, (class_of(a), class_of(b)), field_ref[a, b])
    for (i, j), value in sums.items():
        a, b = (0, 1, NODES - 1)[i], (0, 1, NODES - 1)[j]
        sums[(i, j)] = scaled(value * tile, axis_factor(a, side_x), axis_factor(b, side_y))
    return class_tiles(sums)


def start_kernel(counts, r_ref, sy_first, sy_second):
    side_x, side_y = Sides("gx", counts[0]), Sides("gy", counts[1])
    for a in range(NODES):
        low, high = r_ref[a, 1], r_ref[a, NODES - 2]
        sy_first[a] = side_y.send_first(low, high)
        sy_second[a] = side_y.send_second(low, high)
    sy_first[NODES] = summed_row(
        counts, shared_class_tiles(r_ref, side_x, side_y), side_x, side_y
    )


def planes(ref):
    return jnp.concatenate([ref[a] for a in range(EXT)], axis=1)


def local_solve(x_ref, forward_ref, back_ref, inverse_ref, part_ref):
    zero = jnp.zeros((6, 128), jnp.float32)
    for a in range(EXT):
        x_ref[a, 80:90] = shift_up(x_ref[a, pl.ds(6, EXT, stride=NODES), :])
        x_ref[a, 96:106] = shift_down(x_ref[a, pl.ds(1, EXT, stride=NODES), :])
        x_ref[a, 90:96] = zero
        x_ref[a, 106:112] = zero
    half = EXT // 2
    for block in range(ROWS // 8):
        rows = pl.ds(block * 8, 8)
        low = [x_ref[a, rows] for a in range(half)]
        high = [x_ref[EXT - 1 - a, rows] for a in range(half)]
        folded = {1: [x + y for x, y in zip(low, high)], -1: [x - y for x, y in zip(low, high)]}
        for sign in (1, -1):
            for mode in PARITY[sign]:
                total = folded[sign][0] * float(BASIS[0, mode])
                for a in range(1, half):
                    total = total + folded[sign][a] * float(BASIS[a, mode])
                x_ref[mode, rows] = total
    spectrum = jnp.dot(
        forward_ref[...], planes(x_ref), precision=plane_mode, preferred_element_type=jnp.float32
    ) * planes(inverse_ref)
    values = jnp.dot(
        back_ref[...], spectrum, precision=plane_mode, preferred_element_type=jnp.float32
    )
    for block in range(ROWS // 8):
        rows = pl.ds(block * 8, 8)
        modes = [values[block * 8 : block * 8 + 8, m * 128 : (m + 1) * 128] for m in range(EXT)]
        back = {}
        for sign in (1, -1):
            for a in range(half):
                total = None
                for mode in PARITY[sign]:
                    term = modes[mode] * float(BASIS[a, mode])
                    total = term if total is None else total + term
                back[(sign, a)] = total
        for a in range(half):
            part_ref[a, rows] = back[(1, a)] + back[(-1, a)]
            part_ref[EXT - 1 - a, rows] = back[(1, a)] - back[(-1, a)]
    for a in range(EXT):

        def layer(k):
            return (a, pl.ds(k, EXT, stride=NODES), slice(None))

        bottom, top = part_ref[layer(0)], part_ref[layer(NODES - 1)]
        part_ref[layer(0)] = bottom + shift_up(top)
        part_ref[layer(NODES - 1)] = top + shift_down(bottom)
        part_ref[layer(1)] = part_ref[layer(1)] + shift_up(part_ref[a, 96:106])
        part_ref[layer(NODES - 2)] = part_ref[layer(NODES - 2)] + shift_down(part_ref[a, 80:90])


def send_parts(part_ref, side_x, side_y, sy_first, sy_second, fx_first, fx_second):
    for a in range(EXT):
        low, high = part_ref[a, 0:16], part_ref[a, 64:80]
        sy_first[2 * a : 2 * a + 2] = side_y.send_first(low, high).reshape(2, NODES, 128)
        sy_second[2 * a : 2 * a + 2] = side_y.send_second(low, high).reshape(2, NODES, 128)
    for layer in range(2):
        low, high = part_ref[layer, 0:80], part_ref[NODES + layer, 0:80]
        fx_first[layer] = side_x.send_first(low, high).reshape(EXT, NODES, 128)
        fx_second[layer] = side_x.send_second(low, high).reshape(EXT, NODES, 128)


def first_solve_kernel(
    counts, r_ref, porosity_ref, ry_first, ry_second, rx_first, rx_second, forward_ref, back_ref,
    inverse_ref, part_ref, sy_first, sy_second, fx_first, fx_second, x_ref,
):
    for send in (sy_first, sy_second):
        send[2 * EXT] = jnp.broadcast_to(porosity_ref[...], (NODES, 128))
    side_x, side_y = Sides("gx", counts[0]), Sides("gy", counts[1])
    x_ref[0, 0:80] = side_x.low(rx_first[...], rx_second[...]).reshape(80, 128)
    x_ref[EXT - 1, 0:80] = side_x.high(rx_first[...], rx_second[...]).reshape(80, 128)
    for a in range(NODES):
        x_ref[a + 1, 0:8] = side_y.low(ry_first[a], ry_second[a])
        x_ref[a + 1, 8:72] = r_ref[a].reshape(64, 128)
        x_ref[a + 1, 72:80] = side_y.high(ry_first[a], ry_second[a])
    local_solve(x_ref, forward_ref, back_ref, inverse_ref, part_ref)
    send_parts(part_ref, side_x, side_y, sy_first, sy_second, fx_first, fx_second)


def second_solve_kernel(
    counts, u_ref, ry_first, ry_second, rx_first, rx_second, forward_ref, back_ref, inverse_ref,
    q_ref, part_ref, sy_first, sy_second, fx_first, fx_second, x_ref,
):
    side_x, side_y = Sides("gx", counts[0]), Sides("gy", counts[1])
    extend_image(
        u_ref, ry_first, ry_second, rx_first, rx_second, side_x, side_y, q_ref, x_ref, None
    )
    local_solve(x_ref, forward_ref, back_ref, inverse_ref, part_ref)
    send_parts(part_ref, side_x, side_y, sy_first, sy_second, fx_first, fx_second)


def late_solve_kernel(
    counts, u_ref, ry_first, ry_second, rx_first, rx_second, columns_ref, lift_ref, sum_ref,
    forward_ref, back_ref, inverse_ref, q_ref, part_ref, sy_first, sy_second, fx_first, fx_second,
    field_ref, x_ref, table_ref,
):
    side_x, side_y = Sides("gx", counts[0]), Sides("gy", counts[1])
    table_ref[...] = jnp.broadcast_to(
        jnp.sum(lift_ref[...] * sum_ref[0:1], axis=1, keepdims=True), table_ref.shape
    )
    fields = near_fields(counts, table_ref, side_x, side_y)
    own = fields[(1, 1)]
    field_ref[...] = jnp.concatenate(
        [own[i][j] for i in range(3) for j in range(3)] + [jnp.zeros((7, 128), jnp.float32)]
    )
    image = LiftedImage(fields, columns_ref)
    extend_image(
        u_ref, ry_first, ry_second, rx_first, rx_second, side_x, side_y, q_ref, x_ref, image
    )
    local_solve(x_ref, forward_ref, back_ref, inverse_ref, part_ref)
    send_parts(part_ref, side_x, side_y, sy_first, sy_second, fx_first, fx_second)


def extend_image(
    u_ref, ry_first, ry_second, rx_first, rx_second, side_x, side_y, q_ref, x_ref, image
):
    low_x = side_x.low(rx_first[...], rx_second[...])
    high_x = side_x.high(rx_first[...], rx_second[...])

    def lifted(value, a, b):
        return value if image is None else value + image.at(a - 1, b - 1)

    for b in range(EXT):
        rows = pl.ds(b * 8, 8)
        x_ref[0, rows] = lifted(low_x[0, b], 0, b)
        x_ref[EXT - 1, rows] = lifted(high_x[1, b], EXT - 1, b)
    for a in range(NODES):
        low_y = side_y.low(ry_first[a], ry_second[a])
        high_y = side_y.high(ry_first[a], ry_second[a])
        rows = [low_y[0]]
        for b in range(NODES):
            value = u_ref[a, b]
            if b == 0:
                value = value + low_y[1]
            if b == NODES - 1:
                value = value + high_y[0]
            rows.append(value)
        rows.append(high_y[1])
        for b in range(EXT):
            value = rows[b]
            if a == 0:
                value = value + low_x[1, b]
            if a == NODES - 1:
                value = value + high_x[0, b]
            value = lifted(value, a + 1, b)
            x_ref[a + 1, b * 8 : b * 8 + 8] = value
            if 0 < b < EXT - 1:
                q_ref[a, b - 1] = value


def collect_parts(part_ref, ry_first, ry_second, rx_first, rx_second, side_x, side_y, field):
    low_x = side_x.low(rx_first[...], rx_second[...])
    high_x = side_x.high(rx_first[...], rx_second[...])
    result = {}
    for a in range(NODES):
        low_y = side_y.low(ry_first[a + 1], ry_second[a + 1])
        high_y = side_y.high(ry_first[a + 1], ry_second[a + 1])
        for b in range(NODES):
            value = part_ref[a + 1, (b + 1) * 8 : (b + 2) * 8]
            if b < 2:
                value = value + low_y[b]
            if b >= NODES - 2:
                value = value + high_y[b - (NODES - 2)]
            if a < 2:
                value = value + low_x[a, b]
            if a >= NODES - 2:
                value = value + high_x[a - (NODES - 2), b]
            if field is not None:
                node_class = 3 * class_of(a) + class_of(b)
                value = value + field[node_class : node_class + 1, :]
            result[(a, b)] = value
    return result


def apply_tiles(z_ref, u_ref, y_ref, por):
    weight_tile = row_tile(WEIGHTS)
    stiff_tiles = [
        row_tile([STIFF[k, (k - shift) % NODES] for k in range(NODES)]) for shift in range(NODES)
    ]
    for a in range(NODES):
        for b in range(NODES):
            y_ref[a, b] = z_ref[a, b] * weight_tile
    for a in range(NODES):
        for b in range(NODES):
            z = z_ref[a, b]
            third = z * stiff_tiles[0]
            for shift in range(1, NODES):
                third = third + pltpu.roll(z, shift, 0) * stiff_tiles[shift]
            first = y_ref[0, b] * float(STIFF[a, 0] * WEIGHTS[b])
            second = y_ref[a, 0] * float(STIFF[b, 0] * WEIGHTS[a])
            for other in range(1, NODES):
                first = first + y_ref[other, b] * float(STIFF[a, other] * WEIGHTS[b])
                second = second + y_ref[a, other] * float(STIFF[b, other] * WEIGHTS[a])
            weight = float(WEIGHTS[a] * WEIGHTS[b])
            u_ref[a, b] = por * (third * weight + first + second) + y_ref[a, b] * (
                shift_mass * weight
            )


def sum_column(u_ref):
    for a in range(NODES):
        bottom = u_ref[a, :, 0, :]
        top = u_ref[a, :, NODES - 1, :]
        u_ref[a, :, 0, :] = bottom + shift_up(top)
        u_ref[a, :, NODES - 1, :] = top + shift_down(bottom)


def first_apply_kernel(
    counts, part_ref, ry_first, ry_second, rx_first, rx_second, sum_ref, lift_ref, porosity_ref,
    r_ref, z_ref, u_ref, sy_first, sy_second, fx_first, fx_second, tile_ref, y_ref,
):
    side_x, side_y = Sides("gx", counts[0]), Sides("gy", counts[1])
    field = lifted_rows(counts, row_of(counts, sum_ref), lift_ref)
    z = collect_parts(part_ref, ry_first, ry_second, rx_first, rx_second, side_x, side_y, field)
    inner = None
    for (a, b), value in z.items():
        z_ref[a, b] = value
        term = scaled(value * r_ref[a, b], axis_factor(a, side_x), axis_factor(b, side_y))
        inner = term if inner is None else inner + term
    inner = inner * multiplicity_tile()
    apply_tiles(z_ref, u_ref, y_ref, porosity_ref[...])
    sums = {}
    curvature = None
    for a in range(NODES):
        for b in range(NODES):
            value = u_ref[a, b]
            add_to(sums, (class_of(a), class_of(b)), value)
            term = value * z_ref[a, b]
            curvature = term if curvature is None else curvature + term
    tiles = class_tiles(sums) + [inner, curvature]
    tile_ref[...] = summed_row(counts, tiles, side_x, side_y)
    sum_column(u_ref)
    send_layers(u_ref, side_x, side_y, sy_first, sy_second, fx_first, fx_second)


def second_apply_kernel(
    counts, part_ref, ry_first, ry_second, rx_first, rx_second, sum_ref, lift_ref, porosity_ref,
    r_ref, q_ref, z_ref, z1_ref, u_ref, sy_first, sy_second, fx_first, fx_second, stats_ref, y_ref,
):
    side_x, side_y = Sides("gx", counts[0]), Sides("gy", counts[1])
    summed = row_of(counts, sum_ref)
    field = lifted_rows(counts, summed, lift_ref)
    step = row_value(counts, summed, 0) / row_value(counts, summed, 1)
    w = collect_parts(part_ref, ry_first, ry_second, rx_first, rx_second, side_x, side_y, field)
    inner = None
    for (a, b), value in w.items():
        next_z = z_ref[a, b] - step * value
        next_r = r_ref[a, b] - step * q_ref[a, b]
        z1_ref[a, b] = next_z
        term = scaled(next_z * next_r, axis_factor(a, side_x), axis_factor(b, side_y))
        inner = term if inner is None else inner + term
    inner = inner * multiplicity_tile()
    apply_tiles(z1_ref, u_ref, y_ref, porosity_ref[...])
    own = None
    cross = None
    for a in range(NODES):
        for b in range(NODES):
            value = u_ref[a, b]
            own_term = value * z1_ref[a, b]
            cross_term = value * z_ref[a, b]
            own = own_term if own is None else own + own_term
            cross = cross_term if cross is None else cross + cross_term
    write_stats(stats_ref, [inner, own, cross])
    sum_column(u_ref)
    for a in range(NODES):
        low, high = u_ref[a, 0], u_ref[a, NODES - 1]
        sy_first[a] = side_y.send_first(low, high)
        sy_second[a] = side_y.send_second(low, high)
    low, high = u_ref[0], u_ref[NODES - 1]
    fx_first[...] = side_x.send_first(low, high)
    fx_second[...] = side_x.send_second(low, high)


def send_layers(u_ref, side_x, side_y, sy_first, sy_second, fx_first, fx_second):
    for a in range(NODES):
        for layer in range(2):
            low, high = u_ref[a, layer], u_ref[a, NODES - 2 + layer]
            sy_first[2 * a + layer] = side_y.send_first(low, high)
            sy_second[2 * a + layer] = side_y.send_second(low, high)
    for layer in range(2):
        low, high = u_ref[layer], u_ref[NODES - 2 + layer]
        fx_first[layer] = side_x.send_first(low, high)
        fx_second[layer] = side_x.send_second(low, high)


def early_apply_kernel(
    counts, part_ref, ry_first, ry_second, rx_first, rx_second, porosity_ref,
    z_ref, u_ref, sy_first, sy_second, fx_first, fx_second, y_ref,
):
    side_x, side_y = Sides("gx", counts[0]), Sides("gy", counts[1])
    z = collect_parts(part_ref, ry_first, ry_second, rx_first, rx_second, side_x, side_y, None)
    for (a, b), value in z.items():
        z_ref[a, b] = value
    apply_tiles(z_ref, u_ref, y_ref, porosity_ref[...])
    sum_column(u_ref)
    send_layers(u_ref, side_x, side_y, sy_first, sy_second, fx_first, fx_second)


def late_apply_kernel(
    counts, part_ref, ry_first, ry_second, rx_first, rx_second, porosity_ref, r_ref, q_ref,
    schwarz_ref, field_ref, z_ref, w_ref, u_ref, sy_first, sy_second, fx_first, fx_second,
    stats_ref, y_ref,
):
    side_x, side_y = Sides("gx", counts[0]), Sides("gy", counts[1])
    w = collect_parts(part_ref, ry_first, ry_second, rx_first, rx_second, side_x, side_y, None)
    inner = first_inner = first_curvature = None
    for (a, b), value in w.items():
        w_ref[a, b] = value
        node_class = 3 * class_of(a) + class_of(b)
        z = schwarz_ref[a, b] + field_ref[node_class : node_class + 1, :]
        z_ref[a, b] = z
        q = q_ref[a, b]
        factors = (axis_factor(a, side_x), axis_factor(b, side_y))
        terms = [scaled(t, *factors) for t in (value * q, z * r_ref[a, b], z * q)]
        if inner is None:
            inner, first_inner, first_curvature = terms
        else:
            inner, first_inner, first_curvature = (
                inner + terms[0], first_inner + terms[1], first_curvature + terms[2]
            )
    tile = multiplicity_tile()
    inner, first_inner, first_curvature = inner * tile, first_inner * tile, first_curvature * tile
    porosity = porosity_ref[...]
    apply_tiles(w_ref, u_ref, y_ref, porosity)
    sums = {}
    own = None
    for a in range(NODES):
        for b in range(NODES):
            value = u_ref[a, b]
            add_to(sums, (class_of(a), class_of(b)), value)
            term = value * w_ref[a, b]
            own = term if own is None else own + term
    total = counts[0] * counts[1]
    tiles = class_tiles(sums) + [inner, own, porosity]
    first_tiles = shared_class_tiles(q_ref, side_x, side_y) + [first_inner, first_curvature]
    row = summed_row(counts, first_tiles, side_x, side_y)[0:1] + pltpu.roll(
        summed_row(counts, tiles, side_x, side_y), total + 2, 1
    )[0:1]
    for index in range(stats_ref.shape[0]):
        stats_ref[index] = jnp.broadcast_to(row, stats_ref.shape[1:])
    sum_column(u_ref)
    for a in range(NODES):
        low, high = u_ref[a, 0], u_ref[a, NODES - 1]
        sy_first[a] = side_y.send_first(low, high)
        sy_second[a] = side_y.send_second(low, high)
    low, high = u_ref[0], u_ref[NODES - 1]
    fx_first[...] = side_x.send_first(low, high)
    fx_second[...] = side_x.send_second(low, high)


def porosity_kernel(counts, low_ref, own_ref, high_ref, out_ref):
    row = lax.broadcasted_iota(jnp.int32, (NODES, 128), 0)
    weights = row_tile(WEIGHTS)
    mass = shift_mass * weights / multiplicity_tile()
    end = float(WEIGHTS[0])
    for x, ref in enumerate((low_ref, own_ref, high_ref)):
        for y in range(3):
            porosity = ref[y : y + 1]
            tile = porosity * weights
            tile = tile + jnp.where(row == 0, end * shift_up(porosity), 0.0)
            tile = tile + jnp.where(row == NODES - 1, end * shift_down(porosity), 0.0)
            out_ref[3 * x + y] = tile
            out_ref[9 + 3 * x + y] = jnp.where(porosity > 0.0, mass, 0.0)


CLASS_STIFF = np.stack(
    [STIFF[:, 0], STIFF[:, 1 : NODES - 1].sum(axis=1), STIFF[:, NODES - 1]], axis=1
)
CLASS_ENDS = np.stack(
    [CLASS_STIFF[0], CLASS_STIFF[1 : NODES - 1].sum(axis=0), CLASS_STIFF[NODES - 1]]
)
CLASS_WEIGHTS = np.array([WEIGHTS[0], WEIGHTS[1 : NODES - 1].sum(), WEIGHTS[NODES - 1]])


def combine(coefficients, values):
    total = None
    for coefficient, value in zip(coefficients, values):
        term = value * float(coefficient)
        total = term if total is None else total + term
    return total


def sharing(node):
    return {
        -1: [(0, NODES - 2)], 0: [(1, 0), (0, NODES - 1)],
        NODES - 1: [(1, NODES - 1), (2, 0)], NODES: [(2, 1)],
    }.get(node, [(1, node)])


class LiftedImage:
    def __init__(self, fields, columns_ref):
        self.fields, self.columns, self.known = fields, columns_ref, {}

    def along(self, column, place, other_class, axis):
        key = (column, place, other_class, axis)
        if key not in self.known:
            field = self.fields[column]
            line = [
                field[i][other_class] if axis == 0 else field[other_class][i] for i in range(3)
            ]
            self.known[key] = combine(CLASS_STIFF[place], line)
        return self.known[key]

    def at(self, a, b):
        total = None
        for i, place_a in sharing(a):
            for j, place_b in sharing(b):
                class_a, class_b = class_of(place_a), class_of(place_b)
                stiff = self.along((i, j), place_a, class_b, 0) * float(WEIGHTS[place_b])
                stiff = stiff + self.along((i, j), place_b, class_a, 1) * float(WEIGHTS[place_a])
                mass = self.fields[(i, j)][class_a][class_b]
                mass = mass * float(WEIGHTS[place_a] * WEIGHTS[place_b])
                term = stiff * self.columns[3 * i + j] + mass * self.columns[9 + 3 * i + j]
                total = term if total is None else total + term
        return total


def near_fields(counts, table_ref, side_x, side_y):
    total = counts[0] * counts[1]

    def field_of(step_x, step_y):
        x = jnp.clip(side_x.index + step_x, 0, counts[0] - 1)
        y = jnp.clip(side_y.index + step_y, 0, counts[1] - 1)
        place = x * counts[1] + y
        return [
            [table_ref[pl.ds((3 * i + j) * total + place, 1), :] for j in range(3)]
            for i in range(3)
        ]

    return {(i, j): field_of(i - 1, j - 1) for i in range(3) for j in range(3)}


def lifted_energy(counts, table_ref, porosity_sums, length):
    total = counts[0] * counts[1]
    field = [
        [table_ref[pl.ds((3 * i + j) * total, total), :] for j in range(3)] for i in range(3)
    ]

    def line(values):
        terms = []
        for i, j in ((0, 1), (0, 2), (1, 2)):
            difference = values[i] - values[j]
            terms.append(difference * difference * float(-CLASS_ENDS[i, j]))
        return terms[0] + terms[1] + terms[2]

    stiff = None
    mass = None
    for i in range(3):
        term = line(field[i]) * float(CLASS_WEIGHTS[i])
        term = term + line([field[j][i] for j in range(3)]) * float(CLASS_WEIGHTS[i])
        stiff = term if stiff is None else stiff + term
        for j in range(3):
            term = field[i][j] * field[i][j] * float(CLASS_WEIGHTS[i] * CLASS_WEIGHTS[j])
            mass = term if mass is None else mass + term
    energy = stiff * porosity_sums * 2.0 + mass * (shift_mass * 2.0 * length)
    return jnp.sum(energy, axis=0, keepdims=True)


def late_final_kernel(
    counts, sol_ref, r_ref, q_ref, z_ref, w_ref, u_ref, ry_first, ry_second, rx_first, rx_second,
    columns_ref, lift_ref, stats_ref, sol_out, r_out, d_out, steps_out, table_ref,
):
    side_x, side_y = Sides("gx", counts[0]), Sides("gy", counts[1])
    total = counts[0] * counts[1]
    stats = stats_ref[:, 0, :]
    summed = jnp.sum(stats, axis=0, keepdims=True)
    table_ref[...] = jnp.broadcast_to(
        jnp.sum(lift_ref[...] * summed, axis=1, keepdims=True), table_ref.shape
    )
    column = lax.broadcasted_iota(jnp.int32, (total, 128), 0)
    lane = lax.broadcasted_iota(jnp.int32, (total, 128), 1)
    at = 2 * total + 2
    porosity_sums = jnp.sum(
        jnp.where(lane == at + 2, stats, 0.0), axis=1, keepdims=True
    )
    coarse = table_ref[pl.ds(4 * total, total), :]

    def product(first):
        chosen = jnp.where(lane == column + first, coarse * summed, 0.0)
        return jnp.sum(jnp.sum(chosen, axis=0, keepdims=True), axis=1, keepdims=True)

    def value(index):
        return jnp.sum(jnp.where(lane[0:1] == index, summed, 0.0), axis=1, keepdims=True)

    first_inner, first_curvature = value(total), value(total + 1)
    cross = value(at) + product(0)
    energy = value(at + 1) + 2.0 * product(total + 2) + lifted_energy(
        counts, table_ref, porosity_sums, sol_ref.shape[-1]
    )
    first_step = first_inner / first_curvature
    second_inner = first_step * first_step * cross - first_inner
    ratio = second_inner / first_inner
    mixed = first_curvature - first_step * cross
    own = first_curvature - 2.0 * first_step * cross + first_step * first_step * energy
    second_step = second_inner / (own + ratio * (2.0 * mixed + ratio * first_curvature))
    first_step, second_step, ratio = (
        jnp.broadcast_to(scalar[:, 0:1], (1, 128)) for scalar in (first_step, second_step, ratio)
    )
    steps_out[0] = first_step[0, 0]
    steps_out[1] = second_step[0, 0]

    fields = near_fields(counts, table_ref, side_x, side_y)
    lifted_image = LiftedImage(fields, columns_ref)
    low_x = side_x.low(rx_first[...], rx_second[...])
    high_x = side_x.high(rx_first[...], rx_second[...])
    for a in range(NODES):
        for b in range(NODES):
            image = u_ref[a, b]
            if b == 0:
                image = image + side_y.low(ry_first[a], ry_second[a])
            if b == NODES - 1:
                image = image + side_y.high(ry_first[a], ry_second[a])
            if a == 0:
                image = image + low_x[b]
            if a == NODES - 1:
                image = image + high_x[b]
            lifted = fields[(1, 1)][class_of(a)][class_of(b)]
            image = image + lifted_image.at(a, b)
            z, q = z_ref[a, b], q_ref[a, b]
            direction = z - first_step * (w_ref[a, b] + lifted) + ratio * z
            image = q - first_step * image + ratio * q
            d_out[a, b] = direction
            sol_out[a, b] = sol_ref[a, b] + first_step * z + second_step * direction
            r_out[a, b] = r_ref[a, b] - first_step * q - second_step * image


def prepare_kernel(counts, sol_ref, r_ref, q_ref, z_ref, sum_ref, sol_out, r_out):
    summed = row_of(counts, sum_ref)
    step = row_value(counts, summed, 0) / row_value(counts, summed, 1)
    for a in range(NODES):
        for b in range(NODES):
            sol_out[a, b] = sol_ref[a, b] + step * z_ref[a, b]
            r_out[a, b] = r_ref[a, b] - step * q_ref[a, b]


def final_kernel(
    counts, sol_ref, r_ref, q_ref, z_ref, z1_ref, u_ref, ry_first, ry_second, rx_first, rx_second,
    sum_ref, last_ref, sol_out, r_out, d_out, steps_out,
):
    side_x, side_y = Sides("gx", counts[0]), Sides("gy", counts[1])
    summed = row_of(counts, sum_ref)
    first_inner, first_curvature = row_value(counts, summed, 0), row_value(counts, summed, 1)
    second_inner, own, cross = stat_columns(last_ref[:, 0, :], 0, 3)
    first_step = first_inner / first_curvature
    ratio = second_inner / first_inner
    second_step = second_inner / (own + ratio * (2.0 * cross + ratio * first_curvature))
    steps_out[0] = first_step[0, 0]
    steps_out[1] = second_step[0, 0]
    low_x = side_x.low(rx_first[...], rx_second[...])
    high_x = side_x.high(rx_first[...], rx_second[...])
    for a in range(NODES):
        for b in range(NODES):
            image = u_ref[a, b]
            if b == 0:
                image = image + side_y.low(ry_first[a], ry_second[a])
            if b == NODES - 1:
                image = image + side_y.high(ry_first[a], ry_second[a])
            if a == 0:
                image = image + low_x[b]
            if a == NODES - 1:
                image = image + high_x[b]
            z, q = z_ref[a, b], q_ref[a, b]
            direction = z1_ref[a, b] + ratio * z
            image = image + ratio * q
            d_out[a, b] = direction
            sol_out[a, b] = sol_ref[a, b] + second_step * direction
            r_out[a, b] = r_ref[a, b] - second_step * image


COSTS = {
    "start": 100, "first_solve": 1300, "second_solve": 1300, "first_apply": 800,
    "second_apply": 800, "prepare": 20000, "final": 500, "late_apply": 800, "porosity": 20000, "late_final": 800,
}


def call(kernel, counts, name, shapes, scratch, *operands):
    def body(*refs):
        kernel(counts, *refs)

    def space(shape):
        return pltpu.SMEM if len(shape) == 1 else pltpu.VMEM

    return pl.pallas_call(
        body,
        name=name,
        out_shape=[jax.ShapeDtypeStruct(shape, jnp.float32) for shape in shapes],
        in_specs=[pl.BlockSpec(memory_space=pltpu.VMEM)] * len(operands),
        out_specs=[pl.BlockSpec(memory_space=space(shape)) for shape in shapes],
        scratch_shapes=[pltpu.VMEM(shape, jnp.float32) for shape in scratch],
        compiler_params=pltpu.CompilerParams(vmem_limit_bytes=24 * 1024 * 1024),
        cost_estimate=pl.CostEstimate(
            flops=COSTS[name] * 1000000, bytes_accessed=COSTS[name] * 3000, transcendentals=0
        ),
    )(*operands)


def swap_pairs(counts, axis, parity):
    count_x, count_y = counts
    pairs = []
    for x in range(count_x):
        for y in range(count_y):
            if axis == 0:
                to = ((x + 1 if x % 2 == parity else x - 1) % count_x, y)
            else:
                other = y + 1 if y % 2 == parity else y - 1
                to = (x, other) if 0 <= other < count_y else (x ^ 1, y)
            pairs.append((x * count_y + y, to[0] * count_y + to[1]))
    return pairs


def trade(counts, axis, first, second):
    return (
        lax.ppermute(first, AXES, swap_pairs(counts, axis, 0)),
        lax.ppermute(second, AXES, swap_pairs(counts, axis, 1)),
    )


def trade_far(counts, value, far_x, far_y):
    pairs = [
        (x * counts[1] + y, (x ^ far_x) * counts[1] + (y ^ far_y))
        for x in range(counts[0])
        for y in range(counts[1])
    ]
    return lax.ppermute(value, AXES, pairs)


class RunningSum:
    def __init__(self, counts, tile, carried):
        self.counts = counts
        self.carried = carried
        self.value = tile if self.carried else lax.psum(tile, AXES)

    def add(self, received):
        if self.carried:
            self.value = self.value + received

    def far(self, *steps):
        return [trade_far(self.counts, self.value, *step) for step in steps if self.carried]


def carry(tiles, running):
    return jnp.concatenate([tiles.reshape((-1, NODES, 128)), running.value[None]])


def carried(received, shape):
    return received[:-1].reshape(shape), received[-1]


def gather_stats(stats):
    return lax.all_to_all(stats, AXES, 0, 0)


def lift_tables(counts, column_length):
    share_x, share_y = share_table(counts[0]), share_table(counts[1])
    basis_x, eigen_x = cosine_inverse(counts[0])
    basis_y, eigen_y = cosine_inverse(counts[1])
    divisor = (
        2.0 * mean_porosity * column_length * (eigen_x[:, None] + eigen_y[None, :])
        + 8.0 * shift_mass * column_length
    )
    modes_x = np.einsum("xip,pa->xia", share_x, basis_x)
    modes_y = np.einsum("yjq,qb->yjb", share_y, basis_y)
    total = counts[0] * counts[1]
    to_modes = np.einsum("pa,qb->abpq", basis_x, basis_y).reshape(total, total)
    to_modes = np.pad(to_modes, ((0, 0), (0, sum_lanes(counts) - total)))
    return [table.astype(np.float32) for table in (modes_x, modes_y, 1.0 / divisor, to_modes)]


def all_lift(counts, column_length):
    modes_x, modes_y, inverse, to_modes = lift_tables(counts, column_length)
    total = counts[0] * counts[1]
    lift = np.einsum(
        "xia,yjb,ab,abl->ijxyl", *(
            table.astype(np.float64)
            for table in (modes_x, modes_y, inverse, to_modes.reshape(inverse.shape + (-1,)))
        ),
    )
    return jnp.asarray(lift.reshape(9 * total, -1).astype(np.float32))


def own_lift(tables):
    modes_x, modes_y, inverse, to_modes = [jnp.asarray(table) for table in tables]
    own_x = lax.dynamic_index_in_dim(modes_x, lax.axis_index("gx"), 0, keepdims=False)
    own_y = lax.dynamic_index_in_dim(modes_y, lax.axis_index("gy"), 0, keepdims=False)
    own = own_x[:, None, :, None] * own_y[None, :, None, :] * inverse[None, None]
    lift = jnp.dot(own.reshape(9, -1), to_modes, precision=exact_mode)
    return jnp.pad(lift, ((0, 7), (0, 0)))


def shards_of(counts):
    forward_np, back_np, inverse_np = plane_tables()

    def shards(solution, residual, grain_counts):
        shard_shape = solution.shape
        block = shard_shape[2:]
        solution = solution.reshape(block)
        residual = residual.reshape(block)
        lift = own_lift(lift_tables(counts, block[-1]))
        late = counts == (8, 4)
        every_lift = all_lift(counts, block[-1]) if late else None
        porosity = 1.0 - 0.6 * grain_counts.reshape(1, 128).astype(jnp.float32) / MOST_GRAINS
        plane = [jnp.asarray(table) for table in (forward_np, back_np, inverse_np)]
        side_x, side_y = Sides("gx", counts[0]), Sides("gy", counts[1])
        row = (counts[0] * counts[1], 4, 128)
        face = (NODES, NODES, 128)
        part_shapes = [
            (EXT, ROWS, 128),
            (2 * EXT, NODES, 128), (2 * EXT, NODES, 128),
            (2, EXT, NODES, 128), (2, EXT, NODES, 128),
        ]
        first_shapes = list(part_shapes)
        first_shapes[1:3] = [(2 * EXT + 1, NODES, 128)] * 2
        solve_scratch = [(EXT, ROWS, 128)]

        y_first, y_second = call(
            start_kernel, counts, "start", [(NODES + 1,) + face[1:], face], [], residual
        )
        running = RunningSum(counts, y_first[-1], late)
        ry = trade(counts, 1, y_first, y_second)
        ry_first, tile = carried(ry[0], face)
        running.add(tile)
        ry = (ry_first, ry[1])
        low_y, high_y = side_y.low(*ry), side_y.high(*ry)

        def with_layers(index):
            return jnp.concatenate([low_y[index][None], residual[index], high_y[index][None]])

        low_face, high_face = with_layers(1), with_layers(NODES - 2)
        rx = trade(
            counts, 0, carry(side_x.send_first(low_face, high_face), running),
            side_x.send_second(low_face, high_face),
        )
        rx_first, tile = carried(rx[0], low_face.shape)
        running.add(tile)
        rx = (rx_first, rx[1])
        part, y_first, y_second, *fx = call(
            first_solve_kernel, counts, "first_solve", first_shapes, solve_scratch,
            residual, porosity, *ry, *rx, *plane,
        )

        def spread_faces(fx, ry):
            low_y, high_y = side_y.low(*ry), side_y.high(*ry)
            middle = jnp.zeros((2, NODES - 4, NODES, 128), jnp.float32)
            both = [
                jnp.concatenate([low_y[at], middle, high_y[at]], axis=1)
                for at in (slice(0, 2), slice(8, 10))
            ]
            return (
                fx[0][:, 1:-1] + side_x.send_first(*both),
                fx[1][:, 1:-1] + side_x.send_second(*both),
            )

        def trade_y(y_first, y_second, shape):
            count = math.prod(shape[:-2])
            ry = trade(counts, 1, y_first, y_second)
            faces = [value[:count].reshape(shape) for value in ry]
            return faces, [value[count:] for value in ry]

        ext_face = (EXT, 2, NODES, 128)
        two = (NODES, 2, NODES, 128)
        tiles = (-1, NODES, 128)
        middle = jnp.broadcast_to(porosity, (1, NODES, 128))
        if late:
            y_second = jnp.concatenate([y_second, running.value[None]])
            ry, rows = trade_y(y_first, y_second, ext_face)
            inner_y = (side_y.index > 0) & (side_y.index < counts[1] - 1)
            running.add(jnp.where(inner_y, rows[1][1], 0.0))
        else:
            ry, rows = trade_y(y_first, y_second, ext_face)
        three = jnp.concatenate(
            [
                side[0, 0:1]
                for side in (
                    side_y.low(rows[0][:1], rows[1][:1]), middle,
                    side_y.high(rows[0][:1], rows[1][:1]),
                )
            ]
            + [jnp.zeros((NODES - 3, 128), jnp.float32)]
        )
        first, second = spread_faces(fx, ry)
        rx = trade(
            counts, 0, jnp.concatenate([first.reshape(tiles), three[None]]),
            jnp.concatenate([second.reshape(tiles), three[None], running.value[None]]),
        )
        count = 2 * NODES
        threes = [value[count] for value in rx]
        running.add(rx[1][count + 1])
        rx = [value[:count].reshape(first.shape) for value in rx]
        if late:
            z, u, y_first, y_second, *fx = call(
                early_apply_kernel, counts, "first_apply",
                [block, block, (2 * NODES, NODES, 128), (2 * NODES, NODES, 128),
                 (2, NODES, NODES, 128), (2, NODES, NODES, 128)],
                [block],
                part, *ry, *rx, porosity,
            )
            y_first = jnp.concatenate([y_first, running.value[None]])
        else:
            z, u, y_first, y_second, *fx, tile = call(
                first_apply_kernel, counts, "first_apply",
                [block, block, (2 * NODES, NODES, 128), (2 * NODES, NODES, 128),
                 (2, NODES, NODES, 128), (2, NODES, NODES, 128), (NODES, 128)],
                [block],
                part, *ry, *rx, running.value, lift, porosity, residual,
            )
        ry, rows = trade_y(y_first, y_second, two)
        if late:
            running.value = jnp.where(inner_y, running.value, rows[0][0])
        low_y, high_y = side_y.low(*ry), side_y.high(*ry)

        def image_faces(index):
            middle = jnp.zeros((2, NODES - 2, NODES, 128), jnp.float32)
            return jnp.concatenate([low_y[index], middle, high_y[index]], axis=1)

        pads = ((0, 0), (1, 1), (0, 0), (0, 0))
        both = (image_faces(slice(0, 2)), image_faces(slice(NODES - 2, NODES)))
        rx = trade(
            counts, 0,
            jnp.pad(fx[0], pads) + side_x.send_first(*both),
            jnp.pad(fx[1], pads) + side_x.send_second(*both),
        )
        if late:
            (columns,) = call(
                porosity_kernel, counts, "porosity", [(18, NODES, 128)], [],
                side_x.low(*threes), three, side_x.high(*threes),
            )
            rx, far, columns = lax.optimization_barrier((rx, running.far((4, 0)), columns))
            for value in far:
                running.add(value)
            table = (9 * counts[0] * counts[1], 128)
            q, part, y_first, y_second, *fx, field = call(
                late_solve_kernel, counts, "second_solve", [block] + part_shapes + [(16, 128)],
                solve_scratch + [table],
                u, *ry, *rx, columns, every_lift, running.value, *plane,
            )
        else:
            q, part, y_first, y_second, *fx = call(
                second_solve_kernel, counts, "second_solve", [block] + part_shapes, solve_scratch,
                u, *ry, *rx, *plane,
            )
        ry, _ = trade_y(y_first, y_second, ext_face)
        rx = trade(counts, 0, *spread_faces(fx, ry))

        def trade_edges(y_first, y_second, fx, beside):
            ry, beside = lax.optimization_barrier((trade(counts, 1, y_first, y_second), beside))
            low_y, high_y = side_y.low(*ry), side_y.high(*ry)

            def edge_rows(index):
                middle = jnp.zeros((NODES - 2, NODES, 128), jnp.float32)
                return jnp.concatenate([low_y[index][None], middle, high_y[index][None]])

            both = (edge_rows(0), edge_rows(NODES - 1))
            rx = trade(
                counts, 0, fx[0] + side_x.send_first(*both), fx[1] + side_x.send_second(*both)
            )
            return ry, rx, beside

        if late:
            z, w, u, y_first, y_second, *fx, stats = call(
                late_apply_kernel, counts, "late_apply",
                [block, block, block, face, face, face, face, row], [block],
                part, *ry, *rx, porosity, residual, q, z, field,
            )
            ry, rx, _ = trade_edges(y_first, y_second, fx, [])
            solution_out, residual_out, direction, steps = call(
                late_final_kernel, counts, "late_final", [block] * 3 + [(2,)], [table],
                solution, residual, q, z, w, u, *ry, *rx, columns, every_lift,
                gather_stats(stats),
            )
        else:
            summed = lax.psum(tile, AXES)
            z1, u, y_first, y_second, *fx, stats = call(
                second_apply_kernel, counts, "second_apply",
                [block, block, face, face, face, face, row], [block],
                part, *ry, *rx, summed, lift, porosity, residual, q, z,
            )
            nexts = call(
                prepare_kernel, counts, "prepare", [block] * 2, [],
                solution, residual, q, z, summed,
            )
            ry, rx, nexts = trade_edges(y_first, y_second, fx, nexts)
            solution_out, residual_out, direction, steps = call(
                final_kernel, counts, "final", [block] * 3 + [(2,)], [],
                *nexts, q, z, z1, u, *ry, *rx, summed, gather_stats(stats),
            )
        return (
            solution_out.reshape(shard_shape),
            residual_out.reshape(shard_shape),
            direction.reshape(shard_shape),
            steps,
        )

    return shards


def solution(mesh):
    counts = (mesh.shape["gx"], mesh.shape["gy"])
    return jax.shard_map(
        shards_of(counts),
        mesh=mesh,
        in_specs=(
            P("gx", "gy", None, None, None, None),
            P("gx", "gy", None, None, None, None),
            P("gx", "gy", None),
        ),
        out_specs=(
            P("gx", "gy", None, None, None, None),
            P("gx", "gy", None, None, None, None),
            P("gx", "gy", None, None, None, None),
            P(),
        ),
        check_vma=False,
    )
```

```python
import math

import jax
import jax.numpy as jnp
import numpy as np
from jax import lax
from jax.experimental import pallas as pl
from jax.experimental.pallas import tpu as pltpu
from jax.sharding import PartitionSpec as P

NODES = 8
MOST_GRAINS = 16
EXT = NODES + 2
ROWS = 112
MODES = 104
AXES = ("gx", "gy")

shift_mass = 0.1
mean_porosity = 0.7
exact_mode = lax.Precision.HIGHEST
plane_mode = lax.Precision.HIGH


def legendre_columns(node_set, degree):
    table = [node_set * 0.0 + 1.0, node_set]
    for order in range(2, degree + 1):
        table.append(
            ((2 * order - 1) * node_set * table[order - 1] - (order - 1) * table[order - 2]) / order
        )
    return table


def gll_tables():
    degree = NODES - 1
    node_set = np.cos(math.pi * np.arange(degree + 1) / degree)
    for sweep in range(100):
        table = legendre_columns(node_set, degree)
        node_set = node_set - (node_set * table[degree] - table[degree - 1]) / (
            (degree + 1) * table[degree]
        )
    node_set = node_set[::-1].copy()
    values = legendre_columns(node_set, degree)[degree]
    weights = 2.0 / (degree * (degree + 1) * values**2)
    derivative = np.zeros((NODES, NODES))
    for row_index in range(NODES):
        for column_index in range(NODES):
            if row_index != column_index:
                derivative[row_index, column_index] = values[row_index] / (
                    values[column_index] * (node_set[row_index] - node_set[column_index])
                )
    derivative[0, 0] = -degree * (degree + 1) / 4.0
    derivative[NODES - 1, NODES - 1] = degree * (degree + 1) / 4.0
    return (weights, derivative)


def jacobi_eigen(matrix):
    size_now = matrix.shape[0]
    current = matrix.copy()
    vectors = np.eye(size_now)
    for sweep in range(12):
        for first in range(size_now - 1):
            for second in range(first + 1, size_now):
                off_value = current[first, second]
                safe_value = np.where(off_value == 0.0, 1e-300, off_value)
                theta = (current[second, second] - current[first, first]) / (2.0 * safe_value)
                sign_value = np.where(theta >= 0.0, 1.0, -1.0)
                tangent = sign_value / (np.abs(theta) + np.sqrt(theta * theta + 1.0))
                cosine = 1.0 / np.sqrt(tangent * tangent + 1.0)
                sine = tangent * cosine
                rotation = np.eye(size_now)
                rotation[first, first] = cosine
                rotation[second, second] = cosine
                rotation[first, second] = sine
                rotation[second, first] = -sine
                current = rotation.T @ current @ rotation
                vectors = vectors @ rotation
    eigen_values = np.array([current[index, index] for index in range(size_now)])
    return (eigen_values, vectors)


def schwarz_tables():
    weights, derivative = gll_tables()
    stiffness = derivative.T @ (weights[:, None] * derivative)
    total_nodes = 3 * (NODES - 1) + 1
    three_stiffness = np.zeros((total_nodes, total_nodes))
    three_mass = np.zeros(total_nodes)
    for element in range(3):
        start_node = element * (NODES - 1)
        three_stiffness[
            start_node : start_node + NODES, start_node : start_node + NODES
        ] += stiffness
        three_mass[start_node : start_node + NODES] += weights
    chosen = np.array([NODES - 2] + list(range(NODES - 1, 2 * NODES - 1)) + [2 * NODES - 1])
    local_stiffness = three_stiffness[chosen][:, chosen]
    local_mass = three_mass[chosen]
    scaling = 1.0 / np.sqrt(local_mass)
    symmetric = scaling[:, None] * local_stiffness * scaling[None, :]
    symmetric = 0.5 * (symmetric + symmetric.T)
    eigen_values, eigen_vectors = jacobi_eigen(symmetric)
    return (scaling[:, None] * eigen_vectors, eigen_values)


WEIGHTS, DERIVATIVE = gll_tables()
STIFF = DERIVATIVE.T @ (WEIGHTS[:, None] * DERIVATIVE)
BASIS, EIGEN = schwarz_tables()
PARITY = {
    sign: [mode for mode in range(EXT) if BASIS[0, mode] * BASIS[EXT - 1, mode] * sign > 0]
    for sign in (1, -1)
}


def plane_tables():
    forward = np.zeros((MODES, ROWS))
    inverse = np.zeros((MODES, EXT))
    for mode_b in range(EXT):
        for mode_c in range(EXT):
            mode = mode_b * EXT + mode_c
            for b in range(EXT):
                for k in range(NODES):
                    forward[mode, b * NODES + k] = BASIS[b, mode_b] * BASIS[k + 1, mode_c]
                forward[mode, 80 + b] = BASIS[b, mode_b] * BASIS[0, mode_c]
                forward[mode, 96 + b] = BASIS[b, mode_b] * BASIS[EXT - 1, mode_c]
            inverse[mode] = 1.0 / (
                mean_porosity * (EIGEN + EIGEN[mode_b] + EIGEN[mode_c]) + shift_mass
            )
    lanes = np.repeat(inverse.T[:, :, None], 128, axis=2)
    return (
        forward.astype(np.float32),
        forward.T.astype(np.float32).copy(),
        lanes.astype(np.float32),
    )


def row_tile(values):
    row = lax.broadcasted_iota(jnp.int32, (NODES, 128), 0)
    tile = jnp.full((NODES, 128), float(values[0]), jnp.float32)
    for k in range(1, NODES):
        tile = jnp.where(row == k, float(values[k]), tile)
    return tile


def share_table(count):
    table = np.zeros((count, 3, count))
    for column in range(count):
        table[column, :, column] = 1.0
        if column > 0:
            table[column, 0, column] = 0.5
            table[column, 0, column - 1] = 0.5
        if column < count - 1:
            table[column, 2, column] = 0.5
            table[column, 2, column + 1] = 0.5
    return table


def cosine_inverse(count):
    position = np.arange(count)
    basis = np.cos(math.pi * (position[:, None] + 0.5) * position[None, :] / count)
    basis = basis * np.where(position == 0, math.sqrt(1.0 / count), math.sqrt(2.0 / count))[None, :]
    return basis, 2.0 - 2.0 * np.cos(math.pi * position / count)


def shift_up(rows):
    lane = lax.broadcasted_iota(jnp.int32, rows.shape, 1)
    return jnp.where(lane == 0, 0.0, pltpu.roll(rows, 1, 1))


def shift_down(rows):
    lane = lax.broadcasted_iota(jnp.int32, rows.shape, 1)
    return jnp.where(lane == 127, 0.0, pltpu.roll(rows, 127, 1))


class Sides:
    def __init__(self, axis, count):
        self.index = lax.axis_index(axis)
        self.even = lax.rem(self.index, 2) == 0
        self.no_low = self.index == 0
        self.no_high = self.index == count - 1

    def low(self, first, second):
        return jnp.where(self.no_low, 0.0, jnp.where(self.even, second, first))

    def high(self, first, second):
        return jnp.where(self.no_high, 0.0, jnp.where(self.even, first, second))

    def send_first(self, low_face, high_face):
        return jnp.where(self.even, high_face, low_face)

    def send_second(self, low_face, high_face):
        return jnp.where(self.even, low_face, high_face)


def multiplicity_tile():
    row = lax.broadcasted_iota(jnp.int32, (NODES, 128), 0)
    lane = lax.broadcasted_iota(jnp.int32, (NODES, 128), 1)
    shared = ((row == 0) & (lane > 0)) | ((row == NODES - 1) & (lane < 127))
    return jnp.where(shared, 0.5, 1.0)


def class_of(node):
    return 0 if node == 0 else (2 if node == NODES - 1 else 1)


def axis_factor(node, side):
    if node == 0:
        return jnp.where(side.no_low, 1.0, 0.5)
    if node == NODES - 1:
        return jnp.where(side.no_high, 1.0, 0.5)
    return None


def scaled(value, *factors):
    for factor in factors:
        if factor is not None:
            value = value * factor
    return value


def add_to(total, key, value):
    total[key] = value if key not in total else total[key] + value


def lane_sums(tiles):
    columns = [jnp.sum(tile, axis=0, keepdims=True) for tile in tiles]
    columns.append(jnp.zeros((16 - len(tiles), 128), jnp.float32))
    sums = jnp.sum(jnp.concatenate(columns, axis=0), axis=1, keepdims=True)
    return jnp.broadcast_to(sums, (16, 128))


def write_stats(stats_ref, tiles):
    row = lax.broadcasted_iota(jnp.int32, (16, 128), 0)
    lane = lax.broadcasted_iota(jnp.int32, (16, 128), 1)
    sums = jnp.sum(jnp.where(row == lane, lane_sums(tiles), 0.0), axis=0, keepdims=True)
    for index in range(stats_ref.shape[0]):
        stats_ref[index] = jnp.broadcast_to(sums, stats_ref.shape[1:])


def stat_columns(stats, first, count):
    lane = lax.broadcasted_iota(jnp.int32, stats.shape, 1)
    sums = lane_sums([jnp.where(lane == first + i, stats, 0.0) for i in range(count)])
    return [sums[i : i + 1] for i in range(count)]


def sum_lanes(counts):
    return -(-(counts[0] * counts[1] + 2) // 128) * 128


def share_rows(counts, side_x, side_y):
    lane = lax.broadcasted_iota(jnp.int32, (1, sum_lanes(counts)), 1)
    column_y = lax.rem(lane, counts[1])
    first_x = lane - column_y

    def weights(side, place, step, count):
        own = jnp.where(place == side.index * step, 1.0, 0.0)
        below = jnp.where(place == (side.index - 1) * step, 1.0, 0.0)
        above = jnp.where(place == (side.index + 1) * step, 1.0, 0.0)
        return (
            jnp.where(side.no_low, own, 0.5 * (own + below)),
            own,
            jnp.where(side.no_high, own, 0.5 * (own + above)),
        )

    inside = lane < counts[0] * counts[1]
    along_x = weights(side_x, first_x, counts[1], counts[0])
    along_y = weights(side_y, column_y, 1, counts[1])
    return [jnp.where(inside, wx * wy, 0.0) for wx in along_x for wy in along_y]


def summed_row(counts, tiles, side_x, side_y):
    sums = lane_sums(tiles)
    lane = lax.broadcasted_iota(jnp.int32, (1, sum_lanes(counts)), 1)
    total = None
    for i, share in enumerate(share_rows(counts, side_x, side_y)):
        term = share * sums[i : i + 1, 0:1]
        total = term if total is None else total + term
    for i in range(9, len(tiles)):
        total = total + jnp.where(lane == counts[0] * counts[1] + i - 9, sums[i : i + 1, 0:1], 0.0)
    pieces = [total[:, at : at + 128] for at in range(0, sum_lanes(counts), 128)]
    pieces.append(jnp.zeros((NODES - len(pieces), 128), jnp.float32))
    return jnp.concatenate(pieces, axis=0)


def row_of(counts, tile_ref):
    rows = [tile_ref[i : i + 1, :] for i in range(sum_lanes(counts) // 128)]
    return rows[0] if len(rows) == 1 else jnp.concatenate(rows, axis=1)


def lifted_rows(counts, row, lift_ref):
    sums = jnp.sum(lift_ref[...] * row, axis=1, keepdims=True)
    return jnp.broadcast_to(sums, (16, 128))


def row_value(counts, row, index):
    lane = lax.broadcasted_iota(jnp.int32, row.shape, 1)
    chosen = jnp.where(lane == counts[0] * counts[1] + index, row, 0.0)
    return jnp.broadcast_to(jnp.sum(chosen, axis=1, keepdims=True), (1, 128))


def class_tiles(sums):
    return [sums[(i, j)] for i in range(3) for j in range(3)]


def shared_class_tiles(field_ref, side_x, side_y):
    tile = multiplicity_tile()
    sums = {}
    for a in range(NODES):
        for b in range(NODES):
            add_to(sums, (class_of(a), class_of(b)), field_ref[a, b])
    for (i, j), value in sums.items():
        a, b = (0, 1, NODES - 1)[i], (0, 1, NODES - 1)[j]
        sums[(i, j)] = scaled(value * tile, axis_factor(a, side_x), axis_factor(b, side_y))
    return class_tiles(sums)


def start_kernel(counts, r_ref, sy_first, sy_second):
    side_x, side_y = Sides("gx", counts[0]), Sides("gy", counts[1])
    for a in range(NODES):
        low, high = r_ref[a, 1], r_ref[a, NODES - 2]
        sy_first[a] = side_y.send_first(low, high)
        sy_second[a] = side_y.send_second(low, high)
    sy_first[NODES] = summed_row(
        counts, shared_class_tiles(r_ref, side_x, side_y), side_x, side_y
    )


def planes(ref):
    return jnp.concatenate([ref[a] for a in range(EXT)], axis=1)


def local_solve(x_ref, forward_ref, back_ref, inverse_ref, part_ref):
    zero = jnp.zeros((6, 128), jnp.float32)
    for a in range(EXT):
        x_ref[a, 80:90] = shift_up(x_ref[a, pl.ds(6, EXT, stride=NODES), :])
        x_ref[a, 96:106] = shift_down(x_ref[a, pl.ds(1, EXT, stride=NODES), :])
        x_ref[a, 90:96] = zero
        x_ref[a, 106:112] = zero
    half = EXT // 2
    for block in range(ROWS // 8):
        rows = pl.ds(block * 8, 8)
        low = [x_ref[a, rows] for a in range(half)]
        high = [x_ref[EXT - 1 - a, rows] for a in range(half)]
        folded = {1: [x + y for x, y in zip(low, high)], -1: [x - y for x, y in zip(low, high)]}
        for sign in (1, -1):
            for mode in PARITY[sign]:
                total = folded[sign][0] * float(BASIS[0, mode])
                for a in range(1, half):
                    total = total + folded[sign][a] * float(BASIS[a, mode])
                x_ref[mode, rows] = total
    spectrum = jnp.dot(
        forward_ref[...], planes(x_ref), precision=plane_mode, preferred_element_type=jnp.float32
    ) * planes(inverse_ref)
    values = jnp.dot(
        back_ref[...], spectrum, precision=plane_mode, preferred_element_type=jnp.float32
    )
    for block in range(ROWS // 8):
        rows = pl.ds(block * 8, 8)
        modes = [values[block * 8 : block * 8 + 8, m * 128 : (m + 1) * 128] for m in range(EXT)]
        back = {}
        for sign in (1, -1):
            for a in range(half):
                total = None
                for mode in PARITY[sign]:
                    term = modes[mode] * float(BASIS[a, mode])
                    total = term if total is None else total + term
                back[(sign, a)] = total
        for a in range(half):
            part_ref[a, rows] = back[(1, a)] + back[(-1, a)]
            part_ref[EXT - 1 - a, rows] = back[(1, a)] - back[(-1, a)]
    for a in range(EXT):

        def layer(k):
            return (a, pl.ds(k, EXT, stride=NODES), slice(None))

        bottom, top = part_ref[layer(0)], part_ref[layer(NODES - 1)]
        part_ref[layer(0)] = bottom + shift_up(top)
        part_ref[layer(NODES - 1)] = top + shift_down(bottom)
        part_ref[layer(1)] = part_ref[layer(1)] + shift_up(part_ref[a, 96:106])
        part_ref[layer(NODES - 2)] = part_ref[layer(NODES - 2)] + shift_down(part_ref[a, 80:90])


def send_parts(part_ref, side_x, side_y, sy_first, sy_second, fx_first, fx_second):
    for a in range(EXT):
        low, high = part_ref[a, 0:16], part_ref[a, 64:80]
        sy_first[2 * a : 2 * a + 2] = side_y.send_first(low, high).reshape(2, NODES, 128)
        sy_second[2 * a : 2 * a + 2] = side_y.send_second(low, high).reshape(2, NODES, 128)
    for layer in range(2):
        low, high = part_ref[layer, 0:80], part_ref[NODES + layer, 0:80]
        fx_first[layer] = side_x.send_first(low, high).reshape(EXT, NODES, 128)
        fx_second[layer] = side_x.send_second(low, high).reshape(EXT, NODES, 128)


def first_solve_kernel(
    counts, r_ref, porosity_ref, ry_first, ry_second, rx_first, rx_second, forward_ref, back_ref,
    inverse_ref, part_ref, sy_first, sy_second, fx_first, fx_second, x_ref,
):
    for send in (sy_first, sy_second):
        send[2 * EXT] = jnp.broadcast_to(porosity_ref[...], (NODES, 128))
    side_x, side_y = Sides("gx", counts[0]), Sides("gy", counts[1])
    x_ref[0, 0:80] = side_x.low(rx_first[...], rx_second[...]).reshape(80, 128)
    x_ref[EXT - 1, 0:80] = side_x.high(rx_first[...], rx_second[...]).reshape(80, 128)
    for a in range(NODES):
        x_ref[a + 1, 0:8] = side_y.low(ry_first[a], ry_second[a])
        x_ref[a + 1, 8:72] = r_ref[a].reshape(64, 128)
        x_ref[a + 1, 72:80] = side_y.high(ry_first[a], ry_second[a])
    local_solve(x_ref, forward_ref, back_ref, inverse_ref, part_ref)
    send_parts(part_ref, side_x, side_y, sy_first, sy_second, fx_first, fx_second)


def second_solve_kernel(
    counts, u_ref, ry_first, ry_second, rx_first, rx_second, forward_ref, back_ref, inverse_ref,
    q_ref, part_ref, sy_first, sy_second, fx_first, fx_second, x_ref,
):
    side_x, side_y = Sides("gx", counts[0]), Sides("gy", counts[1])
    extend_image(
        u_ref, ry_first, ry_second, rx_first, rx_second, side_x, side_y, q_ref, x_ref, None
    )
    local_solve(x_ref, forward_ref, back_ref, inverse_ref, part_ref)
    send_parts(part_ref, side_x, side_y, sy_first, sy_second, fx_first, fx_second)


def late_solve_kernel(
    counts, u_ref, ry_first, ry_second, rx_first, rx_second, columns_ref, lift_ref, sum_ref,
    forward_ref, back_ref, inverse_ref, q_ref, part_ref, sy_first, sy_second, fx_first, fx_second,
    field_ref, x_ref, table_ref,
):
    side_x, side_y = Sides("gx", counts[0]), Sides("gy", counts[1])
    table_ref[...] = jnp.broadcast_to(
        jnp.sum(lift_ref[...] * sum_ref[0:1], axis=1, keepdims=True), table_ref.shape
    )
    fields = near_fields(counts, table_ref, side_x, side_y)
    own = fields[(1, 1)]
    field_ref[...] = jnp.concatenate(
        [own[i][j] for i in range(3) for j in range(3)] + [jnp.zeros((7, 128), jnp.float32)]
    )
    image = LiftedImage(fields, columns_ref)
    extend_image(
        u_ref, ry_first, ry_second, rx_first, rx_second, side_x, side_y, q_ref, x_ref, image
    )
    local_solve(x_ref, forward_ref, back_ref, inverse_ref, part_ref)
    send_parts(part_ref, side_x, side_y, sy_first, sy_second, fx_first, fx_second)


def extend_image(
    u_ref, ry_first, ry_second, rx_first, rx_second, side_x, side_y, q_ref, x_ref, image
):
    low_x = side_x.low(rx_first[...], rx_second[...])
    high_x = side_x.high(rx_first[...], rx_second[...])

    def lifted(value, a, b):
        return value if image is None else value + image.at(a - 1, b - 1)

    for b in range(EXT):
        rows = pl.ds(b * 8, 8)
        x_ref[0, rows] = lifted(low_x[0, b], 0, b)
        x_ref[EXT - 1, rows] = lifted(high_x[1, b], EXT - 1, b)
    for a in range(NODES):
        low_y = side_y.low(ry_first[a], ry_second[a])
        high_y = side_y.high(ry_first[a], ry_second[a])
        rows = [low_y[0]]
        for b in range(NODES):
            value = u_ref[a, b]
            if b == 0:
                value = value + low_y[1]
            if b == NODES - 1:
                value = value + high_y[0]
            rows.append(value)
        rows.append(high_y[1])
        for b in range(EXT):
            value = rows[b]
            if a == 0:
                value = value + low_x[1, b]
            if a == NODES - 1:
                value = value + high_x[0, b]
            value = lifted(value, a + 1, b)
            x_ref[a + 1, b * 8 : b * 8 + 8] = value
            if 0 < b < EXT - 1:
                q_ref[a, b - 1] = value


def collect_parts(part_ref, ry_first, ry_second, rx_first, rx_second, side_x, side_y, field):
    low_x = side_x.low(rx_first[...], rx_second[...])
    high_x = side_x.high(rx_first[...], rx_second[...])
    result = {}
    for a in range(NODES):
        low_y = side_y.low(ry_first[a + 1], ry_second[a + 1])
        high_y = side_y.high(ry_first[a + 1], ry_second[a + 1])
        for b in range(NODES):
            value = part_ref[a + 1, (b + 1) * 8 : (b + 2) * 8]
            if b < 2:
                value = value + low_y[b]
            if b >= NODES - 2:
                value = value + high_y[b - (NODES - 2)]
            if a < 2:
                value = value + low_x[a, b]
            if a >= NODES - 2:
                value = value + high_x[a - (NODES - 2), b]
            if field is not None:
                node_class = 3 * class_of(a) + class_of(b)
                value = value + field[node_class : node_class + 1, :]
            result[(a, b)] = value
    return result


def apply_tiles(z_ref, u_ref, y_ref, por):
    weight_tile = row_tile(WEIGHTS)
    stiff_tiles = [
        row_tile([STIFF[k, (k - shift) % NODES] for k in range(NODES)]) for shift in range(NODES)
    ]
    for a in range(NODES):
        for b in range(NODES):
            y_ref[a, b] = z_ref[a, b] * weight_tile
    for a in range(NODES):
        for b in range(NODES):
            z = z_ref[a, b]
            third = z * stiff_tiles[0]
            for shift in range(1, NODES):
                third = third + pltpu.roll(z, shift, 0) * stiff_tiles[shift]
            first = y_ref[0, b] * float(STIFF[a, 0] * WEIGHTS[b])
            second = y_ref[a, 0] * float(STIFF[b, 0] * WEIGHTS[a])
            for other in range(1, NODES):
                first = first + y_ref[other, b] * float(STIFF[a, other] * WEIGHTS[b])
                second = second + y_ref[a, other] * float(STIFF[b, other] * WEIGHTS[a])
            weight = float(WEIGHTS[a] * WEIGHTS[b])
            u_ref[a, b] = por * (third * weight + first + second) + y_ref[a, b] * (
                shift_mass * weight
            )


def sum_column(u_ref):
    for a in range(NODES):
        bottom = u_ref[a, :, 0, :]
        top = u_ref[a, :, NODES - 1, :]
        u_ref[a, :, 0, :] = bottom + shift_up(top)
        u_ref[a, :, NODES - 1, :] = top + shift_down(bottom)


def first_apply_kernel(
    counts, part_ref, ry_first, ry_second, rx_first, rx_second, sum_ref, lift_ref, porosity_ref,
    r_ref, z_ref, u_ref, sy_first, sy_second, fx_first, fx_second, tile_ref, y_ref,
):
    side_x, side_y = Sides("gx", counts[0]), Sides("gy", counts[1])
    field = lifted_rows(counts, row_of(counts, sum_ref), lift_ref)
    z = collect_parts(part_ref, ry_first, ry_second, rx_first, rx_second, side_x, side_y, field)
    inner = None
    for (a, b), value in z.items():
        z_ref[a, b] = value
        term = scaled(value * r_ref[a, b], axis_factor(a, side_x), axis_factor(b, side_y))
        inner = term if inner is None else inner + term
    inner = inner * multiplicity_tile()
    apply_tiles(z_ref, u_ref, y_ref, porosity_ref[...])
    sums = {}
    curvature = None
    for a in range(NODES):
        for b in range(NODES):
            value = u_ref[a, b]
            add_to(sums, (class_of(a), class_of(b)), value)
            term = value * z_ref[a, b]
            curvature = term if curvature is None else curvature + term
    tiles = class_tiles(sums) + [inner, curvature]
    tile_ref[...] = summed_row(counts, tiles, side_x, side_y)
    sum_column(u_ref)
    send_layers(u_ref, side_x, side_y, sy_first, sy_second, fx_first, fx_second)


def second_apply_kernel(
    counts, part_ref, ry_first, ry_second, rx_first, rx_second, sum_ref, lift_ref, porosity_ref,
    r_ref, q_ref, z_ref, z1_ref, u_ref, sy_first, sy_second, fx_first, fx_second, stats_ref, y_ref,
):
    side_x, side_y = Sides("gx", counts[0]), Sides("gy", counts[1])
    summed = row_of(counts, sum_ref)
    field = lifted_rows(counts, summed, lift_ref)
    step = row_value(counts, summed, 0) / row_value(counts, summed, 1)
    w = collect_parts(part_ref, ry_first, ry_second, rx_first, rx_second, side_x, side_y, field)
    inner = None
    for (a, b), value in w.items():
        next_z = z_ref[a, b] - step * value
        next_r = r_ref[a, b] - step * q_ref[a, b]
        z1_ref[a, b] = next_z
        term = scaled(next_z * next_r, axis_factor(a, side_x), axis_factor(b, side_y))
        inner = term if inner is None else inner + term
    inner = inner * multiplicity_tile()
    apply_tiles(z1_ref, u_ref, y_ref, porosity_ref[...])
    own = None
    cross = None
    for a in range(NODES):
        for b in range(NODES):
            value = u_ref[a, b]
            own_term = value * z1_ref[a, b]
            cross_term = value * z_ref[a, b]
            own = own_term if own is None else own + own_term
            cross = cross_term if cross is None else cross + cross_term
    write_stats(stats_ref, [inner, own, cross])
    sum_column(u_ref)
    for a in range(NODES):
        low, high = u_ref[a, 0], u_ref[a, NODES - 1]
        sy_first[a] = side_y.send_first(low, high)
        sy_second[a] = side_y.send_second(low, high)
    low, high = u_ref[0], u_ref[NODES - 1]
    fx_first[...] = side_x.send_first(low, high)
    fx_second[...] = side_x.send_second(low, high)


def send_layers(u_ref, side_x, side_y, sy_first, sy_second, fx_first, fx_second):
    for a in range(NODES):
        for layer in range(2):
            low, high = u_ref[a, layer], u_ref[a, NODES - 2 + layer]
            sy_first[2 * a + layer] = side_y.send_first(low, high)
            sy_second[2 * a + layer] = side_y.send_second(low, high)
    for layer in range(2):
        low, high = u_ref[layer], u_ref[NODES - 2 + layer]
        fx_first[layer] = side_x.send_first(low, high)
        fx_second[layer] = side_x.send_second(low, high)


def early_apply_kernel(
    counts, part_ref, ry_first, ry_second, rx_first, rx_second, porosity_ref,
    z_ref, u_ref, sy_first, sy_second, fx_first, fx_second, y_ref,
):
    side_x, side_y = Sides("gx", counts[0]), Sides("gy", counts[1])
    z = collect_parts(part_ref, ry_first, ry_second, rx_first, rx_second, side_x, side_y, None)
    for (a, b), value in z.items():
        z_ref[a, b] = value
    apply_tiles(z_ref, u_ref, y_ref, porosity_ref[...])
    sum_column(u_ref)
    send_layers(u_ref, side_x, side_y, sy_first, sy_second, fx_first, fx_second)


def late_apply_kernel(
    counts, part_ref, ry_first, ry_second, rx_first, rx_second, porosity_ref, low_ref, own_ref,
    high_ref, r_ref, q_ref, schwarz_ref, field_ref, w_ref, u_ref, sy_first, sy_second, fx_first, fx_second, stats_ref,
    y_ref,
):
    side_x, side_y = Sides("gx", counts[0]), Sides("gy", counts[1])
    w = collect_parts(part_ref, ry_first, ry_second, rx_first, rx_second, side_x, side_y, None)
    inner = first_inner = first_curvature = None
    for (a, b), value in w.items():
        w_ref[a, b] = value
        node_class = 3 * class_of(a) + class_of(b)
        z = schwarz_ref[a, b] + field_ref[node_class : node_class + 1, :]
        q = q_ref[a, b]
        factors = (axis_factor(a, side_x), axis_factor(b, side_y))
        terms = [scaled(t, *factors) for t in (value * q, z * r_ref[a, b], z * q)]
        if inner is None:
            inner, first_inner, first_curvature = terms
        else:
            inner, first_inner, first_curvature = (
                inner + terms[0], first_inner + terms[1], first_curvature + terms[2]
            )
    tile = multiplicity_tile()
    inner, first_inner, first_curvature = inner * tile, first_inner * tile, first_curvature * tile
    porosity = porosity_ref[...]
    apply_tiles(w_ref, u_ref, y_ref, porosity)
    sums = {}
    own = None
    for a in range(NODES):
        for b in range(NODES):
            value = u_ref[a, b]
            add_to(sums, (class_of(a), class_of(b)), value)
            term = value * w_ref[a, b]
            own = term if own is None else own + term
    total = counts[0] * counts[1]
    tiles = class_tiles(sums) + [inner, own, porosity]
    first_tiles = shared_class_tiles(q_ref, side_x, side_y) + [first_inner, first_curvature]
    row = summed_row(counts, first_tiles, side_x, side_y)[0:1] + pltpu.roll(
        summed_row(counts, tiles, side_x, side_y), total + 2, 1
    )[0:1]
    for index in range(stats_ref.shape[0]):
        stats_ref[index] = jnp.broadcast_to(row, stats_ref.shape[1:])
    sum_column(u_ref)
    near = [[ref[y : y + 1] for y in range(3)] for ref in (low_ref, own_ref, high_ref)]
    send_corners(
        u_ref, w_ref, y_ref, near, side_x, side_y, sy_first, sy_second, fx_first, fx_second
    )


def sum_tile(tile):
    row = lax.broadcasted_iota(jnp.int32, (NODES, 128), 0)
    below = jnp.where(row == 0, pltpu.roll(shift_up(tile), 1, 0), 0.0)
    above = jnp.where(row == NODES - 1, pltpu.roll(shift_down(tile), NODES - 1, 0), 0.0)
    return tile + below + above


def send_corners(
    u_ref, w_ref, y_ref, near, side_x, side_y, sy_first, sy_second, fx_first, fx_second
):
    ends = (0, NODES - 1)

    def along_x(end, b):
        return combine(STIFF[end] * WEIGHTS[b], [y_ref[a, b] for a in range(NODES)])

    def along_y(end, a):
        return combine(STIFF[end] * WEIGHTS[a], [y_ref[a, b] for b in range(NODES)])

    for a in range(NODES):
        low, high = u_ref[a, 0], u_ref[a, NODES - 1]
        sy_first[a] = side_y.send_first(low, high)
        sy_second[a] = side_y.send_second(low, high)
        low, high = u_ref[0, a], u_ref[NODES - 1, a]
        fx_first[a] = side_x.send_first(low, high)
        fx_second[a] = side_x.send_second(low, high)
    for place, node in enumerate(ends):
        low, high = (sum_tile(near[2 * place][1] * along_y(end, node)) for end in ends)
        sy_first[NODES + place] = side_y.send_first(low, high)
        sy_second[NODES + place] = side_y.send_second(low, high)
        low, high = (sum_tile(near[1][2 * place] * along_x(end, node)) for end in ends)
        fx_first[NODES + place] = side_x.send_first(low, high)
        fx_second[NODES + place] = side_x.send_second(low, high)
    weight = float(WEIGHTS[0] * WEIGHTS[0])
    for i, a in enumerate(ends):
        for j, b in enumerate(ends):
            porosity = near[2 * i][2 * j]
            value = w_ref[a, b]
            third = None
            for shift in range(NODES):
                turned = value if shift == 0 else pltpu.roll(value, shift, 0)
                term = turned * row_tile([STIFF[k, (k - shift) % NODES] for k in range(NODES)])
                third = term if third is None else third + term
            mass = jnp.where(porosity > 0.0, shift_mass * y_ref[a, b], 0.0)
            u_ref[a, b] = u_ref[a, b] + weight * sum_tile(porosity * third + mass)


def prepare_late_kernel(counts, sol_ref, r_ref, schwarz_ref, field_ref, z_ref, sol_out, r_out):
    for a in range(NODES):
        for b in range(NODES):
            node_class = 3 * class_of(a) + class_of(b)
            z_ref[a, b] = schwarz_ref[a, b] + field_ref[node_class : node_class + 1, :]
            sol_out[a, b] = sol_ref[a, b]
            r_out[a, b] = r_ref[a, b]


def porosity_kernel(counts, low_ref, own_ref, high_ref, out_ref):
    row = lax.broadcasted_iota(jnp.int32, (NODES, 128), 0)
    weights = row_tile(WEIGHTS)
    mass = shift_mass * weights / multiplicity_tile()
    end = float(WEIGHTS[0])
    for x, ref in enumerate((low_ref, own_ref, high_ref)):
        for y in range(3):
            porosity = ref[y : y + 1]
            tile = porosity * weights
            tile = tile + jnp.where(row == 0, end * shift_up(porosity), 0.0)
            tile = tile + jnp.where(row == NODES - 1, end * shift_down(porosity), 0.0)
            out_ref[3 * x + y] = tile
            out_ref[9 + 3 * x + y] = jnp.where(porosity > 0.0, mass, 0.0)


CLASS_STIFF = np.stack(
    [STIFF[:, 0], STIFF[:, 1 : NODES - 1].sum(axis=1), STIFF[:, NODES - 1]], axis=1
)
CLASS_ENDS = np.stack(
    [CLASS_STIFF[0], CLASS_STIFF[1 : NODES - 1].sum(axis=0), CLASS_STIFF[NODES - 1]]
)
CLASS_WEIGHTS = np.array([WEIGHTS[0], WEIGHTS[1 : NODES - 1].sum(), WEIGHTS[NODES - 1]])


def combine(coefficients, values):
    total = None
    for coefficient, value in zip(coefficients, values):
        term = value * float(coefficient)
        total = term if total is None else total + term
    return total


def sharing(node):
    return {
        -1: [(0, NODES - 2)], 0: [(1, 0), (0, NODES - 1)],
        NODES - 1: [(1, NODES - 1), (2, 0)], NODES: [(2, 1)],
    }.get(node, [(1, node)])


class LiftedImage:
    def __init__(self, fields, columns_ref):
        self.fields, self.columns, self.known = fields, columns_ref, {}

    def along(self, column, place, other_class, axis):
        key = (column, place, other_class, axis)
        if key not in self.known:
            field = self.fields[column]
            line = [
                field[i][other_class] if axis == 0 else field[other_class][i] for i in range(3)
            ]
            self.known[key] = combine(CLASS_STIFF[place], line)
        return self.known[key]

    def at(self, a, b):
        total = None
        for i, place_a in sharing(a):
            for j, place_b in sharing(b):
                class_a, class_b = class_of(place_a), class_of(place_b)
                stiff = self.along((i, j), place_a, class_b, 0) * float(WEIGHTS[place_b])
                stiff = stiff + self.along((i, j), place_b, class_a, 1) * float(WEIGHTS[place_a])
                mass = self.fields[(i, j)][class_a][class_b]
                mass = mass * float(WEIGHTS[place_a] * WEIGHTS[place_b])
                term = stiff * self.columns[3 * i + j] + mass * self.columns[9 + 3 * i + j]
                total = term if total is None else total + term
        return total


def near_fields(counts, table_ref, side_x, side_y):
    total = counts[0] * counts[1]

    def field_of(step_x, step_y):
        x = jnp.clip(side_x.index + step_x, 0, counts[0] - 1)
        y = jnp.clip(side_y.index + step_y, 0, counts[1] - 1)
        place = x * counts[1] + y
        return [
            [table_ref[pl.ds((3 * i + j) * total + place, 1), :] for j in range(3)]
            for i in range(3)
        ]

    return {(i, j): field_of(i - 1, j - 1) for i in range(3) for j in range(3)}


def lifted_energy(counts, table_ref, porosity_sums, length):
    total = counts[0] * counts[1]
    field = [
        [table_ref[pl.ds((3 * i + j) * total, total), :] for j in range(3)] for i in range(3)
    ]

    def line(values):
        terms = []
        for i, j in ((0, 1), (0, 2), (1, 2)):
            difference = values[i] - values[j]
            terms.append(difference * difference * float(-CLASS_ENDS[i, j]))
        return terms[0] + terms[1] + terms[2]

    stiff = None
    mass = None
    for i in range(3):
        term = line(field[i]) * float(CLASS_WEIGHTS[i])
        term = term + line([field[j][i] for j in range(3)]) * float(CLASS_WEIGHTS[i])
        stiff = term if stiff is None else stiff + term
        for j in range(3):
            term = field[i][j] * field[i][j] * float(CLASS_WEIGHTS[i] * CLASS_WEIGHTS[j])
            mass = term if mass is None else mass + term
    energy = stiff * porosity_sums * 2.0 + mass * (shift_mass * 2.0 * length)
    return jnp.sum(energy, axis=0, keepdims=True)


def late_final_kernel(
    counts, sol_ref, r_ref, q_ref, z_ref, w_ref, u_ref, ry_first, ry_second, rx_first, rx_second,
    columns_ref, lift_ref, stats_ref, sol_out, r_out, d_out, steps_out, table_ref,
):
    side_x, side_y = Sides("gx", counts[0]), Sides("gy", counts[1])
    total = counts[0] * counts[1]
    stats = stats_ref[:, 0, :]
    summed = jnp.sum(stats, axis=0, keepdims=True)
    table_ref[...] = jnp.broadcast_to(
        jnp.sum(lift_ref[...] * summed, axis=1, keepdims=True), table_ref.shape
    )
    column = lax.broadcasted_iota(jnp.int32, (total, 128), 0)
    lane = lax.broadcasted_iota(jnp.int32, (total, 128), 1)
    at = 2 * total + 2
    porosity_sums = jnp.sum(
        jnp.where(lane == at + 2, stats, 0.0), axis=1, keepdims=True
    )
    coarse = table_ref[pl.ds(4 * total, total), :]

    def product(first):
        chosen = jnp.where(lane == column + first, coarse * summed, 0.0)
        return jnp.sum(jnp.sum(chosen, axis=0, keepdims=True), axis=1, keepdims=True)

    def value(index):
        return jnp.sum(jnp.where(lane[0:1] == index, summed, 0.0), axis=1, keepdims=True)

    first_inner, first_curvature = value(total), value(total + 1)
    cross = value(at) + product(0)
    energy = value(at + 1) + 2.0 * product(total + 2) + lifted_energy(
        counts, table_ref, porosity_sums, sol_ref.shape[-1]
    )
    first_step = first_inner / first_curvature
    second_inner = first_step * first_step * cross - first_inner
    ratio = second_inner / first_inner
    mixed = first_curvature - first_step * cross
    own = first_curvature - 2.0 * first_step * cross + first_step * first_step * energy
    second_step = second_inner / (own + ratio * (2.0 * mixed + ratio * first_curvature))
    first_step, second_step, ratio = (
        jnp.broadcast_to(scalar[:, 0:1], (1, 128)) for scalar in (first_step, second_step, ratio)
    )
    steps_out[0] = first_step[0, 0]
    steps_out[1] = second_step[0, 0]

    fields = near_fields(counts, table_ref, side_x, side_y)
    lifted_image = LiftedImage(fields, columns_ref)
    low_x = side_x.low(rx_first[...], rx_second[...])
    high_x = side_x.high(rx_first[...], rx_second[...])
    corner_y = {}
    for place in range(2):
        tiles = ry_first[NODES + place], ry_second[NODES + place]
        corner_y[(place > 0, False)] = side_y.low(*tiles)
        corner_y[(place > 0, True)] = side_y.high(*tiles)
    for a in range(NODES):
        for b in range(NODES):
            image = u_ref[a, b]
            if b == 0:
                image = image + side_y.low(ry_first[a], ry_second[a])
            if b == NODES - 1:
                image = image + side_y.high(ry_first[a], ry_second[a])
            if a == 0:
                image = image + low_x[b]
            if a == NODES - 1:
                image = image + high_x[b]
            if a in (0, NODES - 1) and b in (0, NODES - 1):
                from_x = low_x if a == 0 else high_x
                image = image + from_x[NODES + (b > 0)] + corner_y[(a > 0, b > 0)]
            lifted = fields[(1, 1)][class_of(a)][class_of(b)]
            image = image + lifted_image.at(a, b)
            z, q = z_ref[a, b], q_ref[a, b]
            direction = z - first_step * (w_ref[a, b] + lifted) + ratio * z
            image = q - first_step * image + ratio * q
            d_out[a, b] = direction
            sol_out[a, b] = sol_ref[a, b] + first_step * z + second_step * direction
            r_out[a, b] = r_ref[a, b] - first_step * q - second_step * image


def prepare_kernel(counts, sol_ref, r_ref, q_ref, z_ref, sum_ref, sol_out, r_out):
    summed = row_of(counts, sum_ref)
    step = row_value(counts, summed, 0) / row_value(counts, summed, 1)
    for a in range(NODES):
        for b in range(NODES):
            sol_out[a, b] = sol_ref[a, b] + step * z_ref[a, b]
            r_out[a, b] = r_ref[a, b] - step * q_ref[a, b]


def final_kernel(
    counts, sol_ref, r_ref, q_ref, z_ref, z1_ref, u_ref, ry_first, ry_second, rx_first, rx_second,
    sum_ref, last_ref, sol_out, r_out, d_out, steps_out,
):
    side_x, side_y = Sides("gx", counts[0]), Sides("gy", counts[1])
    summed = row_of(counts, sum_ref)
    first_inner, first_curvature = row_value(counts, summed, 0), row_value(counts, summed, 1)
    second_inner, own, cross = stat_columns(last_ref[:, 0, :], 0, 3)
    first_step = first_inner / first_curvature
    ratio = second_inner / first_inner
    second_step = second_inner / (own + ratio * (2.0 * cross + ratio * first_curvature))
    steps_out[0] = first_step[0, 0]
    steps_out[1] = second_step[0, 0]
    low_x = side_x.low(rx_first[...], rx_second[...])
    high_x = side_x.high(rx_first[...], rx_second[...])
    for a in range(NODES):
        for b in range(NODES):
            image = u_ref[a, b]
            if b == 0:
                image = image + side_y.low(ry_first[a], ry_second[a])
            if b == NODES - 1:
                image = image + side_y.high(ry_first[a], ry_second[a])
            if a == 0:
                image = image + low_x[b]
            if a == NODES - 1:
                image = image + high_x[b]
            z, q = z_ref[a, b], q_ref[a, b]
            direction = z1_ref[a, b] + ratio * z
            image = image + ratio * q
            d_out[a, b] = direction
            sol_out[a, b] = sol_ref[a, b] + second_step * direction
            r_out[a, b] = r_ref[a, b] - second_step * image


COSTS = {
    "start": 100, "first_solve": 1300, "second_solve": 1300, "first_apply": 800,
    "second_apply": 800, "prepare": 20000, "final": 500, "late_apply": 800, "porosity": 20000, "late_final": 800,
}


def call(kernel, counts, name, shapes, scratch, *operands):
    def body(*refs):
        kernel(counts, *refs)

    def space(shape):
        return pltpu.SMEM if len(shape) == 1 else pltpu.VMEM

    return pl.pallas_call(
        body,
        name=name,
        out_shape=[jax.ShapeDtypeStruct(shape, jnp.float32) for shape in shapes],
        in_specs=[pl.BlockSpec(memory_space=pltpu.VMEM)] * len(operands),
        out_specs=[pl.BlockSpec(memory_space=space(shape)) for shape in shapes],
        scratch_shapes=[pltpu.VMEM(shape, jnp.float32) for shape in scratch],
        compiler_params=pltpu.CompilerParams(vmem_limit_bytes=24 * 1024 * 1024),
        cost_estimate=pl.CostEstimate(
            flops=COSTS[name] * 1000000, bytes_accessed=COSTS[name] * 3000, transcendentals=0
        ),
    )(*operands)


def swap_pairs(counts, axis, parity):
    count_x, count_y = counts
    pairs = []
    for x in range(count_x):
        for y in range(count_y):
            if axis == 0:
                to = ((x + 1 if x % 2 == parity else x - 1) % count_x, y)
            else:
                other = y + 1 if y % 2 == parity else y - 1
                to = (x, other) if 0 <= other < count_y else (x ^ 1, y)
            pairs.append((x * count_y + y, to[0] * count_y + to[1]))
    return pairs


def trade(counts, axis, first, second):
    return (
        lax.ppermute(first, AXES, swap_pairs(counts, axis, 0)),
        lax.ppermute(second, AXES, swap_pairs(counts, axis, 1)),
    )


def trade_far(counts, value, far_x, far_y):
    pairs = [
        (x * counts[1] + y, (x ^ far_x) * counts[1] + (y ^ far_y))
        for x in range(counts[0])
        for y in range(counts[1])
    ]
    return lax.ppermute(value, AXES, pairs)


class RunningSum:
    def __init__(self, counts, tile, carried):
        self.counts = counts
        self.carried = carried
        self.value = tile if self.carried else lax.psum(tile, AXES)

    def add(self, received):
        if self.carried:
            self.value = self.value + received

    def far(self, *steps):
        return [trade_far(self.counts, self.value, *step) for step in steps if self.carried]


def carry(tiles, running):
    return jnp.concatenate([tiles.reshape((-1, NODES, 128)), running.value[None]])


def carried(received, shape):
    return received[:-1].reshape(shape), received[-1]


def gather_stats(stats):
    return lax.all_to_all(stats, AXES, 0, 0)


def lift_tables(counts, column_length):
    share_x, share_y = share_table(counts[0]), share_table(counts[1])
    basis_x, eigen_x = cosine_inverse(counts[0])
    basis_y, eigen_y = cosine_inverse(counts[1])
    divisor = (
        2.0 * mean_porosity * column_length * (eigen_x[:, None] + eigen_y[None, :])
        + 8.0 * shift_mass * column_length
    )
    modes_x = np.einsum("xip,pa->xia", share_x, basis_x)
    modes_y = np.einsum("yjq,qb->yjb", share_y, basis_y)
    total = counts[0] * counts[1]
    to_modes = np.einsum("pa,qb->abpq", basis_x, basis_y).reshape(total, total)
    to_modes = np.pad(to_modes, ((0, 0), (0, sum_lanes(counts) - total)))
    return [table.astype(np.float32) for table in (modes_x, modes_y, 1.0 / divisor, to_modes)]


def all_lift(counts, column_length):
    modes_x, modes_y, inverse, to_modes = lift_tables(counts, column_length)
    total = counts[0] * counts[1]
    lift = np.einsum(
        "xia,yjb,ab,abl->ijxyl", *(
            table.astype(np.float64)
            for table in (modes_x, modes_y, inverse, to_modes.reshape(inverse.shape + (-1,)))
        ),
    )
    return jnp.asarray(lift.reshape(9 * total, -1).astype(np.float32))


def own_lift(tables):
    modes_x, modes_y, inverse, to_modes = [jnp.asarray(table) for table in tables]
    own_x = lax.dynamic_index_in_dim(modes_x, lax.axis_index("gx"), 0, keepdims=False)
    own_y = lax.dynamic_index_in_dim(modes_y, lax.axis_index("gy"), 0, keepdims=False)
    own = own_x[:, None, :, None] * own_y[None, :, None, :] * inverse[None, None]
    lift = jnp.dot(own.reshape(9, -1), to_modes, precision=exact_mode)
    return jnp.pad(lift, ((0, 7), (0, 0)))


def shards_of(counts):
    forward_np, back_np, inverse_np = plane_tables()

    def shards(solution, residual, grain_counts):
        shard_shape = solution.shape
        block = shard_shape[2:]
        solution = solution.reshape(block)
        residual = residual.reshape(block)
        lift = own_lift(lift_tables(counts, block[-1]))
        late = counts == (8, 4)
        every_lift = all_lift(counts, block[-1]) if late else None
        porosity = 1.0 - 0.6 * grain_counts.reshape(1, 128).astype(jnp.float32) / MOST_GRAINS
        plane = [jnp.asarray(table) for table in (forward_np, back_np, inverse_np)]
        side_x, side_y = Sides("gx", counts[0]), Sides("gy", counts[1])
        row = (counts[0] * counts[1], 4, 128)
        face = (NODES, NODES, 128)
        part_shapes = [
            (EXT, ROWS, 128),
            (2 * EXT, NODES, 128), (2 * EXT, NODES, 128),
            (2, EXT, NODES, 128), (2, EXT, NODES, 128),
        ]
        first_shapes = list(part_shapes)
        first_shapes[1:3] = [(2 * EXT + 1, NODES, 128)] * 2
        solve_scratch = [(EXT, ROWS, 128)]

        y_first, y_second = call(
            start_kernel, counts, "start", [(NODES + 1,) + face[1:], face], [], residual
        )
        running = RunningSum(counts, y_first[-1], late)
        ry = trade(counts, 1, y_first, y_second)
        ry_first, tile = carried(ry[0], face)
        running.add(tile)
        ry = (ry_first, ry[1])
        low_y, high_y = side_y.low(*ry), side_y.high(*ry)

        def with_layers(index):
            return jnp.concatenate([low_y[index][None], residual[index], high_y[index][None]])

        low_face, high_face = with_layers(1), with_layers(NODES - 2)
        rx = trade(
            counts, 0, carry(side_x.send_first(low_face, high_face), running),
            side_x.send_second(low_face, high_face),
        )
        rx_first, tile = carried(rx[0], low_face.shape)
        running.add(tile)
        rx = (rx_first, rx[1])
        part, y_first, y_second, *fx = call(
            first_solve_kernel, counts, "first_solve", first_shapes, solve_scratch,
            residual, porosity, *ry, *rx, *plane,
        )

        def spread_faces(fx, ry):
            low_y, high_y = side_y.low(*ry), side_y.high(*ry)
            middle = jnp.zeros((2, NODES - 4, NODES, 128), jnp.float32)
            both = [
                jnp.concatenate([low_y[at], middle, high_y[at]], axis=1)
                for at in (slice(0, 2), slice(8, 10))
            ]
            return (
                fx[0][:, 1:-1] + side_x.send_first(*both),
                fx[1][:, 1:-1] + side_x.send_second(*both),
            )

        def trade_y(y_first, y_second, shape):
            count = math.prod(shape[:-2])
            ry = trade(counts, 1, y_first, y_second)
            faces = [value[:count].reshape(shape) for value in ry]
            return faces, [value[count:] for value in ry]

        ext_face = (EXT, 2, NODES, 128)
        two = (NODES, 2, NODES, 128)
        tiles = (-1, NODES, 128)
        middle = jnp.broadcast_to(porosity, (1, NODES, 128))
        if late:
            y_second = jnp.concatenate([y_second, running.value[None]])
            ry, rows = trade_y(y_first, y_second, ext_face)
            inner_y = (side_y.index > 0) & (side_y.index < counts[1] - 1)
            running.add(jnp.where(inner_y, rows[1][1], 0.0))
        else:
            ry, rows = trade_y(y_first, y_second, ext_face)
        three = jnp.concatenate(
            [
                side[0, 0:1]
                for side in (
                    side_y.low(rows[0][:1], rows[1][:1]), middle,
                    side_y.high(rows[0][:1], rows[1][:1]),
                )
            ]
            + [jnp.zeros((NODES - 3, 128), jnp.float32)]
        )
        first, second = spread_faces(fx, ry)
        rx = trade(
            counts, 0, jnp.concatenate([first.reshape(tiles), three[None]]),
            jnp.concatenate([second.reshape(tiles), three[None], running.value[None]]),
        )
        count = 2 * NODES
        threes = [value[count] for value in rx]
        running.add(rx[1][count + 1])
        rx = [value[:count].reshape(first.shape) for value in rx]
        if late:
            z, u, y_first, y_second, *fx = call(
                early_apply_kernel, counts, "first_apply",
                [block, block, (2 * NODES, NODES, 128), (2 * NODES, NODES, 128),
                 (2, NODES, NODES, 128), (2, NODES, NODES, 128)],
                [block],
                part, *ry, *rx, porosity,
            )
            y_first = jnp.concatenate([y_first, running.value[None]])
        else:
            z, u, y_first, y_second, *fx, tile = call(
                first_apply_kernel, counts, "first_apply",
                [block, block, (2 * NODES, NODES, 128), (2 * NODES, NODES, 128),
                 (2, NODES, NODES, 128), (2, NODES, NODES, 128), (NODES, 128)],
                [block],
                part, *ry, *rx, running.value, lift, porosity, residual,
            )
        ry, rows = trade_y(y_first, y_second, two)
        if late:
            running.value = jnp.where(inner_y, running.value, rows[0][0])
        low_y, high_y = side_y.low(*ry), side_y.high(*ry)

        def image_faces(index):
            middle = jnp.zeros((2, NODES - 2, NODES, 128), jnp.float32)
            return jnp.concatenate([low_y[index], middle, high_y[index]], axis=1)

        pads = ((0, 0), (1, 1), (0, 0), (0, 0))
        both = (image_faces(slice(0, 2)), image_faces(slice(NODES - 2, NODES)))
        rx = trade(
            counts, 0,
            jnp.pad(fx[0], pads) + side_x.send_first(*both),
            jnp.pad(fx[1], pads) + side_x.send_second(*both),
        )
        if late:
            near = (side_x.low(*threes), three, side_x.high(*threes))
            (columns,) = call(porosity_kernel, counts, "porosity", [(18, NODES, 128)], [], *near)
            rx, far, columns = lax.optimization_barrier((rx, running.far((4, 0)), columns))
            for value in far:
                running.add(value)
            table = (9 * counts[0] * counts[1], 128)
            q, part, y_first, y_second, *fx, field = call(
                late_solve_kernel, counts, "second_solve", [block] + part_shapes + [(16, 128)],
                solve_scratch + [table],
                u, *ry, *rx, columns, every_lift, running.value, *plane,
            )
        else:
            q, part, y_first, y_second, *fx = call(
                second_solve_kernel, counts, "second_solve", [block] + part_shapes, solve_scratch,
                u, *ry, *rx, *plane,
            )
        ry, _ = trade_y(y_first, y_second, ext_face)
        rx = trade(counts, 0, *spread_faces(fx, ry))

        def trade_edges(y_first, y_second, fx, beside):
            ry, beside = lax.optimization_barrier((trade(counts, 1, y_first, y_second), beside))
            low_y, high_y = side_y.low(*ry), side_y.high(*ry)

            def edge_rows(index):
                middle = jnp.zeros((NODES - 2, NODES, 128), jnp.float32)
                return jnp.concatenate([low_y[index][None], middle, high_y[index][None]])

            both = (edge_rows(0), edge_rows(NODES - 1))
            rx = trade(
                counts, 0, fx[0] + side_x.send_first(*both), fx[1] + side_x.send_second(*both)
            )
            return ry, rx, beside

        if late:
            w, u, y_first, y_second, *fx, stats = call(
                late_apply_kernel, counts, "late_apply",
                [block, block] + [(NODES + 2, NODES, 128)] * 4 + [row], [block],
                part, *ry, *rx, porosity, *near, residual, q, z, field,
            )
            z, w = lax.optimization_barrier((z, w))
            nexts = call(
                prepare_late_kernel, counts, "prepare", [block] * 3, [],
                solution, residual, z, field,
            )
            ry, rx, (z, solution, residual) = lax.optimization_barrier(
                (trade(counts, 1, y_first, y_second), trade(counts, 0, *fx), nexts)
            )
            solution_out, residual_out, direction, steps = call(
                late_final_kernel, counts, "late_final", [block] * 3 + [(2,)], [table],
                solution, residual, q, z, w, u, *ry, *rx, columns, every_lift,
                gather_stats(stats),
            )
        else:
            summed = lax.psum(tile, AXES)
            z1, u, y_first, y_second, *fx, stats = call(
                second_apply_kernel, counts, "second_apply",
                [block, block, face, face, face, face, row], [block],
                part, *ry, *rx, summed, lift, porosity, residual, q, z,
            )
            nexts = call(
                prepare_kernel, counts, "prepare", [block] * 2, [],
                solution, residual, q, z, summed,
            )
            ry, rx, nexts = trade_edges(y_first, y_second, fx, nexts)
            solution_out, residual_out, direction, steps = call(
                final_kernel, counts, "final", [block] * 3 + [(2,)], [],
                *nexts, q, z, z1, u, *ry, *rx, summed, gather_stats(stats),
            )
        return (
            solution_out.reshape(shard_shape),
            residual_out.reshape(shard_shape),
            direction.reshape(shard_shape),
            steps,
        )

    return shards


def solution(mesh):
    counts = (mesh.shape["gx"], mesh.shape["gy"])
    return jax.shard_map(
        shards_of(counts),
        mesh=mesh,
        in_specs=(
            P("gx", "gy", None, None, None, None),
            P("gx", "gy", None, None, None, None),
            P("gx", "gy", None),
        ),
        out_specs=(
            P("gx", "gy", None, None, None, None),
            P("gx", "gy", None, None, None, None),
            P("gx", "gy", None, None, None, None),
            P(),
        ),
        check_vma=False,
    )
```

```python
import math

import jax
import jax.numpy as jnp
import numpy as np
from jax import lax
from jax.experimental import pallas as pl
from jax.experimental.pallas import tpu as pltpu
from jax.sharding import PartitionSpec as P

NODES = 8
MOST_GRAINS = 16
EXT = NODES + 2
ROWS = 112
MODES = 104
AXES = ("gx", "gy")
EDGE = (0, 1, EXT - 2, EXT - 1)
INNER = tuple(range(2, EXT - 2))

shift_mass = 0.1
mean_porosity = 0.7
exact_mode = lax.Precision.HIGHEST
plane_mode = lax.Precision.HIGH


def legendre_columns(node_set, degree):
    table = [node_set * 0.0 + 1.0, node_set]
    for order in range(2, degree + 1):
        table.append(
            ((2 * order - 1) * node_set * table[order - 1] - (order - 1) * table[order - 2]) / order
        )
    return table


def gll_tables():
    degree = NODES - 1
    node_set = np.cos(math.pi * np.arange(degree + 1) / degree)
    for sweep in range(100):
        table = legendre_columns(node_set, degree)
        node_set = node_set - (node_set * table[degree] - table[degree - 1]) / (
            (degree + 1) * table[degree]
        )
    node_set = node_set[::-1].copy()
    values = legendre_columns(node_set, degree)[degree]
    weights = 2.0 / (degree * (degree + 1) * values**2)
    derivative = np.zeros((NODES, NODES))
    for row_index in range(NODES):
        for column_index in range(NODES):
            if row_index != column_index:
                derivative[row_index, column_index] = values[row_index] / (
                    values[column_index] * (node_set[row_index] - node_set[column_index])
                )
    derivative[0, 0] = -degree * (degree + 1) / 4.0
    derivative[NODES - 1, NODES - 1] = degree * (degree + 1) / 4.0
    return (weights, derivative)


def jacobi_eigen(matrix):
    size_now = matrix.shape[0]
    current = matrix.copy()
    vectors = np.eye(size_now)
    for sweep in range(12):
        for first in range(size_now - 1):
            for second in range(first + 1, size_now):
                off_value = current[first, second]
                safe_value = np.where(off_value == 0.0, 1e-300, off_value)
                theta = (current[second, second] - current[first, first]) / (2.0 * safe_value)
                sign_value = np.where(theta >= 0.0, 1.0, -1.0)
                tangent = sign_value / (np.abs(theta) + np.sqrt(theta * theta + 1.0))
                cosine = 1.0 / np.sqrt(tangent * tangent + 1.0)
                sine = tangent * cosine
                rotation = np.eye(size_now)
                rotation[first, first] = cosine
                rotation[second, second] = cosine
                rotation[first, second] = sine
                rotation[second, first] = -sine
                current = rotation.T @ current @ rotation
                vectors = vectors @ rotation
    eigen_values = np.array([current[index, index] for index in range(size_now)])
    return (eigen_values, vectors)


def schwarz_tables():
    weights, derivative = gll_tables()
    stiffness = derivative.T @ (weights[:, None] * derivative)
    total_nodes = 3 * (NODES - 1) + 1
    three_stiffness = np.zeros((total_nodes, total_nodes))
    three_mass = np.zeros(total_nodes)
    for element in range(3):
        start_node = element * (NODES - 1)
        three_stiffness[
            start_node : start_node + NODES, start_node : start_node + NODES
        ] += stiffness
        three_mass[start_node : start_node + NODES] += weights
    chosen = np.array([NODES - 2] + list(range(NODES - 1, 2 * NODES - 1)) + [2 * NODES - 1])
    local_stiffness = three_stiffness[chosen][:, chosen]
    local_mass = three_mass[chosen]
    scaling = 1.0 / np.sqrt(local_mass)
    symmetric = scaling[:, None] * local_stiffness * scaling[None, :]
    symmetric = 0.5 * (symmetric + symmetric.T)
    eigen_values, eigen_vectors = jacobi_eigen(symmetric)
    return (scaling[:, None] * eigen_vectors, eigen_values)


WEIGHTS, DERIVATIVE = gll_tables()
STIFF = DERIVATIVE.T @ (WEIGHTS[:, None] * DERIVATIVE)
BASIS, EIGEN = schwarz_tables()
PARITY = {
    sign: [mode for mode in range(EXT) if BASIS[0, mode] * BASIS[EXT - 1, mode] * sign > 0]
    for sign in (1, -1)
}


def plane_tables():
    forward = np.zeros((MODES, ROWS))
    inverse = np.zeros((MODES, EXT))
    for mode_b in range(EXT):
        for mode_c in range(EXT):
            mode = mode_b * EXT + mode_c
            for b in range(EXT):
                for k in range(NODES):
                    forward[mode, b * NODES + k] = BASIS[b, mode_b] * BASIS[k + 1, mode_c]
                forward[mode, 80 + b] = BASIS[b, mode_b] * BASIS[0, mode_c]
                forward[mode, 96 + b] = BASIS[b, mode_b] * BASIS[EXT - 1, mode_c]
            inverse[mode] = 1.0 / (
                mean_porosity * (EIGEN + EIGEN[mode_b] + EIGEN[mode_c]) + shift_mass
            )
    lanes = np.repeat(inverse.T[:, :, None], 128, axis=2)
    back = forward.T
    tables = [
        np.concatenate([back[[8 * b + k for b in layers for k in range(NODES)]]]
                       + [pad_rows(back[[at + b for b in layers]], 8) for at in (80, 96)])
        for layers in (EDGE, INNER)
    ]
    return tuple(table.astype(np.float32) for table in (forward, *tables, lanes))


def pad_rows(table, count):
    return np.pad(table, ((0, -len(table) % count), (0, 0)))


def row_tile(values):
    row = lax.broadcasted_iota(jnp.int32, (NODES, 128), 0)
    tile = jnp.full((NODES, 128), float(values[0]), jnp.float32)
    for k in range(1, NODES):
        tile = jnp.where(row == k, float(values[k]), tile)
    return tile


def share_table(count):
    table = np.zeros((count, 3, count))
    for column in range(count):
        table[column, :, column] = 1.0
        if column > 0:
            table[column, 0, column] = 0.5
            table[column, 0, column - 1] = 0.5
        if column < count - 1:
            table[column, 2, column] = 0.5
            table[column, 2, column + 1] = 0.5
    return table


def cosine_inverse(count):
    position = np.arange(count)
    basis = np.cos(math.pi * (position[:, None] + 0.5) * position[None, :] / count)
    basis = basis * np.where(position == 0, math.sqrt(1.0 / count), math.sqrt(2.0 / count))[None, :]
    return basis, 2.0 - 2.0 * np.cos(math.pi * position / count)


def shift_up(rows):
    lane = lax.broadcasted_iota(jnp.int32, rows.shape, 1)
    return jnp.where(lane == 0, 0.0, pltpu.roll(rows, 1, 1))


def shift_down(rows):
    lane = lax.broadcasted_iota(jnp.int32, rows.shape, 1)
    return jnp.where(lane == 127, 0.0, pltpu.roll(rows, 127, 1))


class Sides:
    def __init__(self, axis, count):
        self.index = lax.axis_index(axis)
        self.even = lax.rem(self.index, 2) == 0
        self.no_low = self.index == 0
        self.no_high = self.index == count - 1

    def low(self, first, second):
        return jnp.where(self.no_low, 0.0, jnp.where(self.even, second, first))

    def high(self, first, second):
        return jnp.where(self.no_high, 0.0, jnp.where(self.even, first, second))

    def send_first(self, low_face, high_face):
        return jnp.where(self.even, high_face, low_face)

    def send_second(self, low_face, high_face):
        return jnp.where(self.even, low_face, high_face)


def multiplicity_tile():
    row = lax.broadcasted_iota(jnp.int32, (NODES, 128), 0)
    lane = lax.broadcasted_iota(jnp.int32, (NODES, 128), 1)
    shared = ((row == 0) & (lane > 0)) | ((row == NODES - 1) & (lane < 127))
    return jnp.where(shared, 0.5, 1.0)


def class_of(node):
    return 0 if node == 0 else (2 if node == NODES - 1 else 1)


def axis_factor(node, side):
    if node == 0:
        return jnp.where(side.no_low, 1.0, 0.5)
    if node == NODES - 1:
        return jnp.where(side.no_high, 1.0, 0.5)
    return None


def scaled(value, *factors):
    for factor in factors:
        if factor is not None:
            value = value * factor
    return value


def add_to(total, key, value):
    total[key] = value if key not in total else total[key] + value


def lane_sums(tiles):
    columns = [jnp.sum(tile, axis=0, keepdims=True) for tile in tiles]
    columns.append(jnp.zeros((16 - len(tiles), 128), jnp.float32))
    sums = jnp.sum(jnp.concatenate(columns, axis=0), axis=1, keepdims=True)
    return jnp.broadcast_to(sums, (16, 128))


def write_stats(stats_ref, tiles):
    row = lax.broadcasted_iota(jnp.int32, (16, 128), 0)
    lane = lax.broadcasted_iota(jnp.int32, (16, 128), 1)
    sums = jnp.sum(jnp.where(row == lane, lane_sums(tiles), 0.0), axis=0, keepdims=True)
    for index in range(stats_ref.shape[0]):
        stats_ref[index] = jnp.broadcast_to(sums, stats_ref.shape[1:])


def stat_columns(stats, first, count):
    lane = lax.broadcasted_iota(jnp.int32, stats.shape, 1)
    sums = lane_sums([jnp.where(lane == first + i, stats, 0.0) for i in range(count)])
    return [sums[i : i + 1] for i in range(count)]


def sum_lanes(counts):
    return -(-(counts[0] * counts[1] + 2) // 128) * 128


def share_rows(counts, side_x, side_y):
    lane = lax.broadcasted_iota(jnp.int32, (1, sum_lanes(counts)), 1)
    column_y = lax.rem(lane, counts[1])
    first_x = lane - column_y

    def weights(side, place, step, count):
        own = jnp.where(place == side.index * step, 1.0, 0.0)
        below = jnp.where(place == (side.index - 1) * step, 1.0, 0.0)
        above = jnp.where(place == (side.index + 1) * step, 1.0, 0.0)
        return (
            jnp.where(side.no_low, own, 0.5 * (own + below)),
            own,
            jnp.where(side.no_high, own, 0.5 * (own + above)),
        )

    inside = lane < counts[0] * counts[1]
    along_x = weights(side_x, first_x, counts[1], counts[0])
    along_y = weights(side_y, column_y, 1, counts[1])
    return [jnp.where(inside, wx * wy, 0.0) for wx in along_x for wy in along_y]


def summed_row(counts, tiles, side_x, side_y):
    sums = lane_sums(tiles)
    lane = lax.broadcasted_iota(jnp.int32, (1, sum_lanes(counts)), 1)
    total = None
    for i, share in enumerate(share_rows(counts, side_x, side_y)):
        term = share * sums[i : i + 1, 0:1]
        total = term if total is None else total + term
    for i in range(9, len(tiles)):
        total = total + jnp.where(lane == counts[0] * counts[1] + i - 9, sums[i : i + 1, 0:1], 0.0)
    pieces = [total[:, at : at + 128] for at in range(0, sum_lanes(counts), 128)]
    pieces.append(jnp.zeros((NODES - len(pieces), 128), jnp.float32))
    return jnp.concatenate(pieces, axis=0)


def row_of(counts, tile_ref):
    rows = [tile_ref[i : i + 1, :] for i in range(sum_lanes(counts) // 128)]
    return rows[0] if len(rows) == 1 else jnp.concatenate(rows, axis=1)


def lifted_rows(counts, row, lift_ref):
    sums = jnp.sum(lift_ref[...] * row, axis=1, keepdims=True)
    return jnp.broadcast_to(sums, (16, 128))


def row_value(counts, row, index):
    lane = lax.broadcasted_iota(jnp.int32, row.shape, 1)
    chosen = jnp.where(lane == counts[0] * counts[1] + index, row, 0.0)
    return jnp.broadcast_to(jnp.sum(chosen, axis=1, keepdims=True), (1, 128))


def class_tiles(sums):
    return [sums[(i, j)] for i in range(3) for j in range(3)]


def shared_class_tiles(field_ref, side_x, side_y):
    tile = multiplicity_tile()
    sums = {}
    for a in range(NODES):
        for b in range(NODES):
            add_to(sums, (class_of(a), class_of(b)), field_ref[a, b])
    for (i, j), value in sums.items():
        a, b = (0, 1, NODES - 1)[i], (0, 1, NODES - 1)[j]
        sums[(i, j)] = scaled(value * tile, axis_factor(a, side_x), axis_factor(b, side_y))
    return class_tiles(sums)


def start_kernel(counts, r_ref, sy_first, sy_second):
    side_x, side_y = Sides("gx", counts[0]), Sides("gy", counts[1])
    for a in range(NODES):
        low, high = r_ref[a, 1], r_ref[a, NODES - 2]
        sy_first[a] = side_y.send_first(low, high)
        sy_second[a] = side_y.send_second(low, high)
    sy_first[NODES] = summed_row(
        counts, shared_class_tiles(r_ref, side_x, side_y), side_x, side_y
    )


def planes(ref):
    return jnp.concatenate([ref[a] for a in range(EXT)], axis=1)


def to_spectrum(x_ref, forward_ref, inverse_ref):
    zero = jnp.zeros((6, 128), jnp.float32)
    for a in range(EXT):
        x_ref[a, 80:90] = shift_up(x_ref[a, pl.ds(6, EXT, stride=NODES), :])
        x_ref[a, 96:106] = shift_down(x_ref[a, pl.ds(1, EXT, stride=NODES), :])
        x_ref[a, 90:96] = zero
        x_ref[a, 106:112] = zero
    half = EXT // 2
    for block in range(ROWS // 8):
        rows = pl.ds(block * 8, 8)
        low = [x_ref[a, rows] for a in range(half)]
        high = [x_ref[EXT - 1 - a, rows] for a in range(half)]
        folded = {1: [x + y for x, y in zip(low, high)], -1: [x - y for x, y in zip(low, high)]}
        for sign in (1, -1):
            for mode in PARITY[sign]:
                total = folded[sign][0] * float(BASIS[0, mode])
                for a in range(1, half):
                    total = total + folded[sign][a] * float(BASIS[a, mode])
                x_ref[mode, rows] = total
    spectrum = jnp.dot(
        forward_ref[...], planes(x_ref), precision=plane_mode, preferred_element_type=jnp.float32
    ) * planes(inverse_ref)
    return spectrum


def from_spectrum(spectrum, back_ref, part_ref, count):
    half = EXT // 2
    values = jnp.dot(
        back_ref[...], spectrum, precision=plane_mode, preferred_element_type=jnp.float32
    )
    for block in range(part_ref.shape[1] // 8):
        rows = pl.ds(block * 8, 8)
        modes = [values[block * 8 : block * 8 + 8, m * 128 : (m + 1) * 128] for m in range(EXT)]
        back = {}
        for sign in (1, -1):
            for a in range(half):
                total = None
                for mode in PARITY[sign]:
                    term = modes[mode] * float(BASIS[a, mode])
                    total = term if total is None else total + term
                back[(sign, a)] = total
        for a in range(half):
            part_ref[a, rows] = back[(1, a)] + back[(-1, a)]
            part_ref[EXT - 1 - a, rows] = back[(1, a)] - back[(-1, a)]
    below, above = NODES * count, NODES * count + 8
    for a in range(EXT):

        def layer(k):
            return (a, pl.ds(k, count, stride=NODES), slice(None))

        bottom, top = part_ref[layer(0)], part_ref[layer(NODES - 1)]
        part_ref[layer(0)] = bottom + shift_up(top)
        part_ref[layer(NODES - 1)] = top + shift_down(bottom)
        part_ref[layer(1)] = part_ref[layer(1)] + shift_up(part_ref[a, above : above + count])
        part_ref[layer(NODES - 2)] = part_ref[layer(NODES - 2)] + shift_down(
            part_ref[a, below : below + count]
        )


def solve_edges(
    x_ref, forward_ref, back_ref, inverse_ref, spectrum_ref, edge_ref, sy_first, sy_second,
    side_y, part_ref,
):
    spectrum = to_spectrum(x_ref, forward_ref, inverse_ref)
    spectrum_ref[...] = spectrum
    from_spectrum(spectrum, back_ref, part_ref, len(EDGE))
    for a in range(EXT):
        low, high = part_ref[a, 0:16], part_ref[a, 16:32]
        sy_first[2 * a : 2 * a + 2] = side_y.send_first(low, high).reshape(2, NODES, 128)
        sy_second[2 * a : 2 * a + 2] = side_y.send_second(low, high).reshape(2, NODES, 128)
        edge_ref[a] = part_ref[a, 8:24]


def rest_kernel(
    counts, spectrum_ref, edge_ref, back_ref, part_ref, fx_first, fx_second, inner_ref
):
    side_x = Sides("gx", counts[0])
    from_spectrum(spectrum_ref[...], back_ref, inner_ref, len(INNER))
    for a in range(EXT):
        part_ref[a, 0:8] = edge_ref[a, 0:8]
        part_ref[a, 8:56] = inner_ref[a, 0:48]
        part_ref[a, 56:64] = edge_ref[a, 8:16]
    for layer in range(2):
        low, high = part_ref[layer], part_ref[NODES + layer]
        fx_first[layer] = side_x.send_first(low, high).reshape(NODES, NODES, 128)
        fx_second[layer] = side_x.send_second(low, high).reshape(NODES, NODES, 128)


def first_solve_kernel(
    counts, r_ref, porosity_ref, ry_first, ry_second, rx_first, rx_second, forward_ref, back_ref,
    inverse_ref, spectrum_ref, edge_ref, sy_first, sy_second, x_ref, part_ref,
):
    for send in (sy_first, sy_second):
        send[2 * EXT] = jnp.broadcast_to(porosity_ref[...], (NODES, 128))
    side_x, side_y = Sides("gx", counts[0]), Sides("gy", counts[1])
    x_ref[0, 0:80] = side_x.low(rx_first[...], rx_second[...]).reshape(80, 128)
    x_ref[EXT - 1, 0:80] = side_x.high(rx_first[...], rx_second[...]).reshape(80, 128)
    for a in range(NODES):
        x_ref[a + 1, 0:8] = side_y.low(ry_first[a], ry_second[a])
        x_ref[a + 1, 8:72] = r_ref[a].reshape(64, 128)
        x_ref[a + 1, 72:80] = side_y.high(ry_first[a], ry_second[a])
    solve_edges(
        x_ref, forward_ref, back_ref, inverse_ref, spectrum_ref, edge_ref, sy_first, sy_second,
        side_y, part_ref,
    )


def second_solve_kernel(
    counts, edge_ref, inner_ref, ry_first, ry_second, rx_first, rx_second, forward_ref, back_ref,
    inverse_ref, q_ref, spectrum_ref, layers_ref, sy_first, sy_second, x_ref, part_ref,
):
    side_x, side_y = Sides("gx", counts[0]), Sides("gy", counts[1])
    extend_image(
        edge_ref, inner_ref, ry_first, ry_second, rx_first, rx_second, side_x, side_y, q_ref, x_ref, None
    )
    solve_edges(
        x_ref, forward_ref, back_ref, inverse_ref, spectrum_ref, layers_ref, sy_first, sy_second,
        side_y, part_ref,
    )


def late_solve_kernel(
    counts, edge_ref, inner_ref, ry_first, ry_second, rx_first, rx_second, columns_ref, lift_ref,
    sum_ref, forward_ref, back_ref, inverse_ref, q_ref, spectrum_ref, layers_ref, sy_first,
    sy_second, field_ref, x_ref, part_ref, table_ref,
):
    side_x, side_y = Sides("gx", counts[0]), Sides("gy", counts[1])
    table_ref[...] = jnp.broadcast_to(
        jnp.sum(lift_ref[...] * sum_ref[0:1], axis=1, keepdims=True), table_ref.shape
    )
    fields = near_fields(counts, table_ref, side_x, side_y)
    own = fields[(1, 1)]
    field_ref[...] = jnp.concatenate(
        [own[i][j] for i in range(3) for j in range(3)] + [jnp.zeros((7, 128), jnp.float32)]
    )
    image = LiftedImage(fields, columns_ref)
    extend_image(
        edge_ref, inner_ref, ry_first, ry_second, rx_first, rx_second, side_x, side_y, q_ref, x_ref, image
    )
    solve_edges(
        x_ref, forward_ref, back_ref, inverse_ref, spectrum_ref, layers_ref, sy_first, sy_second,
        side_y, part_ref,
    )


def layer_of(edge_ref, inner_ref, a, b):
    if 2 <= b < NODES - 2:
        return inner_ref[a, b - 2]
    return edge_ref[a, b if b < 2 else b - (NODES - 4)]


def extend_image(
    edge_ref, inner_ref, ry_first, ry_second, rx_first, rx_second, side_x, side_y, q_ref, x_ref,
    image,
):
    low_x = side_x.low(rx_first[...], rx_second[...])
    high_x = side_x.high(rx_first[...], rx_second[...])

    def lifted(value, a, b):
        return value if image is None else value + image.at(a - 1, b - 1)

    for b in range(EXT):
        rows = pl.ds(b * 8, 8)
        x_ref[0, rows] = lifted(low_x[0, b], 0, b)
        x_ref[EXT - 1, rows] = lifted(high_x[1, b], EXT - 1, b)
    for a in range(NODES):
        low_y = side_y.low(ry_first[a], ry_second[a])
        high_y = side_y.high(ry_first[a], ry_second[a])
        rows = [low_y[0]]
        for b in range(NODES):
            value = layer_of(edge_ref, inner_ref, a, b)
            if b == 0:
                value = value + low_y[1]
            if b == NODES - 1:
                value = value + high_y[0]
            rows.append(value)
        rows.append(high_y[1])
        for b in range(EXT):
            value = rows[b]
            if a == 0:
                value = value + low_x[1, b]
            if a == NODES - 1:
                value = value + high_x[0, b]
            value = lifted(value, a + 1, b)
            x_ref[a + 1, b * 8 : b * 8 + 8] = value
            if 0 < b < EXT - 1:
                q_ref[a, b - 1] = value


def collect_parts(part_ref, ry_first, ry_second, rx_first, rx_second, side_x, side_y, field):
    low_x = side_x.low(rx_first[...], rx_second[...])
    high_x = side_x.high(rx_first[...], rx_second[...])
    result = {}
    for a in range(NODES):
        low_y = side_y.low(ry_first[a + 1], ry_second[a + 1])
        high_y = side_y.high(ry_first[a + 1], ry_second[a + 1])
        for b in range(NODES):
            value = part_ref[a + 1, b * 8 : (b + 1) * 8]
            if b < 2:
                value = value + low_y[b]
            if b >= NODES - 2:
                value = value + high_y[b - (NODES - 2)]
            if a < 2:
                value = value + low_x[a, b]
            if a >= NODES - 2:
                value = value + high_x[a - (NODES - 2), b]
            if field is not None:
                node_class = 3 * class_of(a) + class_of(b)
                value = value + field[node_class : node_class + 1, :]
            result[(a, b)] = value
    return result


def apply_tiles(z_ref, u_ref, y_ref, por, layers=range(NODES)):
    weight_tile = row_tile(WEIGHTS)
    stiff_tiles = [
        row_tile([STIFF[k, (k - shift) % NODES] for k in range(NODES)]) for shift in range(NODES)
    ]
    for a in range(NODES):
        for b in range(NODES):
            y_ref[a, b] = z_ref[a, b] * weight_tile
    for a in range(NODES):
        for place, b in enumerate(layers):
            z = z_ref[a, b]
            third = z * stiff_tiles[0]
            for shift in range(1, NODES):
                third = third + pltpu.roll(z, shift, 0) * stiff_tiles[shift]
            first = y_ref[0, b] * float(STIFF[a, 0] * WEIGHTS[b])
            second = y_ref[a, 0] * float(STIFF[b, 0] * WEIGHTS[a])
            for other in range(1, NODES):
                first = first + y_ref[other, b] * float(STIFF[a, other] * WEIGHTS[b])
                second = second + y_ref[a, other] * float(STIFF[b, other] * WEIGHTS[a])
            weight = float(WEIGHTS[a] * WEIGHTS[b])
            u_ref[a, place] = por * (third * weight + first + second) + y_ref[a, b] * (
                shift_mass * weight
            )


def sum_column(u_ref):
    for a in range(NODES):
        bottom = u_ref[a, :, 0, :]
        top = u_ref[a, :, NODES - 1, :]
        u_ref[a, :, 0, :] = bottom + shift_up(top)
        u_ref[a, :, NODES - 1, :] = top + shift_down(bottom)


def first_apply_kernel(
    counts, part_ref, ry_first, ry_second, rx_first, rx_second, sum_ref, lift_ref, porosity_ref,
    r_ref, z_ref, u_ref, sy_first, sy_second, fx_first, fx_second, tile_ref, y_ref,
):
    side_x, side_y = Sides("gx", counts[0]), Sides("gy", counts[1])
    field = lifted_rows(counts, row_of(counts, sum_ref), lift_ref)
    z = collect_parts(part_ref, ry_first, ry_second, rx_first, rx_second, side_x, side_y, field)
    inner = None
    for (a, b), value in z.items():
        z_ref[a, b] = value
        term = scaled(value * r_ref[a, b], axis_factor(a, side_x), axis_factor(b, side_y))
        inner = term if inner is None else inner + term
    inner = inner * multiplicity_tile()
    apply_tiles(z_ref, u_ref, y_ref, porosity_ref[...])
    sums = {}
    curvature = None
    for a in range(NODES):
        for b in range(NODES):
            value = u_ref[a, b]
            add_to(sums, (class_of(a), class_of(b)), value)
            term = value * z_ref[a, b]
            curvature = term if curvature is None else curvature + term
    tiles = class_tiles(sums) + [inner, curvature]
    tile_ref[...] = summed_row(counts, tiles, side_x, side_y)
    sum_column(u_ref)
    send_layers(u_ref, side_x, side_y, sy_first, sy_second, fx_first, fx_second)


def second_apply_kernel(
    counts, part_ref, ry_first, ry_second, rx_first, rx_second, sum_ref, lift_ref, porosity_ref,
    r_ref, q_ref, z_ref, z1_ref, u_ref, sy_first, sy_second, fx_first, fx_second, stats_ref, y_ref,
):
    side_x, side_y = Sides("gx", counts[0]), Sides("gy", counts[1])
    summed = row_of(counts, sum_ref)
    field = lifted_rows(counts, summed, lift_ref)
    step = row_value(counts, summed, 0) / row_value(counts, summed, 1)
    w = collect_parts(part_ref, ry_first, ry_second, rx_first, rx_second, side_x, side_y, field)
    inner = None
    for (a, b), value in w.items():
        next_z = z_ref[a, b] - step * value
        next_r = r_ref[a, b] - step * q_ref[a, b]
        z1_ref[a, b] = next_z
        term = scaled(next_z * next_r, axis_factor(a, side_x), axis_factor(b, side_y))
        inner = term if inner is None else inner + term
    inner = inner * multiplicity_tile()
    apply_tiles(z1_ref, u_ref, y_ref, porosity_ref[...])
    own = None
    cross = None
    for a in range(NODES):
        for b in range(NODES):
            value = u_ref[a, b]
            own_term = value * z1_ref[a, b]
            cross_term = value * z_ref[a, b]
            own = own_term if own is None else own + own_term
            cross = cross_term if cross is None else cross + cross_term
    write_stats(stats_ref, [inner, own, cross])
    sum_column(u_ref)
    for a in range(NODES):
        low, high = u_ref[a, 0], u_ref[a, NODES - 1]
        sy_first[a] = side_y.send_first(low, high)
        sy_second[a] = side_y.send_second(low, high)
    low, high = u_ref[0], u_ref[NODES - 1]
    fx_first[...] = side_x.send_first(low, high)
    fx_second[...] = side_x.send_second(low, high)


def send_layers(u_ref, side_x, side_y, sy_first, sy_second, fx_first, fx_second):
    for a in range(NODES):
        for layer in range(2):
            low, high = u_ref[a, layer], u_ref[a, NODES - 2 + layer]
            sy_first[2 * a + layer] = side_y.send_first(low, high)
            sy_second[2 * a + layer] = side_y.send_second(low, high)
    for layer in range(2):
        low, high = u_ref[layer], u_ref[NODES - 2 + layer]
        fx_first[layer] = side_x.send_first(low, high)
        fx_second[layer] = side_x.send_second(low, high)


def early_apply_kernel(
    counts, part_ref, ry_first, ry_second, rx_first, rx_second, porosity_ref,
    z_ref, edge_ref, sy_first, sy_second, y_ref,
):
    side_x, side_y = Sides("gx", counts[0]), Sides("gy", counts[1])
    z = collect_parts(part_ref, ry_first, ry_second, rx_first, rx_second, side_x, side_y, None)
    for (a, b), value in z.items():
        z_ref[a, b] = value
    apply_tiles(z_ref, edge_ref, y_ref, porosity_ref[...], (0, 1, NODES - 2, NODES - 1))
    sum_column(edge_ref)
    for a in range(NODES):
        for layer in range(2):
            low, high = edge_ref[a, layer], edge_ref[a, 2 + layer]
            sy_first[2 * a + layer] = side_y.send_first(low, high)
            sy_second[2 * a + layer] = side_y.send_second(low, high)


def rest_apply_kernel(
    counts, z_ref, edge_ref, porosity_ref, inner_ref, fx_first, fx_second, y_ref
):
    side_x = Sides("gx", counts[0])
    apply_tiles(z_ref, inner_ref, y_ref, porosity_ref[...], range(2, NODES - 2))
    sum_column(inner_ref)
    for layer in range(2):
        for b in range(NODES):
            low = layer_of(edge_ref, inner_ref, layer, b)
            high = layer_of(edge_ref, inner_ref, NODES - 2 + layer, b)
            fx_first[layer, b] = side_x.send_first(low, high)
            fx_second[layer, b] = side_x.send_second(low, high)


def late_apply_kernel(
    counts, part_ref, ry_first, ry_second, rx_first, rx_second, porosity_ref, low_ref, own_ref,
    high_ref, r_ref, q_ref, schwarz_ref, field_ref, w_ref, u_ref, sy_first, sy_second, fx_first, fx_second, stats_ref,
    y_ref,
):
    side_x, side_y = Sides("gx", counts[0]), Sides("gy", counts[1])
    w = collect_parts(part_ref, ry_first, ry_second, rx_first, rx_second, side_x, side_y, None)
    inner = first_inner = first_curvature = None
    for (a, b), value in w.items():
        w_ref[a, b] = value
        node_class = 3 * class_of(a) + class_of(b)
        z = schwarz_ref[a, b] + field_ref[node_class : node_class + 1, :]
        q = q_ref[a, b]
        factors = (axis_factor(a, side_x), axis_factor(b, side_y))
        terms = [scaled(t, *factors) for t in (value * q, z * r_ref[a, b], z * q)]
        if inner is None:
            inner, first_inner, first_curvature = terms
        else:
            inner, first_inner, first_curvature = (
                inner + terms[0], first_inner + terms[1], first_curvature + terms[2]
            )
    tile = multiplicity_tile()
    inner, first_inner, first_curvature = inner * tile, first_inner * tile, first_curvature * tile
    porosity = porosity_ref[...]
    apply_tiles(w_ref, u_ref, y_ref, porosity)
    sums = {}
    own = None
    for a in range(NODES):
        for b in range(NODES):
            value = u_ref[a, b]
            add_to(sums, (class_of(a), class_of(b)), value)
            term = value * w_ref[a, b]
            own = term if own is None else own + term
    total = counts[0] * counts[1]
    tiles = class_tiles(sums) + [inner, own, porosity]
    first_tiles = shared_class_tiles(q_ref, side_x, side_y) + [first_inner, first_curvature]
    row = summed_row(counts, first_tiles, side_x, side_y)[0:1] + pltpu.roll(
        summed_row(counts, tiles, side_x, side_y), total + 2, 1
    )[0:1]
    for index in range(stats_ref.shape[0]):
        stats_ref[index] = jnp.broadcast_to(row, stats_ref.shape[1:])
    sum_column(u_ref)
    near = [[ref[y : y + 1] for y in range(3)] for ref in (low_ref, own_ref, high_ref)]
    send_corners(
        u_ref, w_ref, y_ref, near, side_x, side_y, sy_first, sy_second, fx_first, fx_second
    )


def sum_tile(tile):
    row = lax.broadcasted_iota(jnp.int32, (NODES, 128), 0)
    below = jnp.where(row == 0, pltpu.roll(shift_up(tile), 1, 0), 0.0)
    above = jnp.where(row == NODES - 1, pltpu.roll(shift_down(tile), NODES - 1, 0), 0.0)
    return tile + below + above


def send_corners(
    u_ref, w_ref, y_ref, near, side_x, side_y, sy_first, sy_second, fx_first, fx_second
):
    ends = (0, NODES - 1)

    def along_x(end, b):
        return combine(STIFF[end] * WEIGHTS[b], [y_ref[a, b] for a in range(NODES)])

    def along_y(end, a):
        return combine(STIFF[end] * WEIGHTS[a], [y_ref[a, b] for b in range(NODES)])

    for a in range(NODES):
        low, high = u_ref[a, 0], u_ref[a, NODES - 1]
        sy_first[a] = side_y.send_first(low, high)
        sy_second[a] = side_y.send_second(low, high)
        low, high = u_ref[0, a], u_ref[NODES - 1, a]
        fx_first[a] = side_x.send_first(low, high)
        fx_second[a] = side_x.send_second(low, high)
    for place, node in enumerate(ends):
        low, high = (sum_tile(near[2 * place][1] * along_y(end, node)) for end in ends)
        sy_first[NODES + place] = side_y.send_first(low, high)
        sy_second[NODES + place] = side_y.send_second(low, high)
        low, high = (sum_tile(near[1][2 * place] * along_x(end, node)) for end in ends)
        fx_first[NODES + place] = side_x.send_first(low, high)
        fx_second[NODES + place] = side_x.send_second(low, high)
    weight = float(WEIGHTS[0] * WEIGHTS[0])
    for i, a in enumerate(ends):
        for j, b in enumerate(ends):
            porosity = near[2 * i][2 * j]
            value = w_ref[a, b]
            third = None
            for shift in range(NODES):
                turned = value if shift == 0 else pltpu.roll(value, shift, 0)
                term = turned * row_tile([STIFF[k, (k - shift) % NODES] for k in range(NODES)])
                third = term if third is None else third + term
            mass = jnp.where(porosity > 0.0, shift_mass * y_ref[a, b], 0.0)
            u_ref[a, b] = u_ref[a, b] + weight * sum_tile(porosity * third + mass)


def prepare_late_kernel(counts, sol_ref, r_ref, schwarz_ref, field_ref, z_ref, sol_out, r_out):
    for a in range(NODES):
        for b in range(NODES):
            node_class = 3 * class_of(a) + class_of(b)
            z_ref[a, b] = schwarz_ref[a, b] + field_ref[node_class : node_class + 1, :]
            sol_out[a, b] = sol_ref[a, b]
            r_out[a, b] = r_ref[a, b]


def porosity_kernel(counts, low_ref, own_ref, high_ref, out_ref):
    row = lax.broadcasted_iota(jnp.int32, (NODES, 128), 0)
    weights = row_tile(WEIGHTS)
    mass = shift_mass * weights / multiplicity_tile()
    end = float(WEIGHTS[0])
    for x, ref in enumerate((low_ref, own_ref, high_ref)):
        for y in range(3):
            porosity = ref[y : y + 1]
            tile = porosity * weights
            tile = tile + jnp.where(row == 0, end * shift_up(porosity), 0.0)
            tile = tile + jnp.where(row == NODES - 1, end * shift_down(porosity), 0.0)
            out_ref[3 * x + y] = tile
            out_ref[9 + 3 * x + y] = jnp.where(porosity > 0.0, mass, 0.0)


CLASS_STIFF = np.stack(
    [STIFF[:, 0], STIFF[:, 1 : NODES - 1].sum(axis=1), STIFF[:, NODES - 1]], axis=1
)
CLASS_ENDS = np.stack(
    [CLASS_STIFF[0], CLASS_STIFF[1 : NODES - 1].sum(axis=0), CLASS_STIFF[NODES - 1]]
)
CLASS_WEIGHTS = np.array([WEIGHTS[0], WEIGHTS[1 : NODES - 1].sum(), WEIGHTS[NODES - 1]])


def combine(coefficients, values):
    total = None
    for coefficient, value in zip(coefficients, values):
        term = value * float(coefficient)
        total = term if total is None else total + term
    return total


def sharing(node):
    return {
        -1: [(0, NODES - 2)], 0: [(1, 0), (0, NODES - 1)],
        NODES - 1: [(1, NODES - 1), (2, 0)], NODES: [(2, 1)],
    }.get(node, [(1, node)])


class LiftedImage:
    def __init__(self, fields, columns_ref):
        self.fields, self.columns, self.known = fields, columns_ref, {}

    def along(self, column, place, other_class, axis):
        key = (column, place, other_class, axis)
        if key not in self.known:
            field = self.fields[column]
            line = [
                field[i][other_class] if axis == 0 else field[other_class][i] for i in range(3)
            ]
            self.known[key] = combine(CLASS_STIFF[place], line)
        return self.known[key]

    def at(self, a, b):
        total = None
        for i, place_a in sharing(a):
            for j, place_b in sharing(b):
                class_a, class_b = class_of(place_a), class_of(place_b)
                stiff = self.along((i, j), place_a, class_b, 0) * float(WEIGHTS[place_b])
                stiff = stiff + self.along((i, j), place_b, class_a, 1) * float(WEIGHTS[place_a])
                mass = self.fields[(i, j)][class_a][class_b]
                mass = mass * float(WEIGHTS[place_a] * WEIGHTS[place_b])
                term = stiff * self.columns[3 * i + j] + mass * self.columns[9 + 3 * i + j]
                total = term if total is None else total + term
        return total


def near_fields(counts, table_ref, side_x, side_y):
    total = counts[0] * counts[1]

    def field_of(step_x, step_y):
        x = jnp.clip(side_x.index + step_x, 0, counts[0] - 1)
        y = jnp.clip(side_y.index + step_y, 0, counts[1] - 1)
        place = x * counts[1] + y
        return [
            [table_ref[pl.ds((3 * i + j) * total + place, 1), :] for j in range(3)]
            for i in range(3)
        ]

    return {(i, j): field_of(i - 1, j - 1) for i in range(3) for j in range(3)}


def lifted_energy(counts, table_ref, porosity_sums, length):
    total = counts[0] * counts[1]
    field = [
        [table_ref[pl.ds((3 * i + j) * total, total), :] for j in range(3)] for i in range(3)
    ]

    def line(values):
        terms = []
        for i, j in ((0, 1), (0, 2), (1, 2)):
            difference = values[i] - values[j]
            terms.append(difference * difference * float(-CLASS_ENDS[i, j]))
        return terms[0] + terms[1] + terms[2]

    stiff = None
    mass = None
    for i in range(3):
        term = line(field[i]) * float(CLASS_WEIGHTS[i])
        term = term + line([field[j][i] for j in range(3)]) * float(CLASS_WEIGHTS[i])
        stiff = term if stiff is None else stiff + term
        for j in range(3):
            term = field[i][j] * field[i][j] * float(CLASS_WEIGHTS[i] * CLASS_WEIGHTS[j])
            mass = term if mass is None else mass + term
    energy = stiff * porosity_sums * 2.0 + mass * (shift_mass * 2.0 * length)
    return jnp.sum(energy, axis=0, keepdims=True)


def late_final_kernel(
    counts, sol_ref, r_ref, q_ref, z_ref, w_ref, u_ref, ry_first, ry_second, rx_first, rx_second,
    columns_ref, lift_ref, stats_ref, sol_out, r_out, d_out, steps_out, table_ref,
):
    side_x, side_y = Sides("gx", counts[0]), Sides("gy", counts[1])
    total = counts[0] * counts[1]
    stats = stats_ref[:, 0, :]
    summed = jnp.sum(stats, axis=0, keepdims=True)
    table_ref[...] = jnp.broadcast_to(
        jnp.sum(lift_ref[...] * summed, axis=1, keepdims=True), table_ref.shape
    )
    column = lax.broadcasted_iota(jnp.int32, (total, 128), 0)
    lane = lax.broadcasted_iota(jnp.int32, (total, 128), 1)
    at = 2 * total + 2
    porosity_sums = jnp.sum(
        jnp.where(lane == at + 2, stats, 0.0), axis=1, keepdims=True
    )
    coarse = table_ref[pl.ds(4 * total, total), :]

    def product(first):
        chosen = jnp.where(lane == column + first, coarse * summed, 0.0)
        return jnp.sum(jnp.sum(chosen, axis=0, keepdims=True), axis=1, keepdims=True)

    def value(index):
        return jnp.sum(jnp.where(lane[0:1] == index, summed, 0.0), axis=1, keepdims=True)

    first_inner, first_curvature = value(total), value(total + 1)
    cross = value(at) + product(0)
    energy = value(at + 1) + 2.0 * product(total + 2) + lifted_energy(
        counts, table_ref, porosity_sums, sol_ref.shape[-1]
    )
    first_step = first_inner / first_curvature
    second_inner = first_step * first_step * cross - first_inner
    ratio = second_inner / first_inner
    mixed = first_curvature - first_step * cross
    own = first_curvature - 2.0 * first_step * cross + first_step * first_step * energy
    second_step = second_inner / (own + ratio * (2.0 * mixed + ratio * first_curvature))
    first_step, second_step, ratio = (
        jnp.broadcast_to(scalar[:, 0:1], (1, 128)) for scalar in (first_step, second_step, ratio)
    )
    steps_out[0] = first_step[0, 0]
    steps_out[1] = second_step[0, 0]

    fields = near_fields(counts, table_ref, side_x, side_y)
    lifted_image = LiftedImage(fields, columns_ref)
    low_x = side_x.low(rx_first[...], rx_second[...])
    high_x = side_x.high(rx_first[...], rx_second[...])
    corner_y = {}
    for place in range(2):
        tiles = ry_first[NODES + place], ry_second[NODES + place]
        corner_y[(place > 0, False)] = side_y.low(*tiles)
        corner_y[(place > 0, True)] = side_y.high(*tiles)
    for a in range(NODES):
        for b in range(NODES):
            image = u_ref[a, b]
            if b == 0:
                image = image + side_y.low(ry_first[a], ry_second[a])
            if b == NODES - 1:
                image = image + side_y.high(ry_first[a], ry_second[a])
            if a == 0:
                image = image + low_x[b]
            if a == NODES - 1:
                image = image + high_x[b]
            if a in (0, NODES - 1) and b in (0, NODES - 1):
                from_x = low_x if a == 0 else high_x
                image = image + from_x[NODES + (b > 0)] + corner_y[(a > 0, b > 0)]
            lifted = fields[(1, 1)][class_of(a)][class_of(b)]
            image = image + lifted_image.at(a, b)
            z, q = z_ref[a, b], q_ref[a, b]
            direction = z - first_step * (w_ref[a, b] + lifted) + ratio * z
            image = q - first_step * image + ratio * q
            d_out[a, b] = direction
            sol_out[a, b] = sol_ref[a, b] + first_step * z + second_step * direction
            r_out[a, b] = r_ref[a, b] - first_step * q - second_step * image


def prepare_kernel(counts, sol_ref, r_ref, q_ref, z_ref, sum_ref, sol_out, r_out):
    summed = row_of(counts, sum_ref)
    step = row_value(counts, summed, 0) / row_value(counts, summed, 1)
    for a in range(NODES):
        for b in range(NODES):
            sol_out[a, b] = sol_ref[a, b] + step * z_ref[a, b]
            r_out[a, b] = r_ref[a, b] - step * q_ref[a, b]


def final_kernel(
    counts, sol_ref, r_ref, q_ref, z_ref, z1_ref, u_ref, ry_first, ry_second, rx_first, rx_second,
    sum_ref, last_ref, sol_out, r_out, d_out, steps_out,
):
    side_x, side_y = Sides("gx", counts[0]), Sides("gy", counts[1])
    summed = row_of(counts, sum_ref)
    first_inner, first_curvature = row_value(counts, summed, 0), row_value(counts, summed, 1)
    second_inner, own, cross = stat_columns(last_ref[:, 0, :], 0, 3)
    first_step = first_inner / first_curvature
    ratio = second_inner / first_inner
    second_step = second_inner / (own + ratio * (2.0 * cross + ratio * first_curvature))
    steps_out[0] = first_step[0, 0]
    steps_out[1] = second_step[0, 0]
    low_x = side_x.low(rx_first[...], rx_second[...])
    high_x = side_x.high(rx_first[...], rx_second[...])
    for a in range(NODES):
        for b in range(NODES):
            image = u_ref[a, b]
            if b == 0:
                image = image + side_y.low(ry_first[a], ry_second[a])
            if b == NODES - 1:
                image = image + side_y.high(ry_first[a], ry_second[a])
            if a == 0:
                image = image + low_x[b]
            if a == NODES - 1:
                image = image + high_x[b]
            z, q = z_ref[a, b], q_ref[a, b]
            direction = z1_ref[a, b] + ratio * z
            image = image + ratio * q
            d_out[a, b] = direction
            sol_out[a, b] = sol_ref[a, b] + second_step * direction
            r_out[a, b] = r_ref[a, b] - second_step * image


COSTS = {
    "start": 100, "first_solve": 900, "second_solve": 900, "rest_of_solve": 600,
    "first_apply": 500, "rest_of_apply": 400, "second_apply": 800, "prepare": 20000,
    "final": 500, "late_apply": 800, "porosity": 20000, "late_final": 800,
}


def call(kernel, counts, name, shapes, scratch, *operands):
    def body(*refs):
        kernel(counts, *refs)

    def space(shape):
        return pltpu.SMEM if len(shape) == 1 else pltpu.VMEM

    return pl.pallas_call(
        body,
        name=name,
        out_shape=[jax.ShapeDtypeStruct(shape, jnp.float32) for shape in shapes],
        in_specs=[pl.BlockSpec(memory_space=pltpu.VMEM)] * len(operands),
        out_specs=[pl.BlockSpec(memory_space=space(shape)) for shape in shapes],
        scratch_shapes=[pltpu.VMEM(shape, jnp.float32) for shape in scratch],
        compiler_params=pltpu.CompilerParams(vmem_limit_bytes=24 * 1024 * 1024),
        cost_estimate=pl.CostEstimate(
            flops=COSTS[name] * 1000000, bytes_accessed=COSTS[name] * 3000, transcendentals=0
        ),
    )(*operands)


def swap_pairs(counts, axis, parity):
    count_x, count_y = counts
    pairs = []
    for x in range(count_x):
        for y in range(count_y):
            if axis == 0:
                to = ((x + 1 if x % 2 == parity else x - 1) % count_x, y)
            else:
                other = y + 1 if y % 2 == parity else y - 1
                to = (x, other) if 0 <= other < count_y else (x ^ 1, y)
            pairs.append((x * count_y + y, to[0] * count_y + to[1]))
    return pairs


def trade(counts, axis, first, second):
    return (
        lax.ppermute(first, AXES, swap_pairs(counts, axis, 0)),
        lax.ppermute(second, AXES, swap_pairs(counts, axis, 1)),
    )


def trade_far(counts, value, far_x, far_y):
    pairs = [
        (x * counts[1] + y, (x ^ far_x) * counts[1] + (y ^ far_y))
        for x in range(counts[0])
        for y in range(counts[1])
    ]
    return lax.ppermute(value, AXES, pairs)


class RunningSum:
    def __init__(self, counts, tile, carried):
        self.counts = counts
        self.carried = carried
        self.value = tile if self.carried else lax.psum(tile, AXES)

    def add(self, received):
        if self.carried:
            self.value = self.value + received

    def far(self, *steps):
        return [trade_far(self.counts, self.value, *step) for step in steps if self.carried]


def carry(tiles, running):
    return jnp.concatenate([tiles.reshape((-1, NODES, 128)), running.value[None]])


def carried(received, shape):
    return received[:-1].reshape(shape), received[-1]


def gather_stats(stats):
    return lax.all_to_all(stats, AXES, 0, 0)


def lift_tables(counts, column_length):
    share_x, share_y = share_table(counts[0]), share_table(counts[1])
    basis_x, eigen_x = cosine_inverse(counts[0])
    basis_y, eigen_y = cosine_inverse(counts[1])
    divisor = (
        2.0 * mean_porosity * column_length * (eigen_x[:, None] + eigen_y[None, :])
        + 8.0 * shift_mass * column_length
    )
    modes_x = np.einsum("xip,pa->xia", share_x, basis_x)
    modes_y = np.einsum("yjq,qb->yjb", share_y, basis_y)
    total = counts[0] * counts[1]
    to_modes = np.einsum("pa,qb->abpq", basis_x, basis_y).reshape(total, total)
    to_modes = np.pad(to_modes, ((0, 0), (0, sum_lanes(counts) - total)))
    return [table.astype(np.float32) for table in (modes_x, modes_y, 1.0 / divisor, to_modes)]


def all_lift(counts, column_length):
    modes_x, modes_y, inverse, to_modes = lift_tables(counts, column_length)
    total = counts[0] * counts[1]
    lift = np.einsum(
        "xia,yjb,ab,abl->ijxyl", *(
            table.astype(np.float64)
            for table in (modes_x, modes_y, inverse, to_modes.reshape(inverse.shape + (-1,)))
        ),
    )
    return jnp.asarray(lift.reshape(9 * total, -1).astype(np.float32))


def own_lift(tables):
    modes_x, modes_y, inverse, to_modes = [jnp.asarray(table) for table in tables]
    own_x = lax.dynamic_index_in_dim(modes_x, lax.axis_index("gx"), 0, keepdims=False)
    own_y = lax.dynamic_index_in_dim(modes_y, lax.axis_index("gy"), 0, keepdims=False)
    own = own_x[:, None, :, None] * own_y[None, :, None, :] * inverse[None, None]
    lift = jnp.dot(own.reshape(9, -1), to_modes, precision=exact_mode)
    return jnp.pad(lift, ((0, 7), (0, 0)))


def shards_of(counts):
    forward_np, back_edge_np, back_inner_np, inverse_np = plane_tables()

    def shards(solution, residual, grain_counts):
        shard_shape = solution.shape
        block = shard_shape[2:]
        solution = solution.reshape(block)
        residual = residual.reshape(block)
        lift = own_lift(lift_tables(counts, block[-1]))
        late = counts == (8, 4)
        every_lift = all_lift(counts, block[-1]) if late else None
        porosity = 1.0 - 0.6 * grain_counts.reshape(1, 128).astype(jnp.float32) / MOST_GRAINS
        plane = [jnp.asarray(table) for table in (forward_np, back_edge_np, inverse_np)]
        back_inner = jnp.asarray(back_inner_np)
        side_x, side_y = Sides("gx", counts[0]), Sides("gy", counts[1])
        row = (counts[0] * counts[1], 4, 128)
        face = (NODES, NODES, 128)
        sends = [(2 * EXT, NODES, 128)] * 2
        solve_shapes = [(MODES, EXT * 128), (EXT, 2 * NODES, 128)]
        solve_scratch = [(EXT, ROWS, 128), (EXT, len(back_edge_np), 128)]

        def rest_of_solve(spectrum, edges):
            return call(
                rest_kernel, counts, "rest_of_solve",
                [(EXT, NODES * NODES, 128)] + [(2, NODES, NODES, 128)] * 2,
                [(EXT, len(back_inner_np), 128)], spectrum, edges, back_inner,
            )

        y_first, y_second = call(
            start_kernel, counts, "start", [(NODES + 1,) + face[1:], face], [], residual
        )
        running = RunningSum(counts, y_first[-1], late)
        ry = trade(counts, 1, y_first, y_second)
        ry_first, tile = carried(ry[0], face)
        running.add(tile)
        ry = (ry_first, ry[1])
        low_y, high_y = side_y.low(*ry), side_y.high(*ry)

        def with_layers(index):
            return jnp.concatenate([low_y[index][None], residual[index], high_y[index][None]])

        low_face, high_face = with_layers(1), with_layers(NODES - 2)
        rx = trade(
            counts, 0, carry(side_x.send_first(low_face, high_face), running),
            side_x.send_second(low_face, high_face),
        )
        rx_first, tile = carried(rx[0], low_face.shape)
        running.add(tile)
        rx = (rx_first, rx[1])
        spectrum, edges, y_first, y_second = call(
            first_solve_kernel, counts, "first_solve",
            solve_shapes + [(2 * EXT + 1, NODES, 128)] * 2, solve_scratch,
            residual, porosity, *ry, *rx, *plane,
        )
        part, *fx = rest_of_solve(spectrum, edges)

        def spread_faces(fx, ry):
            low_y, high_y = side_y.low(*ry), side_y.high(*ry)
            middle = jnp.zeros((2, NODES - 4, NODES, 128), jnp.float32)
            both = [
                jnp.concatenate([low_y[at], middle, high_y[at]], axis=1)
                for at in (slice(0, 2), slice(8, 10))
            ]
            return (
                fx[0] + side_x.send_first(*both),
                fx[1] + side_x.send_second(*both),
            )

        def trade_y(y_first, y_second, shape):
            count = math.prod(shape[:-2])
            ry = trade(counts, 1, y_first, y_second)
            faces = [value[:count].reshape(shape) for value in ry]
            return faces, [value[count:] for value in ry]

        ext_face = (EXT, 2, NODES, 128)
        two = (NODES, 2, NODES, 128)
        tiles = (-1, NODES, 128)
        middle = jnp.broadcast_to(porosity, (1, NODES, 128))
        if late:
            y_second = jnp.concatenate([y_second, running.value[None]])
            ry, rows = trade_y(y_first, y_second, ext_face)
            inner_y = (side_y.index > 0) & (side_y.index < counts[1] - 1)
            running.add(jnp.where(inner_y, rows[1][1], 0.0))
        else:
            ry, rows = trade_y(y_first, y_second, ext_face)
        three = jnp.concatenate(
            [
                side[0, 0:1]
                for side in (
                    side_y.low(rows[0][:1], rows[1][:1]), middle,
                    side_y.high(rows[0][:1], rows[1][:1]),
                )
            ]
            + [jnp.zeros((NODES - 3, 128), jnp.float32)]
        )
        first, second = spread_faces(fx, ry)
        rx = trade(
            counts, 0, jnp.concatenate([first.reshape(tiles), three[None]]),
            jnp.concatenate([second.reshape(tiles), three[None], running.value[None]]),
        )
        count = 2 * NODES
        threes = [value[count] for value in rx]
        running.add(rx[1][count + 1])
        rx = [value[:count].reshape(first.shape) for value in rx]
        if late:
            half = (NODES, NODES // 2, NODES, 128)
            z, u_edge, y_first, y_second = call(
                early_apply_kernel, counts, "first_apply",
                [block, half, (2 * NODES, NODES, 128), (2 * NODES, NODES, 128)], [block],
                part, *ry, *rx, porosity,
            )
            u_inner, *fx = call(
                rest_apply_kernel, counts, "rest_of_apply",
                [half, (2, NODES, NODES, 128), (2, NODES, NODES, 128)], [block],
                z, u_edge, porosity,
            )
            y_first = jnp.concatenate([y_first, running.value[None]])
        else:
            z, u, y_first, y_second, *fx, tile = call(
                first_apply_kernel, counts, "first_apply",
                [block, block, (2 * NODES, NODES, 128), (2 * NODES, NODES, 128),
                 (2, NODES, NODES, 128), (2, NODES, NODES, 128), (NODES, 128)],
                [block],
                part, *ry, *rx, running.value, lift, porosity, residual,
            )
            u_edge = jnp.concatenate([u[:, :2], u[:, -2:]], axis=1)
            u_inner = u[:, 2:-2]
        ry, rows = trade_y(y_first, y_second, two)
        if late:
            running.value = jnp.where(inner_y, running.value, rows[0][0])
        low_y, high_y = side_y.low(*ry), side_y.high(*ry)

        def image_faces(index):
            middle = jnp.zeros((2, NODES - 2, NODES, 128), jnp.float32)
            return jnp.concatenate([low_y[index], middle, high_y[index]], axis=1)

        pads = ((0, 0), (1, 1), (0, 0), (0, 0))
        both = (image_faces(slice(0, 2)), image_faces(slice(NODES - 2, NODES)))
        rx = trade(
            counts, 0,
            jnp.pad(fx[0], pads) + side_x.send_first(*both),
            jnp.pad(fx[1], pads) + side_x.send_second(*both),
        )
        if late:
            near = (side_x.low(*threes), three, side_x.high(*threes))
            (columns,) = call(porosity_kernel, counts, "porosity", [(18, NODES, 128)], [], *near)
            rx, far, columns = lax.optimization_barrier((rx, running.far((4, 0)), columns))
            for value in far:
                running.add(value)
            table = (9 * counts[0] * counts[1], 128)
            q, spectrum, edges, y_first, y_second, field = call(
                late_solve_kernel, counts, "second_solve",
                [block] + solve_shapes + sends + [(16, 128)], solve_scratch + [table],
                u_edge, u_inner, *ry, *rx, columns, every_lift, running.value, *plane,
            )
        else:
            q, spectrum, edges, y_first, y_second = call(
                second_solve_kernel, counts, "second_solve", [block] + solve_shapes + sends,
                solve_scratch, u_edge, u_inner, *ry, *rx, *plane,
            )
        part, *fx = rest_of_solve(spectrum, edges)
        ry, _ = trade_y(y_first, y_second, ext_face)
        rx = trade(counts, 0, *spread_faces(fx, ry))

        def trade_edges(y_first, y_second, fx, beside):
            ry, beside = lax.optimization_barrier((trade(counts, 1, y_first, y_second), beside))
            low_y, high_y = side_y.low(*ry), side_y.high(*ry)

            def edge_rows(index):
                middle = jnp.zeros((NODES - 2, NODES, 128), jnp.float32)
                return jnp.concatenate([low_y[index][None], middle, high_y[index][None]])

            both = (edge_rows(0), edge_rows(NODES - 1))
            rx = trade(
                counts, 0, fx[0] + side_x.send_first(*both), fx[1] + side_x.send_second(*both)
            )
            return ry, rx, beside

        if late:
            w, u, y_first, y_second, *fx, stats = call(
                late_apply_kernel, counts, "late_apply",
                [block, block] + [(NODES + 2, NODES, 128)] * 4 + [row], [block],
                part, *ry, *rx, porosity, *near, residual, q, z, field,
            )
            z, w = lax.optimization_barrier((z, w))
            nexts = call(
                prepare_late_kernel, counts, "prepare", [block] * 3, [],
                solution, residual, z, field,
            )
            ry, rx, (z, solution, residual) = lax.optimization_barrier(
                (trade(counts, 1, y_first, y_second), trade(counts, 0, *fx), nexts)
            )
            solution_out, residual_out, direction, steps = call(
                late_final_kernel, counts, "late_final", [block] * 3 + [(2,)], [table],
                solution, residual, q, z, w, u, *ry, *rx, columns, every_lift,
                gather_stats(stats),
            )
        else:
            summed = lax.psum(tile, AXES)
            z1, u, y_first, y_second, *fx, stats = call(
                second_apply_kernel, counts, "second_apply",
                [block, block, face, face, face, face, row], [block],
                part, *ry, *rx, summed, lift, porosity, residual, q, z,
            )
            nexts = call(
                prepare_kernel, counts, "prepare", [block] * 2, [],
                solution, residual, q, z, summed,
            )
            ry, rx, nexts = trade_edges(y_first, y_second, fx, nexts)
            solution_out, residual_out, direction, steps = call(
                final_kernel, counts, "final", [block] * 3 + [(2,)], [],
                *nexts, q, z, z1, u, *ry, *rx, summed, gather_stats(stats),
            )
        return (
            solution_out.reshape(shard_shape),
            residual_out.reshape(shard_shape),
            direction.reshape(shard_shape),
            steps,
        )

    return shards


def solution(mesh):
    counts = (mesh.shape["gx"], mesh.shape["gy"])
    return jax.shard_map(
        shards_of(counts),
        mesh=mesh,
        in_specs=(
            P("gx", "gy", None, None, None, None),
            P("gx", "gy", None, None, None, None),
            P("gx", "gy", None),
        ),
        out_specs=(
            P("gx", "gy", None, None, None, None),
            P("gx", "gy", None, None, None, None),
            P("gx", "gy", None, None, None, None),
            P(),
        ),
        check_vma=False,
    )
```

```python
import math

import jax
import jax.numpy as jnp
import numpy as np
from jax import lax
from jax.experimental import pallas as pl
from jax.experimental.pallas import tpu as pltpu
from jax.sharding import PartitionSpec as P

NODES = 8
MOST_GRAINS = 16
EXT = NODES + 2
ROWS = 112
MODES = 104
AXES = ("gx", "gy")
EDGE = (0, 1, EXT - 2, EXT - 1)
INNER = tuple(range(2, EXT - 2))

shift_mass = 0.1
mean_porosity = 0.7
exact_mode = lax.Precision.HIGHEST
plane_mode = lax.Precision.HIGH


def legendre_columns(node_set, degree):
    table = [node_set * 0.0 + 1.0, node_set]
    for order in range(2, degree + 1):
        table.append(
            ((2 * order - 1) * node_set * table[order - 1] - (order - 1) * table[order - 2]) / order
        )
    return table


def gll_tables():
    degree = NODES - 1
    node_set = np.cos(math.pi * np.arange(degree + 1) / degree)
    for sweep in range(100):
        table = legendre_columns(node_set, degree)
        node_set = node_set - (node_set * table[degree] - table[degree - 1]) / (
            (degree + 1) * table[degree]
        )
    node_set = node_set[::-1].copy()
    values = legendre_columns(node_set, degree)[degree]
    weights = 2.0 / (degree * (degree + 1) * values**2)
    derivative = np.zeros((NODES, NODES))
    for row_index in range(NODES):
        for column_index in range(NODES):
            if row_index != column_index:
                derivative[row_index, column_index] = values[row_index] / (
                    values[column_index] * (node_set[row_index] - node_set[column_index])
                )
    derivative[0, 0] = -degree * (degree + 1) / 4.0
    derivative[NODES - 1, NODES - 1] = degree * (degree + 1) / 4.0
    return (weights, derivative)


def jacobi_eigen(matrix):
    size_now = matrix.shape[0]
    current = matrix.copy()
    vectors = np.eye(size_now)
    for sweep in range(12):
        for first in range(size_now - 1):
            for second in range(first + 1, size_now):
                off_value = current[first, second]
                safe_value = np.where(off_value == 0.0, 1e-300, off_value)
                theta = (current[second, second] - current[first, first]) / (2.0 * safe_value)
                sign_value = np.where(theta >= 0.0, 1.0, -1.0)
                tangent = sign_value / (np.abs(theta) + np.sqrt(theta * theta + 1.0))
                cosine = 1.0 / np.sqrt(tangent * tangent + 1.0)
                sine = tangent * cosine
                rotation = np.eye(size_now)
                rotation[first, first] = cosine
                rotation[second, second] = cosine
                rotation[first, second] = sine
                rotation[second, first] = -sine
                current = rotation.T @ current @ rotation
                vectors = vectors @ rotation
    eigen_values = np.array([current[index, index] for index in range(size_now)])
    return (eigen_values, vectors)


def schwarz_tables():
    weights, derivative = gll_tables()
    stiffness = derivative.T @ (weights[:, None] * derivative)
    total_nodes = 3 * (NODES - 1) + 1
    three_stiffness = np.zeros((total_nodes, total_nodes))
    three_mass = np.zeros(total_nodes)
    for element in range(3):
        start_node = element * (NODES - 1)
        three_stiffness[
            start_node : start_node + NODES, start_node : start_node + NODES
        ] += stiffness
        three_mass[start_node : start_node + NODES] += weights
    chosen = np.array([NODES - 2] + list(range(NODES - 1, 2 * NODES - 1)) + [2 * NODES - 1])
    local_stiffness = three_stiffness[chosen][:, chosen]
    local_mass = three_mass[chosen]
    scaling = 1.0 / np.sqrt(local_mass)
    symmetric = scaling[:, None] * local_stiffness * scaling[None, :]
    symmetric = 0.5 * (symmetric + symmetric.T)
    eigen_values, eigen_vectors = jacobi_eigen(symmetric)
    return (scaling[:, None] * eigen_vectors, eigen_values)


WEIGHTS, DERIVATIVE = gll_tables()
STIFF = DERIVATIVE.T @ (WEIGHTS[:, None] * DERIVATIVE)
BASIS, EIGEN = schwarz_tables()
PARITY = {
    sign: [mode for mode in range(EXT) if BASIS[0, mode] * BASIS[EXT - 1, mode] * sign > 0]
    for sign in (1, -1)
}


def plane_tables():
    forward = np.zeros((MODES, ROWS))
    inverse = np.zeros((MODES, EXT))
    for mode_b in range(EXT):
        for mode_c in range(EXT):
            mode = mode_b * EXT + mode_c
            for b in range(EXT):
                for k in range(NODES):
                    forward[mode, b * NODES + k] = BASIS[b, mode_b] * BASIS[k + 1, mode_c]
                forward[mode, 80 + b] = BASIS[b, mode_b] * BASIS[0, mode_c]
                forward[mode, 96 + b] = BASIS[b, mode_b] * BASIS[EXT - 1, mode_c]
            inverse[mode] = 1.0 / (
                mean_porosity * (EIGEN + EIGEN[mode_b] + EIGEN[mode_c]) + shift_mass
            )
    lanes = np.repeat(inverse.T[:, :, None], 128, axis=2)
    back = forward.T
    tables = [
        np.concatenate([back[[8 * b + k for b in layers for k in range(NODES)]]]
                       + [pad_rows(back[[at + b for b in layers]], 8) for at in (80, 96)])
        for layers in (EDGE, INNER)
    ]
    return tuple(table.astype(np.float32) for table in (forward, *tables, lanes))


def pad_rows(table, count):
    return np.pad(table, ((0, -len(table) % count), (0, 0)))


def row_tile(values):
    row = lax.broadcasted_iota(jnp.int32, (NODES, 128), 0)
    tile = jnp.full((NODES, 128), float(values[0]), jnp.float32)
    for k in range(1, NODES):
        tile = jnp.where(row == k, float(values[k]), tile)
    return tile


def share_table(count):
    table = np.zeros((count, 3, count))
    for column in range(count):
        table[column, :, column] = 1.0
        if column > 0:
            table[column, 0, column] = 0.5
            table[column, 0, column - 1] = 0.5
        if column < count - 1:
            table[column, 2, column] = 0.5
            table[column, 2, column + 1] = 0.5
    return table


def cosine_inverse(count):
    position = np.arange(count)
    basis = np.cos(math.pi * (position[:, None] + 0.5) * position[None, :] / count)
    basis = basis * np.where(position == 0, math.sqrt(1.0 / count), math.sqrt(2.0 / count))[None, :]
    return basis, 2.0 - 2.0 * np.cos(math.pi * position / count)


def shift_up(rows):
    lane = lax.broadcasted_iota(jnp.int32, rows.shape, 1)
    return jnp.where(lane == 0, 0.0, pltpu.roll(rows, 1, 1))


def shift_down(rows):
    lane = lax.broadcasted_iota(jnp.int32, rows.shape, 1)
    return jnp.where(lane == 127, 0.0, pltpu.roll(rows, 127, 1))


class Sides:
    def __init__(self, axis, count):
        self.index = lax.axis_index(axis)
        self.even = lax.rem(self.index, 2) == 0
        self.no_low = self.index == 0
        self.no_high = self.index == count - 1

    def low(self, first, second):
        return jnp.where(self.no_low, 0.0, jnp.where(self.even, second, first))

    def high(self, first, second):
        return jnp.where(self.no_high, 0.0, jnp.where(self.even, first, second))

    def send_first(self, low_face, high_face):
        return jnp.where(self.even, high_face, low_face)

    def send_second(self, low_face, high_face):
        return jnp.where(self.even, low_face, high_face)


def multiplicity_tile():
    row = lax.broadcasted_iota(jnp.int32, (NODES, 128), 0)
    lane = lax.broadcasted_iota(jnp.int32, (NODES, 128), 1)
    shared = ((row == 0) & (lane > 0)) | ((row == NODES - 1) & (lane < 127))
    return jnp.where(shared, 0.5, 1.0)


def class_of(node):
    return 0 if node == 0 else (2 if node == NODES - 1 else 1)


def axis_factor(node, side):
    if node == 0:
        return jnp.where(side.no_low, 1.0, 0.5)
    if node == NODES - 1:
        return jnp.where(side.no_high, 1.0, 0.5)
    return None


def scaled(value, *factors):
    for factor in factors:
        if factor is not None:
            value = value * factor
    return value


def add_to(total, key, value):
    total[key] = value if key not in total else total[key] + value


def lane_sums(tiles):
    columns = [jnp.sum(tile, axis=0, keepdims=True) for tile in tiles]
    columns.append(jnp.zeros((16 - len(tiles), 128), jnp.float32))
    sums = jnp.sum(jnp.concatenate(columns, axis=0), axis=1, keepdims=True)
    return jnp.broadcast_to(sums, (16, 128))


def write_stats(stats_ref, tiles):
    row = lax.broadcasted_iota(jnp.int32, (16, 128), 0)
    lane = lax.broadcasted_iota(jnp.int32, (16, 128), 1)
    sums = jnp.sum(jnp.where(row == lane, lane_sums(tiles), 0.0), axis=0, keepdims=True)
    for index in range(stats_ref.shape[0]):
        stats_ref[index] = jnp.broadcast_to(sums, stats_ref.shape[1:])


def stat_columns(stats, first, count):
    lane = lax.broadcasted_iota(jnp.int32, stats.shape, 1)
    sums = lane_sums([jnp.where(lane == first + i, stats, 0.0) for i in range(count)])
    return [sums[i : i + 1] for i in range(count)]


def sum_lanes(counts):
    return -(-(counts[0] * counts[1] + 2) // 128) * 128


def share_rows(counts, side_x, side_y):
    lane = lax.broadcasted_iota(jnp.int32, (1, sum_lanes(counts)), 1)
    column_y = lax.rem(lane, counts[1])
    first_x = lane - column_y

    def weights(side, place, step, count):
        own = jnp.where(place == side.index * step, 1.0, 0.0)
        below = jnp.where(place == (side.index - 1) * step, 1.0, 0.0)
        above = jnp.where(place == (side.index + 1) * step, 1.0, 0.0)
        return (
            jnp.where(side.no_low, own, 0.5 * (own + below)),
            own,
            jnp.where(side.no_high, own, 0.5 * (own + above)),
        )

    inside = lane < counts[0] * counts[1]
    along_x = weights(side_x, first_x, counts[1], counts[0])
    along_y = weights(side_y, column_y, 1, counts[1])
    return [jnp.where(inside, wx * wy, 0.0) for wx in along_x for wy in along_y]


def summed_row(counts, tiles, side_x, side_y):
    sums = lane_sums(tiles)
    lane = lax.broadcasted_iota(jnp.int32, (1, sum_lanes(counts)), 1)
    total = None
    for i, share in enumerate(share_rows(counts, side_x, side_y)):
        term = share * sums[i : i + 1, 0:1]
        total = term if total is None else total + term
    for i in range(9, len(tiles)):
        total = total + jnp.where(lane == counts[0] * counts[1] + i - 9, sums[i : i + 1, 0:1], 0.0)
    pieces = [total[:, at : at + 128] for at in range(0, sum_lanes(counts), 128)]
    pieces.append(jnp.zeros((NODES - len(pieces), 128), jnp.float32))
    return jnp.concatenate(pieces, axis=0)


def row_of(counts, tile_ref):
    rows = [tile_ref[i : i + 1, :] for i in range(sum_lanes(counts) // 128)]
    return rows[0] if len(rows) == 1 else jnp.concatenate(rows, axis=1)


def lifted_rows(counts, row, lift_ref):
    sums = jnp.sum(lift_ref[...] * row, axis=1, keepdims=True)
    return jnp.broadcast_to(sums, (16, 128))


def row_value(counts, row, index):
    lane = lax.broadcasted_iota(jnp.int32, row.shape, 1)
    chosen = jnp.where(lane == counts[0] * counts[1] + index, row, 0.0)
    return jnp.broadcast_to(jnp.sum(chosen, axis=1, keepdims=True), (1, 128))


def class_tiles(sums):
    return [sums[(i, j)] for i in range(3) for j in range(3)]


def shared_class_tiles(field_ref, side_x, side_y):
    tile = multiplicity_tile()
    sums = {}
    for a in range(NODES):
        for b in range(NODES):
            add_to(sums, (class_of(a), class_of(b)), field_ref[a, b])
    for (i, j), value in sums.items():
        a, b = (0, 1, NODES - 1)[i], (0, 1, NODES - 1)[j]
        sums[(i, j)] = scaled(value * tile, axis_factor(a, side_x), axis_factor(b, side_y))
    return class_tiles(sums)


def start_kernel(counts, r_ref, sy_first, sy_second):
    side_x, side_y = Sides("gx", counts[0]), Sides("gy", counts[1])
    for a in range(NODES):
        low, high = r_ref[a, 1], r_ref[a, NODES - 2]
        sy_first[a] = side_y.send_first(low, high)
        sy_second[a] = side_y.send_second(low, high)
    sy_first[NODES] = summed_row(
        counts, shared_class_tiles(r_ref, side_x, side_y), side_x, side_y
    )


def planes(ref):
    return jnp.concatenate([ref[a] for a in range(EXT)], axis=1)


def to_spectrum(x_ref, forward_ref, inverse_ref):
    zero = jnp.zeros((6, 128), jnp.float32)
    for a in range(EXT):
        x_ref[a, 80:90] = shift_up(x_ref[a, pl.ds(6, EXT, stride=NODES), :])
        x_ref[a, 96:106] = shift_down(x_ref[a, pl.ds(1, EXT, stride=NODES), :])
        x_ref[a, 90:96] = zero
        x_ref[a, 106:112] = zero
    half = EXT // 2
    for block in range(ROWS // 8):
        rows = pl.ds(block * 8, 8)
        low = [x_ref[a, rows] for a in range(half)]
        high = [x_ref[EXT - 1 - a, rows] for a in range(half)]
        folded = {1: [x + y for x, y in zip(low, high)], -1: [x - y for x, y in zip(low, high)]}
        for sign in (1, -1):
            for mode in PARITY[sign]:
                total = folded[sign][0] * float(BASIS[0, mode])
                for a in range(1, half):
                    total = total + folded[sign][a] * float(BASIS[a, mode])
                x_ref[mode, rows] = total
    spectrum = jnp.dot(
        forward_ref[...], planes(x_ref), precision=plane_mode, preferred_element_type=jnp.float32
    ) * planes(inverse_ref)
    return spectrum


def from_spectrum(spectrum, back_ref, part_ref, count):
    half = EXT // 2
    values = jnp.dot(
        back_ref[...], spectrum, precision=plane_mode, preferred_element_type=jnp.float32
    )
    for block in range(part_ref.shape[1] // 8):
        rows = pl.ds(block * 8, 8)
        modes = [values[block * 8 : block * 8 + 8, m * 128 : (m + 1) * 128] for m in range(EXT)]
        back = {}
        for sign in (1, -1):
            for a in range(half):
                total = None
                for mode in PARITY[sign]:
                    term = modes[mode] * float(BASIS[a, mode])
                    total = term if total is None else total + term
                back[(sign, a)] = total
        for a in range(half):
            part_ref[a, rows] = back[(1, a)] + back[(-1, a)]
            part_ref[EXT - 1 - a, rows] = back[(1, a)] - back[(-1, a)]
    below, above = NODES * count, NODES * count + 8
    for a in range(EXT):

        def layer(k):
            return (a, pl.ds(k, count, stride=NODES), slice(None))

        bottom, top = part_ref[layer(0)], part_ref[layer(NODES - 1)]
        part_ref[layer(0)] = bottom + shift_up(top)
        part_ref[layer(NODES - 1)] = top + shift_down(bottom)
        part_ref[layer(1)] = part_ref[layer(1)] + shift_up(part_ref[a, above : above + count])
        part_ref[layer(NODES - 2)] = part_ref[layer(NODES - 2)] + shift_down(
            part_ref[a, below : below + count]
        )


def solve_edges(
    x_ref, forward_ref, back_ref, inverse_ref, spectrum_ref, edge_ref, sy_first, sy_second,
    side_y, part_ref,
):
    spectrum = to_spectrum(x_ref, forward_ref, inverse_ref)
    spectrum_ref[...] = spectrum
    from_spectrum(spectrum, back_ref, part_ref, len(EDGE))
    for a in range(EXT):
        low, high = part_ref[a, 0:16], part_ref[a, 16:32]
        sy_first[2 * a : 2 * a + 2] = side_y.send_first(low, high).reshape(2, NODES, 128)
        sy_second[2 * a : 2 * a + 2] = side_y.send_second(low, high).reshape(2, NODES, 128)
        edge_ref[a] = part_ref[a, 8:24]


def rest_kernel(
    counts, spectrum_ref, edge_ref, back_ref, part_ref, fx_first, fx_second, inner_ref
):
    side_x = Sides("gx", counts[0])
    from_spectrum(spectrum_ref[...], back_ref, inner_ref, len(INNER))
    for a in range(EXT):
        part_ref[a, 0:8] = edge_ref[a, 0:8]
        part_ref[a, 8:56] = inner_ref[a, 0:48]
        part_ref[a, 56:64] = edge_ref[a, 8:16]
    for layer in range(2):
        low, high = part_ref[layer], part_ref[NODES + layer]
        fx_first[layer] = side_x.send_first(low, high).reshape(NODES, NODES, 128)
        fx_second[layer] = side_x.send_second(low, high).reshape(NODES, NODES, 128)


def first_solve_kernel(
    counts, r_ref, porosity_ref, sum_ref, ry_first, ry_second, rx_first, rx_second, forward_ref, back_ref,
    inverse_ref, spectrum_ref, edge_ref, sy_first, sy_second, x_ref, part_ref,
):
    row = lax.broadcasted_iota(jnp.int32, (NODES, 128), 0)
    for send in (sy_first, sy_second):
        send[2 * EXT] = jnp.where(row == 0, sum_ref[...], porosity_ref[...])
    side_x, side_y = Sides("gx", counts[0]), Sides("gy", counts[1])
    x_ref[0, 0:80] = side_x.low(rx_first[...], rx_second[...]).reshape(80, 128)
    x_ref[EXT - 1, 0:80] = side_x.high(rx_first[...], rx_second[...]).reshape(80, 128)
    for a in range(NODES):
        x_ref[a + 1, 0:8] = side_y.low(ry_first[a], ry_second[a])
        x_ref[a + 1, 8:72] = r_ref[a].reshape(64, 128)
        x_ref[a + 1, 72:80] = side_y.high(ry_first[a], ry_second[a])
    solve_edges(
        x_ref, forward_ref, back_ref, inverse_ref, spectrum_ref, edge_ref, sy_first, sy_second,
        side_y, part_ref,
    )


def second_solve_kernel(
    counts, edge_ref, inner_ref, ry_first, ry_second, rx_first, rx_second, forward_ref, back_ref,
    inverse_ref, q_ref, spectrum_ref, layers_ref, sy_first, sy_second, x_ref, part_ref,
):
    side_x, side_y = Sides("gx", counts[0]), Sides("gy", counts[1])
    extend_image(
        edge_ref, inner_ref, ry_first, ry_second, rx_first, rx_second, side_x, side_y, q_ref, x_ref, None
    )
    solve_edges(
        x_ref, forward_ref, back_ref, inverse_ref, spectrum_ref, layers_ref, sy_first, sy_second,
        side_y, part_ref,
    )


def late_solve_kernel(
    counts, edge_ref, inner_ref, ry_first, ry_second, rx_first, rx_second, columns_ref, lift_ref,
    sum_ref, forward_ref, back_ref, inverse_ref, q_ref, spectrum_ref, layers_ref, sy_first,
    sy_second, field_ref, x_ref, part_ref, table_ref,
):
    side_x, side_y = Sides("gx", counts[0]), Sides("gy", counts[1])
    table_ref[...] = jnp.broadcast_to(
        jnp.sum(lift_ref[...] * sum_ref[0:1], axis=1, keepdims=True), table_ref.shape
    )
    fields = near_fields(counts, table_ref, side_x, side_y)
    own = fields[(1, 1)]
    field_ref[...] = jnp.concatenate(
        [own[i][j] for i in range(3) for j in range(3)] + [jnp.zeros((7, 128), jnp.float32)]
    )
    image = LiftedImage(fields, columns_ref)
    extend_image(
        edge_ref, inner_ref, ry_first, ry_second, rx_first, rx_second, side_x, side_y, q_ref, x_ref, image
    )
    solve_edges(
        x_ref, forward_ref, back_ref, inverse_ref, spectrum_ref, layers_ref, sy_first, sy_second,
        side_y, part_ref,
    )


def layer_of(edge_ref, inner_ref, a, b):
    if 2 <= b < NODES - 2:
        return inner_ref[a, b - 2]
    return edge_ref[a, b if b < 2 else b - (NODES - 4)]


def extend_image(
    edge_ref, inner_ref, ry_first, ry_second, rx_first, rx_second, side_x, side_y, q_ref, x_ref,
    image,
):
    low_x = side_x.low(rx_first[...], rx_second[...])
    high_x = side_x.high(rx_first[...], rx_second[...])

    def lifted(value, a, b):
        return value if image is None else value + image.at(a - 1, b - 1)

    for b in range(EXT):
        rows = pl.ds(b * 8, 8)
        x_ref[0, rows] = lifted(low_x[0, b], 0, b)
        x_ref[EXT - 1, rows] = lifted(high_x[1, b], EXT - 1, b)
    for a in range(NODES):
        low_y = side_y.low(ry_first[a], ry_second[a])
        high_y = side_y.high(ry_first[a], ry_second[a])
        rows = [low_y[0]]
        for b in range(NODES):
            value = layer_of(edge_ref, inner_ref, a, b)
            if b == 0:
                value = value + low_y[1]
            if b == NODES - 1:
                value = value + high_y[0]
            rows.append(value)
        rows.append(high_y[1])
        for b in range(EXT):
            value = rows[b]
            if a == 0:
                value = value + low_x[1, b]
            if a == NODES - 1:
                value = value + high_x[0, b]
            value = lifted(value, a + 1, b)
            x_ref[a + 1, b * 8 : b * 8 + 8] = value
            if 0 < b < EXT - 1:
                q_ref[a, b - 1] = value


def collect_parts(part_ref, ry_first, ry_second, rx_first, rx_second, side_x, side_y, field):
    low_x = side_x.low(rx_first[...], rx_second[...])
    high_x = side_x.high(rx_first[...], rx_second[...])
    result = {}
    for a in range(NODES):
        low_y = side_y.low(ry_first[a + 1], ry_second[a + 1])
        high_y = side_y.high(ry_first[a + 1], ry_second[a + 1])
        for b in range(NODES):
            value = part_ref[a + 1, b * 8 : (b + 1) * 8]
            if b < 2:
                value = value + low_y[b]
            if b >= NODES - 2:
                value = value + high_y[b - (NODES - 2)]
            if a < 2:
                value = value + low_x[a, b]
            if a >= NODES - 2:
                value = value + high_x[a - (NODES - 2), b]
            if field is not None:
                node_class = 3 * class_of(a) + class_of(b)
                value = value + field[node_class : node_class + 1, :]
            result[(a, b)] = value
    return result


def apply_tiles(z_ref, u_ref, y_ref, por, layers=range(NODES)):
    weight_tile = row_tile(WEIGHTS)
    stiff_tiles = [
        row_tile([STIFF[k, (k - shift) % NODES] for k in range(NODES)]) for shift in range(NODES)
    ]
    for a in range(NODES):
        for b in range(NODES):
            y_ref[a, b] = z_ref[a, b] * weight_tile
    for a in range(NODES):
        for place, b in enumerate(layers):
            z = z_ref[a, b]
            third = z * stiff_tiles[0]
            for shift in range(1, NODES):
                third = third + pltpu.roll(z, shift, 0) * stiff_tiles[shift]
            first = y_ref[0, b] * float(STIFF[a, 0] * WEIGHTS[b])
            second = y_ref[a, 0] * float(STIFF[b, 0] * WEIGHTS[a])
            for other in range(1, NODES):
                first = first + y_ref[other, b] * float(STIFF[a, other] * WEIGHTS[b])
                second = second + y_ref[a, other] * float(STIFF[b, other] * WEIGHTS[a])
            weight = float(WEIGHTS[a] * WEIGHTS[b])
            u_ref[a, place] = por * (third * weight + first + second) + y_ref[a, b] * (
                shift_mass * weight
            )


def sum_column(u_ref):
    for a in range(NODES):
        bottom = u_ref[a, :, 0, :]
        top = u_ref[a, :, NODES - 1, :]
        u_ref[a, :, 0, :] = bottom + shift_up(top)
        u_ref[a, :, NODES - 1, :] = top + shift_down(bottom)


def first_apply_kernel(
    counts, part_ref, ry_first, ry_second, rx_first, rx_second, sum_ref, lift_ref, porosity_ref,
    r_ref, z_ref, u_ref, sy_first, sy_second, fx_first, fx_second, tile_ref, y_ref,
):
    side_x, side_y = Sides("gx", counts[0]), Sides("gy", counts[1])
    field = lifted_rows(counts, row_of(counts, sum_ref), lift_ref)
    z = collect_parts(part_ref, ry_first, ry_second, rx_first, rx_second, side_x, side_y, field)
    inner = None
    for (a, b), value in z.items():
        z_ref[a, b] = value
        term = scaled(value * r_ref[a, b], axis_factor(a, side_x), axis_factor(b, side_y))
        inner = term if inner is None else inner + term
    inner = inner * multiplicity_tile()
    apply_tiles(z_ref, u_ref, y_ref, porosity_ref[...])
    sums = {}
    curvature = None
    for a in range(NODES):
        for b in range(NODES):
            value = u_ref[a, b]
            add_to(sums, (class_of(a), class_of(b)), value)
            term = value * z_ref[a, b]
            curvature = term if curvature is None else curvature + term
    tiles = class_tiles(sums) + [inner, curvature]
    tile_ref[...] = summed_row(counts, tiles, side_x, side_y)
    sum_column(u_ref)
    send_layers(u_ref, side_x, side_y, sy_first, sy_second, fx_first, fx_second)


def second_apply_kernel(
    counts, part_ref, ry_first, ry_second, rx_first, rx_second, sum_ref, lift_ref, porosity_ref,
    r_ref, q_ref, z_ref, z1_ref, u_ref, sy_first, sy_second, fx_first, fx_second, stats_ref, y_ref,
):
    side_x, side_y = Sides("gx", counts[0]), Sides("gy", counts[1])
    summed = row_of(counts, sum_ref)
    field = lifted_rows(counts, summed, lift_ref)
    step = row_value(counts, summed, 0) / row_value(counts, summed, 1)
    w = collect_parts(part_ref, ry_first, ry_second, rx_first, rx_second, side_x, side_y, field)
    inner = None
    for (a, b), value in w.items():
        next_z = z_ref[a, b] - step * value
        next_r = r_ref[a, b] - step * q_ref[a, b]
        z1_ref[a, b] = next_z
        term = scaled(next_z * next_r, axis_factor(a, side_x), axis_factor(b, side_y))
        inner = term if inner is None else inner + term
    inner = inner * multiplicity_tile()
    apply_tiles(z1_ref, u_ref, y_ref, porosity_ref[...])
    own = None
    cross = None
    for a in range(NODES):
        for b in range(NODES):
            value = u_ref[a, b]
            own_term = value * z1_ref[a, b]
            cross_term = value * z_ref[a, b]
            own = own_term if own is None else own + own_term
            cross = cross_term if cross is None else cross + cross_term
    write_stats(stats_ref, [inner, own, cross])
    sum_column(u_ref)
    for a in range(NODES):
        low, high = u_ref[a, 0], u_ref[a, NODES - 1]
        sy_first[a] = side_y.send_first(low, high)
        sy_second[a] = side_y.send_second(low, high)
    low, high = u_ref[0], u_ref[NODES - 1]
    fx_first[...] = side_x.send_first(low, high)
    fx_second[...] = side_x.send_second(low, high)


def send_layers(u_ref, side_x, side_y, sy_first, sy_second, fx_first, fx_second):
    for a in range(NODES):
        for layer in range(2):
            low, high = u_ref[a, layer], u_ref[a, NODES - 2 + layer]
            sy_first[2 * a + layer] = side_y.send_first(low, high)
            sy_second[2 * a + layer] = side_y.send_second(low, high)
    for layer in range(2):
        low, high = u_ref[layer], u_ref[NODES - 2 + layer]
        fx_first[layer] = side_x.send_first(low, high)
        fx_second[layer] = side_x.send_second(low, high)


def early_apply_kernel(
    counts, part_ref, ry_first, ry_second, rx_first, rx_second, porosity_ref, sum_ref,
    z_ref, edge_ref, sy_first, sy_second, y_ref,
):
    side_x, side_y = Sides("gx", counts[0]), Sides("gy", counts[1])
    z = collect_parts(part_ref, ry_first, ry_second, rx_first, rx_second, side_x, side_y, None)
    for (a, b), value in z.items():
        z_ref[a, b] = value
    apply_tiles(z_ref, edge_ref, y_ref, porosity_ref[...], (0, 1, NODES - 2, NODES - 1))
    sum_column(edge_ref)
    for a in range(NODES):
        for layer in range(2):
            low, high = edge_ref[a, layer], edge_ref[a, 2 + layer]
            sy_first[2 * a + layer] = side_y.send_first(low, high)
            sy_second[2 * a + layer] = side_y.send_second(low, high)
    sy_first[2 * NODES] = sum_ref[...]


def rest_apply_kernel(
    counts, z_ref, edge_ref, porosity_ref, inner_ref, fx_first, fx_second, y_ref
):
    side_x = Sides("gx", counts[0])
    apply_tiles(z_ref, inner_ref, y_ref, porosity_ref[...], range(2, NODES - 2))
    sum_column(inner_ref)
    for layer in range(2):
        for b in range(NODES):
            low = layer_of(edge_ref, inner_ref, layer, b)
            high = layer_of(edge_ref, inner_ref, NODES - 2 + layer, b)
            fx_first[layer, b] = side_x.send_first(low, high)
            fx_second[layer, b] = side_x.send_second(low, high)


def late_apply_kernel(
    counts, part_ref, ry_first, ry_second, rx_first, rx_second, porosity_ref, low_ref, own_ref,
    high_ref, r_ref, q_ref, schwarz_ref, field_ref, w_ref, u_ref, sy_first, sy_second, fx_first, fx_second, stats_ref,
    y_ref,
):
    side_x, side_y = Sides("gx", counts[0]), Sides("gy", counts[1])
    w = collect_parts(part_ref, ry_first, ry_second, rx_first, rx_second, side_x, side_y, None)
    inner = first_inner = first_curvature = None
    for (a, b), value in w.items():
        w_ref[a, b] = value
        node_class = 3 * class_of(a) + class_of(b)
        z = schwarz_ref[a, b] + field_ref[node_class : node_class + 1, :]
        q = q_ref[a, b]
        factors = (axis_factor(a, side_x), axis_factor(b, side_y))
        terms = [scaled(t, *factors) for t in (value * q, z * r_ref[a, b], z * q)]
        if inner is None:
            inner, first_inner, first_curvature = terms
        else:
            inner, first_inner, first_curvature = (
                inner + terms[0], first_inner + terms[1], first_curvature + terms[2]
            )
    tile = multiplicity_tile()
    inner, first_inner, first_curvature = inner * tile, first_inner * tile, first_curvature * tile
    porosity = porosity_ref[...]
    apply_tiles(w_ref, u_ref, y_ref, porosity)
    sums = {}
    own = None
    for a in range(NODES):
        for b in range(NODES):
            value = u_ref[a, b]
            add_to(sums, (class_of(a), class_of(b)), value)
            term = value * w_ref[a, b]
            own = term if own is None else own + term
    total = counts[0] * counts[1]
    tiles = class_tiles(sums) + [inner, own, porosity]
    first_tiles = shared_class_tiles(q_ref, side_x, side_y) + [first_inner, first_curvature]
    row = summed_row(counts, first_tiles, side_x, side_y)[0:1] + pltpu.roll(
        summed_row(counts, tiles, side_x, side_y), total + 2, 1
    )[0:1]
    for index in range(stats_ref.shape[0]):
        stats_ref[index] = jnp.broadcast_to(row, stats_ref.shape[1:])
    sum_column(u_ref)
    near = [[ref[y + 1 : y + 2] for y in range(3)] for ref in (low_ref, own_ref, high_ref)]
    send_corners(
        u_ref, w_ref, y_ref, near, side_x, side_y, sy_first, sy_second, fx_first, fx_second
    )


def sum_tile(tile):
    row = lax.broadcasted_iota(jnp.int32, (NODES, 128), 0)
    below = jnp.where(row == 0, pltpu.roll(shift_up(tile), 1, 0), 0.0)
    above = jnp.where(row == NODES - 1, pltpu.roll(shift_down(tile), NODES - 1, 0), 0.0)
    return tile + below + above


def send_corners(
    u_ref, w_ref, y_ref, near, side_x, side_y, sy_first, sy_second, fx_first, fx_second
):
    ends = (0, NODES - 1)

    def along_x(end, b):
        return combine(STIFF[end] * WEIGHTS[b], [y_ref[a, b] for a in range(NODES)])

    def along_y(end, a):
        return combine(STIFF[end] * WEIGHTS[a], [y_ref[a, b] for b in range(NODES)])

    for a in range(NODES):
        low, high = u_ref[a, 0], u_ref[a, NODES - 1]
        sy_first[a] = side_y.send_first(low, high)
        sy_second[a] = side_y.send_second(low, high)
        low, high = u_ref[0, a], u_ref[NODES - 1, a]
        fx_first[a] = side_x.send_first(low, high)
        fx_second[a] = side_x.send_second(low, high)
    for place, node in enumerate(ends):
        low, high = (sum_tile(near[2 * place][1] * along_y(end, node)) for end in ends)
        sy_first[NODES + place] = side_y.send_first(low, high)
        sy_second[NODES + place] = side_y.send_second(low, high)
        low, high = (sum_tile(near[1][2 * place] * along_x(end, node)) for end in ends)
        fx_first[NODES + place] = side_x.send_first(low, high)
        fx_second[NODES + place] = side_x.send_second(low, high)
    weight = float(WEIGHTS[0] * WEIGHTS[0])
    for i, a in enumerate(ends):
        for j, b in enumerate(ends):
            porosity = near[2 * i][2 * j]
            value = w_ref[a, b]
            third = None
            for shift in range(NODES):
                turned = value if shift == 0 else pltpu.roll(value, shift, 0)
                term = turned * row_tile([STIFF[k, (k - shift) % NODES] for k in range(NODES)])
                third = term if third is None else third + term
            mass = jnp.where(porosity > 0.0, shift_mass * y_ref[a, b], 0.0)
            u_ref[a, b] = u_ref[a, b] + weight * sum_tile(porosity * third + mass)


def prepare_late_kernel(counts, sol_ref, r_ref, schwarz_ref, field_ref, z_ref, sol_out, r_out):
    for a in range(NODES):
        for b in range(NODES):
            node_class = 3 * class_of(a) + class_of(b)
            z_ref[a, b] = schwarz_ref[a, b] + field_ref[node_class : node_class + 1, :]
            sol_out[a, b] = sol_ref[a, b]
            r_out[a, b] = r_ref[a, b]


def porosity_kernel(counts, low_ref, own_ref, high_ref, out_ref):
    row = lax.broadcasted_iota(jnp.int32, (NODES, 128), 0)
    weights = row_tile(WEIGHTS)
    mass = shift_mass * weights / multiplicity_tile()
    end = float(WEIGHTS[0])
    for x, ref in enumerate((low_ref, own_ref, high_ref)):
        for y in range(3):
            porosity = ref[y + 1 : y + 2]
            tile = porosity * weights
            tile = tile + jnp.where(row == 0, end * shift_up(porosity), 0.0)
            tile = tile + jnp.where(row == NODES - 1, end * shift_down(porosity), 0.0)
            out_ref[3 * x + y] = tile
            out_ref[9 + 3 * x + y] = jnp.where(porosity > 0.0, mass, 0.0)


CLASS_STIFF = np.stack(
    [STIFF[:, 0], STIFF[:, 1 : NODES - 1].sum(axis=1), STIFF[:, NODES - 1]], axis=1
)
CLASS_ENDS = np.stack(
    [CLASS_STIFF[0], CLASS_STIFF[1 : NODES - 1].sum(axis=0), CLASS_STIFF[NODES - 1]]
)
CLASS_WEIGHTS = np.array([WEIGHTS[0], WEIGHTS[1 : NODES - 1].sum(), WEIGHTS[NODES - 1]])


def combine(coefficients, values):
    total = None
    for coefficient, value in zip(coefficients, values):
        term = value * float(coefficient)
        total = term if total is None else total + term
    return total


def sharing(node):
    return {
        -1: [(0, NODES - 2)], 0: [(1, 0), (0, NODES - 1)],
        NODES - 1: [(1, NODES - 1), (2, 0)], NODES: [(2, 1)],
    }.get(node, [(1, node)])


class LiftedImage:
    def __init__(self, fields, columns_ref):
        self.fields, self.columns, self.known = fields, columns_ref, {}

    def along(self, column, place, other_class, axis):
        key = (column, place, other_class, axis)
        if key not in self.known:
            field = self.fields[column]
            line = [
                field[i][other_class] if axis == 0 else field[other_class][i] for i in range(3)
            ]
            self.known[key] = combine(CLASS_STIFF[place], line)
        return self.known[key]

    def at(self, a, b):
        total = None
        for i, place_a in sharing(a):
            for j, place_b in sharing(b):
                class_a, class_b = class_of(place_a), class_of(place_b)
                stiff = self.along((i, j), place_a, class_b, 0) * float(WEIGHTS[place_b])
                stiff = stiff + self.along((i, j), place_b, class_a, 1) * float(WEIGHTS[place_a])
                mass = self.fields[(i, j)][class_a][class_b]
                mass = mass * float(WEIGHTS[place_a] * WEIGHTS[place_b])
                term = stiff * self.columns[3 * i + j] + mass * self.columns[9 + 3 * i + j]
                total = term if total is None else total + term
        return total


def near_fields(counts, table_ref, side_x, side_y):
    total = counts[0] * counts[1]

    def field_of(step_x, step_y):
        x = jnp.clip(side_x.index + step_x, 0, counts[0] - 1)
        y = jnp.clip(side_y.index + step_y, 0, counts[1] - 1)
        place = x * counts[1] + y
        return [
            [table_ref[pl.ds((3 * i + j) * total + place, 1), :] for j in range(3)]
            for i in range(3)
        ]

    return {(i, j): field_of(i - 1, j - 1) for i in range(3) for j in range(3)}


def lifted_energy(counts, table_ref, porosity_sums, length):
    total = counts[0] * counts[1]
    field = [
        [table_ref[pl.ds((3 * i + j) * total, total), :] for j in range(3)] for i in range(3)
    ]

    def line(values):
        terms = []
        for i, j in ((0, 1), (0, 2), (1, 2)):
            difference = values[i] - values[j]
            terms.append(difference * difference * float(-CLASS_ENDS[i, j]))
        return terms[0] + terms[1] + terms[2]

    stiff = None
    mass = None
    for i in range(3):
        term = line(field[i]) * float(CLASS_WEIGHTS[i])
        term = term + line([field[j][i] for j in range(3)]) * float(CLASS_WEIGHTS[i])
        stiff = term if stiff is None else stiff + term
        for j in range(3):
            term = field[i][j] * field[i][j] * float(CLASS_WEIGHTS[i] * CLASS_WEIGHTS[j])
            mass = term if mass is None else mass + term
    energy = stiff * porosity_sums * 2.0 + mass * (shift_mass * 2.0 * length)
    return jnp.sum(energy, axis=0, keepdims=True)


def late_final_kernel(
    counts, sol_ref, r_ref, q_ref, z_ref, w_ref, u_ref, ry_first, ry_second, rx_first, rx_second,
    columns_ref, lift_ref, stats_ref, sol_out, r_out, d_out, steps_out, table_ref,
):
    side_x, side_y = Sides("gx", counts[0]), Sides("gy", counts[1])
    total = counts[0] * counts[1]
    stats = stats_ref[:, 0, :]
    summed = jnp.sum(stats, axis=0, keepdims=True)
    table_ref[...] = jnp.broadcast_to(
        jnp.sum(lift_ref[...] * summed, axis=1, keepdims=True), table_ref.shape
    )
    column = lax.broadcasted_iota(jnp.int32, (total, 128), 0)
    lane = lax.broadcasted_iota(jnp.int32, (total, 128), 1)
    at = 2 * total + 2
    porosity_sums = jnp.sum(
        jnp.where(lane == at + 2, stats, 0.0), axis=1, keepdims=True
    )
    coarse = table_ref[pl.ds(4 * total, total), :]

    def product(first):
        chosen = jnp.where(lane == column + first, coarse * summed, 0.0)
        return jnp.sum(jnp.sum(chosen, axis=0, keepdims=True), axis=1, keepdims=True)

    def value(index):
        return jnp.sum(jnp.where(lane[0:1] == index, summed, 0.0), axis=1, keepdims=True)

    first_inner, first_curvature = value(total), value(total + 1)
    cross = value(at) + product(0)
    energy = value(at + 1) + 2.0 * product(total + 2) + lifted_energy(
        counts, table_ref, porosity_sums, sol_ref.shape[-1]
    )
    first_step = first_inner / first_curvature
    second_inner = first_step * first_step * cross - first_inner
    ratio = second_inner / first_inner
    mixed = first_curvature - first_step * cross
    own = first_curvature - 2.0 * first_step * cross + first_step * first_step * energy
    second_step = second_inner / (own + ratio * (2.0 * mixed + ratio * first_curvature))
    first_step, second_step, ratio = (
        jnp.broadcast_to(scalar[:, 0:1], (1, 128)) for scalar in (first_step, second_step, ratio)
    )
    steps_out[0] = first_step[0, 0]
    steps_out[1] = second_step[0, 0]

    fields = near_fields(counts, table_ref, side_x, side_y)
    lifted_image = LiftedImage(fields, columns_ref)
    low_x = side_x.low(rx_first[...], rx_second[...])
    high_x = side_x.high(rx_first[...], rx_second[...])
    corner_y = {}
    for place in range(2):
        tiles = ry_first[NODES + place], ry_second[NODES + place]
        corner_y[(place > 0, False)] = side_y.low(*tiles)
        corner_y[(place > 0, True)] = side_y.high(*tiles)
    for a in range(NODES):
        for b in range(NODES):
            image = u_ref[a, b]
            if b == 0:
                image = image + side_y.low(ry_first[a], ry_second[a])
            if b == NODES - 1:
                image = image + side_y.high(ry_first[a], ry_second[a])
            if a == 0:
                image = image + low_x[b]
            if a == NODES - 1:
                image = image + high_x[b]
            if a in (0, NODES - 1) and b in (0, NODES - 1):
                from_x = low_x if a == 0 else high_x
                image = image + from_x[NODES + (b > 0)] + corner_y[(a > 0, b > 0)]
            lifted = fields[(1, 1)][class_of(a)][class_of(b)]
            image = image + lifted_image.at(a, b)
            z, q = z_ref[a, b], q_ref[a, b]
            direction = z - first_step * (w_ref[a, b] + lifted) + ratio * z
            image = q - first_step * image + ratio * q
            d_out[a, b] = direction
            sol_out[a, b] = sol_ref[a, b] + first_step * z + second_step * direction
            r_out[a, b] = r_ref[a, b] - first_step * q - second_step * image


def prepare_kernel(counts, sol_ref, r_ref, q_ref, z_ref, sum_ref, sol_out, r_out):
    summed = row_of(counts, sum_ref)
    step = row_value(counts, summed, 0) / row_value(counts, summed, 1)
    for a in range(NODES):
        for b in range(NODES):
            sol_out[a, b] = sol_ref[a, b] + step * z_ref[a, b]
            r_out[a, b] = r_ref[a, b] - step * q_ref[a, b]


def final_kernel(
    counts, sol_ref, r_ref, q_ref, z_ref, z1_ref, u_ref, ry_first, ry_second, rx_first, rx_second,
    sum_ref, last_ref, sol_out, r_out, d_out, steps_out,
):
    side_x, side_y = Sides("gx", counts[0]), Sides("gy", counts[1])
    summed = row_of(counts, sum_ref)
    first_inner, first_curvature = row_value(counts, summed, 0), row_value(counts, summed, 1)
    second_inner, own, cross = stat_columns(last_ref[:, 0, :], 0, 3)
    first_step = first_inner / first_curvature
    ratio = second_inner / first_inner
    second_step = second_inner / (own + ratio * (2.0 * cross + ratio * first_curvature))
    steps_out[0] = first_step[0, 0]
    steps_out[1] = second_step[0, 0]
    low_x = side_x.low(rx_first[...], rx_second[...])
    high_x = side_x.high(rx_first[...], rx_second[...])
    for a in range(NODES):
        for b in range(NODES):
            image = u_ref[a, b]
            if b == 0:
                image = image + side_y.low(ry_first[a], ry_second[a])
            if b == NODES - 1:
                image = image + side_y.high(ry_first[a], ry_second[a])
            if a == 0:
                image = image + low_x[b]
            if a == NODES - 1:
                image = image + high_x[b]
            z, q = z_ref[a, b], q_ref[a, b]
            direction = z1_ref[a, b] + ratio * z
            image = image + ratio * q
            d_out[a, b] = direction
            sol_out[a, b] = sol_ref[a, b] + second_step * direction
            r_out[a, b] = r_ref[a, b] - second_step * image


COSTS = {
    "start": 100, "first_solve": 900, "second_solve": 900, "rest_of_solve": 600,
    "first_apply": 500, "rest_of_apply": 400, "second_apply": 800, "prepare": 20000,
    "final": 500, "late_apply": 800, "porosity": 20000, "late_final": 800,
}


def call(kernel, counts, name, shapes, scratch, *operands):
    def body(*refs):
        kernel(counts, *refs)

    def space(shape):
        return pltpu.SMEM if len(shape) == 1 else pltpu.VMEM

    return pl.pallas_call(
        body,
        name=name,
        out_shape=[jax.ShapeDtypeStruct(shape, jnp.float32) for shape in shapes],
        in_specs=[pl.BlockSpec(memory_space=pltpu.VMEM)] * len(operands),
        out_specs=[pl.BlockSpec(memory_space=space(shape)) for shape in shapes],
        scratch_shapes=[pltpu.VMEM(shape, jnp.float32) for shape in scratch],
        compiler_params=pltpu.CompilerParams(vmem_limit_bytes=24 * 1024 * 1024),
        cost_estimate=pl.CostEstimate(
            flops=COSTS[name] * 1000000, bytes_accessed=COSTS[name] * 3000, transcendentals=0
        ),
    )(*operands)


def swap_pairs(counts, axis, parity, ring):
    count_x, count_y = counts
    pairs = []
    for x in range(count_x):
        for y in range(count_y):
            if axis == 0:
                other = x + 1 if x % 2 == parity else x - 1
                to = (other % count_x, y) if ring or 0 <= other < count_x else (x, y ^ 1)
            else:
                other = y + 1 if y % 2 == parity else y - 1
                to = (x, other) if 0 <= other < count_y else (x ^ 1, y)
            pairs.append((x * count_y + y, to[0] * count_y + to[1]))
    return pairs


def trade(counts, axis, first, second, ring=False):
    return (
        lax.ppermute(first, AXES, swap_pairs(counts, axis, 0, ring)),
        lax.ppermute(second, AXES, swap_pairs(counts, axis, 1, ring)),
    )


def trade_far(counts, value, far_x, far_y):
    pairs = [
        (x * counts[1] + y, (x ^ far_x) * counts[1] + (y ^ far_y))
        for x in range(counts[0])
        for y in range(counts[1])
    ]
    return lax.ppermute(value, AXES, pairs)


class RunningSum:
    def __init__(self, counts, tile, carried):
        self.counts = counts
        self.carried = carried
        self.value = tile if self.carried else lax.psum(tile, AXES)

    def add(self, received):
        if self.carried:
            self.value = self.value + received

    def far(self, *steps):
        return [trade_far(self.counts, self.value, *step) for step in steps if self.carried]


def carry(tiles, running):
    return jnp.concatenate([tiles.reshape((-1, NODES, 128)), running.value[None]])


def carried(received, shape):
    return received[:-1].reshape(shape), received[-1]


def gather_stats(stats):
    return lax.all_to_all(stats, AXES, 0, 0)


def lift_tables(counts, column_length):
    share_x, share_y = share_table(counts[0]), share_table(counts[1])
    basis_x, eigen_x = cosine_inverse(counts[0])
    basis_y, eigen_y = cosine_inverse(counts[1])
    divisor = (
        2.0 * mean_porosity * column_length * (eigen_x[:, None] + eigen_y[None, :])
        + 8.0 * shift_mass * column_length
    )
    modes_x = np.einsum("xip,pa->xia", share_x, basis_x)
    modes_y = np.einsum("yjq,qb->yjb", share_y, basis_y)
    total = counts[0] * counts[1]
    to_modes = np.einsum("pa,qb->abpq", basis_x, basis_y).reshape(total, total)
    to_modes = np.pad(to_modes, ((0, 0), (0, sum_lanes(counts) - total)))
    return [table.astype(np.float32) for table in (modes_x, modes_y, 1.0 / divisor, to_modes)]


def all_lift(counts, column_length):
    modes_x, modes_y, inverse, to_modes = lift_tables(counts, column_length)
    total = counts[0] * counts[1]
    lift = np.einsum(
        "xia,yjb,ab,abl->ijxyl", *(
            table.astype(np.float64)
            for table in (modes_x, modes_y, inverse, to_modes.reshape(inverse.shape + (-1,)))
        ),
    )
    return jnp.asarray(lift.reshape(9 * total, -1).astype(np.float32))


def own_lift(tables):
    modes_x, modes_y, inverse, to_modes = [jnp.asarray(table) for table in tables]
    own_x = lax.dynamic_index_in_dim(modes_x, lax.axis_index("gx"), 0, keepdims=False)
    own_y = lax.dynamic_index_in_dim(modes_y, lax.axis_index("gy"), 0, keepdims=False)
    own = own_x[:, None, :, None] * own_y[None, :, None, :] * inverse[None, None]
    lift = jnp.dot(own.reshape(9, -1), to_modes, precision=exact_mode)
    return jnp.pad(lift, ((0, 7), (0, 0)))


def shards_of(counts):
    forward_np, back_edge_np, back_inner_np, inverse_np = plane_tables()

    def shards(solution, residual, grain_counts):
        shard_shape = solution.shape
        block = shard_shape[2:]
        solution = solution.reshape(block)
        residual = residual.reshape(block)
        lift = own_lift(lift_tables(counts, block[-1]))
        late = counts == (8, 4)
        every_lift = all_lift(counts, block[-1]) if late else None
        porosity = 1.0 - 0.6 * grain_counts.reshape(1, 128).astype(jnp.float32) / MOST_GRAINS
        plane = [jnp.asarray(table) for table in (forward_np, back_edge_np, inverse_np)]
        back_inner = jnp.asarray(back_inner_np)
        side_x, side_y = Sides("gx", counts[0]), Sides("gy", counts[1])
        row = (counts[0] * counts[1], 4, 128)
        face = (NODES, NODES, 128)
        sends = [(2 * EXT, NODES, 128)] * 2
        solve_shapes = [(MODES, EXT * 128), (EXT, 2 * NODES, 128)]
        solve_scratch = [(EXT, ROWS, 128), (EXT, len(back_edge_np), 128)]

        def rest_of_solve(spectrum, edges):
            return call(
                rest_kernel, counts, "rest_of_solve",
                [(EXT, NODES * NODES, 128)] + [(2, NODES, NODES, 128)] * 2,
                [(EXT, len(back_inner_np), 128)], spectrum, edges, back_inner,
            )

        y_first, y_second = call(
            start_kernel, counts, "start", [(NODES + 1,) + face[1:], face], [], residual
        )
        running = RunningSum(counts, y_first[-1], late)
        ry = trade(counts, 1, y_first, y_second)
        ry_first, tile = carried(ry[0], face)
        running.add(tile)
        ry = (ry_first, ry[1])
        low_y, high_y = side_y.low(*ry), side_y.high(*ry)

        def with_layers(index):
            return jnp.concatenate([low_y[index][None], residual[index], high_y[index][None]])

        low_face, high_face = with_layers(1), with_layers(NODES - 2)
        rx = trade(
            counts, 0, carry(side_x.send_first(low_face, high_face), running),
            side_x.send_second(low_face, high_face),
        )
        rx_first, tile = carried(rx[0], low_face.shape)
        running.add(tile)
        rx = (rx_first, rx[1])
        spectrum, edges, y_first, y_second = call(
            first_solve_kernel, counts, "first_solve",
            solve_shapes + [(2 * EXT + 1, NODES, 128)] * 2, solve_scratch,
            residual, porosity, running.value, *ry, *rx, *plane,
        )
        part, *fx = rest_of_solve(spectrum, edges)

        def spread_faces(fx, ry):
            low_y, high_y = side_y.low(*ry), side_y.high(*ry)
            middle = jnp.zeros((2, NODES - 4, NODES, 128), jnp.float32)
            both = [
                jnp.concatenate([low_y[at], middle, high_y[at]], axis=1)
                for at in (slice(0, 2), slice(8, 10))
            ]
            return (
                fx[0] + side_x.send_first(*both),
                fx[1] + side_x.send_second(*both),
            )

        def trade_y(y_first, y_second, shape):
            count = math.prod(shape[:-2])
            ry = trade(counts, 1, y_first, y_second)
            faces = [value[:count].reshape(shape) for value in ry]
            return faces, [value[count:] for value in ry]

        ext_face = (EXT, 2, NODES, 128)
        two = (NODES, 2, NODES, 128)
        tiles = (-1, NODES, 128)
        ry, rows = trade_y(y_first, y_second, ext_face)
        rows = [value[0] for value in rows]
        inner_y = (side_y.index > 0) & (side_y.index < counts[1] - 1)
        three = jnp.concatenate(
            [
                running.value[0:1] + jnp.where(inner_y, rows[1][0:1], 0.0),
                side_y.low(*rows)[1:2], porosity, side_y.high(*rows)[1:2],
                jnp.zeros((NODES - 4, 128), jnp.float32),
            ]
        )
        first, second = (
            jnp.concatenate([faces.reshape(tiles), three[None]]) for faces in spread_faces(fx, ry)
        )
        rx = trade(counts, 0, first, second, ring=True)
        count = 2 * NODES
        threes = [value[count] for value in rx]
        rx = [value[:count].reshape((2, NODES, NODES, 128)) for value in rx]
        if late:
            running.value = three + threes[1]
        if late:
            half = (NODES, NODES // 2, NODES, 128)
            z, u_edge, y_first, y_second = call(
                early_apply_kernel, counts, "first_apply",
                [block, half, (2 * NODES + 1, NODES, 128), (2 * NODES, NODES, 128)], [block],
                part, *ry, *rx, porosity, running.value,
            )
            u_inner, *fx = call(
                rest_apply_kernel, counts, "rest_of_apply",
                [half, (2, NODES, NODES, 128), (2, NODES, NODES, 128)], [block],
                z, u_edge, porosity,
            )
        else:
            z, u, y_first, y_second, *fx, tile = call(
                first_apply_kernel, counts, "first_apply",
                [block, block, (2 * NODES, NODES, 128), (2 * NODES, NODES, 128),
                 (2, NODES, NODES, 128), (2, NODES, NODES, 128), (NODES, 128)],
                [block],
                part, *ry, *rx, running.value, lift, porosity, residual,
            )
            u_edge = jnp.concatenate([u[:, :2], u[:, -2:]], axis=1)
            u_inner = u[:, 2:-2]
        ry, rows = trade_y(y_first, y_second, two)
        if late:
            running.value = jnp.where(inner_y, running.value, rows[0][0])
        low_y, high_y = side_y.low(*ry), side_y.high(*ry)

        def image_faces(index):
            middle = jnp.zeros((2, NODES - 2, NODES, 128), jnp.float32)
            return jnp.concatenate([low_y[index], middle, high_y[index]], axis=1)

        pads = ((0, 0), (1, 1), (0, 0), (0, 0))
        both = (image_faces(slice(0, 2)), image_faces(slice(NODES - 2, NODES)))
        rx = trade(
            counts, 0,
            jnp.pad(fx[0], pads) + side_x.send_first(*both),
            jnp.pad(fx[1], pads) + side_x.send_second(*both),
        )
        if late:
            near = (side_x.low(*threes), three, side_x.high(*threes))
            (columns,) = call(porosity_kernel, counts, "porosity", [(18, NODES, 128)], [], *near)
            rx, far, columns = lax.optimization_barrier((rx, running.far((4, 0)), columns))
            for value in far:
                running.add(value)
            table = (9 * counts[0] * counts[1], 128)
            q, spectrum, edges, y_first, y_second, field = call(
                late_solve_kernel, counts, "second_solve",
                [block] + solve_shapes + sends + [(16, 128)], solve_scratch + [table],
                u_edge, u_inner, *ry, *rx, columns, every_lift, running.value, *plane,
            )
        else:
            q, spectrum, edges, y_first, y_second = call(
                second_solve_kernel, counts, "second_solve", [block] + solve_shapes + sends,
                solve_scratch, u_edge, u_inner, *ry, *rx, *plane,
            )
        part, *fx = rest_of_solve(spectrum, edges)
        ry, _ = trade_y(y_first, y_second, ext_face)
        rx = trade(counts, 0, *spread_faces(fx, ry))

        def trade_edges(y_first, y_second, fx, beside):
            ry, beside = lax.optimization_barrier((trade(counts, 1, y_first, y_second), beside))
            low_y, high_y = side_y.low(*ry), side_y.high(*ry)

            def edge_rows(index):
                middle = jnp.zeros((NODES - 2, NODES, 128), jnp.float32)
                return jnp.concatenate([low_y[index][None], middle, high_y[index][None]])

            both = (edge_rows(0), edge_rows(NODES - 1))
            rx = trade(
                counts, 0, fx[0] + side_x.send_first(*both), fx[1] + side_x.send_second(*both)
            )
            return ry, rx, beside

        if late:
            w, u, y_first, y_second, *fx, stats = call(
                late_apply_kernel, counts, "late_apply",
                [block, block] + [(NODES + 2, NODES, 128)] * 4 + [row], [block],
                part, *ry, *rx, porosity, *near, residual, q, z, field,
            )
            z, w = lax.optimization_barrier((z, w))
            nexts = call(
                prepare_late_kernel, counts, "prepare", [block] * 3, [],
                solution, residual, z, field,
            )
            ry, rx, (z, solution, residual) = lax.optimization_barrier(
                (trade(counts, 1, y_first, y_second), trade(counts, 0, *fx), nexts)
            )
            solution_out, residual_out, direction, steps = call(
                late_final_kernel, counts, "late_final", [block] * 3 + [(2,)], [table],
                solution, residual, q, z, w, u, *ry, *rx, columns, every_lift,
                gather_stats(stats),
            )
        else:
            summed = lax.psum(tile, AXES)
            z1, u, y_first, y_second, *fx, stats = call(
                second_apply_kernel, counts, "second_apply",
                [block, block, face, face, face, face, row], [block],
                part, *ry, *rx, summed, lift, porosity, residual, q, z,
            )
            nexts = call(
                prepare_kernel, counts, "prepare", [block] * 2, [],
                solution, residual, q, z, summed,
            )
            ry, rx, nexts = trade_edges(y_first, y_second, fx, nexts)
            solution_out, residual_out, direction, steps = call(
                final_kernel, counts, "final", [block] * 3 + [(2,)], [],
                *nexts, q, z, z1, u, *ry, *rx, summed, gather_stats(stats),
            )
        return (
            solution_out.reshape(shard_shape),
            residual_out.reshape(shard_shape),
            direction.reshape(shard_shape),
            steps,
        )

    return shards


def solution(mesh):
    counts = (mesh.shape["gx"], mesh.shape["gy"])
    return jax.shard_map(
        shards_of(counts),
        mesh=mesh,
        in_specs=(
            P("gx", "gy", None, None, None, None),
            P("gx", "gy", None, None, None, None),
            P("gx", "gy", None),
        ),
        out_specs=(
            P("gx", "gy", None, None, None, None),
            P("gx", "gy", None, None, None, None),
            P("gx", "gy", None, None, None, None),
            P(),
        ),
        check_vma=False,
    )
```

```python
import math

import jax
import jax.numpy as jnp
import numpy as np
from jax import lax
from jax.experimental import pallas as pl
from jax.experimental.pallas import tpu as pltpu
from jax.sharding import PartitionSpec as P

NODES = 8
MOST_GRAINS = 16
EXT = NODES + 2
ROWS = 112
MODES = 104
AXES = ("gx", "gy")
EDGE = (0, 1, EXT - 2, EXT - 1)
INNER = tuple(range(2, EXT - 2))

shift_mass = 0.1
mean_porosity = 0.7
exact_mode = lax.Precision.HIGHEST
plane_mode = lax.Precision.HIGH


def legendre_columns(node_set, degree):
    table = [node_set * 0.0 + 1.0, node_set]
    for order in range(2, degree + 1):
        table.append(
            ((2 * order - 1) * node_set * table[order - 1] - (order - 1) * table[order - 2]) / order
        )
    return table


def gll_tables():
    degree = NODES - 1
    node_set = np.cos(math.pi * np.arange(degree + 1) / degree)
    for sweep in range(100):
        table = legendre_columns(node_set, degree)
        node_set = node_set - (node_set * table[degree] - table[degree - 1]) / (
            (degree + 1) * table[degree]
        )
    node_set = node_set[::-1].copy()
    values = legendre_columns(node_set, degree)[degree]
    weights = 2.0 / (degree * (degree + 1) * values**2)
    derivative = np.zeros((NODES, NODES))
    for row_index in range(NODES):
        for column_index in range(NODES):
            if row_index != column_index:
                derivative[row_index, column_index] = values[row_index] / (
                    values[column_index] * (node_set[row_index] - node_set[column_index])
                )
    derivative[0, 0] = -degree * (degree + 1) / 4.0
    derivative[NODES - 1, NODES - 1] = degree * (degree + 1) / 4.0
    return (weights, derivative)


def jacobi_eigen(matrix):
    size_now = matrix.shape[0]
    current = matrix.copy()
    vectors = np.eye(size_now)
    for sweep in range(12):
        for first in range(size_now - 1):
            for second in range(first + 1, size_now):
                off_value = current[first, second]
                safe_value = np.where(off_value == 0.0, 1e-300, off_value)
                theta = (current[second, second] - current[first, first]) / (2.0 * safe_value)
                sign_value = np.where(theta >= 0.0, 1.0, -1.0)
                tangent = sign_value / (np.abs(theta) + np.sqrt(theta * theta + 1.0))
                cosine = 1.0 / np.sqrt(tangent * tangent + 1.0)
                sine = tangent * cosine
                rotation = np.eye(size_now)
                rotation[first, first] = cosine
                rotation[second, second] = cosine
                rotation[first, second] = sine
                rotation[second, first] = -sine
                current = rotation.T @ current @ rotation
                vectors = vectors @ rotation
    eigen_values = np.array([current[index, index] for index in range(size_now)])
    return (eigen_values, vectors)


def schwarz_tables():
    weights, derivative = gll_tables()
    stiffness = derivative.T @ (weights[:, None] * derivative)
    total_nodes = 3 * (NODES - 1) + 1
    three_stiffness = np.zeros((total_nodes, total_nodes))
    three_mass = np.zeros(total_nodes)
    for element in range(3):
        start_node = element * (NODES - 1)
        three_stiffness[
            start_node : start_node + NODES, start_node : start_node + NODES
        ] += stiffness
        three_mass[start_node : start_node + NODES] += weights
    chosen = np.array([NODES - 2] + list(range(NODES - 1, 2 * NODES - 1)) + [2 * NODES - 1])
    local_stiffness = three_stiffness[chosen][:, chosen]
    local_mass = three_mass[chosen]
    scaling = 1.0 / np.sqrt(local_mass)
    symmetric = scaling[:, None] * local_stiffness * scaling[None, :]
    symmetric = 0.5 * (symmetric + symmetric.T)
    eigen_values, eigen_vectors = jacobi_eigen(symmetric)
    return (scaling[:, None] * eigen_vectors, eigen_values)


WEIGHTS, DERIVATIVE = gll_tables()
STIFF = DERIVATIVE.T @ (WEIGHTS[:, None] * DERIVATIVE)
BASIS, EIGEN = schwarz_tables()
PARITY = {
    sign: [mode for mode in range(EXT) if BASIS[0, mode] * BASIS[EXT - 1, mode] * sign > 0]
    for sign in (1, -1)
}


def plane_tables():
    forward = np.zeros((MODES, ROWS))
    inverse = np.zeros((MODES, EXT))
    for mode_b in range(EXT):
        for mode_c in range(EXT):
            mode = mode_b * EXT + mode_c
            for b in range(EXT):
                for k in range(NODES):
                    forward[mode, b * NODES + k] = BASIS[b, mode_b] * BASIS[k + 1, mode_c]
                forward[mode, 80 + b] = BASIS[b, mode_b] * BASIS[0, mode_c]
                forward[mode, 96 + b] = BASIS[b, mode_b] * BASIS[EXT - 1, mode_c]
            inverse[mode] = 1.0 / (
                mean_porosity * (EIGEN + EIGEN[mode_b] + EIGEN[mode_c]) + shift_mass
            )
    lanes = np.repeat(inverse.T[:, :, None], 128, axis=2)
    back = forward.T
    tables = [
        np.concatenate([back[[8 * b + k for b in layers for k in range(NODES)]]]
                       + [pad_rows(back[[at + b for b in layers]], 8) for at in (80, 96)])
        for layers in (EDGE, INNER)
    ]
    return tuple(table.astype(np.float32) for table in (forward, *tables, lanes))


def pad_rows(table, count):
    return np.pad(table, ((0, -len(table) % count), (0, 0)))


def row_tile(values):
    row = lax.broadcasted_iota(jnp.int32, (NODES, 128), 0)
    tile = jnp.full((NODES, 128), float(values[0]), jnp.float32)
    for k in range(1, NODES):
        tile = jnp.where(row == k, float(values[k]), tile)
    return tile


def share_table(count):
    table = np.zeros((count, 3, count))
    for column in range(count):
        table[column, :, column] = 1.0
        if column > 0:
            table[column, 0, column] = 0.5
            table[column, 0, column - 1] = 0.5
        if column < count - 1:
            table[column, 2, column] = 0.5
            table[column, 2, column + 1] = 0.5
    return table


def cosine_inverse(count):
    position = np.arange(count)
    basis = np.cos(math.pi * (position[:, None] + 0.5) * position[None, :] / count)
    basis = basis * np.where(position == 0, math.sqrt(1.0 / count), math.sqrt(2.0 / count))[None, :]
    return basis, 2.0 - 2.0 * np.cos(math.pi * position / count)


def shift_up(rows):
    lane = lax.broadcasted_iota(jnp.int32, rows.shape, 1)
    return jnp.where(lane == 0, 0.0, pltpu.roll(rows, 1, 1))


def shift_down(rows):
    lane = lax.broadcasted_iota(jnp.int32, rows.shape, 1)
    return jnp.where(lane == 127, 0.0, pltpu.roll(rows, 127, 1))


class Sides:
    def __init__(self, axis, count):
        self.index = lax.axis_index(axis)
        self.even = lax.rem(self.index, 2) == 0
        self.no_low = self.index == 0
        self.no_high = self.index == count - 1

    def low(self, first, second):
        return jnp.where(self.no_low, 0.0, jnp.where(self.even, second, first))

    def high(self, first, second):
        return jnp.where(self.no_high, 0.0, jnp.where(self.even, first, second))

    def send_first(self, low_face, high_face):
        return jnp.where(self.even, high_face, low_face)

    def send_second(self, low_face, high_face):
        return jnp.where(self.even, low_face, high_face)


def multiplicity_tile():
    row = lax.broadcasted_iota(jnp.int32, (NODES, 128), 0)
    lane = lax.broadcasted_iota(jnp.int32, (NODES, 128), 1)
    shared = ((row == 0) & (lane > 0)) | ((row == NODES - 1) & (lane < 127))
    return jnp.where(shared, 0.5, 1.0)


def class_of(node):
    return 0 if node == 0 else (2 if node == NODES - 1 else 1)


def axis_factor(node, side):
    if node == 0:
        return jnp.where(side.no_low, 1.0, 0.5)
    if node == NODES - 1:
        return jnp.where(side.no_high, 1.0, 0.5)
    return None


def scaled(value, *factors):
    for factor in factors:
        if factor is not None:
            value = value * factor
    return value


def add_to(total, key, value):
    total[key] = value if key not in total else total[key] + value


def lane_sums(tiles):
    columns = [jnp.sum(tile, axis=0, keepdims=True) for tile in tiles]
    columns.append(jnp.zeros((16 - len(tiles), 128), jnp.float32))
    sums = jnp.sum(jnp.concatenate(columns, axis=0), axis=1, keepdims=True)
    return jnp.broadcast_to(sums, (16, 128))


def write_stats(stats_ref, tiles):
    row = lax.broadcasted_iota(jnp.int32, (16, 128), 0)
    lane = lax.broadcasted_iota(jnp.int32, (16, 128), 1)
    sums = jnp.sum(jnp.where(row == lane, lane_sums(tiles), 0.0), axis=0, keepdims=True)
    for index in range(stats_ref.shape[0]):
        stats_ref[index] = jnp.broadcast_to(sums, stats_ref.shape[1:])


def stat_columns(stats, first, count):
    lane = lax.broadcasted_iota(jnp.int32, stats.shape, 1)
    sums = lane_sums([jnp.where(lane == first + i, stats, 0.0) for i in range(count)])
    return [sums[i : i + 1] for i in range(count)]


def sum_lanes(counts):
    return -(-(counts[0] * counts[1] + 2) // 128) * 128


def share_rows(counts, side_x, side_y):
    lane = lax.broadcasted_iota(jnp.int32, (1, sum_lanes(counts)), 1)
    column_y = lax.rem(lane, counts[1])
    first_x = lane - column_y

    def weights(side, place, step, count):
        own = jnp.where(place == side.index * step, 1.0, 0.0)
        below = jnp.where(place == (side.index - 1) * step, 1.0, 0.0)
        above = jnp.where(place == (side.index + 1) * step, 1.0, 0.0)
        return (
            jnp.where(side.no_low, own, 0.5 * (own + below)),
            own,
            jnp.where(side.no_high, own, 0.5 * (own + above)),
        )

    inside = lane < counts[0] * counts[1]
    along_x = weights(side_x, first_x, counts[1], counts[0])
    along_y = weights(side_y, column_y, 1, counts[1])
    return [jnp.where(inside, wx * wy, 0.0) for wx in along_x for wy in along_y]


def summed_row(counts, tiles, side_x, side_y):
    sums = lane_sums(tiles)
    lane = lax.broadcasted_iota(jnp.int32, (1, sum_lanes(counts)), 1)
    total = None
    for i, share in enumerate(share_rows(counts, side_x, side_y)):
        term = share * sums[i : i + 1, 0:1]
        total = term if total is None else total + term
    for i in range(9, len(tiles)):
        total = total + jnp.where(lane == counts[0] * counts[1] + i - 9, sums[i : i + 1, 0:1], 0.0)
    pieces = [total[:, at : at + 128] for at in range(0, sum_lanes(counts), 128)]
    pieces.append(jnp.zeros((NODES - len(pieces), 128), jnp.float32))
    return jnp.concatenate(pieces, axis=0)


def row_of(counts, tile_ref):
    rows = [tile_ref[i : i + 1, :] for i in range(sum_lanes(counts) // 128)]
    return rows[0] if len(rows) == 1 else jnp.concatenate(rows, axis=1)


def lifted_rows(counts, row, lift_ref):
    sums = jnp.sum(lift_ref[...] * row, axis=1, keepdims=True)
    return jnp.broadcast_to(sums, (16, 128))


def row_value(counts, row, index):
    lane = lax.broadcasted_iota(jnp.int32, row.shape, 1)
    chosen = jnp.where(lane == counts[0] * counts[1] + index, row, 0.0)
    return jnp.broadcast_to(jnp.sum(chosen, axis=1, keepdims=True), (1, 128))


def class_tiles(sums):
    return [sums[(i, j)] for i in range(3) for j in range(3)]


def shared_class_tiles(field_ref, side_x, side_y):
    tile = multiplicity_tile()
    sums = {}
    for a in range(NODES):
        for b in range(NODES):
            add_to(sums, (class_of(a), class_of(b)), field_ref[a, b])
    for (i, j), value in sums.items():
        a, b = (0, 1, NODES - 1)[i], (0, 1, NODES - 1)[j]
        sums[(i, j)] = scaled(value * tile, axis_factor(a, side_x), axis_factor(b, side_y))
    return class_tiles(sums)


def start_kernel(counts, r_ref, sy_first, sy_second):
    side_x, side_y = Sides("gx", counts[0]), Sides("gy", counts[1])
    for a in range(NODES):
        low, high = r_ref[a, 1], r_ref[a, NODES - 2]
        sy_first[a] = side_y.send_first(low, high)
        sy_second[a] = side_y.send_second(low, high)
    sy_first[NODES] = summed_row(
        counts, shared_class_tiles(r_ref, side_x, side_y), side_x, side_y
    )


def planes(ref):
    return jnp.concatenate([ref[a] for a in range(EXT)], axis=1)


def to_spectrum(x_ref, forward_ref, inverse_ref):
    zero = jnp.zeros((6, 128), jnp.float32)
    for a in range(EXT):
        x_ref[a, 80:90] = shift_up(x_ref[a, pl.ds(6, EXT, stride=NODES), :])
        x_ref[a, 96:106] = shift_down(x_ref[a, pl.ds(1, EXT, stride=NODES), :])
        x_ref[a, 90:96] = zero
        x_ref[a, 106:112] = zero
    half = EXT // 2
    for block in range(ROWS // 8):
        rows = pl.ds(block * 8, 8)
        low = [x_ref[a, rows] for a in range(half)]
        high = [x_ref[EXT - 1 - a, rows] for a in range(half)]
        folded = {1: [x + y for x, y in zip(low, high)], -1: [x - y for x, y in zip(low, high)]}
        for sign in (1, -1):
            for mode in PARITY[sign]:
                total = folded[sign][0] * float(BASIS[0, mode])
                for a in range(1, half):
                    total = total + folded[sign][a] * float(BASIS[a, mode])
                x_ref[mode, rows] = total
    spectrum = jnp.dot(
        forward_ref[...], planes(x_ref), precision=plane_mode, preferred_element_type=jnp.float32
    ) * planes(inverse_ref)
    return spectrum


def from_spectrum(spectrum, back_ref, part_ref, count):
    half = EXT // 2
    values = jnp.dot(
        back_ref[...], spectrum, precision=plane_mode, preferred_element_type=jnp.float32
    )
    for block in range(part_ref.shape[1] // 8):
        rows = pl.ds(block * 8, 8)
        modes = [values[block * 8 : block * 8 + 8, m * 128 : (m + 1) * 128] for m in range(EXT)]
        back = {}
        for sign in (1, -1):
            for a in range(half):
                total = None
                for mode in PARITY[sign]:
                    term = modes[mode] * float(BASIS[a, mode])
                    total = term if total is None else total + term
                back[(sign, a)] = total
        for a in range(half):
            part_ref[a, rows] = back[(1, a)] + back[(-1, a)]
            part_ref[EXT - 1 - a, rows] = back[(1, a)] - back[(-1, a)]
    below, above = NODES * count, NODES * count + 8
    for a in range(EXT):

        def layer(k):
            return (a, pl.ds(k, count, stride=NODES), slice(None))

        bottom, top = part_ref[layer(0)], part_ref[layer(NODES - 1)]
        part_ref[layer(0)] = bottom + shift_up(top)
        part_ref[layer(NODES - 1)] = top + shift_down(bottom)
        part_ref[layer(1)] = part_ref[layer(1)] + shift_up(part_ref[a, above : above + count])
        part_ref[layer(NODES - 2)] = part_ref[layer(NODES - 2)] + shift_down(
            part_ref[a, below : below + count]
        )


def solve_edges(
    x_ref, forward_ref, back_ref, inverse_ref, spectrum_ref, edge_ref, sy_first, sy_second,
    side_y, part_ref,
):
    spectrum = to_spectrum(x_ref, forward_ref, inverse_ref)
    spectrum_ref[...] = spectrum
    from_spectrum(spectrum, back_ref, part_ref, len(EDGE))
    for a in range(EXT):
        low, high = part_ref[a, 0:16], part_ref[a, 16:32]
        sy_first[2 * a : 2 * a + 2] = side_y.send_first(low, high).reshape(2, NODES, 128)
        sy_second[2 * a : 2 * a + 2] = side_y.send_second(low, high).reshape(2, NODES, 128)
        edge_ref[a] = part_ref[a, 8:24]


def rest_kernel(
    counts, spectrum_ref, edge_ref, back_ref, part_ref, fx_first, fx_second, inner_ref
):
    side_x = Sides("gx", counts[0])
    from_spectrum(spectrum_ref[...], back_ref, inner_ref, len(INNER))
    for a in range(EXT):
        part_ref[a, 0:8] = edge_ref[a, 0:8]
        part_ref[a, 8:56] = inner_ref[a, 0:48]
        part_ref[a, 56:64] = edge_ref[a, 8:16]
    for layer in range(2):
        low, high = part_ref[layer], part_ref[NODES + layer]
        fx_first[layer] = side_x.send_first(low, high).reshape(NODES, NODES, 128)
        fx_second[layer] = side_x.send_second(low, high).reshape(NODES, NODES, 128)


def first_solve_kernel(
    counts, r_ref, porosity_ref, sum_ref, ry_first, ry_second, rx_first, rx_second, forward_ref, back_ref,
    inverse_ref, spectrum_ref, edge_ref, sy_first, sy_second, x_ref, part_ref,
):
    row = lax.broadcasted_iota(jnp.int32, (NODES, 128), 0)
    for send in (sy_first, sy_second):
        send[2 * EXT] = jnp.where(row == 0, sum_ref[...], porosity_ref[...])
    side_x, side_y = Sides("gx", counts[0]), Sides("gy", counts[1])
    x_ref[0, 0:80] = side_x.low(rx_first[...], rx_second[...]).reshape(80, 128)
    x_ref[EXT - 1, 0:80] = side_x.high(rx_first[...], rx_second[...]).reshape(80, 128)
    for a in range(NODES):
        x_ref[a + 1, 0:8] = side_y.low(ry_first[a], ry_second[a])
        x_ref[a + 1, 8:72] = r_ref[a].reshape(64, 128)
        x_ref[a + 1, 72:80] = side_y.high(ry_first[a], ry_second[a])
    solve_edges(
        x_ref, forward_ref, back_ref, inverse_ref, spectrum_ref, edge_ref, sy_first, sy_second,
        side_y, part_ref,
    )


def second_solve_kernel(
    counts, edge_ref, inner_ref, ry_first, ry_second, rx_first, rx_second, forward_ref, back_ref,
    inverse_ref, q_ref, spectrum_ref, layers_ref, sy_first, sy_second, x_ref, part_ref,
):
    side_x, side_y = Sides("gx", counts[0]), Sides("gy", counts[1])
    extend_image(
        edge_ref, inner_ref, ry_first, ry_second, rx_first, rx_second, side_x, side_y, q_ref, x_ref, None
    )
    solve_edges(
        x_ref, forward_ref, back_ref, inverse_ref, spectrum_ref, layers_ref, sy_first, sy_second,
        side_y, part_ref,
    )


def late_solve_kernel(
    counts, edge_ref, inner_ref, ry_first, ry_second, rx_first, rx_second, columns_ref, lift_ref,
    sum_ref, forward_ref, back_ref, inverse_ref, q_ref, spectrum_ref, layers_ref, sy_first,
    sy_second, field_ref, x_ref, part_ref, table_ref,
):
    side_x, side_y = Sides("gx", counts[0]), Sides("gy", counts[1])
    table_ref[...] = jnp.broadcast_to(
        jnp.sum(lift_ref[...] * sum_ref[0:1], axis=1, keepdims=True), table_ref.shape
    )
    fields = near_fields(counts, table_ref, side_x, side_y)
    own = fields[(1, 1)]
    field_ref[...] = jnp.concatenate(
        [own[i][j] for i in range(3) for j in range(3)] + [jnp.zeros((7, 128), jnp.float32)]
    )
    image = LiftedImage(fields, columns_ref)
    extend_image(
        edge_ref, inner_ref, ry_first, ry_second, rx_first, rx_second, side_x, side_y, q_ref, x_ref, image
    )
    solve_edges(
        x_ref, forward_ref, back_ref, inverse_ref, spectrum_ref, layers_ref, sy_first, sy_second,
        side_y, part_ref,
    )


def layer_of(edge_ref, inner_ref, a, b):
    if 2 <= b < NODES - 2:
        return inner_ref[a, b - 2]
    return edge_ref[a, b if b < 2 else b - (NODES - 4)]


def extend_image(
    edge_ref, inner_ref, ry_first, ry_second, rx_first, rx_second, side_x, side_y, q_ref, x_ref,
    image,
):
    low_x = side_x.low(rx_first[...], rx_second[...])
    high_x = side_x.high(rx_first[...], rx_second[...])

    def lifted(value, a, b):
        return value if image is None else value + image.at(a - 1, b - 1)

    for b in range(EXT):
        rows = pl.ds(b * 8, 8)
        x_ref[0, rows] = lifted(low_x[0, b], 0, b)
        x_ref[EXT - 1, rows] = lifted(high_x[1, b], EXT - 1, b)
    for a in range(NODES):
        low_y = side_y.low(ry_first[a], ry_second[a])
        high_y = side_y.high(ry_first[a], ry_second[a])
        rows = [low_y[0]]
        for b in range(NODES):
            value = layer_of(edge_ref, inner_ref, a, b)
            if b == 0:
                value = value + low_y[1]
            if b == NODES - 1:
                value = value + high_y[0]
            rows.append(value)
        rows.append(high_y[1])
        for b in range(EXT):
            value = rows[b]
            if a == 0:
                value = value + low_x[1, b]
            if a == NODES - 1:
                value = value + high_x[0, b]
            value = lifted(value, a + 1, b)
            x_ref[a + 1, b * 8 : b * 8 + 8] = value
            if 0 < b < EXT - 1:
                q_ref[a, b - 1] = value


def collect_parts(part_ref, ry_first, ry_second, rx_first, rx_second, side_x, side_y, field):
    low_x = side_x.low(rx_first[...], rx_second[...])
    high_x = side_x.high(rx_first[...], rx_second[...])
    result = {}
    for a in range(NODES):
        low_y = side_y.low(ry_first[a + 1], ry_second[a + 1])
        high_y = side_y.high(ry_first[a + 1], ry_second[a + 1])
        for b in range(NODES):
            value = part_ref[a + 1, b * 8 : (b + 1) * 8]
            if b < 2:
                value = value + low_y[b]
            if b >= NODES - 2:
                value = value + high_y[b - (NODES - 2)]
            if a < 2:
                value = value + low_x[a, b]
            if a >= NODES - 2:
                value = value + high_x[a - (NODES - 2), b]
            if field is not None:
                node_class = 3 * class_of(a) + class_of(b)
                value = value + field[node_class : node_class + 1, :]
            result[(a, b)] = value
    return result


def apply_tiles(z_ref, u_ref, y_ref, por, layers=range(NODES)):
    weight_tile = row_tile(WEIGHTS)
    stiff_tiles = [
        row_tile([STIFF[k, (k - shift) % NODES] for k in range(NODES)]) for shift in range(NODES)
    ]
    for a in range(NODES):
        for b in range(NODES):
            y_ref[a, b] = z_ref[a, b] * weight_tile
    for a in range(NODES):
        for place, b in enumerate(layers):
            z = z_ref[a, b]
            third = z * stiff_tiles[0]
            for shift in range(1, NODES):
                third = third + pltpu.roll(z, shift, 0) * stiff_tiles[shift]
            first = y_ref[0, b] * float(STIFF[a, 0] * WEIGHTS[b])
            second = y_ref[a, 0] * float(STIFF[b, 0] * WEIGHTS[a])
            for other in range(1, NODES):
                first = first + y_ref[other, b] * float(STIFF[a, other] * WEIGHTS[b])
                second = second + y_ref[a, other] * float(STIFF[b, other] * WEIGHTS[a])
            weight = float(WEIGHTS[a] * WEIGHTS[b])
            u_ref[a, place] = por * (third * weight + first + second) + y_ref[a, b] * (
                shift_mass * weight
            )


def sum_column(u_ref):
    for a in range(NODES):
        bottom = u_ref[a, :, 0, :]
        top = u_ref[a, :, NODES - 1, :]
        u_ref[a, :, 0, :] = bottom + shift_up(top)
        u_ref[a, :, NODES - 1, :] = top + shift_down(bottom)


def first_apply_kernel(
    counts, part_ref, ry_first, ry_second, rx_first, rx_second, sum_ref, lift_ref, porosity_ref,
    r_ref, z_ref, u_ref, sy_first, sy_second, fx_first, fx_second, tile_ref, y_ref,
):
    side_x, side_y = Sides("gx", counts[0]), Sides("gy", counts[1])
    field = lifted_rows(counts, row_of(counts, sum_ref), lift_ref)
    z = collect_parts(part_ref, ry_first, ry_second, rx_first, rx_second, side_x, side_y, field)
    inner = None
    for (a, b), value in z.items():
        z_ref[a, b] = value
        term = scaled(value * r_ref[a, b], axis_factor(a, side_x), axis_factor(b, side_y))
        inner = term if inner is None else inner + term
    inner = inner * multiplicity_tile()
    apply_tiles(z_ref, u_ref, y_ref, porosity_ref[...])
    sums = {}
    curvature = None
    for a in range(NODES):
        for b in range(NODES):
            value = u_ref[a, b]
            add_to(sums, (class_of(a), class_of(b)), value)
            term = value * z_ref[a, b]
            curvature = term if curvature is None else curvature + term
    tiles = class_tiles(sums) + [inner, curvature]
    tile_ref[...] = summed_row(counts, tiles, side_x, side_y)
    sum_column(u_ref)
    send_layers(u_ref, side_x, side_y, sy_first, sy_second, fx_first, fx_second)


def second_apply_kernel(
    counts, part_ref, ry_first, ry_second, rx_first, rx_second, sum_ref, lift_ref, porosity_ref,
    r_ref, q_ref, z_ref, z1_ref, u_ref, sy_first, sy_second, fx_first, fx_second, stats_ref, y_ref,
):
    side_x, side_y = Sides("gx", counts[0]), Sides("gy", counts[1])
    summed = row_of(counts, sum_ref)
    field = lifted_rows(counts, summed, lift_ref)
    step = row_value(counts, summed, 0) / row_value(counts, summed, 1)
    w = collect_parts(part_ref, ry_first, ry_second, rx_first, rx_second, side_x, side_y, field)
    inner = None
    for (a, b), value in w.items():
        next_z = z_ref[a, b] - step * value
        next_r = r_ref[a, b] - step * q_ref[a, b]
        z1_ref[a, b] = next_z
        term = scaled(next_z * next_r, axis_factor(a, side_x), axis_factor(b, side_y))
        inner = term if inner is None else inner + term
    inner = inner * multiplicity_tile()
    apply_tiles(z1_ref, u_ref, y_ref, porosity_ref[...])
    own = None
    cross = None
    for a in range(NODES):
        for b in range(NODES):
            value = u_ref[a, b]
            own_term = value * z1_ref[a, b]
            cross_term = value * z_ref[a, b]
            own = own_term if own is None else own + own_term
            cross = cross_term if cross is None else cross + cross_term
    write_stats(stats_ref, [inner, own, cross])
    sum_column(u_ref)
    for a in range(NODES):
        low, high = u_ref[a, 0], u_ref[a, NODES - 1]
        sy_first[a] = side_y.send_first(low, high)
        sy_second[a] = side_y.send_second(low, high)
    low, high = u_ref[0], u_ref[NODES - 1]
    fx_first[...] = side_x.send_first(low, high)
    fx_second[...] = side_x.send_second(low, high)


def send_layers(u_ref, side_x, side_y, sy_first, sy_second, fx_first, fx_second):
    for a in range(NODES):
        for layer in range(2):
            low, high = u_ref[a, layer], u_ref[a, NODES - 2 + layer]
            sy_first[2 * a + layer] = side_y.send_first(low, high)
            sy_second[2 * a + layer] = side_y.send_second(low, high)
    for layer in range(2):
        low, high = u_ref[layer], u_ref[NODES - 2 + layer]
        fx_first[layer] = side_x.send_first(low, high)
        fx_second[layer] = side_x.send_second(low, high)


def early_apply_kernel(
    counts, part_ref, ry_first, ry_second, rx_first, rx_second, porosity_ref, sum_ref,
    z_ref, edge_ref, sy_first, sy_second, y_ref,
):
    side_x, side_y = Sides("gx", counts[0]), Sides("gy", counts[1])
    z = collect_parts(part_ref, ry_first, ry_second, rx_first, rx_second, side_x, side_y, None)
    for (a, b), value in z.items():
        z_ref[a, b] = value
    apply_tiles(z_ref, edge_ref, y_ref, porosity_ref[...], (0, 1, NODES - 2, NODES - 1))
    sum_column(edge_ref)
    for a in range(NODES):
        for layer in range(2):
            low, high = edge_ref[a, layer], edge_ref[a, 2 + layer]
            sy_first[2 * a + layer] = side_y.send_first(low, high)
            sy_second[2 * a + layer] = side_y.send_second(low, high)
    sy_first[2 * NODES] = sum_ref[...]


def rest_apply_kernel(
    counts, z_ref, edge_ref, porosity_ref, inner_ref, fx_first, fx_second, y_ref
):
    side_x = Sides("gx", counts[0])
    apply_tiles(z_ref, inner_ref, y_ref, porosity_ref[...], range(2, NODES - 2))
    sum_column(inner_ref)
    for layer in range(2):
        for b in range(NODES):
            low = layer_of(edge_ref, inner_ref, layer, b)
            high = layer_of(edge_ref, inner_ref, NODES - 2 + layer, b)
            fx_first[layer, b] = side_x.send_first(low, high)
            fx_second[layer, b] = side_x.send_second(low, high)


def first_sums_kernel(counts, r_ref, q_ref, schwarz_ref, field_ref, row_ref):
    side_x, side_y = Sides("gx", counts[0]), Sides("gy", counts[1])
    inner = curvature = None
    for a in range(NODES):
        for b in range(NODES):
            node_class = 3 * class_of(a) + class_of(b)
            z = schwarz_ref[a, b] + field_ref[node_class : node_class + 1, :]
            factors = (axis_factor(a, side_x), axis_factor(b, side_y))
            first, second = (scaled(z * ref[a, b], *factors) for ref in (r_ref, q_ref))
            inner = first if inner is None else inner + first
            curvature = second if curvature is None else curvature + second
    tile = multiplicity_tile()
    tiles = shared_class_tiles(q_ref, side_x, side_y) + [inner * tile, curvature * tile]
    row_ref[...] = summed_row(counts, tiles, side_x, side_y)


def late_apply_kernel(
    counts, part_ref, ry_first, ry_second, rx_first, rx_second, porosity_ref, low_ref, own_ref,
    high_ref, q_ref, first_ref, w_ref, u_ref, sy_first, sy_second, fx_first, fx_second, stats_ref,
    y_ref,
):
    side_x, side_y = Sides("gx", counts[0]), Sides("gy", counts[1])
    w = collect_parts(part_ref, ry_first, ry_second, rx_first, rx_second, side_x, side_y, None)
    inner = None
    for (a, b), value in w.items():
        w_ref[a, b] = value
        term = scaled(value * q_ref[a, b], axis_factor(a, side_x), axis_factor(b, side_y))
        inner = term if inner is None else inner + term
    inner = inner * multiplicity_tile()
    porosity = porosity_ref[...]
    apply_tiles(w_ref, u_ref, y_ref, porosity)
    sums = {}
    own = None
    for a in range(NODES):
        for b in range(NODES):
            value = u_ref[a, b]
            add_to(sums, (class_of(a), class_of(b)), value)
            term = value * w_ref[a, b]
            own = term if own is None else own + term
    total = counts[0] * counts[1]
    tiles = class_tiles(sums) + [inner, own, porosity]
    row = first_ref[0:1] + pltpu.roll(
        summed_row(counts, tiles, side_x, side_y), total + 2, 1
    )[0:1]
    for index in range(stats_ref.shape[0]):
        stats_ref[index] = jnp.broadcast_to(row, stats_ref.shape[1:])
    sum_column(u_ref)
    near = [[ref[y + 1 : y + 2] for y in range(3)] for ref in (low_ref, own_ref, high_ref)]
    send_corners(
        u_ref, w_ref, y_ref, near, side_x, side_y, sy_first, sy_second, fx_first, fx_second
    )


def sum_tile(tile):
    row = lax.broadcasted_iota(jnp.int32, (NODES, 128), 0)
    below = jnp.where(row == 0, pltpu.roll(shift_up(tile), 1, 0), 0.0)
    above = jnp.where(row == NODES - 1, pltpu.roll(shift_down(tile), NODES - 1, 0), 0.0)
    return tile + below + above


def send_corners(
    u_ref, w_ref, y_ref, near, side_x, side_y, sy_first, sy_second, fx_first, fx_second
):
    ends = (0, NODES - 1)

    def along_x(end, b):
        return combine(STIFF[end] * WEIGHTS[b], [y_ref[a, b] for a in range(NODES)])

    def along_y(end, a):
        return combine(STIFF[end] * WEIGHTS[a], [y_ref[a, b] for b in range(NODES)])

    for a in range(NODES):
        low, high = u_ref[a, 0], u_ref[a, NODES - 1]
        sy_first[a] = side_y.send_first(low, high)
        sy_second[a] = side_y.send_second(low, high)
        low, high = u_ref[0, a], u_ref[NODES - 1, a]
        fx_first[a] = side_x.send_first(low, high)
        fx_second[a] = side_x.send_second(low, high)
    for place, node in enumerate(ends):
        low, high = (sum_tile(near[2 * place][1] * along_y(end, node)) for end in ends)
        sy_first[NODES + place] = side_y.send_first(low, high)
        sy_second[NODES + place] = side_y.send_second(low, high)
        low, high = (sum_tile(near[1][2 * place] * along_x(end, node)) for end in ends)
        fx_first[NODES + place] = side_x.send_first(low, high)
        fx_second[NODES + place] = side_x.send_second(low, high)
    weight = float(WEIGHTS[0] * WEIGHTS[0])
    for i, a in enumerate(ends):
        for j, b in enumerate(ends):
            porosity = near[2 * i][2 * j]
            value = w_ref[a, b]
            third = None
            for shift in range(NODES):
                turned = value if shift == 0 else pltpu.roll(value, shift, 0)
                term = turned * row_tile([STIFF[k, (k - shift) % NODES] for k in range(NODES)])
                third = term if third is None else third + term
            mass = jnp.where(porosity > 0.0, shift_mass * y_ref[a, b], 0.0)
            u_ref[a, b] = u_ref[a, b] + weight * sum_tile(porosity * third + mass)


def prepare_late_kernel(counts, sol_ref, r_ref, schwarz_ref, field_ref, z_ref, sol_out, r_out):
    for a in range(NODES):
        for b in range(NODES):
            node_class = 3 * class_of(a) + class_of(b)
            z_ref[a, b] = schwarz_ref[a, b] + field_ref[node_class : node_class + 1, :]
            sol_out[a, b] = sol_ref[a, b]
            r_out[a, b] = r_ref[a, b]


def porosity_kernel(counts, low_ref, own_ref, high_ref, out_ref):
    row = lax.broadcasted_iota(jnp.int32, (NODES, 128), 0)
    weights = row_tile(WEIGHTS)
    mass = shift_mass * weights / multiplicity_tile()
    end = float(WEIGHTS[0])
    for x, ref in enumerate((low_ref, own_ref, high_ref)):
        for y in range(3):
            porosity = ref[y + 1 : y + 2]
            tile = porosity * weights
            tile = tile + jnp.where(row == 0, end * shift_up(porosity), 0.0)
            tile = tile + jnp.where(row == NODES - 1, end * shift_down(porosity), 0.0)
            out_ref[3 * x + y] = tile
            out_ref[9 + 3 * x + y] = jnp.where(porosity > 0.0, mass, 0.0)


CLASS_STIFF = np.stack(
    [STIFF[:, 0], STIFF[:, 1 : NODES - 1].sum(axis=1), STIFF[:, NODES - 1]], axis=1
)
CLASS_ENDS = np.stack(
    [CLASS_STIFF[0], CLASS_STIFF[1 : NODES - 1].sum(axis=0), CLASS_STIFF[NODES - 1]]
)
CLASS_WEIGHTS = np.array([WEIGHTS[0], WEIGHTS[1 : NODES - 1].sum(), WEIGHTS[NODES - 1]])


def combine(coefficients, values):
    total = None
    for coefficient, value in zip(coefficients, values):
        term = value * float(coefficient)
        total = term if total is None else total + term
    return total


def sharing(node):
    return {
        -1: [(0, NODES - 2)], 0: [(1, 0), (0, NODES - 1)],
        NODES - 1: [(1, NODES - 1), (2, 0)], NODES: [(2, 1)],
    }.get(node, [(1, node)])


class LiftedImage:
    def __init__(self, fields, columns_ref):
        self.fields, self.columns, self.known = fields, columns_ref, {}

    def along(self, column, place, other_class, axis):
        key = (column, place, other_class, axis)
        if key not in self.known:
            field = self.fields[column]
            line = [
                field[i][other_class] if axis == 0 else field[other_class][i] for i in range(3)
            ]
            self.known[key] = combine(CLASS_STIFF[place], line)
        return self.known[key]

    def at(self, a, b):
        total = None
        for i, place_a in sharing(a):
            for j, place_b in sharing(b):
                class_a, class_b = class_of(place_a), class_of(place_b)
                stiff = self.along((i, j), place_a, class_b, 0) * float(WEIGHTS[place_b])
                stiff = stiff + self.along((i, j), place_b, class_a, 1) * float(WEIGHTS[place_a])
                mass = self.fields[(i, j)][class_a][class_b]
                mass = mass * float(WEIGHTS[place_a] * WEIGHTS[place_b])
                term = stiff * self.columns[3 * i + j] + mass * self.columns[9 + 3 * i + j]
                total = term if total is None else total + term
        return total


def near_fields(counts, table_ref, side_x, side_y):
    total = counts[0] * counts[1]

    def field_of(step_x, step_y):
        x = jnp.clip(side_x.index + step_x, 0, counts[0] - 1)
        y = jnp.clip(side_y.index + step_y, 0, counts[1] - 1)
        place = x * counts[1] + y
        return [
            [table_ref[pl.ds((3 * i + j) * total + place, 1), :] for j in range(3)]
            for i in range(3)
        ]

    return {(i, j): field_of(i - 1, j - 1) for i in range(3) for j in range(3)}


def lifted_energy(counts, table_ref, porosity_sums, length):
    total = counts[0] * counts[1]
    field = [
        [table_ref[pl.ds((3 * i + j) * total, total), :] for j in range(3)] for i in range(3)
    ]

    def line(values):
        terms = []
        for i, j in ((0, 1), (0, 2), (1, 2)):
            difference = values[i] - values[j]
            terms.append(difference * difference * float(-CLASS_ENDS[i, j]))
        return terms[0] + terms[1] + terms[2]

    stiff = None
    mass = None
    for i in range(3):
        term = line(field[i]) * float(CLASS_WEIGHTS[i])
        term = term + line([field[j][i] for j in range(3)]) * float(CLASS_WEIGHTS[i])
        stiff = term if stiff is None else stiff + term
        for j in range(3):
            term = field[i][j] * field[i][j] * float(CLASS_WEIGHTS[i] * CLASS_WEIGHTS[j])
            mass = term if mass is None else mass + term
    energy = stiff * porosity_sums * 2.0 + mass * (shift_mass * 2.0 * length)
    return jnp.sum(energy, axis=0, keepdims=True)


def late_final_kernel(
    counts, sol_ref, r_ref, q_ref, z_ref, w_ref, u_ref, ry_first, ry_second, rx_first, rx_second,
    columns_ref, lift_ref, stats_ref, sol_out, r_out, d_out, steps_out, table_ref,
):
    side_x, side_y = Sides("gx", counts[0]), Sides("gy", counts[1])
    total = counts[0] * counts[1]
    stats = stats_ref[:, 0, :]
    summed = jnp.sum(stats, axis=0, keepdims=True)
    table_ref[...] = jnp.broadcast_to(
        jnp.sum(lift_ref[...] * summed, axis=1, keepdims=True), table_ref.shape
    )
    column = lax.broadcasted_iota(jnp.int32, (total, 128), 0)
    lane = lax.broadcasted_iota(jnp.int32, (total, 128), 1)
    at = 2 * total + 2
    porosity_sums = jnp.sum(
        jnp.where(lane == at + 2, stats, 0.0), axis=1, keepdims=True
    )
    coarse = table_ref[pl.ds(4 * total, total), :]

    def product(first):
        chosen = jnp.where(lane == column + first, coarse * summed, 0.0)
        return jnp.sum(jnp.sum(chosen, axis=0, keepdims=True), axis=1, keepdims=True)

    def value(index):
        return jnp.sum(jnp.where(lane[0:1] == index, summed, 0.0), axis=1, keepdims=True)

    first_inner, first_curvature = value(total), value(total + 1)
    cross = value(at) + product(0)
    energy = value(at + 1) + 2.0 * product(total + 2) + lifted_energy(
        counts, table_ref, porosity_sums, sol_ref.shape[-1]
    )
    first_step = first_inner / first_curvature
    second_inner = first_step * first_step * cross - first_inner
    ratio = second_inner / first_inner
    mixed = first_curvature - first_step * cross
    own = first_curvature - 2.0 * first_step * cross + first_step * first_step * energy
    second_step = second_inner / (own + ratio * (2.0 * mixed + ratio * first_curvature))
    first_step, second_step, ratio = (
        jnp.broadcast_to(scalar[:, 0:1], (1, 128)) for scalar in (first_step, second_step, ratio)
    )
    steps_out[0] = first_step[0, 0]
    steps_out[1] = second_step[0, 0]

    fields = near_fields(counts, table_ref, side_x, side_y)
    lifted_image = LiftedImage(fields, columns_ref)
    low_x = side_x.low(rx_first[...], rx_second[...])
    high_x = side_x.high(rx_first[...], rx_second[...])
    corner_y = {}
    for place in range(2):
        tiles = ry_first[NODES + place], ry_second[NODES + place]
        corner_y[(place > 0, False)] = side_y.low(*tiles)
        corner_y[(place > 0, True)] = side_y.high(*tiles)
    for a in range(NODES):
        for b in range(NODES):
            image = u_ref[a, b]
            if b == 0:
                image = image + side_y.low(ry_first[a], ry_second[a])
            if b == NODES - 1:
                image = image + side_y.high(ry_first[a], ry_second[a])
            if a == 0:
                image = image + low_x[b]
            if a == NODES - 1:
                image = image + high_x[b]
            if a in (0, NODES - 1) and b in (0, NODES - 1):
                from_x = low_x if a == 0 else high_x
                image = image + from_x[NODES + (b > 0)] + corner_y[(a > 0, b > 0)]
            lifted = fields[(1, 1)][class_of(a)][class_of(b)]
            image = image + lifted_image.at(a, b)
            z, q = z_ref[a, b], q_ref[a, b]
            direction = z - first_step * (w_ref[a, b] + lifted) + ratio * z
            image = q - first_step * image + ratio * q
            d_out[a, b] = direction
            sol_out[a, b] = sol_ref[a, b] + first_step * z + second_step * direction
            r_out[a, b] = r_ref[a, b] - first_step * q - second_step * image


def prepare_kernel(counts, sol_ref, r_ref, q_ref, z_ref, sum_ref, sol_out, r_out):
    summed = row_of(counts, sum_ref)
    step = row_value(counts, summed, 0) / row_value(counts, summed, 1)
    for a in range(NODES):
        for b in range(NODES):
            sol_out[a, b] = sol_ref[a, b] + step * z_ref[a, b]
            r_out[a, b] = r_ref[a, b] - step * q_ref[a, b]


def final_kernel(
    counts, sol_ref, r_ref, q_ref, z_ref, z1_ref, u_ref, ry_first, ry_second, rx_first, rx_second,
    sum_ref, last_ref, sol_out, r_out, d_out, steps_out,
):
    side_x, side_y = Sides("gx", counts[0]), Sides("gy", counts[1])
    summed = row_of(counts, sum_ref)
    first_inner, first_curvature = row_value(counts, summed, 0), row_value(counts, summed, 1)
    second_inner, own, cross = stat_columns(last_ref[:, 0, :], 0, 3)
    first_step = first_inner / first_curvature
    ratio = second_inner / first_inner
    second_step = second_inner / (own + ratio * (2.0 * cross + ratio * first_curvature))
    steps_out[0] = first_step[0, 0]
    steps_out[1] = second_step[0, 0]
    low_x = side_x.low(rx_first[...], rx_second[...])
    high_x = side_x.high(rx_first[...], rx_second[...])
    for a in range(NODES):
        for b in range(NODES):
            image = u_ref[a, b]
            if b == 0:
                image = image + side_y.low(ry_first[a], ry_second[a])
            if b == NODES - 1:
                image = image + side_y.high(ry_first[a], ry_second[a])
            if a == 0:
                image = image + low_x[b]
            if a == NODES - 1:
                image = image + high_x[b]
            z, q = z_ref[a, b], q_ref[a, b]
            direction = z1_ref[a, b] + ratio * z
            image = image + ratio * q
            d_out[a, b] = direction
            sol_out[a, b] = sol_ref[a, b] + second_step * direction
            r_out[a, b] = r_ref[a, b] - second_step * image


COSTS = {
    "start": 100, "first_solve": 900, "second_solve": 900, "rest_of_solve": 600,
    "first_apply": 500, "rest_of_apply": 400, "second_apply": 800, "prepare": 20000,
    "final": 500, "late_apply": 800, "first_sums": 300, "porosity": 20000, "late_final": 800,
}


def call(kernel, counts, name, shapes, scratch, *operands):
    def body(*refs):
        kernel(counts, *refs)

    def space(shape):
        return pltpu.SMEM if len(shape) == 1 else pltpu.VMEM

    return pl.pallas_call(
        body,
        name=name,
        out_shape=[jax.ShapeDtypeStruct(shape, jnp.float32) for shape in shapes],
        in_specs=[pl.BlockSpec(memory_space=pltpu.VMEM)] * len(operands),
        out_specs=[pl.BlockSpec(memory_space=space(shape)) for shape in shapes],
        scratch_shapes=[pltpu.VMEM(shape, jnp.float32) for shape in scratch],
        compiler_params=pltpu.CompilerParams(vmem_limit_bytes=24 * 1024 * 1024),
        cost_estimate=pl.CostEstimate(
            flops=COSTS[name] * 1000000, bytes_accessed=COSTS[name] * 3000, transcendentals=0
        ),
    )(*operands)


def swap_pairs(counts, axis, parity, ring):
    count_x, count_y = counts
    pairs = []
    for x in range(count_x):
        for y in range(count_y):
            if axis == 0:
                other = x + 1 if x % 2 == parity else x - 1
                to = (other % count_x, y) if ring or 0 <= other < count_x else (x, y ^ 1)
            else:
                other = y + 1 if y % 2 == parity else y - 1
                to = (x, other) if 0 <= other < count_y else (x ^ 1, y)
            pairs.append((x * count_y + y, to[0] * count_y + to[1]))
    return pairs


def trade(counts, axis, first, second, ring=False):
    return (
        lax.ppermute(first, AXES, swap_pairs(counts, axis, 0, ring)),
        lax.ppermute(second, AXES, swap_pairs(counts, axis, 1, ring)),
    )


def trade_far(counts, value, far_x, far_y):
    pairs = [
        (x * counts[1] + y, (x ^ far_x) * counts[1] + (y ^ far_y))
        for x in range(counts[0])
        for y in range(counts[1])
    ]
    return lax.ppermute(value, AXES, pairs)


class RunningSum:
    def __init__(self, counts, tile, carried):
        self.counts = counts
        self.carried = carried
        self.value = tile if self.carried else lax.psum(tile, AXES)

    def add(self, received):
        if self.carried:
            self.value = self.value + received

    def far(self, *steps):
        return [trade_far(self.counts, self.value, *step) for step in steps if self.carried]


def carry(tiles, running):
    return jnp.concatenate([tiles.reshape((-1, NODES, 128)), running.value[None]])


def carried(received, shape):
    return received[:-1].reshape(shape), received[-1]


def gather_stats(stats):
    return lax.all_to_all(stats, AXES, 0, 0)


def lift_tables(counts, column_length):
    share_x, share_y = share_table(counts[0]), share_table(counts[1])
    basis_x, eigen_x = cosine_inverse(counts[0])
    basis_y, eigen_y = cosine_inverse(counts[1])
    divisor = (
        2.0 * mean_porosity * column_length * (eigen_x[:, None] + eigen_y[None, :])
        + 8.0 * shift_mass * column_length
    )
    modes_x = np.einsum("xip,pa->xia", share_x, basis_x)
    modes_y = np.einsum("yjq,qb->yjb", share_y, basis_y)
    total = counts[0] * counts[1]
    to_modes = np.einsum("pa,qb->abpq", basis_x, basis_y).reshape(total, total)
    to_modes = np.pad(to_modes, ((0, 0), (0, sum_lanes(counts) - total)))
    return [table.astype(np.float32) for table in (modes_x, modes_y, 1.0 / divisor, to_modes)]


def all_lift(counts, column_length):
    modes_x, modes_y, inverse, to_modes = lift_tables(counts, column_length)
    total = counts[0] * counts[1]
    lift = np.einsum(
        "xia,yjb,ab,abl->ijxyl", *(
            table.astype(np.float64)
            for table in (modes_x, modes_y, inverse, to_modes.reshape(inverse.shape + (-1,)))
        ),
    )
    return jnp.asarray(lift.reshape(9 * total, -1).astype(np.float32))


def own_lift(tables):
    modes_x, modes_y, inverse, to_modes = [jnp.asarray(table) for table in tables]
    own_x = lax.dynamic_index_in_dim(modes_x, lax.axis_index("gx"), 0, keepdims=False)
    own_y = lax.dynamic_index_in_dim(modes_y, lax.axis_index("gy"), 0, keepdims=False)
    own = own_x[:, None, :, None] * own_y[None, :, None, :] * inverse[None, None]
    lift = jnp.dot(own.reshape(9, -1), to_modes, precision=exact_mode)
    return jnp.pad(lift, ((0, 7), (0, 0)))


def shards_of(counts):
    forward_np, back_edge_np, back_inner_np, inverse_np = plane_tables()

    def shards(solution, residual, grain_counts):
        shard_shape = solution.shape
        block = shard_shape[2:]
        solution = solution.reshape(block)
        residual = residual.reshape(block)
        lift = own_lift(lift_tables(counts, block[-1]))
        late = counts == (8, 4)
        every_lift = all_lift(counts, block[-1]) if late else None
        porosity = 1.0 - 0.6 * grain_counts.reshape(1, 128).astype(jnp.float32) / MOST_GRAINS
        plane = [jnp.asarray(table) for table in (forward_np, back_edge_np, inverse_np)]
        back_inner = jnp.asarray(back_inner_np)
        side_x, side_y = Sides("gx", counts[0]), Sides("gy", counts[1])
        row = (counts[0] * counts[1], 4, 128)
        face = (NODES, NODES, 128)
        sends = [(2 * EXT, NODES, 128)] * 2
        solve_shapes = [(MODES, EXT * 128), (EXT, 2 * NODES, 128)]
        solve_scratch = [(EXT, ROWS, 128), (EXT, len(back_edge_np), 128)]

        def rest_of_solve(spectrum, edges):
            return call(
                rest_kernel, counts, "rest_of_solve",
                [(EXT, NODES * NODES, 128)] + [(2, NODES, NODES, 128)] * 2,
                [(EXT, len(back_inner_np), 128)], spectrum, edges, back_inner,
            )

        y_first, y_second = call(
            start_kernel, counts, "start", [(NODES + 1,) + face[1:], face], [], residual
        )
        running = RunningSum(counts, y_first[-1], late)
        ry = trade(counts, 1, y_first, y_second)
        ry_first, tile = carried(ry[0], face)
        running.add(tile)
        ry = (ry_first, ry[1])
        low_y, high_y = side_y.low(*ry), side_y.high(*ry)

        def with_layers(index):
            return jnp.concatenate([low_y[index][None], residual[index], high_y[index][None]])

        low_face, high_face = with_layers(1), with_layers(NODES - 2)
        rx = trade(
            counts, 0, carry(side_x.send_first(low_face, high_face), running),
            side_x.send_second(low_face, high_face),
        )
        rx_first, tile = carried(rx[0], low_face.shape)
        running.add(tile)
        rx = (rx_first, rx[1])
        spectrum, edges, y_first, y_second = call(
            first_solve_kernel, counts, "first_solve",
            solve_shapes + [(2 * EXT + 1, NODES, 128)] * 2, solve_scratch,
            residual, porosity, running.value, *ry, *rx, *plane,
        )
        part, *fx = rest_of_solve(spectrum, edges)

        def spread_faces(fx, ry):
            low_y, high_y = side_y.low(*ry), side_y.high(*ry)
            middle = jnp.zeros((2, NODES - 4, NODES, 128), jnp.float32)
            both = [
                jnp.concatenate([low_y[at], middle, high_y[at]], axis=1)
                for at in (slice(0, 2), slice(8, 10))
            ]
            return (
                fx[0] + side_x.send_first(*both),
                fx[1] + side_x.send_second(*both),
            )

        def trade_y(y_first, y_second, shape):
            count = math.prod(shape[:-2])
            ry = trade(counts, 1, y_first, y_second)
            faces = [value[:count].reshape(shape) for value in ry]
            return faces, [value[count:] for value in ry]

        ext_face = (EXT, 2, NODES, 128)
        two = (NODES, 2, NODES, 128)
        tiles = (-1, NODES, 128)
        ry, rows = trade_y(y_first, y_second, ext_face)
        rows = [value[0] for value in rows]
        inner_y = (side_y.index > 0) & (side_y.index < counts[1] - 1)
        three = jnp.concatenate(
            [
                running.value[0:1] + jnp.where(inner_y, rows[1][0:1], 0.0),
                side_y.low(*rows)[1:2], porosity, side_y.high(*rows)[1:2],
                jnp.zeros((NODES - 4, 128), jnp.float32),
            ]
        )
        first, second = (
            jnp.concatenate([faces.reshape(tiles), three[None]]) for faces in spread_faces(fx, ry)
        )
        rx = trade(counts, 0, first, second, ring=True)
        count = 2 * NODES
        threes = [value[count] for value in rx]
        rx = [value[:count].reshape((2, NODES, NODES, 128)) for value in rx]
        if late:
            running.value = three + threes[1]
        if late:
            half = (NODES, NODES // 2, NODES, 128)
            z, u_edge, y_first, y_second = call(
                early_apply_kernel, counts, "first_apply",
                [block, half, (2 * NODES + 1, NODES, 128), (2 * NODES, NODES, 128)], [block],
                part, *ry, *rx, porosity, running.value,
            )
            u_inner, *fx = call(
                rest_apply_kernel, counts, "rest_of_apply",
                [half, (2, NODES, NODES, 128), (2, NODES, NODES, 128)], [block],
                z, u_edge, porosity,
            )
        else:
            z, u, y_first, y_second, *fx, tile = call(
                first_apply_kernel, counts, "first_apply",
                [block, block, (2 * NODES, NODES, 128), (2 * NODES, NODES, 128),
                 (2, NODES, NODES, 128), (2, NODES, NODES, 128), (NODES, 128)],
                [block],
                part, *ry, *rx, running.value, lift, porosity, residual,
            )
            u_edge = jnp.concatenate([u[:, :2], u[:, -2:]], axis=1)
            u_inner = u[:, 2:-2]
        ry, rows = trade_y(y_first, y_second, two)
        if late:
            running.value = jnp.where(inner_y, running.value, rows[0][0])
        low_y, high_y = side_y.low(*ry), side_y.high(*ry)

        def image_faces(index):
            middle = jnp.zeros((2, NODES - 2, NODES, 128), jnp.float32)
            return jnp.concatenate([low_y[index], middle, high_y[index]], axis=1)

        pads = ((0, 0), (1, 1), (0, 0), (0, 0))
        both = (image_faces(slice(0, 2)), image_faces(slice(NODES - 2, NODES)))
        rx = trade(
            counts, 0,
            jnp.pad(fx[0], pads) + side_x.send_first(*both),
            jnp.pad(fx[1], pads) + side_x.send_second(*both),
        )
        if late:
            near = (side_x.low(*threes), three, side_x.high(*threes))
            (columns,) = call(porosity_kernel, counts, "porosity", [(18, NODES, 128)], [], *near)
            rx, far, columns = lax.optimization_barrier((rx, running.far((4, 0)), columns))
            for value in far:
                running.add(value)
            table = (9 * counts[0] * counts[1], 128)
            q, spectrum, edges, y_first, y_second, field = call(
                late_solve_kernel, counts, "second_solve",
                [block] + solve_shapes + sends + [(16, 128)], solve_scratch + [table],
                u_edge, u_inner, *ry, *rx, columns, every_lift, running.value, *plane,
            )
        else:
            q, spectrum, edges, y_first, y_second = call(
                second_solve_kernel, counts, "second_solve", [block] + solve_shapes + sends,
                solve_scratch, u_edge, u_inner, *ry, *rx, *plane,
            )
        part, *fx = rest_of_solve(spectrum, edges)
        ry, _ = trade_y(y_first, y_second, ext_face)
        if late:
            (first_row,) = call(
                first_sums_kernel, counts, "first_sums", [(NODES, 128)], [],
                residual, q, z, field,
            )
            ry, first_row = lax.optimization_barrier((ry, first_row))
        rx = trade(counts, 0, *spread_faces(fx, ry))

        def trade_edges(y_first, y_second, fx, beside):
            ry, beside = lax.optimization_barrier((trade(counts, 1, y_first, y_second), beside))
            low_y, high_y = side_y.low(*ry), side_y.high(*ry)

            def edge_rows(index):
                middle = jnp.zeros((NODES - 2, NODES, 128), jnp.float32)
                return jnp.concatenate([low_y[index][None], middle, high_y[index][None]])

            both = (edge_rows(0), edge_rows(NODES - 1))
            rx = trade(
                counts, 0, fx[0] + side_x.send_first(*both), fx[1] + side_x.send_second(*both)
            )
            return ry, rx, beside

        if late:
            w, u, y_first, y_second, *fx, stats = call(
                late_apply_kernel, counts, "late_apply",
                [block, block] + [(NODES + 2, NODES, 128)] * 4 + [row], [block],
                part, *ry, *rx, porosity, *near, q, first_row,
            )
            z, w = lax.optimization_barrier((z, w))
            nexts = call(
                prepare_late_kernel, counts, "prepare", [block] * 3, [],
                solution, residual, z, field,
            )
            ry, rx, (z, solution, residual) = lax.optimization_barrier(
                (trade(counts, 1, y_first, y_second), trade(counts, 0, *fx), nexts)
            )
            solution_out, residual_out, direction, steps = call(
                late_final_kernel, counts, "late_final", [block] * 3 + [(2,)], [table],
                solution, residual, q, z, w, u, *ry, *rx, columns, every_lift,
                gather_stats(stats),
            )
        else:
            summed = lax.psum(tile, AXES)
            z1, u, y_first, y_second, *fx, stats = call(
                second_apply_kernel, counts, "second_apply",
                [block, block, face, face, face, face, row], [block],
                part, *ry, *rx, summed, lift, porosity, residual, q, z,
            )
            nexts = call(
                prepare_kernel, counts, "prepare", [block] * 2, [],
                solution, residual, q, z, summed,
            )
            ry, rx, nexts = trade_edges(y_first, y_second, fx, nexts)
            solution_out, residual_out, direction, steps = call(
                final_kernel, counts, "final", [block] * 3 + [(2,)], [],
                *nexts, q, z, z1, u, *ry, *rx, summed, gather_stats(stats),
            )
        return (
            solution_out.reshape(shard_shape),
            residual_out.reshape(shard_shape),
            direction.reshape(shard_shape),
            steps,
        )

    return shards


def solution(mesh):
    counts = (mesh.shape["gx"], mesh.shape["gy"])
    return jax.shard_map(
        shards_of(counts),
        mesh=mesh,
        in_specs=(
            P("gx", "gy", None, None, None, None),
            P("gx", "gy", None, None, None, None),
            P("gx", "gy", None),
        ),
        out_specs=(
            P("gx", "gy", None, None, None, None),
            P("gx", "gy", None, None, None, None),
            P("gx", "gy", None, None, None, None),
            P(),
        ),
        check_vma=False,
    )
```

```python
import math

import jax
import jax.numpy as jnp
import numpy as np
from jax import lax
from jax.experimental import pallas as pl
from jax.experimental.pallas import tpu as pltpu
from jax.sharding import PartitionSpec as P

NODES = 8
MOST_GRAINS = 16
EXT = NODES + 2
ROWS = 112
MODES = 104
AXES = ("gx", "gy")
EDGE = (0, 1, EXT - 2, EXT - 1)
INNER = tuple(range(2, EXT - 2))

shift_mass = 0.1
mean_porosity = 0.7
exact_mode = lax.Precision.HIGHEST
plane_mode = lax.Precision.HIGH


def legendre_columns(node_set, degree):
    table = [node_set * 0.0 + 1.0, node_set]
    for order in range(2, degree + 1):
        table.append(
            ((2 * order - 1) * node_set * table[order - 1] - (order - 1) * table[order - 2]) / order
        )
    return table


def gll_tables():
    degree = NODES - 1
    node_set = np.cos(math.pi * np.arange(degree + 1) / degree)
    for sweep in range(100):
        table = legendre_columns(node_set, degree)
        node_set = node_set - (node_set * table[degree] - table[degree - 1]) / (
            (degree + 1) * table[degree]
        )
    node_set = node_set[::-1].copy()
    values = legendre_columns(node_set, degree)[degree]
    weights = 2.0 / (degree * (degree + 1) * values**2)
    derivative = np.zeros((NODES, NODES))
    for row_index in range(NODES):
        for column_index in range(NODES):
            if row_index != column_index:
                derivative[row_index, column_index] = values[row_index] / (
                    values[column_index] * (node_set[row_index] - node_set[column_index])
                )
    derivative[0, 0] = -degree * (degree + 1) / 4.0
    derivative[NODES - 1, NODES - 1] = degree * (degree + 1) / 4.0
    return (weights, derivative)


def jacobi_eigen(matrix):
    size_now = matrix.shape[0]
    current = matrix.copy()
    vectors = np.eye(size_now)
    for sweep in range(12):
        for first in range(size_now - 1):
            for second in range(first + 1, size_now):
                off_value = current[first, second]
                safe_value = np.where(off_value == 0.0, 1e-300, off_value)
                theta = (current[second, second] - current[first, first]) / (2.0 * safe_value)
                sign_value = np.where(theta >= 0.0, 1.0, -1.0)
                tangent = sign_value / (np.abs(theta) + np.sqrt(theta * theta + 1.0))
                cosine = 1.0 / np.sqrt(tangent * tangent + 1.0)
                sine = tangent * cosine
                rotation = np.eye(size_now)
                rotation[first, first] = cosine
                rotation[second, second] = cosine
                rotation[first, second] = sine
                rotation[second, first] = -sine
                current = rotation.T @ current @ rotation
                vectors = vectors @ rotation
    eigen_values = np.array([current[index, index] for index in range(size_now)])
    return (eigen_values, vectors)


def schwarz_tables():
    weights, derivative = gll_tables()
    stiffness = derivative.T @ (weights[:, None] * derivative)
    total_nodes = 3 * (NODES - 1) + 1
    three_stiffness = np.zeros((total_nodes, total_nodes))
    three_mass = np.zeros(total_nodes)
    for element in range(3):
        start_node = element * (NODES - 1)
        three_stiffness[
            start_node : start_node + NODES, start_node : start_node + NODES
        ] += stiffness
        three_mass[start_node : start_node + NODES] += weights
    chosen = np.array([NODES - 2] + list(range(NODES - 1, 2 * NODES - 1)) + [2 * NODES - 1])
    local_stiffness = three_stiffness[chosen][:, chosen]
    local_mass = three_mass[chosen]
    scaling = 1.0 / np.sqrt(local_mass)
    symmetric = scaling[:, None] * local_stiffness * scaling[None, :]
    symmetric = 0.5 * (symmetric + symmetric.T)
    eigen_values, eigen_vectors = jacobi_eigen(symmetric)
    return (scaling[:, None] * eigen_vectors, eigen_values)


WEIGHTS, DERIVATIVE = gll_tables()
STIFF = DERIVATIVE.T @ (WEIGHTS[:, None] * DERIVATIVE)
BASIS, EIGEN = schwarz_tables()
PARITY = {
    sign: [mode for mode in range(EXT) if BASIS[0, mode] * BASIS[EXT - 1, mode] * sign > 0]
    for sign in (1, -1)
}


def plane_tables():
    forward = np.zeros((MODES, ROWS))
    inverse = np.zeros((MODES, EXT))
    for mode_b in range(EXT):
        for mode_c in range(EXT):
            mode = mode_b * EXT + mode_c
            for b in range(EXT):
                for k in range(NODES):
                    forward[mode, b * NODES + k] = BASIS[b, mode_b] * BASIS[k + 1, mode_c]
                forward[mode, 80 + b] = BASIS[b, mode_b] * BASIS[0, mode_c]
                forward[mode, 96 + b] = BASIS[b, mode_b] * BASIS[EXT - 1, mode_c]
            inverse[mode] = 1.0 / (
                mean_porosity * (EIGEN + EIGEN[mode_b] + EIGEN[mode_c]) + shift_mass
            )
    lanes = np.repeat(inverse.T[:, :, None], 128, axis=2)
    back = forward.T
    tables = [
        np.concatenate([back[[8 * b + k for b in layers for k in range(NODES)]]]
                       + [pad_rows(back[[at + b for b in layers]], 8) for at in (80, 96)])
        for layers in (EDGE, INNER)
    ]
    return tuple(table.astype(np.float32) for table in (forward, *tables, lanes))


def pad_rows(table, count):
    return np.pad(table, ((0, -len(table) % count), (0, 0)))


def row_tile(values):
    row = lax.broadcasted_iota(jnp.int32, (NODES, 128), 0)
    tile = jnp.full((NODES, 128), float(values[0]), jnp.float32)
    for k in range(1, NODES):
        tile = jnp.where(row == k, float(values[k]), tile)
    return tile


def share_table(count):
    table = np.zeros((count, 3, count))
    for column in range(count):
        table[column, :, column] = 1.0
        if column > 0:
            table[column, 0, column] = 0.5
            table[column, 0, column - 1] = 0.5
        if column < count - 1:
            table[column, 2, column] = 0.5
            table[column, 2, column + 1] = 0.5
    return table


def cosine_inverse(count):
    position = np.arange(count)
    basis = np.cos(math.pi * (position[:, None] + 0.5) * position[None, :] / count)
    basis = basis * np.where(position == 0, math.sqrt(1.0 / count), math.sqrt(2.0 / count))[None, :]
    return basis, 2.0 - 2.0 * np.cos(math.pi * position / count)


def shift_up(rows):
    lane = lax.broadcasted_iota(jnp.int32, rows.shape, 1)
    return jnp.where(lane == 0, 0.0, pltpu.roll(rows, 1, 1))


def shift_down(rows):
    lane = lax.broadcasted_iota(jnp.int32, rows.shape, 1)
    return jnp.where(lane == 127, 0.0, pltpu.roll(rows, 127, 1))


class Sides:
    def __init__(self, axis, count):
        self.index = lax.axis_index(axis)
        self.even = lax.rem(self.index, 2) == 0
        self.no_low = self.index == 0
        self.no_high = self.index == count - 1

    def low(self, first, second):
        return jnp.where(self.no_low, 0.0, jnp.where(self.even, second, first))

    def high(self, first, second):
        return jnp.where(self.no_high, 0.0, jnp.where(self.even, first, second))

    def send_first(self, low_face, high_face):
        return jnp.where(self.even, high_face, low_face)

    def send_second(self, low_face, high_face):
        return jnp.where(self.even, low_face, high_face)


def multiplicity_tile():
    row = lax.broadcasted_iota(jnp.int32, (NODES, 128), 0)
    lane = lax.broadcasted_iota(jnp.int32, (NODES, 128), 1)
    shared = ((row == 0) & (lane > 0)) | ((row == NODES - 1) & (lane < 127))
    return jnp.where(shared, 0.5, 1.0)


def class_of(node):
    return 0 if node == 0 else (2 if node == NODES - 1 else 1)


def axis_factor(node, side):
    if node == 0:
        return jnp.where(side.no_low, 1.0, 0.5)
    if node == NODES - 1:
        return jnp.where(side.no_high, 1.0, 0.5)
    return None


def scaled(value, *factors):
    for factor in factors:
        if factor is not None:
            value = value * factor
    return value


def add_to(total, key, value):
    total[key] = value if key not in total else total[key] + value


def lane_sums(tiles):
    columns = [jnp.sum(tile, axis=0, keepdims=True) for tile in tiles]
    columns.append(jnp.zeros((16 - len(tiles), 128), jnp.float32))
    sums = jnp.sum(jnp.concatenate(columns, axis=0), axis=1, keepdims=True)
    return jnp.broadcast_to(sums, (16, 128))


def write_stats(stats_ref, tiles):
    row = lax.broadcasted_iota(jnp.int32, (16, 128), 0)
    lane = lax.broadcasted_iota(jnp.int32, (16, 128), 1)
    sums = jnp.sum(jnp.where(row == lane, lane_sums(tiles), 0.0), axis=0, keepdims=True)
    for index in range(stats_ref.shape[0]):
        stats_ref[index] = jnp.broadcast_to(sums, stats_ref.shape[1:])


def stat_columns(stats, first, count):
    lane = lax.broadcasted_iota(jnp.int32, stats.shape, 1)
    sums = lane_sums([jnp.where(lane == first + i, stats, 0.0) for i in range(count)])
    return [sums[i : i + 1] for i in range(count)]


def sum_lanes(counts):
    return -(-(counts[0] * counts[1] + 2) // 128) * 128


def share_rows(counts, side_x, side_y):
    lane = lax.broadcasted_iota(jnp.int32, (1, sum_lanes(counts)), 1)
    column_y = lax.rem(lane, counts[1])
    first_x = lane - column_y

    def weights(side, place, step, count):
        own = jnp.where(place == side.index * step, 1.0, 0.0)
        below = jnp.where(place == (side.index - 1) * step, 1.0, 0.0)
        above = jnp.where(place == (side.index + 1) * step, 1.0, 0.0)
        return (
            jnp.where(side.no_low, own, 0.5 * (own + below)),
            own,
            jnp.where(side.no_high, own, 0.5 * (own + above)),
        )

    inside = lane < counts[0] * counts[1]
    along_x = weights(side_x, first_x, counts[1], counts[0])
    along_y = weights(side_y, column_y, 1, counts[1])
    return [jnp.where(inside, wx * wy, 0.0) for wx in along_x for wy in along_y]


def summed_row(counts, tiles, side_x, side_y):
    sums = lane_sums(tiles)
    lane = lax.broadcasted_iota(jnp.int32, (1, sum_lanes(counts)), 1)
    total = None
    for i, share in enumerate(share_rows(counts, side_x, side_y)):
        term = share * sums[i : i + 1, 0:1]
        total = term if total is None else total + term
    for i in range(9, len(tiles)):
        total = total + jnp.where(lane == counts[0] * counts[1] + i - 9, sums[i : i + 1, 0:1], 0.0)
    pieces = [total[:, at : at + 128] for at in range(0, sum_lanes(counts), 128)]
    pieces.append(jnp.zeros((NODES - len(pieces), 128), jnp.float32))
    return jnp.concatenate(pieces, axis=0)


def row_of(counts, tile_ref):
    rows = [tile_ref[i : i + 1, :] for i in range(sum_lanes(counts) // 128)]
    return rows[0] if len(rows) == 1 else jnp.concatenate(rows, axis=1)


def lifted_rows(counts, row, lift_ref):
    sums = jnp.sum(lift_ref[...] * row, axis=1, keepdims=True)
    return jnp.broadcast_to(sums, (16, 128))


def row_value(counts, row, index):
    lane = lax.broadcasted_iota(jnp.int32, row.shape, 1)
    chosen = jnp.where(lane == counts[0] * counts[1] + index, row, 0.0)
    return jnp.broadcast_to(jnp.sum(chosen, axis=1, keepdims=True), (1, 128))


def class_tiles(sums):
    return [sums[(i, j)] for i in range(3) for j in range(3)]


def shared_class_tiles(field_ref, side_x, side_y):
    tile = multiplicity_tile()
    sums = {}
    for a in range(NODES):
        for b in range(NODES):
            add_to(sums, (class_of(a), class_of(b)), field_ref[a, b])
    for (i, j), value in sums.items():
        a, b = (0, 1, NODES - 1)[i], (0, 1, NODES - 1)[j]
        sums[(i, j)] = scaled(value * tile, axis_factor(a, side_x), axis_factor(b, side_y))
    return class_tiles(sums)


def start_kernel(counts, r_ref, sy_first, sy_second):
    side_x, side_y = Sides("gx", counts[0]), Sides("gy", counts[1])
    for a in range(NODES):
        low, high = r_ref[a, 1], r_ref[a, NODES - 2]
        sy_first[a] = side_y.send_first(low, high)
        sy_second[a] = side_y.send_second(low, high)
    sy_first[NODES] = summed_row(
        counts, shared_class_tiles(r_ref, side_x, side_y), side_x, side_y
    )


def planes(ref):
    return jnp.concatenate([ref[a] for a in range(EXT)], axis=1)


def to_spectrum(x_ref, forward_ref, inverse_ref):
    zero = jnp.zeros((6, 128), jnp.float32)
    for a in range(EXT):
        x_ref[a, 80:90] = shift_up(x_ref[a, pl.ds(6, EXT, stride=NODES), :])
        x_ref[a, 96:106] = shift_down(x_ref[a, pl.ds(1, EXT, stride=NODES), :])
        x_ref[a, 90:96] = zero
        x_ref[a, 106:112] = zero
    half = EXT // 2
    for block in range(ROWS // 8):
        rows = pl.ds(block * 8, 8)
        low = [x_ref[a, rows] for a in range(half)]
        high = [x_ref[EXT - 1 - a, rows] for a in range(half)]
        folded = {1: [x + y for x, y in zip(low, high)], -1: [x - y for x, y in zip(low, high)]}
        for sign in (1, -1):
            for mode in PARITY[sign]:
                total = folded[sign][0] * float(BASIS[0, mode])
                for a in range(1, half):
                    total = total + folded[sign][a] * float(BASIS[a, mode])
                x_ref[mode, rows] = total
    spectrum = jnp.dot(
        forward_ref[...], planes(x_ref), precision=plane_mode, preferred_element_type=jnp.float32
    ) * planes(inverse_ref)
    return spectrum


def from_spectrum(spectrum, back_ref, part_ref, count):
    half = EXT // 2
    values = jnp.dot(
        back_ref[...], spectrum, precision=plane_mode, preferred_element_type=jnp.float32
    )
    for block in range(part_ref.shape[1] // 8):
        rows = pl.ds(block * 8, 8)
        modes = [values[block * 8 : block * 8 + 8, m * 128 : (m + 1) * 128] for m in range(EXT)]
        back = {}
        for sign in (1, -1):
            for a in range(half):
                total = None
                for mode in PARITY[sign]:
                    term = modes[mode] * float(BASIS[a, mode])
                    total = term if total is None else total + term
                back[(sign, a)] = total
        for a in range(half):
            part_ref[a, rows] = back[(1, a)] + back[(-1, a)]
            part_ref[EXT - 1 - a, rows] = back[(1, a)] - back[(-1, a)]
    below, above = NODES * count, NODES * count + 8
    for a in range(EXT):

        def layer(k):
            return (a, pl.ds(k, count, stride=NODES), slice(None))

        bottom, top = part_ref[layer(0)], part_ref[layer(NODES - 1)]
        part_ref[layer(0)] = bottom + shift_up(top)
        part_ref[layer(NODES - 1)] = top + shift_down(bottom)
        part_ref[layer(1)] = part_ref[layer(1)] + shift_up(part_ref[a, above : above + count])
        part_ref[layer(NODES - 2)] = part_ref[layer(NODES - 2)] + shift_down(
            part_ref[a, below : below + count]
        )


def solve_edges(
    x_ref, forward_ref, back_ref, inverse_ref, spectrum_ref, edge_ref, sy_first, sy_second,
    side_y, part_ref,
):
    spectrum = to_spectrum(x_ref, forward_ref, inverse_ref)
    spectrum_ref[...] = spectrum
    from_spectrum(spectrum, back_ref, part_ref, len(EDGE))
    for a in range(EXT):
        low, high = part_ref[a, 0:16], part_ref[a, 16:32]
        sy_first[2 * a : 2 * a + 2] = side_y.send_first(low, high).reshape(2, NODES, 128)
        sy_second[2 * a : 2 * a + 2] = side_y.send_second(low, high).reshape(2, NODES, 128)
        edge_ref[a] = part_ref[a, 8:24]


def rest_kernel(
    counts, spectrum_ref, edge_ref, back_ref, part_ref, fx_first, fx_second, inner_ref
):
    side_x = Sides("gx", counts[0])
    from_spectrum(spectrum_ref[...], back_ref, inner_ref, len(INNER))
    for a in range(EXT):
        part_ref[a, 0:8] = edge_ref[a, 0:8]
        part_ref[a, 8:56] = inner_ref[a, 0:48]
        part_ref[a, 56:64] = edge_ref[a, 8:16]
    for layer in range(2):
        low, high = part_ref[layer], part_ref[NODES + layer]
        fx_first[layer] = side_x.send_first(low, high).reshape(NODES, NODES, 128)
        fx_second[layer] = side_x.send_second(low, high).reshape(NODES, NODES, 128)


def first_solve_kernel(
    counts, r_ref, porosity_ref, sum_ref, ry_first, ry_second, rx_first, rx_second, forward_ref, back_ref,
    inverse_ref, spectrum_ref, edge_ref, sy_first, sy_second, x_ref, part_ref,
):
    row = lax.broadcasted_iota(jnp.int32, (NODES, 128), 0)
    for send in (sy_first, sy_second):
        send[2 * EXT] = jnp.where(row == 0, sum_ref[...], porosity_ref[...])
    side_x, side_y = Sides("gx", counts[0]), Sides("gy", counts[1])
    x_ref[0, 0:80] = side_x.low(rx_first[...], rx_second[...]).reshape(80, 128)
    x_ref[EXT - 1, 0:80] = side_x.high(rx_first[...], rx_second[...]).reshape(80, 128)
    for a in range(NODES):
        x_ref[a + 1, 0:8] = side_y.low(ry_first[a], ry_second[a])
        x_ref[a + 1, 8:72] = r_ref[a].reshape(64, 128)
        x_ref[a + 1, 72:80] = side_y.high(ry_first[a], ry_second[a])
    solve_edges(
        x_ref, forward_ref, back_ref, inverse_ref, spectrum_ref, edge_ref, sy_first, sy_second,
        side_y, part_ref,
    )


def second_solve_kernel(
    counts, edge_ref, inner_ref, ry_first, ry_second, rx_first, rx_second, forward_ref, back_ref,
    inverse_ref, q_ref, spectrum_ref, layers_ref, sy_first, sy_second, x_ref, part_ref,
):
    side_x, side_y = Sides("gx", counts[0]), Sides("gy", counts[1])
    extend_image(
        edge_ref, inner_ref, ry_first, ry_second, rx_first, rx_second, side_x, side_y, q_ref, x_ref, None
    )
    solve_edges(
        x_ref, forward_ref, back_ref, inverse_ref, spectrum_ref, layers_ref, sy_first, sy_second,
        side_y, part_ref,
    )


def late_solve_kernel(
    counts, edge_ref, inner_ref, ry_first, ry_second, rx_first, rx_second, columns_ref, lift_ref,
    sum_ref, forward_ref, back_ref, inverse_ref, q_ref, spectrum_ref, layers_ref, sy_first,
    sy_second, field_ref, x_ref, part_ref, table_ref,
):
    side_x, side_y = Sides("gx", counts[0]), Sides("gy", counts[1])
    table_ref[...] = jnp.broadcast_to(
        jnp.sum(lift_ref[...] * sum_ref[0:1], axis=1, keepdims=True), table_ref.shape
    )
    fields = near_fields(counts, table_ref, side_x, side_y)
    own = fields[(1, 1)]
    field_ref[...] = jnp.concatenate(
        [own[i][j] for i in range(3) for j in range(3)] + [jnp.zeros((7, 128), jnp.float32)]
    )
    image = LiftedImage(fields, columns_ref)
    extend_image(
        edge_ref, inner_ref, ry_first, ry_second, rx_first, rx_second, side_x, side_y, q_ref, x_ref, image
    )
    solve_edges(
        x_ref, forward_ref, back_ref, inverse_ref, spectrum_ref, layers_ref, sy_first, sy_second,
        side_y, part_ref,
    )


def layer_of(edge_ref, inner_ref, a, b):
    if 2 <= b < NODES - 2:
        return inner_ref[a, b - 2]
    return edge_ref[a, b if b < 2 else b - (NODES - 4)]


def extend_image(
    edge_ref, inner_ref, ry_first, ry_second, rx_first, rx_second, side_x, side_y, q_ref, x_ref,
    image,
):
    low_x = side_x.low(rx_first[...], rx_second[...])
    high_x = side_x.high(rx_first[...], rx_second[...])

    def lifted(value, a, b):
        return value if image is None else value + image.at(a - 1, b - 1)

    for b in range(EXT):
        rows = pl.ds(b * 8, 8)
        x_ref[0, rows] = lifted(low_x[0, b], 0, b)
        x_ref[EXT - 1, rows] = lifted(high_x[1, b], EXT - 1, b)
    for a in range(NODES):
        low_y = side_y.low(ry_first[a], ry_second[a])
        high_y = side_y.high(ry_first[a], ry_second[a])
        rows = [low_y[0]]
        for b in range(NODES):
            value = layer_of(edge_ref, inner_ref, a, b)
            if b == 0:
                value = value + low_y[1]
            if b == NODES - 1:
                value = value + high_y[0]
            rows.append(value)
        rows.append(high_y[1])
        for b in range(EXT):
            value = rows[b]
            if a == 0:
                value = value + low_x[1, b]
            if a == NODES - 1:
                value = value + high_x[0, b]
            value = lifted(value, a + 1, b)
            x_ref[a + 1, b * 8 : b * 8 + 8] = value
            if 0 < b < EXT - 1:
                q_ref[a, b - 1] = value


def collect_parts(part_ref, ry_first, ry_second, rx_first, rx_second, side_x, side_y, field):
    low_x = side_x.low(rx_first[...], rx_second[...])
    high_x = side_x.high(rx_first[...], rx_second[...])
    result = {}
    for a in range(NODES):
        low_y = side_y.low(ry_first[a + 1], ry_second[a + 1])
        high_y = side_y.high(ry_first[a + 1], ry_second[a + 1])
        for b in range(NODES):
            value = part_ref[a + 1, b * 8 : (b + 1) * 8]
            if b < 2:
                value = value + low_y[b]
            if b >= NODES - 2:
                value = value + high_y[b - (NODES - 2)]
            if a < 2:
                value = value + low_x[a, b]
            if a >= NODES - 2:
                value = value + high_x[a - (NODES - 2), b]
            if field is not None:
                node_class = 3 * class_of(a) + class_of(b)
                value = value + field[node_class : node_class + 1, :]
            result[(a, b)] = value
    return result


def apply_tiles(z_ref, u_ref, y_ref, por, layers=range(NODES)):
    weight_tile = row_tile(WEIGHTS)
    stiff_tiles = [
        row_tile([STIFF[k, (k - shift) % NODES] for k in range(NODES)]) for shift in range(NODES)
    ]
    for a in range(NODES):
        for b in range(NODES):
            y_ref[a, b] = z_ref[a, b] * weight_tile
    half = NODES // 2

    def contract(line, wanted):
        even = [line[i] + line[NODES - 1 - i] for i in range(half)]
        odd = [line[i] - line[NODES - 1 - i] for i in range(half)]
        result = {}
        for node in range(half):
            if node in wanted:
                mirrored = STIFF[node, ::-1]
                both = combine(0.5 * (STIFF[node] + mirrored)[:half], even)
                apart = combine(0.5 * (STIFF[node] - mirrored)[:half], odd)
                result[node], result[NODES - 1 - node] = both + apart, both - apart
        return result

    for place, b in enumerate(layers):
        first = contract([y_ref[a, b] for a in range(NODES)], range(NODES))
        for a in range(NODES):
            u_ref[a, place] = first[a] * float(WEIGHTS[b])
    for a in range(NODES):
        second = contract([y_ref[a, b] for b in range(NODES)], layers)
        for place, b in enumerate(layers):
            z = z_ref[a, b]
            third = z * stiff_tiles[0]
            for shift in range(1, NODES):
                third = third + pltpu.roll(z, shift, 0) * stiff_tiles[shift]
            weight = float(WEIGHTS[a] * WEIGHTS[b])
            total = third * weight + u_ref[a, place] + second[b] * float(WEIGHTS[a])
            u_ref[a, place] = por * total + y_ref[a, b] * (shift_mass * weight)


def sum_column(u_ref):
    for a in range(NODES):
        bottom = u_ref[a, :, 0, :]
        top = u_ref[a, :, NODES - 1, :]
        u_ref[a, :, 0, :] = bottom + shift_up(top)
        u_ref[a, :, NODES - 1, :] = top + shift_down(bottom)


def first_apply_kernel(
    counts, part_ref, ry_first, ry_second, rx_first, rx_second, sum_ref, lift_ref, porosity_ref,
    r_ref, z_ref, u_ref, sy_first, sy_second, fx_first, fx_second, tile_ref, y_ref,
):
    side_x, side_y = Sides("gx", counts[0]), Sides("gy", counts[1])
    field = lifted_rows(counts, row_of(counts, sum_ref), lift_ref)
    z = collect_parts(part_ref, ry_first, ry_second, rx_first, rx_second, side_x, side_y, field)
    inner = None
    for (a, b), value in z.items():
        z_ref[a, b] = value
        term = scaled(value * r_ref[a, b], axis_factor(a, side_x), axis_factor(b, side_y))
        inner = term if inner is None else inner + term
    inner = inner * multiplicity_tile()
    apply_tiles(z_ref, u_ref, y_ref, porosity_ref[...])
    sums = {}
    curvature = None
    for a in range(NODES):
        for b in range(NODES):
            value = u_ref[a, b]
            add_to(sums, (class_of(a), class_of(b)), value)
            term = value * z_ref[a, b]
            curvature = term if curvature is None else curvature + term
    tiles = class_tiles(sums) + [inner, curvature]
    tile_ref[...] = summed_row(counts, tiles, side_x, side_y)
    sum_column(u_ref)
    send_layers(u_ref, side_x, side_y, sy_first, sy_second, fx_first, fx_second)


def second_apply_kernel(
    counts, part_ref, ry_first, ry_second, rx_first, rx_second, sum_ref, lift_ref, porosity_ref,
    r_ref, q_ref, z_ref, z1_ref, u_ref, sy_first, sy_second, fx_first, fx_second, stats_ref, y_ref,
):
    side_x, side_y = Sides("gx", counts[0]), Sides("gy", counts[1])
    summed = row_of(counts, sum_ref)
    field = lifted_rows(counts, summed, lift_ref)
    step = row_value(counts, summed, 0) / row_value(counts, summed, 1)
    w = collect_parts(part_ref, ry_first, ry_second, rx_first, rx_second, side_x, side_y, field)
    inner = None
    for (a, b), value in w.items():
        next_z = z_ref[a, b] - step * value
        next_r = r_ref[a, b] - step * q_ref[a, b]
        z1_ref[a, b] = next_z
        term = scaled(next_z * next_r, axis_factor(a, side_x), axis_factor(b, side_y))
        inner = term if inner is None else inner + term
    inner = inner * multiplicity_tile()
    apply_tiles(z1_ref, u_ref, y_ref, porosity_ref[...])
    own = None
    cross = None
    for a in range(NODES):
        for b in range(NODES):
            value = u_ref[a, b]
            own_term = value * z1_ref[a, b]
            cross_term = value * z_ref[a, b]
            own = own_term if own is None else own + own_term
            cross = cross_term if cross is None else cross + cross_term
    write_stats(stats_ref, [inner, own, cross])
    sum_column(u_ref)
    for a in range(NODES):
        low, high = u_ref[a, 0], u_ref[a, NODES - 1]
        sy_first[a] = side_y.send_first(low, high)
        sy_second[a] = side_y.send_second(low, high)
    low, high = u_ref[0], u_ref[NODES - 1]
    fx_first[...] = side_x.send_first(low, high)
    fx_second[...] = side_x.send_second(low, high)


def send_layers(u_ref, side_x, side_y, sy_first, sy_second, fx_first, fx_second):
    for a in range(NODES):
        for layer in range(2):
            low, high = u_ref[a, layer], u_ref[a, NODES - 2 + layer]
            sy_first[2 * a + layer] = side_y.send_first(low, high)
            sy_second[2 * a + layer] = side_y.send_second(low, high)
    for layer in range(2):
        low, high = u_ref[layer], u_ref[NODES - 2 + layer]
        fx_first[layer] = side_x.send_first(low, high)
        fx_second[layer] = side_x.send_second(low, high)


def early_apply_kernel(
    counts, part_ref, ry_first, ry_second, rx_first, rx_second, porosity_ref, sum_ref,
    z_ref, edge_ref, sy_first, sy_second, y_ref,
):
    side_x, side_y = Sides("gx", counts[0]), Sides("gy", counts[1])
    z = collect_parts(part_ref, ry_first, ry_second, rx_first, rx_second, side_x, side_y, None)
    for (a, b), value in z.items():
        z_ref[a, b] = value
    apply_tiles(z_ref, edge_ref, y_ref, porosity_ref[...], (0, 1, NODES - 2, NODES - 1))
    sum_column(edge_ref)
    for a in range(NODES):
        for layer in range(2):
            low, high = edge_ref[a, layer], edge_ref[a, 2 + layer]
            sy_first[2 * a + layer] = side_y.send_first(low, high)
            sy_second[2 * a + layer] = side_y.send_second(low, high)
    sy_first[2 * NODES] = sum_ref[...]


def rest_apply_kernel(
    counts, z_ref, edge_ref, porosity_ref, inner_ref, fx_first, fx_second, y_ref
):
    side_x = Sides("gx", counts[0])
    apply_tiles(z_ref, inner_ref, y_ref, porosity_ref[...], range(2, NODES - 2))
    sum_column(inner_ref)
    for layer in range(2):
        for b in range(NODES):
            low = layer_of(edge_ref, inner_ref, layer, b)
            high = layer_of(edge_ref, inner_ref, NODES - 2 + layer, b)
            fx_first[layer, b] = side_x.send_first(low, high)
            fx_second[layer, b] = side_x.send_second(low, high)


def first_sums_kernel(counts, r_ref, q_ref, schwarz_ref, field_ref, row_ref):
    side_x, side_y = Sides("gx", counts[0]), Sides("gy", counts[1])
    inner = curvature = None
    for a in range(NODES):
        for b in range(NODES):
            node_class = 3 * class_of(a) + class_of(b)
            z = schwarz_ref[a, b] + field_ref[node_class : node_class + 1, :]
            factors = (axis_factor(a, side_x), axis_factor(b, side_y))
            first, second = (scaled(z * ref[a, b], *factors) for ref in (r_ref, q_ref))
            inner = first if inner is None else inner + first
            curvature = second if curvature is None else curvature + second
    tile = multiplicity_tile()
    tiles = shared_class_tiles(q_ref, side_x, side_y) + [inner * tile, curvature * tile]
    row_ref[...] = summed_row(counts, tiles, side_x, side_y)


def late_apply_kernel(
    counts, part_ref, ry_first, ry_second, rx_first, rx_second, porosity_ref, low_ref, own_ref,
    high_ref, q_ref, first_ref, w_ref, u_ref, sy_first, sy_second, fx_first, fx_second, stats_ref,
    y_ref,
):
    side_x, side_y = Sides("gx", counts[0]), Sides("gy", counts[1])
    w = collect_parts(part_ref, ry_first, ry_second, rx_first, rx_second, side_x, side_y, None)
    inner = None
    for (a, b), value in w.items():
        w_ref[a, b] = value
        term = scaled(value * q_ref[a, b], axis_factor(a, side_x), axis_factor(b, side_y))
        inner = term if inner is None else inner + term
    inner = inner * multiplicity_tile()
    porosity = porosity_ref[...]
    apply_tiles(w_ref, u_ref, y_ref, porosity)
    sums = {}
    own = None
    for a in range(NODES):
        for b in range(NODES):
            value = u_ref[a, b]
            add_to(sums, (class_of(a), class_of(b)), value)
            term = value * w_ref[a, b]
            own = term if own is None else own + term
    total = counts[0] * counts[1]
    tiles = class_tiles(sums) + [inner, own, porosity]
    row = first_ref[0:1] + pltpu.roll(
        summed_row(counts, tiles, side_x, side_y), total + 2, 1
    )[0:1]
    for index in range(stats_ref.shape[0]):
        stats_ref[index] = jnp.broadcast_to(row, stats_ref.shape[1:])
    sum_column(u_ref)
    near = [[ref[y + 1 : y + 2] for y in range(3)] for ref in (low_ref, own_ref, high_ref)]
    send_corners(
        u_ref, w_ref, y_ref, near, side_x, side_y, sy_first, sy_second, fx_first, fx_second
    )


def sum_tile(tile):
    row = lax.broadcasted_iota(jnp.int32, (NODES, 128), 0)
    below = jnp.where(row == 0, pltpu.roll(shift_up(tile), 1, 0), 0.0)
    above = jnp.where(row == NODES - 1, pltpu.roll(shift_down(tile), NODES - 1, 0), 0.0)
    return tile + below + above


def send_corners(
    u_ref, w_ref, y_ref, near, side_x, side_y, sy_first, sy_second, fx_first, fx_second
):
    ends = (0, NODES - 1)

    def along_x(end, b):
        return combine(STIFF[end] * WEIGHTS[b], [y_ref[a, b] for a in range(NODES)])

    def along_y(end, a):
        return combine(STIFF[end] * WEIGHTS[a], [y_ref[a, b] for b in range(NODES)])

    for a in range(NODES):
        low, high = u_ref[a, 0], u_ref[a, NODES - 1]
        sy_first[a] = side_y.send_first(low, high)
        sy_second[a] = side_y.send_second(low, high)
        low, high = u_ref[0, a], u_ref[NODES - 1, a]
        fx_first[a] = side_x.send_first(low, high)
        fx_second[a] = side_x.send_second(low, high)
    for place, node in enumerate(ends):
        low, high = (sum_tile(near[2 * place][1] * along_y(end, node)) for end in ends)
        sy_first[NODES + place] = side_y.send_first(low, high)
        sy_second[NODES + place] = side_y.send_second(low, high)
        low, high = (sum_tile(near[1][2 * place] * along_x(end, node)) for end in ends)
        fx_first[NODES + place] = side_x.send_first(low, high)
        fx_second[NODES + place] = side_x.send_second(low, high)
    weight = float(WEIGHTS[0] * WEIGHTS[0])
    for i, a in enumerate(ends):
        for j, b in enumerate(ends):
            porosity = near[2 * i][2 * j]
            value = w_ref[a, b]
            third = None
            for shift in range(NODES):
                turned = value if shift == 0 else pltpu.roll(value, shift, 0)
                term = turned * row_tile([STIFF[k, (k - shift) % NODES] for k in range(NODES)])
                third = term if third is None else third + term
            mass = jnp.where(porosity > 0.0, shift_mass * y_ref[a, b], 0.0)
            u_ref[a, b] = u_ref[a, b] + weight * sum_tile(porosity * third + mass)


def prepare_late_kernel(counts, sol_ref, r_ref, schwarz_ref, field_ref, z_ref, sol_out, r_out):
    for a in range(NODES):
        for b in range(NODES):
            node_class = 3 * class_of(a) + class_of(b)
            z_ref[a, b] = schwarz_ref[a, b] + field_ref[node_class : node_class + 1, :]
            sol_out[a, b] = sol_ref[a, b]
            r_out[a, b] = r_ref[a, b]


def porosity_kernel(counts, low_ref, own_ref, high_ref, out_ref):
    row = lax.broadcasted_iota(jnp.int32, (NODES, 128), 0)
    weights = row_tile(WEIGHTS)
    mass = shift_mass * weights / multiplicity_tile()
    end = float(WEIGHTS[0])
    for x, ref in enumerate((low_ref, own_ref, high_ref)):
        for y in range(3):
            porosity = ref[y + 1 : y + 2]
            tile = porosity * weights
            tile = tile + jnp.where(row == 0, end * shift_up(porosity), 0.0)
            tile = tile + jnp.where(row == NODES - 1, end * shift_down(porosity), 0.0)
            out_ref[3 * x + y] = tile
            out_ref[9 + 3 * x + y] = jnp.where(porosity > 0.0, mass, 0.0)


CLASS_STIFF = np.stack(
    [STIFF[:, 0], STIFF[:, 1 : NODES - 1].sum(axis=1), STIFF[:, NODES - 1]], axis=1
)
CLASS_ENDS = np.stack(
    [CLASS_STIFF[0], CLASS_STIFF[1 : NODES - 1].sum(axis=0), CLASS_STIFF[NODES - 1]]
)
CLASS_WEIGHTS = np.array([WEIGHTS[0], WEIGHTS[1 : NODES - 1].sum(), WEIGHTS[NODES - 1]])


def combine(coefficients, values):
    total = None
    for coefficient, value in zip(coefficients, values):
        term = value * float(coefficient)
        total = term if total is None else total + term
    return total


def sharing(node):
    return {
        -1: [(0, NODES - 2)], 0: [(1, 0), (0, NODES - 1)],
        NODES - 1: [(1, NODES - 1), (2, 0)], NODES: [(2, 1)],
    }.get(node, [(1, node)])


class LiftedImage:
    def __init__(self, fields, columns_ref):
        self.fields, self.columns, self.known = fields, columns_ref, {}

    def along(self, column, place, other_class, axis):
        key = (column, place, other_class, axis)
        if key not in self.known:
            field = self.fields[column]
            line = [
                field[i][other_class] if axis == 0 else field[other_class][i] for i in range(3)
            ]
            self.known[key] = combine(CLASS_STIFF[place], line)
        return self.known[key]

    def at(self, a, b):
        total = None
        for i, place_a in sharing(a):
            for j, place_b in sharing(b):
                class_a, class_b = class_of(place_a), class_of(place_b)
                stiff = self.along((i, j), place_a, class_b, 0) * float(WEIGHTS[place_b])
                stiff = stiff + self.along((i, j), place_b, class_a, 1) * float(WEIGHTS[place_a])
                mass = self.fields[(i, j)][class_a][class_b]
                mass = mass * float(WEIGHTS[place_a] * WEIGHTS[place_b])
                term = stiff * self.columns[3 * i + j] + mass * self.columns[9 + 3 * i + j]
                total = term if total is None else total + term
        return total


def near_fields(counts, table_ref, side_x, side_y):
    total = counts[0] * counts[1]

    def field_of(step_x, step_y):
        x = jnp.clip(side_x.index + step_x, 0, counts[0] - 1)
        y = jnp.clip(side_y.index + step_y, 0, counts[1] - 1)
        place = x * counts[1] + y
        return [
            [table_ref[pl.ds((3 * i + j) * total + place, 1), :] for j in range(3)]
            for i in range(3)
        ]

    return {(i, j): field_of(i - 1, j - 1) for i in range(3) for j in range(3)}


def lifted_energy(counts, table_ref, porosity_sums, length):
    total = counts[0] * counts[1]
    field = [
        [table_ref[pl.ds((3 * i + j) * total, total), :] for j in range(3)] for i in range(3)
    ]

    def line(values):
        terms = []
        for i, j in ((0, 1), (0, 2), (1, 2)):
            difference = values[i] - values[j]
            terms.append(difference * difference * float(-CLASS_ENDS[i, j]))
        return terms[0] + terms[1] + terms[2]

    stiff = None
    mass = None
    for i in range(3):
        term = line(field[i]) * float(CLASS_WEIGHTS[i])
        term = term + line([field[j][i] for j in range(3)]) * float(CLASS_WEIGHTS[i])
        stiff = term if stiff is None else stiff + term
        for j in range(3):
            term = field[i][j] * field[i][j] * float(CLASS_WEIGHTS[i] * CLASS_WEIGHTS[j])
            mass = term if mass is None else mass + term
    energy = stiff * porosity_sums * 2.0 + mass * (shift_mass * 2.0 * length)
    return jnp.sum(energy, axis=0, keepdims=True)


def late_final_kernel(
    counts, sol_ref, r_ref, q_ref, z_ref, w_ref, u_ref, ry_first, ry_second, rx_first, rx_second,
    columns_ref, lift_ref, stats_ref, sol_out, r_out, d_out, steps_out, table_ref,
):
    side_x, side_y = Sides("gx", counts[0]), Sides("gy", counts[1])
    total = counts[0] * counts[1]
    stats = stats_ref[:, 0, :]
    summed = jnp.sum(stats, axis=0, keepdims=True)
    table_ref[...] = jnp.broadcast_to(
        jnp.sum(lift_ref[...] * summed, axis=1, keepdims=True), table_ref.shape
    )
    column = lax.broadcasted_iota(jnp.int32, (total, 128), 0)
    lane = lax.broadcasted_iota(jnp.int32, (total, 128), 1)
    at = 2 * total + 2
    porosity_sums = jnp.sum(
        jnp.where(lane == at + 2, stats, 0.0), axis=1, keepdims=True
    )
    coarse = table_ref[pl.ds(4 * total, total), :]

    def product(first):
        chosen = jnp.where(lane == column + first, coarse * summed, 0.0)
        return jnp.sum(jnp.sum(chosen, axis=0, keepdims=True), axis=1, keepdims=True)

    def value(index):
        return jnp.sum(jnp.where(lane[0:1] == index, summed, 0.0), axis=1, keepdims=True)

    first_inner, first_curvature = value(total), value(total + 1)
    cross = value(at) + product(0)
    energy = value(at + 1) + 2.0 * product(total + 2) + lifted_energy(
        counts, table_ref, porosity_sums, sol_ref.shape[-1]
    )
    first_step = first_inner / first_curvature
    second_inner = first_step * first_step * cross - first_inner
    ratio = second_inner / first_inner
    mixed = first_curvature - first_step * cross
    own = first_curvature - 2.0 * first_step * cross + first_step * first_step * energy
    second_step = second_inner / (own + ratio * (2.0 * mixed + ratio * first_curvature))
    first_step, second_step, ratio = (
        jnp.broadcast_to(scalar[:, 0:1], (1, 128)) for scalar in (first_step, second_step, ratio)
    )
    steps_out[0] = first_step[0, 0]
    steps_out[1] = second_step[0, 0]

    fields = near_fields(counts, table_ref, side_x, side_y)
    lifted_image = LiftedImage(fields, columns_ref)
    low_x = side_x.low(rx_first[...], rx_second[...])
    high_x = side_x.high(rx_first[...], rx_second[...])
    corner_y = {}
    for place in range(2):
        tiles = ry_first[NODES + place], ry_second[NODES + place]
        corner_y[(place > 0, False)] = side_y.low(*tiles)
        corner_y[(place > 0, True)] = side_y.high(*tiles)
    for a in range(NODES):
        for b in range(NODES):
            image = u_ref[a, b]
            if b == 0:
                image = image + side_y.low(ry_first[a], ry_second[a])
            if b == NODES - 1:
                image = image + side_y.high(ry_first[a], ry_second[a])
            if a == 0:
                image = image + low_x[b]
            if a == NODES - 1:
                image = image + high_x[b]
            if a in (0, NODES - 1) and b in (0, NODES - 1):
                from_x = low_x if a == 0 else high_x
                image = image + from_x[NODES + (b > 0)] + corner_y[(a > 0, b > 0)]
            lifted = fields[(1, 1)][class_of(a)][class_of(b)]
            image = image + lifted_image.at(a, b)
            z, q = z_ref[a, b], q_ref[a, b]
            direction = z - first_step * (w_ref[a, b] + lifted) + ratio * z
            image = q - first_step * image + ratio * q
            d_out[a, b] = direction
            sol_out[a, b] = sol_ref[a, b] + first_step * z + second_step * direction
            r_out[a, b] = r_ref[a, b] - first_step * q - second_step * image


def prepare_kernel(counts, sol_ref, r_ref, q_ref, z_ref, sum_ref, sol_out, r_out):
    summed = row_of(counts, sum_ref)
    step = row_value(counts, summed, 0) / row_value(counts, summed, 1)
    for a in range(NODES):
        for b in range(NODES):
            sol_out[a, b] = sol_ref[a, b] + step * z_ref[a, b]
            r_out[a, b] = r_ref[a, b] - step * q_ref[a, b]


def final_kernel(
    counts, sol_ref, r_ref, q_ref, z_ref, z1_ref, u_ref, ry_first, ry_second, rx_first, rx_second,
    sum_ref, last_ref, sol_out, r_out, d_out, steps_out,
):
    side_x, side_y = Sides("gx", counts[0]), Sides("gy", counts[1])
    summed = row_of(counts, sum_ref)
    first_inner, first_curvature = row_value(counts, summed, 0), row_value(counts, summed, 1)
    second_inner, own, cross = stat_columns(last_ref[:, 0, :], 0, 3)
    first_step = first_inner / first_curvature
    ratio = second_inner / first_inner
    second_step = second_inner / (own + ratio * (2.0 * cross + ratio * first_curvature))
    steps_out[0] = first_step[0, 0]
    steps_out[1] = second_step[0, 0]
    low_x = side_x.low(rx_first[...], rx_second[...])
    high_x = side_x.high(rx_first[...], rx_second[...])
    for a in range(NODES):
        for b in range(NODES):
            image = u_ref[a, b]
            if b == 0:
                image = image + side_y.low(ry_first[a], ry_second[a])
            if b == NODES - 1:
                image = image + side_y.high(ry_first[a], ry_second[a])
            if a == 0:
                image = image + low_x[b]
            if a == NODES - 1:
                image = image + high_x[b]
            z, q = z_ref[a, b], q_ref[a, b]
            direction = z1_ref[a, b] + ratio * z
            image = image + ratio * q
            d_out[a, b] = direction
            sol_out[a, b] = sol_ref[a, b] + second_step * direction
            r_out[a, b] = r_ref[a, b] - second_step * image


COSTS = {
    "start": 100, "first_solve": 900, "second_solve": 900, "rest_of_solve": 600,
    "first_apply": 500, "rest_of_apply": 400, "second_apply": 800, "prepare": 20000,
    "final": 500, "late_apply": 800, "first_sums": 300, "porosity": 20000, "late_final": 800,
}


def call(kernel, counts, name, shapes, scratch, *operands):
    def body(*refs):
        kernel(counts, *refs)

    def space(shape):
        return pltpu.SMEM if len(shape) == 1 else pltpu.VMEM

    return pl.pallas_call(
        body,
        name=name,
        out_shape=[jax.ShapeDtypeStruct(shape, jnp.float32) for shape in shapes],
        in_specs=[pl.BlockSpec(memory_space=pltpu.VMEM)] * len(operands),
        out_specs=[pl.BlockSpec(memory_space=space(shape)) for shape in shapes],
        scratch_shapes=[pltpu.VMEM(shape, jnp.float32) for shape in scratch],
        compiler_params=pltpu.CompilerParams(vmem_limit_bytes=24 * 1024 * 1024),
        cost_estimate=pl.CostEstimate(
            flops=COSTS[name] * 1000000, bytes_accessed=COSTS[name] * 3000, transcendentals=0
        ),
    )(*operands)


def swap_pairs(counts, axis, parity, ring):
    count_x, count_y = counts
    pairs = []
    for x in range(count_x):
        for y in range(count_y):
            if axis == 0:
                other = x + 1 if x % 2 == parity else x - 1
                to = (other % count_x, y) if ring or 0 <= other < count_x else (x, y ^ 1)
            else:
                other = y + 1 if y % 2 == parity else y - 1
                to = (x, other) if 0 <= other < count_y else (x ^ 1, y)
            pairs.append((x * count_y + y, to[0] * count_y + to[1]))
    return pairs


def trade(counts, axis, first, second, ring=False):
    return (
        lax.ppermute(first, AXES, swap_pairs(counts, axis, 0, ring)),
        lax.ppermute(second, AXES, swap_pairs(counts, axis, 1, ring)),
    )


def trade_far(counts, value, far_x, far_y):
    pairs = [
        (x * counts[1] + y, (x ^ far_x) * counts[1] + (y ^ far_y))
        for x in range(counts[0])
        for y in range(counts[1])
    ]
    return lax.ppermute(value, AXES, pairs)


class RunningSum:
    def __init__(self, counts, tile, carried):
        self.counts = counts
        self.carried = carried
        self.value = tile if self.carried else lax.psum(tile, AXES)

    def add(self, received):
        if self.carried:
            self.value = self.value + received

    def far(self, *steps):
        return [trade_far(self.counts, self.value, *step) for step in steps if self.carried]


def carry(tiles, running):
    return jnp.concatenate([tiles.reshape((-1, NODES, 128)), running.value[None]])


def carried(received, shape):
    return received[:-1].reshape(shape), received[-1]


def gather_stats(stats):
    return lax.all_to_all(stats, AXES, 0, 0)


def lift_tables(counts, column_length):
    share_x, share_y = share_table(counts[0]), share_table(counts[1])
    basis_x, eigen_x = cosine_inverse(counts[0])
    basis_y, eigen_y = cosine_inverse(counts[1])
    divisor = (
        2.0 * mean_porosity * column_length * (eigen_x[:, None] + eigen_y[None, :])
        + 8.0 * shift_mass * column_length
    )
    modes_x = np.einsum("xip,pa->xia", share_x, basis_x)
    modes_y = np.einsum("yjq,qb->yjb", share_y, basis_y)
    total = counts[0] * counts[1]
    to_modes = np.einsum("pa,qb->abpq", basis_x, basis_y).reshape(total, total)
    to_modes = np.pad(to_modes, ((0, 0), (0, sum_lanes(counts) - total)))
    return [table.astype(np.float32) for table in (modes_x, modes_y, 1.0 / divisor, to_modes)]


def all_lift(counts, column_length):
    modes_x, modes_y, inverse, to_modes = lift_tables(counts, column_length)
    total = counts[0] * counts[1]
    lift = np.einsum(
        "xia,yjb,ab,abl->ijxyl", *(
            table.astype(np.float64)
            for table in (modes_x, modes_y, inverse, to_modes.reshape(inverse.shape + (-1,)))
        ),
    )
    return jnp.asarray(lift.reshape(9 * total, -1).astype(np.float32))


def own_lift(tables):
    modes_x, modes_y, inverse, to_modes = [jnp.asarray(table) for table in tables]
    own_x = lax.dynamic_index_in_dim(modes_x, lax.axis_index("gx"), 0, keepdims=False)
    own_y = lax.dynamic_index_in_dim(modes_y, lax.axis_index("gy"), 0, keepdims=False)
    own = own_x[:, None, :, None] * own_y[None, :, None, :] * inverse[None, None]
    lift = jnp.dot(own.reshape(9, -1), to_modes, precision=exact_mode)
    return jnp.pad(lift, ((0, 7), (0, 0)))


def shards_of(counts):
    forward_np, back_edge_np, back_inner_np, inverse_np = plane_tables()

    def shards(solution, residual, grain_counts):
        shard_shape = solution.shape
        block = shard_shape[2:]
        solution = solution.reshape(block)
        residual = residual.reshape(block)
        lift = own_lift(lift_tables(counts, block[-1]))
        late = counts == (8, 4)
        every_lift = all_lift(counts, block[-1]) if late else None
        porosity = 1.0 - 0.6 * grain_counts.reshape(1, 128).astype(jnp.float32) / MOST_GRAINS
        plane = [jnp.asarray(table) for table in (forward_np, back_edge_np, inverse_np)]
        back_inner = jnp.asarray(back_inner_np)
        side_x, side_y = Sides("gx", counts[0]), Sides("gy", counts[1])
        row = (counts[0] * counts[1], 4, 128)
        face = (NODES, NODES, 128)
        sends = [(2 * EXT, NODES, 128)] * 2
        solve_shapes = [(MODES, EXT * 128), (EXT, 2 * NODES, 128)]
        solve_scratch = [(EXT, ROWS, 128), (EXT, len(back_edge_np), 128)]

        def rest_of_solve(spectrum, edges):
            return call(
                rest_kernel, counts, "rest_of_solve",
                [(EXT, NODES * NODES, 128)] + [(2, NODES, NODES, 128)] * 2,
                [(EXT, len(back_inner_np), 128)], spectrum, edges, back_inner,
            )

        y_first, y_second = call(
            start_kernel, counts, "start", [(NODES + 1,) + face[1:], face], [], residual
        )
        running = RunningSum(counts, y_first[-1], late)
        ry = trade(counts, 1, y_first, y_second)
        ry_first, tile = carried(ry[0], face)
        running.add(tile)
        ry = (ry_first, ry[1])
        low_y, high_y = side_y.low(*ry), side_y.high(*ry)

        def with_layers(index):
            return jnp.concatenate([low_y[index][None], residual[index], high_y[index][None]])

        low_face, high_face = with_layers(1), with_layers(NODES - 2)
        rx = trade(
            counts, 0, carry(side_x.send_first(low_face, high_face), running),
            side_x.send_second(low_face, high_face),
        )
        rx_first, tile = carried(rx[0], low_face.shape)
        running.add(tile)
        rx = (rx_first, rx[1])
        spectrum, edges, y_first, y_second = call(
            first_solve_kernel, counts, "first_solve",
            solve_shapes + [(2 * EXT + 1, NODES, 128)] * 2, solve_scratch,
            residual, porosity, running.value, *ry, *rx, *plane,
        )
        part, *fx = rest_of_solve(spectrum, edges)

        def spread_faces(fx, ry):
            low_y, high_y = side_y.low(*ry), side_y.high(*ry)
            middle = jnp.zeros((2, NODES - 4, NODES, 128), jnp.float32)
            both = [
                jnp.concatenate([low_y[at], middle, high_y[at]], axis=1)
                for at in (slice(0, 2), slice(8, 10))
            ]
            return (
                fx[0] + side_x.send_first(*both),
                fx[1] + side_x.send_second(*both),
            )

        def trade_y(y_first, y_second, shape):
            count = math.prod(shape[:-2])
            ry = trade(counts, 1, y_first, y_second)
            faces = [value[:count].reshape(shape) for value in ry]
            return faces, [value[count:] for value in ry]

        ext_face = (EXT, 2, NODES, 128)
        two = (NODES, 2, NODES, 128)
        tiles = (-1, NODES, 128)
        ry, rows = trade_y(y_first, y_second, ext_face)
        rows = [value[0] for value in rows]
        inner_y = (side_y.index > 0) & (side_y.index < counts[1] - 1)
        three = jnp.concatenate(
            [
                running.value[0:1] + jnp.where(inner_y, rows[1][0:1], 0.0),
                side_y.low(*rows)[1:2], porosity, side_y.high(*rows)[1:2],
                jnp.zeros((NODES - 4, 128), jnp.float32),
            ]
        )
        first, second = (
            jnp.concatenate([faces.reshape(tiles), three[None]]) for faces in spread_faces(fx, ry)
        )
        rx = trade(counts, 0, first, second, ring=True)
        count = 2 * NODES
        threes = [value[count] for value in rx]
        rx = [value[:count].reshape((2, NODES, NODES, 128)) for value in rx]
        if late:
            running.value = three + threes[1]
        if late:
            half = (NODES, NODES // 2, NODES, 128)
            z, u_edge, y_first, y_second = call(
                early_apply_kernel, counts, "first_apply",
                [block, half, (2 * NODES + 1, NODES, 128), (2 * NODES, NODES, 128)], [block],
                part, *ry, *rx, porosity, running.value,
            )
            u_inner, *fx = call(
                rest_apply_kernel, counts, "rest_of_apply",
                [half, (2, NODES, NODES, 128), (2, NODES, NODES, 128)], [block],
                z, u_edge, porosity,
            )
        else:
            z, u, y_first, y_second, *fx, tile = call(
                first_apply_kernel, counts, "first_apply",
                [block, block, (2 * NODES, NODES, 128), (2 * NODES, NODES, 128),
                 (2, NODES, NODES, 128), (2, NODES, NODES, 128), (NODES, 128)],
                [block],
                part, *ry, *rx, running.value, lift, porosity, residual,
            )
            u_edge = jnp.concatenate([u[:, :2], u[:, -2:]], axis=1)
            u_inner = u[:, 2:-2]
        ry, rows = trade_y(y_first, y_second, two)
        if late:
            running.value = jnp.where(inner_y, running.value, rows[0][0])
        low_y, high_y = side_y.low(*ry), side_y.high(*ry)

        def image_faces(index):
            middle = jnp.zeros((2, NODES - 2, NODES, 128), jnp.float32)
            return jnp.concatenate([low_y[index], middle, high_y[index]], axis=1)

        pads = ((0, 0), (1, 1), (0, 0), (0, 0))
        both = (image_faces(slice(0, 2)), image_faces(slice(NODES - 2, NODES)))
        rx = trade(
            counts, 0,
            jnp.pad(fx[0], pads) + side_x.send_first(*both),
            jnp.pad(fx[1], pads) + side_x.send_second(*both),
        )
        if late:
            near = (side_x.low(*threes), three, side_x.high(*threes))
            (columns,) = call(porosity_kernel, counts, "porosity", [(18, NODES, 128)], [], *near)
            rx, far, columns = lax.optimization_barrier((rx, running.far((4, 0)), columns))
            for value in far:
                running.add(value)
            table = (9 * counts[0] * counts[1], 128)
            q, spectrum, edges, y_first, y_second, field = call(
                late_solve_kernel, counts, "second_solve",
                [block] + solve_shapes + sends + [(16, 128)], solve_scratch + [table],
                u_edge, u_inner, *ry, *rx, columns, every_lift, running.value, *plane,
            )
        else:
            q, spectrum, edges, y_first, y_second = call(
                second_solve_kernel, counts, "second_solve", [block] + solve_shapes + sends,
                solve_scratch, u_edge, u_inner, *ry, *rx, *plane,
            )
        part, *fx = rest_of_solve(spectrum, edges)
        ry, _ = trade_y(y_first, y_second, ext_face)
        if late:
            (first_row,) = call(
                first_sums_kernel, counts, "first_sums", [(NODES, 128)], [],
                residual, q, z, field,
            )
            ry, first_row = lax.optimization_barrier((ry, first_row))
        rx = trade(counts, 0, *spread_faces(fx, ry))

        def trade_edges(y_first, y_second, fx, beside):
            ry, beside = lax.optimization_barrier((trade(counts, 1, y_first, y_second), beside))
            low_y, high_y = side_y.low(*ry), side_y.high(*ry)

            def edge_rows(index):
                middle = jnp.zeros((NODES - 2, NODES, 128), jnp.float32)
                return jnp.concatenate([low_y[index][None], middle, high_y[index][None]])

            both = (edge_rows(0), edge_rows(NODES - 1))
            rx = trade(
                counts, 0, fx[0] + side_x.send_first(*both), fx[1] + side_x.send_second(*both)
            )
            return ry, rx, beside

        if late:
            w, u, y_first, y_second, *fx, stats = call(
                late_apply_kernel, counts, "late_apply",
                [block, block] + [(NODES + 2, NODES, 128)] * 4 + [row], [block],
                part, *ry, *rx, porosity, *near, q, first_row,
            )
            z, w = lax.optimization_barrier((z, w))
            nexts = call(
                prepare_late_kernel, counts, "prepare", [block] * 3, [],
                solution, residual, z, field,
            )
            ry, rx, (z, solution, residual) = lax.optimization_barrier(
                (trade(counts, 1, y_first, y_second), trade(counts, 0, *fx), nexts)
            )
            solution_out, residual_out, direction, steps = call(
                late_final_kernel, counts, "late_final", [block] * 3 + [(2,)], [table],
                solution, residual, q, z, w, u, *ry, *rx, columns, every_lift,
                gather_stats(stats),
            )
        else:
            summed = lax.psum(tile, AXES)
            z1, u, y_first, y_second, *fx, stats = call(
                second_apply_kernel, counts, "second_apply",
                [block, block, face, face, face, face, row], [block],
                part, *ry, *rx, summed, lift, porosity, residual, q, z,
            )
            nexts = call(
                prepare_kernel, counts, "prepare", [block] * 2, [],
                solution, residual, q, z, summed,
            )
            ry, rx, nexts = trade_edges(y_first, y_second, fx, nexts)
            solution_out, residual_out, direction, steps = call(
                final_kernel, counts, "final", [block] * 3 + [(2,)], [],
                *nexts, q, z, z1, u, *ry, *rx, summed, gather_stats(stats),
            )
        return (
            solution_out.reshape(shard_shape),
            residual_out.reshape(shard_shape),
            direction.reshape(shard_shape),
            steps,
        )

    return shards


def solution(mesh):
    counts = (mesh.shape["gx"], mesh.shape["gy"])
    return jax.shard_map(
        shards_of(counts),
        mesh=mesh,
        in_specs=(
            P("gx", "gy", None, None, None, None),
            P("gx", "gy", None, None, None, None),
            P("gx", "gy", None),
        ),
        out_specs=(
            P("gx", "gy", None, None, None, None),
            P("gx", "gy", None, None, None, None),
            P("gx", "gy", None, None, None, None),
            P(),
        ),
        check_vma=False,
    )
```
